32 devices in a mesh: req: 8 (over z, y), tp: 4 (over x, core).
Axes of the slice: x: 2, y: 2, z: 4, core: 2. Of those that a mesh axis runs over, the one named last changes fastest.
Arguments:
- queries: bfloat16 [8192, 2560], P('req', 'tp'), may hold values from -51 to 51
- fresh_keys: bfloat16 [8192, 2560], P('req', 'tp'), may hold values from -5 to 5
- fresh_values: bfloat16 [8192, 2560], P('req', 'tp'), may hold values from -24 to 24
- paged_keys: bfloat16 [128, 128, 2560], P('req', None, 'tp'), may hold values from -6 to 6
- paged_values: bfloat16 [128, 128, 2560], P('req', None, 'tp'), may hold values from -24 to 24
- request_page_table: int32 [64, 8], P('req'), may hold values from 0 to 15, as said below
- live_token_count: int32 [64], P('req'), may hold values from 2 to 128, as said below
- request_adapter_slot: int32 [64], P('req'), may hold values from 0 to 3
- adapters_in_use: int32 [4], replicated, may hold values from 0 to 7, as said below
- adapter_pool_row: int32 [8], replicated, may hold values from 0 to 7, each once
- adapter_down_factors: bfloat16 [8, 16, 2560], P('req', None, 'tp'), may hold values from -0.125 to 0.125
- adapter_up_factors: bfloat16 [8, 16, 2560], P('req'), may hold values from -1.5 to 1.5
- output_weight: bfloat16 [2560, 2560], P('tp'), may hold values from -0.125 to 0.125
- gating: float32 [64, 2560], P('req'), may hold values from 1 to 4
Outputs:
- gated: bfloat16 [8192, 2560], P(('req', 'tp'))
The draws below stay inside these ranges and needn't reach their ends.
Inputs may be any that keep to these rules, and one draw needn't show every extreme that they name: `request_page_table`: A request's 8 pages are distinct. `live_token_count`: some request has all 128 slots live. `adapters_in_use`: 4 distinct adapter ids.
All inputs are finite; a program needn't handle non-finite values.
Results may differ from the reference program's by a relative error of at most 0.0057.
Values may be sent and summed in bfloat16 or wider, within the bound.
No kernel may reach another device: no remote copies, remote signals or barrier semaphores. Data moves between devices by JAX's collectives and lax.ppermute only.
A program may use at most 192 MiB of HBM per device.

```python
import math
import jax
import jax.numpy as jnp
import numpy as np
from jax import lax

HEADS = 20
HD = 128
OUTPUT_FEATURES = 2560
ADAPTER_RANK = 16
PAGE = 128
TOKENS_REQUEST = 128
PAGES_REQ = 8
REQ_DEV = 8
HEAD_FEATURES = 2560
REQUEST_TOTAL = 64
TOKENS = 8192
POOL_DEV = 16
POOL_PAGES = 128
ADAPTER_TOTAL = 8
ACTIVE = 4


def paired_draw(key):
    base = jax.random.fold_in(key, 17)
    key_vals = jnp.clip(jax.random.normal(jax.random.fold_in(base, 1), (TOKENS, HEAD_FEATURES), jnp.float32), -5.0, 5.0)
    query_vals = jnp.clip(jax.random.normal(jax.random.fold_in(base, 2), (TOKENS, HEAD_FEATURES), jnp.float32), -5.0, 5.0)
    return (query_vals, key_vals)


def draw_queries(key, part):
    return paired_draw(key)[0].astype(jnp.bfloat16)


def draw_fresh_keys(key, part):
    return paired_draw(key)[1].astype(jnp.bfloat16)


def draw_request_page_table(key, part):
    request_keys = jax.random.split(jax.random.fold_in(key, 4), REQUEST_TOTAL)
    chosen = jax.vmap(lambda one_key: jax.random.permutation(one_key, POOL_DEV)[:PAGES_REQ])(request_keys)
    return chosen.astype(jnp.int32)


def draw_live_token_count(key, part):
    counts = jax.random.randint(jax.random.fold_in(key, 1), (REQUEST_TOTAL,), 2, TOKENS_REQUEST + 1)
    fullest = jax.random.randint(jax.random.fold_in(key, 2), (), 0, REQUEST_TOTAL)
    return jnp.where(jnp.arange(REQUEST_TOTAL) == fullest, TOKENS_REQUEST, counts).astype(jnp.int32)


def draw_adapters_in_use(key, part):
    middle = jax.random.permutation(jax.random.fold_in(key, 3), ADAPTER_TOTAL - 2)[:ACTIVE - 2].astype(jnp.int32) + 1
    ends = jnp.array([0, ADAPTER_TOTAL - 1], dtype=jnp.int32)
    listed = jnp.concatenate([ends, middle], axis=0)
    order = jax.random.permutation(jax.random.fold_in(key, 5), ACTIVE)
    return listed[order].astype(jnp.int32)


def plant(drawn, rng, smallest, top_value):
    spot = [jax.random.randint(jax.random.fold_in(rng, axis), (), 0, length) for axis, length in enumerate(drawn.shape)]
    longest = drawn.shape.index(max(drawn.shape))
    neighbour = spot[:longest] + [(spot[longest] + 1) % drawn.shape[longest]] + spot[longest + 1:]
    return drawn.at[tuple(spot)].set(smallest).at[tuple(neighbour)].set(top_value)


def shard_levels(own_key, extent, cuts, least, top_value):
    gain = 1.0
    for axis_at, shards_of in cuts:
        draws = jax.random.uniform(jax.random.fold_in(jax.random.fold_in(own_key, 6), axis_at), (shards_of,), jnp.float32, least / len(cuts), top_value / len(cuts))
        gain = gain * jnp.repeat(jnp.exp(draws), extent[axis_at] // shards_of).reshape((-1,) + (1,) * (len(extent) - 1 - axis_at))
    return gain


def rank_bounds(number_of, slope):
    weights = [(1 << 20) // math.isqrt(grade ** slope) + 1 for grade in range(1, number_of + 1)]
    spread = 1 + sum(weights) // (1 << 30)
    return np.cumsum(np.array([max(1, weight // spread) for weight in weights]))


def ranked_ids(key, shape, amount, skew):
    listing = rank_bounds(amount, skew)
    lot = jax.random.randint(jax.random.fold_in(key, 1), shape, 0, int(listing[amount - 1]))
    standing = jnp.searchsorted(jnp.asarray(listing, jnp.int32), lot, side="right")
    return jax.random.permutation(jax.random.fold_in(key, 2), amount)[standing].astype(jnp.int32)


def bell_draw(stream_key, shape, width, most, cuts=(), kind=jnp.bfloat16):
    factor_of = shard_levels(stream_key, shape, cuts, -0.22, 0.18) if cuts else 1.0
    result = jax.random.normal(stream_key, shape, jnp.float32) * width * factor_of
    return jnp.minimum(jnp.maximum(result, -most), most).astype(kind)


def setup_inputs(seed: int = 0) -> dict:
    arg_keys = jax.random.split(jax.random.key(seed), 15)
    queries = draw_queries(jax.random.fold_in(arg_keys[14], 71), 0)
    fresh_keys = draw_fresh_keys(jax.random.fold_in(arg_keys[14], 71), 0)
    fresh_values = bell_draw(arg_keys[2], (TOKENS, HEAD_FEATURES), 4.0, 24.0, ((0, 8), (1, 4)))
    paged_keys = bell_draw(arg_keys[3], (POOL_PAGES, PAGE, HEAD_FEATURES), 1.0, 6.0, ((0, 8), (2, 4)))
    paged_values = bell_draw(arg_keys[4], (POOL_PAGES, PAGE, HEAD_FEATURES), 4.0, 24.0, ((0, 8), (2, 4)))
    request_page_table = draw_request_page_table(jax.random.fold_in(arg_keys[14], 71), 0)
    live_token_count = draw_live_token_count(jax.random.fold_in(arg_keys[14], 71), 0)
    request_adapter_slot = plant(ranked_ids(arg_keys[7], (REQUEST_TOTAL,), ACTIVE, 2), jax.random.fold_in(arg_keys[7], 3), 0, ACTIVE - 1).astype(jnp.int32)
    adapters_in_use = draw_adapters_in_use(jax.random.fold_in(arg_keys[14], 71), 0)
    adapter_pool_row = jax.random.permutation(arg_keys[9], ADAPTER_TOTAL).astype(jnp.int32)
    adapter_down_factors = bell_draw(arg_keys[10], (ADAPTER_TOTAL, ADAPTER_RANK, HEAD_FEATURES), HEAD_FEATURES ** -0.5, 0.125, ((0, 8), (2, 4)))
    adapter_up_factors = bell_draw(arg_keys[11], (ADAPTER_TOTAL, ADAPTER_RANK, OUTPUT_FEATURES), ADAPTER_RANK ** -0.5, 1.5, ((0, 8),))
    output_weight = bell_draw(arg_keys[12], (HEAD_FEATURES, OUTPUT_FEATURES), HEAD_FEATURES ** -0.5, 0.125, ((0, 4),))
    gating = jnp.clip(jnp.exp(math.log(4.0) - 1.3862944 * jax.random.uniform(arg_keys[13], (REQUEST_TOTAL, OUTPUT_FEATURES), jnp.float32) ** shard_levels(arg_keys[13], (REQUEST_TOTAL, OUTPUT_FEATURES), ((0, 8),), -0.2, 0.2)), 1.0, 4.0)
    return dict(queries=queries, fresh_keys=fresh_keys, fresh_values=fresh_values, paged_keys=paged_keys, paged_values=paged_values, request_page_table=request_page_table, live_token_count=live_token_count, request_adapter_slot=request_adapter_slot, adapters_in_use=adapters_in_use, adapter_pool_row=adapter_pool_row, adapter_down_factors=adapter_down_factors, adapter_up_factors=adapter_up_factors, output_weight=output_weight, gating=gating)


def reference(queries, fresh_keys, fresh_values, paged_keys, paged_values, request_page_table, live_token_count, request_adapter_slot, adapters_in_use, adapter_pool_row, adapter_down_factors, adapter_up_factors, output_weight, gating):
    request_ids = jnp.arange(REQUEST_TOTAL, dtype=jnp.int32)
    page_rows = (request_ids // REQ_DEV * POOL_DEV)[:, None] + request_page_table.astype(jnp.int32)
    cached = PAGES_REQ * PAGE

    def attend_request(pieces):
        query, own_keys, own_values, page_index, token_count = pieces
        cached_keys = paged_keys[page_index].reshape(cached, HEAD_FEATURES)
        cached_values = paged_values[page_index].reshape(cached, HEAD_FEATURES)
        keys_all = jnp.concatenate([cached_keys, own_keys], axis=0).astype(jnp.float32).reshape(-1, HEADS, HD)
        values_all = jnp.concatenate([cached_values, own_values], axis=0).astype(jnp.float32).reshape(-1, HEADS, HD)
        query_heads = query.astype(jnp.float32).reshape(TOKENS_REQUEST, HEADS, HD)
        scores = jnp.einsum('qhd,khd->hqk', query_heads, keys_all, precision=lax.Precision.HIGHEST) * (1.0 / math.sqrt(HD))
        key_index = jnp.arange(cached + TOKENS_REQUEST, dtype=jnp.int32)
        usable = (key_index < cached) | (key_index - cached < token_count)
        scores = jnp.where(usable[None, None, :], scores, -1e+30)
        row_peak = lax.optimization_barrier(jnp.max(scores, axis=-1, keepdims=True))
        weights = jnp.exp(scores - row_peak)
        row_total = lax.optimization_barrier(jnp.sum(weights, axis=-1))
        rounded = weights.astype(jnp.bfloat16)
        blended = jnp.einsum('hqk,khd->qhd', rounded.astype(jnp.float32), values_all, precision=lax.Precision.HIGHEST)
        blended = blended / jnp.transpose(row_total)[:, :, None]
        live_slots = jnp.arange(TOKENS_REQUEST, dtype=jnp.int32) < token_count
        blended = jnp.where(live_slots[:, None, None], blended, 0.0)
        return blended.reshape(TOKENS_REQUEST, HEAD_FEATURES).astype(jnp.bfloat16)
    attention_output = lax.map(attend_request, (queries.reshape(REQUEST_TOTAL, TOKENS_REQUEST, HEAD_FEATURES), fresh_keys.reshape(REQUEST_TOTAL, TOKENS_REQUEST, HEAD_FEATURES), fresh_values.reshape(REQUEST_TOTAL, TOKENS_REQUEST, HEAD_FEATURES), page_rows, live_token_count.astype(jnp.int32)))
    adapter_rows = adapter_pool_row[adapters_in_use[request_adapter_slot]]
    down_factor_rows = adapter_down_factors[adapter_rows].astype(jnp.float32)
    up_factor_rows = adapter_up_factors[adapter_rows].astype(jnp.float32)
    rank_activations = jnp.einsum('rsh,rkh->rsk', attention_output.astype(jnp.float32), down_factor_rows, precision=lax.Precision.HIGHEST)
    adapter_term = jnp.einsum('zuh,zhd->zud', rank_activations, up_factor_rows, precision=lax.Precision.HIGHEST)
    projected_output = jnp.dot(attention_output.reshape(TOKENS, HEAD_FEATURES).astype(jnp.float32), output_weight.astype(jnp.float32), precision=lax.Precision.HIGHEST)
    adapter_update = projected_output.reshape(REQUEST_TOTAL, TOKENS_REQUEST, OUTPUT_FEATURES) + adapter_term
    gated = (gating[:, None, :] * adapter_update).astype(jnp.bfloat16)
    return gated.reshape(TOKENS, OUTPUT_FEATURES)
```

```python
import math

import jax
import jax.numpy as jnp
from jax import lax
from jax.experimental import pallas as pl
from jax.experimental.pallas import tpu as pltpu
from jax.sharding import PartitionSpec as P

HD = 128
VMEM_LIMIT = 48 * 1024 * 1024
CHUNKS = 2
MASKED = -1e30
ANY = pl.BlockSpec(memory_space=pl.ANY)


def attend_owner(
    queries,
    fresh_keys,
    fresh_values,
    paged_keys,
    paged_values,
    request_page_table,
    live_token_count,
    first_request,
    request_count,
    after=None,
):
    requests_here, pages = request_page_table.shape
    slots = queries.shape[0] // requests_here
    width = queries.shape[1]
    heads = width // HD
    page_rows = paged_keys.shape[1]
    cached = pages * page_rows
    key_rows = cached + slots
    exponent_scale = math.log2(math.e) / math.sqrt(HD)

    def kernel(table, live, first, q_hbm, fk_hbm, fv_hbm, pk_hbm, pv_hbm, *rest):
        out, q_buf, k_buf, v_buf, sems = rest[-5:]

        def copies(i):
            request = first[0] + i
            rows = pl.ds(pl.multiple_of(request * slots, slots), slots)
            keys = [
                (pk_hbm.at[table[request, j]], k_buf.at[i, pl.ds(j * page_rows, page_rows)])
                for j in range(pages)
            ]
            values = [
                (pv_hbm.at[table[request, j]], v_buf.at[i, pl.ds(j * page_rows, page_rows)])
                for j in range(pages)
            ]
            keys.append((fk_hbm.at[rows], k_buf.at[i, pl.ds(cached, slots)]))
            values.append((fv_hbm.at[rows], v_buf.at[i, pl.ds(cached, slots)]))
            pairs = [(q_hbm.at[rows], q_buf.at[i])] + keys + values
            made = [
                pltpu.make_async_copy(src, dst, sems.at[i, n]) for n, (src, dst) in enumerate(pairs)
            ]
            return made[: 2 + pages], made[2 + pages :]

        for i in range(request_count):
            for group in copies(i):
                for copy in group:
                    copy.start()

        ones = jnp.ones((key_rows, HD), jnp.bfloat16)
        for i in range(request_count):
            live_here = live[first[0] + i]
            usable = lax.broadcasted_iota(jnp.int32, (slots, slots), 1) < live_here
            live_rows = lax.broadcasted_iota(jnp.int32, (slots, HD), 0) < live_here
            key_copies, value_copies = copies(i)
            for copy in key_copies:
                copy.wait()
            for h in range(heads):
                lanes = slice(h * HD, (h + 1) * HD)
                scores = lax.dot_general(
                    q_buf[i, :, lanes],
                    k_buf[i, :, lanes],
                    (((1,), (1,)), ((), ())),
                    preferred_element_type=jnp.float32,
                )
                scores = jnp.concatenate(
                    [scores[:, :cached], jnp.where(usable, scores[:, cached:], MASKED)], axis=1
                )
                peak = jnp.max(scores, axis=1, keepdims=True)
                weights = jnp.exp2((scores - peak) * exponent_scale).astype(jnp.bfloat16)
                if h == 0:
                    for copy in value_copies:
                        copy.wait()
                blended = jnp.dot(
                    weights,
                    jnp.concatenate([v_buf[i, :, lanes], ones], axis=1),
                    preferred_element_type=jnp.float32,
                )
                attended = jnp.where(live_rows, blended[:, :HD] / blended[:, HD:], 0.0)
                out[i * slots : (i + 1) * slots, lanes] = attended.astype(jnp.bfloat16)

    extra = () if after is None else (after,)
    pairs_here = request_count * heads
    return pl.pallas_call(
        kernel,
        grid_spec=pltpu.PrefetchScalarGridSpec(
            num_scalar_prefetch=3,
            grid=(1,),
            in_specs=[ANY] * (5 + len(extra)),
            out_specs=pl.BlockSpec((request_count * slots, width), lambda i, *_: (0, 0)),
            scratch_shapes=[
                pltpu.VMEM((request_count, slots, width), jnp.bfloat16),
                pltpu.VMEM((request_count, key_rows, width), jnp.bfloat16),
                pltpu.VMEM((request_count, key_rows, width), jnp.bfloat16),
                pltpu.SemaphoreType.DMA((request_count, 2 * pages + 3)),
            ],
        ),
        out_shape=jax.ShapeDtypeStruct((request_count * slots, width), jnp.bfloat16),
        compiler_params=pltpu.CompilerParams(vmem_limit_bytes=VMEM_LIMIT),
        cost_estimate=pl.CostEstimate(
            flops=pairs_here * 8 * slots * key_rows * HD,
            bytes_accessed=4 * request_count * (key_rows + slots) * width,
            transcendentals=pairs_here * slots * key_rows,
        ),
        name="attend",
    )(
        request_page_table,
        live_token_count,
        first_request,
        queries,
        fresh_keys,
        fresh_values,
        paged_keys,
        paged_values,
        *extra,
    )


def project_cross(own, other, weight, weight_other, gating, first_request, part, parts):
    rows, width = own.shape
    columns = weight.shape[1] // parts
    block = 640 if columns % 640 == 0 else columns
    steps = columns // block
    slots = rows // 2

    def kernel(first, a, b, w, u, gate, out):
        total = jnp.dot(a[...], w[...], preferred_element_type=jnp.float32)
        total += jnp.dot(b[...], u[...], preferred_element_type=jnp.float32)
        for i in range(2):
            part_rows = slice(i * slots, (i + 1) * slots)
            out[part_rows] = (total[part_rows] * gate[pl.ds(first[0] + i, 1), :]).astype(out.dtype)

    return pl.pallas_call(
        kernel,
        grid_spec=pltpu.PrefetchScalarGridSpec(
            num_scalar_prefetch=1,
            grid=(steps,),
            in_specs=[
                pl.BlockSpec((rows, width), lambda j, *_: (0, 0)),
                pl.BlockSpec((rows, width), lambda j, *_: (0, 0)),
                pl.BlockSpec((width, block), lambda j, *_: (0, part * steps + j)),
                pl.BlockSpec((width, block), lambda j, *_: (0, part * steps + j)),
                pl.BlockSpec((gating.shape[0], block), lambda j, *_: (0, part * steps + j)),
            ],
            out_specs=pl.BlockSpec((rows, block), lambda j, *_: (0, j)),
        ),
        out_shape=jax.ShapeDtypeStruct((rows, columns), jnp.bfloat16),
        compiler_params=pltpu.CompilerParams(vmem_limit_bytes=VMEM_LIMIT),
        cost_estimate=pl.CostEstimate(
            flops=4 * rows * width * columns, bytes_accessed=4 * width * columns, transcendentals=0
        ),
        name="project_cross",
    )(first_request, own, other, weight, weight_other, gating)


def rank_partials(blocks, owners, pool, pool_index):
    rows, width = blocks[0].shape
    slots = rows // 2
    rank = pool.shape[1]
    down_block = (pool.shape[2] - width) // width
    count = len(blocks)

    def kernel(index, owner, *refs):
        downs, ins, outs = refs[: 2 * count], refs[2 * count : 3 * count], refs[3 * count :]
        for n in range(count):
            for i in range(2):
                outs[n][i] = lax.dot_general(
                    downs[2 * n + i][0],
                    ins[n][i * slots : (i + 1) * slots],
                    (((1,), (1,)), ((), ())),
                    preferred_element_type=jnp.float32,
                )

    def down_spec(n, i):
        return pl.BlockSpec(
            (1, rank, width), lambda s, index, owner: (index[2 * owner[n] + i], 0, down_block)
        )

    return pl.pallas_call(
        kernel,
        grid_spec=pltpu.PrefetchScalarGridSpec(
            num_scalar_prefetch=2,
            grid=(1,),
            in_specs=[down_spec(n, i) for n in range(count) for i in range(2)]
            + [pl.BlockSpec((rows, width), lambda s, *_: (0, 0))] * count,
            out_specs=[pl.BlockSpec((2, rank, slots), lambda s, *_: (0, 0, 0))] * count,
        ),
        out_shape=[jax.ShapeDtypeStruct((2, rank, slots), jnp.float32)] * count,
        compiler_params=pltpu.CompilerParams(vmem_limit_bytes=VMEM_LIMIT),
        name="rank_partials",
    )(pool_index, owners, *([pool] * (2 * count)), *blocks)


def project_own(own, other, weight, weight_other, gating, pool, pool_index, first_request, ranks):
    rows, width = own.shape
    columns = weight.shape[1]
    block = 640
    slots = rows // 2
    rank = pool.shape[1]

    def kernel(first, index, a, b, w, u, gate, up_0, up_1, r0, r1, r2, r3, out):
        total = jnp.dot(a[...], w[...], preferred_element_type=jnp.float32)
        total += jnp.dot(b[...], u[...], preferred_element_type=jnp.float32)
        for i, up in enumerate((up_0, up_1)):
            acts = (r0[i] + r1[i]) + (r2[i] + r3[i])
            high = acts.astype(jnp.bfloat16)
            low = (acts - high.astype(jnp.float32)).astype(jnp.bfloat16)
            part_rows = slice(i * slots, (i + 1) * slots)
            update = total[part_rows]
            for piece in (high, low):
                update += lax.dot_general(
                    piece, up[0], (((0,), (0,)), ((), ())), preferred_element_type=jnp.float32
                )
            out[part_rows] = update * gate[pl.ds(first[0] + i, 1), :]

    def up_spec(i):
        return pl.BlockSpec((1, rank, block), lambda j, first, index: (index[first[0] + i], 0, j))

    return pl.pallas_call(
        kernel,
        grid_spec=pltpu.PrefetchScalarGridSpec(
            num_scalar_prefetch=2,
            grid=(columns // block,),
            in_specs=[
                pl.BlockSpec((rows, width), lambda j, *_: (0, 0)),
                pl.BlockSpec((rows, width), lambda j, *_: (0, 0)),
                pl.BlockSpec((width, block), lambda j, *_: (0, j)),
                pl.BlockSpec((width, block), lambda j, *_: (0, j)),
                pl.BlockSpec((gating.shape[0], block), lambda j, *_: (0, j)),
                up_spec(0),
                up_spec(1),
            ]
            + [pl.BlockSpec((2, rank, slots), lambda j, *_: (0, 0, 0))] * 4,
            out_specs=pl.BlockSpec((rows, block), lambda j, *_: (0, j)),
        ),
        out_shape=jax.ShapeDtypeStruct((rows, columns), jnp.float32),
        compiler_params=pltpu.CompilerParams(vmem_limit_bytes=VMEM_LIMIT),
        cost_estimate=pl.CostEstimate(
            flops=4 * rows * width * columns, bytes_accessed=8 * width * columns, transcendentals=0
        ),
        name="project_own",
    )(first_request, pool_index, own, other, weight, weight_other, gating, pool, pool, *ranks)


def add_part(own_sums, received, part, parts, so_far=None):
    rows, columns = own_sums.shape
    wide = columns // parts
    block = 640 if wide % 640 == 0 else wide
    steps = wide // block
    extra = () if so_far is None else (so_far,)

    def kernel(a, b, *rest):
        rest[-1][...] = (a[...] + b[...].astype(jnp.float32)).astype(jnp.bfloat16)

    return pl.pallas_call(
        kernel,
        grid=(steps,),
        in_specs=[
            pl.BlockSpec((rows, block), lambda j: (0, part * steps + j)),
            pl.BlockSpec((rows, block), lambda j: (0, j)),
        ]
        + [ANY] * len(extra),
        out_specs=pl.BlockSpec((rows, block), lambda j: (0, part * steps + j)),
        out_shape=jax.ShapeDtypeStruct((rows, columns), jnp.bfloat16),
        input_output_aliases={2: 0} if extra else {},
        compiler_params=pltpu.CompilerParams(vmem_limit_bytes=VMEM_LIMIT),
        name="add_part",
    )(own_sums, received, *extra)


def body(
    queries,
    fresh_keys,
    fresh_values,
    paged_keys,
    paged_values,
    request_page_table,
    live_token_count,
    request_adapter_slot,
    adapters_in_use,
    adapter_pool_row,
    adapter_down_factors,
    adapter_up_factors,
    output_weight,
    gating,
):
    tp = lax.axis_size("tp")
    holders = lax.axis_size("req")
    me = lax.axis_index("tp").astype(jnp.int32)
    requests_here = live_token_count.shape[0]
    per_owner = requests_here // tp

    def swap(array, flip):
        return lax.ppermute(array, "tp", [(s, s ^ flip) for s in range(tp)])

    weight_other = swap(output_weight, 1)
    factors = jnp.concatenate([adapter_up_factors, adapter_down_factors], axis=2)
    gathered = [factors] + [
        lax.ppermute(factors, "req", [(s, (s + d) % holders) for s in range(holders)])
        for d in range(1, holders)
    ]
    pool = jnp.concatenate(gathered, axis=0)
    pool_row = adapter_pool_row[adapters_in_use[request_adapter_slot]]
    pool_index = jnp.remainder(lax.axis_index("req").astype(jnp.int32) - pool_row, holders)

    def attend(flip, after=None):
        first = ((me ^ flip) * per_owner).reshape(1)
        return attend_owner(
            queries,
            fresh_keys,
            fresh_values,
            paged_keys,
            paged_values,
            request_page_table,
            live_token_count,
            first,
            per_owner,
            after,
        )

    cross_away = attend(3)
    cross_other = swap(cross_away, 1)
    cross_here = attend(2)
    cross_first = ((me ^ 2) * per_owner).reshape(1)
    own_first = (me * per_owner).reshape(1)
    sent = [
        project_cross(
            cross_here, cross_other, output_weight, weight_other, gating, cross_first, n, CHUNKS
        )
        for n in range(CHUNKS)
    ]
    received = [swap(part, 2) for part in sent]
    own_away = attend(1, sent[-1])
    own_other = swap(own_away, 1)
    own_here = attend(0, sent[-1])
    owners = jnp.stack([me ^ 3, me ^ 2, me ^ 1, me])
    ranks = rank_partials([cross_away, cross_here, own_away, own_here], owners, pool, pool_index)
    ranks = [swap(ranks[0], 3), swap(ranks[1], 2), swap(ranks[2], 1), ranks[3]]
    own_sums = project_own(
        own_here,
        own_other,
        output_weight,
        weight_other,
        gating,
        pool,
        pool_index,
        own_first,
        ranks,
    )
    out = None
    for n in range(CHUNKS):
        out = add_part(own_sums, received[n], n, CHUNKS, out)
    return out


def solution(mesh):
    return jax.shard_map(
        body,
        mesh=mesh,
        in_specs=(
            P("req", "tp"),
            P("req", "tp"),
            P("req", "tp"),
            P("req", None, "tp"),
            P("req", None, "tp"),
            P("req", None),
            P("req"),
            P("req"),
            P(),
            P(),
            P("req", None, "tp"),
            P("req", None, None),
            P("tp", None),
            P("req", None),
        ),
        out_specs=P(("req", "tp"), None),
        check_vma=False,
    )
```

```python
import math

import jax
import jax.numpy as jnp
from jax import lax
from jax.experimental import pallas as pl
from jax.experimental.pallas import tpu as pltpu
from jax.sharding import PartitionSpec as P

HD = 128
VMEM_LIMIT = 32 * 1024 * 1024
ATTEND_VMEM_LIMIT = 60 * 1024 * 1024
BLOCK = 256
CUTS = ((0, 5), (5, 10))
MASKED = -1e30
ANY = pl.BlockSpec(memory_space=pl.ANY)
BRIEF = pl.CostEstimate(flops=1000, bytes_accessed=1000, transcendentals=0)
HBM = pl.BlockSpec(memory_space=pltpu.HBM)


def attend_owner(
    queries,
    fresh_keys,
    fresh_values,
    paged_keys,
    paged_values,
    request_page_table,
    live_token_count,
    first_request,
    request_count,
    after=None,
):
    requests_here, pages = request_page_table.shape
    slots = queries.shape[0] // requests_here
    width = queries.shape[1]
    heads = width // HD
    page_rows = paged_keys.shape[1]
    cached = pages * page_rows
    key_rows = cached + slots
    exponent_scale = math.log2(math.e) / math.sqrt(HD)

    def kernel(table, live, first, q_hbm, fk_hbm, fv_hbm, pk_hbm, pv_hbm, *rest):
        out, q_buf, k_buf, v_buf, sems = rest[-5:]

        def copies(i):
            request = first[0] + i
            rows = pl.ds(pl.multiple_of(request * slots, slots), slots)
            keys = [
                (pk_hbm.at[table[request, j]], k_buf.at[i, pl.ds(j * page_rows, page_rows)])
                for j in range(pages)
            ]
            values = [
                (pv_hbm.at[table[request, j]], v_buf.at[i, pl.ds(j * page_rows, page_rows)])
                for j in range(pages)
            ]
            keys.append((fk_hbm.at[rows], k_buf.at[i, pl.ds(cached, slots)]))
            values.append((fv_hbm.at[rows], v_buf.at[i, pl.ds(cached, slots)]))
            pairs = [(q_hbm.at[rows], q_buf.at[i])] + keys + values
            made = [
                pltpu.make_async_copy(src, dst, sems.at[i, n]) for n, (src, dst) in enumerate(pairs)
            ]
            return made[: 2 + pages], made[2 + pages :]

        def wait(group):
            for copy in group:
                copy.wait()

        def score(i, h):
            lanes = slice(h * HD, (h + 1) * HD)
            return lax.dot_general(
                q_buf[i, :, lanes],
                k_buf[i, :, lanes],
                (((1,), (1,)), ((), ())),
                preferred_element_type=jnp.float32,
            )

        def weigh(i, scores):
            usable = lax.broadcasted_iota(jnp.int32, (slots, slots), 1) < live[first[0] + i]
            scores = jnp.concatenate(
                [scores[:, :cached], jnp.where(usable, scores[:, cached:], MASKED)], axis=1
            )
            peak = jnp.max(scores, axis=1, keepdims=True)
            return jnp.exp2((scores - peak) * exponent_scale).astype(jnp.bfloat16)

        def blend(i, h, weights):
            lanes = slice(h * HD, (h + 1) * HD)
            ones = jnp.ones((key_rows, HD), jnp.bfloat16)
            blended = jnp.dot(
                weights,
                jnp.concatenate([v_buf[i, :, lanes], ones], axis=1),
                preferred_element_type=jnp.float32,
            )
            live_rows = lax.broadcasted_iota(jnp.int32, (slots, HD), 0) < live[first[0] + i]
            attended = jnp.where(live_rows, blended[:, :HD] / blended[:, HD:], 0.0)
            out[i * slots : (i + 1) * slots, lanes] = attended.astype(jnp.bfloat16)

        groups = [copies(i) for i in range(request_count)]
        for group in groups:
            for copy in group[0] + group[1]:
                copy.start()
        wait(groups[0][0])
        units = [(i, h) for i in range(request_count) for h in range(heads)]
        scores = score(*units[0])
        wait(groups[0][1])
        for n, (i, h) in enumerate(units):
            later = None
            if n + 1 < len(units):
                if units[n + 1][1] == 0:
                    wait(groups[units[n + 1][0]][0] + groups[units[n + 1][0]][1])
                later = score(*units[n + 1])
            blend(i, h, weigh(i, scores))
            scores = later

    extra = () if after is None else (after,)
    return pl.pallas_call(
        kernel,
        grid_spec=pltpu.PrefetchScalarGridSpec(
            num_scalar_prefetch=3,
            grid=(1,),
            in_specs=[HBM] * 5 + [ANY] * len(extra),
            out_specs=pl.BlockSpec((request_count * slots, width), lambda i, *_: (0, 0)),
            scratch_shapes=[
                pltpu.VMEM((request_count, slots, width), jnp.bfloat16),
                pltpu.VMEM((request_count, key_rows, width), jnp.bfloat16),
                pltpu.VMEM((request_count, key_rows, width), jnp.bfloat16),
                pltpu.SemaphoreType.DMA((request_count, 2 * pages + 3)),
            ],
        ),
        out_shape=jax.ShapeDtypeStruct((request_count * slots, width), jnp.bfloat16),
        compiler_params=pltpu.CompilerParams(vmem_limit_bytes=ATTEND_VMEM_LIMIT),
        cost_estimate=BRIEF,
        name="attend",
    )(
        request_page_table,
        live_token_count,
        first_request,
        queries,
        fresh_keys,
        fresh_values,
        paged_keys,
        paged_values,
        *extra,
    )


def project(own, other, weight, weight_other, begin, end, kind, after=None):
    rows, width = own.shape
    steps = (end - begin) // BLOCK
    at = begin // BLOCK
    extra = () if after is None else (after,)

    def kernel(a, b, w, u, *rest):
        total = jnp.dot(a[...], w[...], preferred_element_type=jnp.float32)
        total += jnp.dot(b[...], u[...], preferred_element_type=jnp.float32)
        rest[-1][...] = total.astype(kind)

    return pl.pallas_call(
        kernel,
        grid=(steps,),
        in_specs=[
            pl.BlockSpec((rows, width), lambda j: (0, 0)),
            pl.BlockSpec((rows, width), lambda j: (0, 0)),
            pl.BlockSpec((width, BLOCK), lambda j: (0, at + j)),
            pl.BlockSpec((width, BLOCK), lambda j: (0, at + j)),
        ]
        + [ANY] * len(extra),
        out_specs=pl.BlockSpec((rows, BLOCK), lambda j: (0, j)),
        out_shape=jax.ShapeDtypeStruct((rows, end - begin), kind),
        compiler_params=pltpu.CompilerParams(vmem_limit_bytes=VMEM_LIMIT),
        cost_estimate=BRIEF,
        name="project",
    )(own, other, weight, weight_other, *extra)


def pool_place(request, req, slot, in_use, pool_row, holders):
    apart = pool_row[in_use[slot[request]]] ^ req[0]
    bits = holders.bit_length() - 1
    place = 0
    for bit in range(bits):
        place += ((apart >> (bits - 1 - bit)) & 1) << bit
    return place


def rank_partials(blocks, owners, pool, lookup):
    rows, width = blocks[0].shape
    slots = rows // 2
    holders, rank = pool.shape[:2]
    down_block = (pool.shape[2] - width) // width
    count = len(blocks)

    def kernel(owner, req, slot, in_use, pool_row, *refs):
        downs, ins, outs = refs[: 2 * count], refs[2 * count : 3 * count], refs[3 * count :]
        for n in range(count):
            for i in range(2):
                outs[n][i] = lax.dot_general(
                    downs[2 * n + i][0],
                    ins[n][i * slots : (i + 1) * slots],
                    (((1,), (1,)), ((), ())),
                    preferred_element_type=jnp.float32,
                )

    def down_spec(n, i):
        return pl.BlockSpec(
            (1, rank, width),
            lambda s, owner, *look: (pool_place(2 * owner[n] + i, *look, holders), 0, down_block),
        )

    return pl.pallas_call(
        kernel,
        grid_spec=pltpu.PrefetchScalarGridSpec(
            num_scalar_prefetch=5,
            grid=(1,),
            in_specs=[down_spec(n, i) for n in range(count) for i in range(2)]
            + [pl.BlockSpec((rows, width), lambda s, *_: (0, 0))] * count,
            out_specs=[pl.BlockSpec((2, rank, slots), lambda s, *_: (0, 0, 0))] * count,
        ),
        out_shape=[jax.ShapeDtypeStruct((2, rank, slots), jnp.float32)] * count,
        compiler_params=pltpu.CompilerParams(vmem_limit_bytes=VMEM_LIMIT),
        cost_estimate=BRIEF,
        name="rank_partials",
    )(owners, *lookup, *([pool] * (2 * count)), *blocks)


def sum_ranks(ranks):
    requests, rank, slots = ranks[0].shape

    def kernel(r0, r1, r2, r3, acts):
        acts[...] = jnp.zeros_like(acts)
        for i in range(requests):
            total = (r0[i] + r1[i]) + (r2[i] + r3[i])
            high = total.astype(jnp.bfloat16).astype(jnp.float32)
            pair = jnp.concatenate([high, total - high], axis=0).T.astype(jnp.bfloat16)
            acts[i * slots : (i + 1) * slots, 2 * rank * i : 2 * rank * (i + 1)] = pair

    return pl.pallas_call(
        kernel,
        out_shape=jax.ShapeDtypeStruct((requests * slots, 2 * requests * rank), jnp.bfloat16),
        compiler_params=pltpu.CompilerParams(vmem_limit_bytes=VMEM_LIMIT),
        cost_estimate=BRIEF,
        name="sum_ranks",
    )(*ranks)


def finish(
    own_sums, received, acts, gating, pools, core, lookup, first_request, begin, end, so_far=None
):
    rows, columns = own_sums.shape
    steps = (end - begin) // BLOCK
    at = begin // BLOCK
    slots = rows // 2
    holders, rank = pools[0].shape[:2]
    half = columns // 2 // BLOCK
    extra = () if so_far is None else (so_far,)

    def kernel(
        first, core, req, slot, in_use, pool_row, sums, part, acts, gate, m0, m1, t0, t1, *rest
    ):
        out = rest[-1]
        mine = (at + pl.program_id(0)) // half == core[0]
        ups = [
            jnp.where(mine, m[0].astype(jnp.float32), t[0].astype(jnp.float32)).astype(jnp.bfloat16)
            for m, t in ((m0, t0), (m1, t1))
        ]
        update = sums[...] + part[...].astype(jnp.float32)
        update += jnp.dot(
            acts[...],
            jnp.concatenate([ups[0], ups[0], ups[1], ups[1]], axis=0),
            preferred_element_type=jnp.float32,
        )
        for i in range(2):
            here = slice(i * slots, (i + 1) * slots)
            out[here] = (update[here] * gate[pl.ds(first[0] + i, 1), :]).astype(jnp.bfloat16)

    def up_spec(i):
        return pl.BlockSpec(
            (1, rank, BLOCK),
            lambda j, first, core, *look: (
                pool_place(first[0] + i, *look, holders),
                0,
                lax.rem(at + j, half),
            ),
        )

    return pl.pallas_call(
        kernel,
        grid_spec=pltpu.PrefetchScalarGridSpec(
            num_scalar_prefetch=6,
            grid=(steps,),
            in_specs=[
                pl.BlockSpec((rows, BLOCK), lambda j, *_: (0, at + j)),
                pl.BlockSpec((rows, BLOCK), lambda j, *_: (0, j)),
                pl.BlockSpec(acts.shape, lambda j, *_: (0, 0)),
                pl.BlockSpec((gating.shape[0], BLOCK), lambda j, *_: (0, at + j)),
                up_spec(0),
                up_spec(1),
                up_spec(0),
                up_spec(1),
            ]
            + [ANY] * len(extra),
            out_specs=pl.BlockSpec((rows, BLOCK), lambda j, *_: (0, at + j)),
        ),
        out_shape=jax.ShapeDtypeStruct((rows, columns), jnp.bfloat16),
        input_output_aliases={14: 0} if extra else {},
        compiler_params=pltpu.CompilerParams(vmem_limit_bytes=VMEM_LIMIT),
        cost_estimate=BRIEF,
        name="finish",
    )(
        first_request,
        core,
        *lookup,
        own_sums,
        received,
        acts,
        gating,
        pools[0],
        pools[0],
        pools[1],
        pools[1],
        *extra,
    )


def body(
    queries,
    fresh_keys,
    fresh_values,
    paged_keys,
    paged_values,
    request_page_table,
    live_token_count,
    request_adapter_slot,
    adapters_in_use,
    adapter_pool_row,
    adapter_down_factors,
    adapter_up_factors,
    output_weight,
    gating,
):
    tp = lax.axis_size("tp")
    holders = lax.axis_size("req")
    me = lax.axis_index("tp").astype(jnp.int32)
    core = lax.rem(me, 2)
    per_owner = live_token_count.shape[0] // tp
    columns = output_weight.shape[1]

    def swap(array, flip):
        return lax.ppermute(array, "tp", [(s, s ^ flip) for s in range(tp)])

    def attend(flip, after=None):
        return attend_owner(
            queries,
            fresh_keys,
            fresh_values,
            paged_keys,
            paged_values,
            request_page_table,
            live_token_count,
            ((me ^ flip) * per_owner).reshape(1),
            per_owner,
            after,
        )

    weight_other = swap(output_weight, 1)
    cross_away = attend(3)
    cross_other = swap(cross_away, 1)
    cross_here = attend(2, cross_away)
    sent = []
    for begin, end in CUTS:
        sent.append(
            project(
                cross_here,
                cross_other,
                output_weight,
                weight_other,
                begin * BLOCK,
                end * BLOCK,
                jnp.bfloat16,
                sent[-1] if sent else None,
            )
        )
    received = [swap(part, 2) for part in sent]

    up_half = lax.dynamic_slice_in_dim(adapter_up_factors, core * (columns // 2), columns // 2, 2)
    pool = jnp.concatenate([up_half, adapter_down_factors], axis=2)
    own_away = attend(1, sent[-1])
    own_other = swap(own_away, 1)
    own_here = attend(0, own_away)
    own_sums = project(
        own_here, own_other, output_weight, weight_other, 0, columns, jnp.float32
    )
    marks = [cross_away, cross_here, sent[-1]]
    apart = holders // 2
    while apart:
        if marks:
            pool, _ = lax.optimization_barrier((pool, marks.pop(0)))
        moved = lax.ppermute(pool, "req", [(s, s ^ apart) for s in range(holders)])
        pool = jnp.concatenate([pool, moved], axis=0)
        apart //= 2
    pool_other = swap(pool[:, :, : columns // 2], 1)
    lookup = (
        lax.axis_index("req").astype(jnp.int32).reshape(1),
        request_adapter_slot,
        adapters_in_use,
        adapter_pool_row,
    )
    owners = jnp.stack([me ^ 3, me ^ 2, me ^ 1, me])
    ranks = rank_partials([cross_away, cross_here, own_away, own_here], owners, pool, lookup)
    acts = sum_ranks([swap(ranks[0], 3), swap(ranks[1], 2), swap(ranks[2], 1), ranks[3]])
    out = None
    for part, (begin, end) in zip(received, CUTS):
        out = finish(
            own_sums,
            part,
            acts,
            gating,
            (pool, pool_other),
            core.reshape(1),
            lookup,
            (me * per_owner).reshape(1),
            begin * BLOCK,
            end * BLOCK,
            out,
        )
    return out


def solution(mesh):
    return jax.shard_map(
        body,
        mesh=mesh,
        in_specs=(
            P("req", "tp"),
            P("req", "tp"),
            P("req", "tp"),
            P("req", None, "tp"),
            P("req", None, "tp"),
            P("req", None),
            P("req"),
            P("req"),
            P(),
            P(),
            P("req", None, "tp"),
            P("req", None, None),
            P("tp", None),
            P("req", None),
        ),
        out_specs=P(("req", "tp"), None),
        check_vma=False,
    )
```

```python
import math

import jax
import jax.numpy as jnp
from jax import lax
from jax.experimental import pallas as pl
from jax.experimental.pallas import tpu as pltpu
from jax.sharding import PartitionSpec as P

HD = 128
VMEM_LIMIT = 32 * 1024 * 1024
ATTEND_VMEM_LIMIT = 60 * 1024 * 1024
BLOCK = 512
CUTS = (4, 1)
MASKED = -1e30
ANY = pl.BlockSpec(memory_space=pl.ANY)
BRIEF = pl.CostEstimate(flops=1000, bytes_accessed=1000, transcendentals=0)
HBM = pl.BlockSpec(memory_space=pltpu.HBM)


def attend_owner(
    queries,
    fresh_keys,
    fresh_values,
    paged_keys,
    paged_values,
    request_page_table,
    live_token_count,
    first_request,
    request_count,
    after=None,
):
    requests_here, pages = request_page_table.shape
    slots = queries.shape[0] // requests_here
    width = queries.shape[1]
    heads = width // HD
    page_rows = paged_keys.shape[1]
    cached = pages * page_rows
    key_rows = cached + slots
    exponent_scale = math.log2(math.e) / math.sqrt(HD)

    def kernel(table, live, first, q_hbm, fk_hbm, fv_hbm, pk_hbm, pv_hbm, *rest):
        out, q_buf, k_buf, v_buf, sems = rest[-5:]

        def copies(i):
            request = first[0] + i
            rows = pl.ds(pl.multiple_of(request * slots, slots), slots)
            keys = [
                (pk_hbm.at[table[request, j]], k_buf.at[i, pl.ds(j * page_rows, page_rows)])
                for j in range(pages)
            ]
            values = [
                (pv_hbm.at[table[request, j]], v_buf.at[i, pl.ds(j * page_rows, page_rows)])
                for j in range(pages)
            ]
            keys.append((fk_hbm.at[rows], k_buf.at[i, pl.ds(cached, slots)]))
            values.append((fv_hbm.at[rows], v_buf.at[i, pl.ds(cached, slots)]))
            pairs = [(q_hbm.at[rows], q_buf.at[i])] + keys + values
            made = [
                pltpu.make_async_copy(src, dst, sems.at[i, n]) for n, (src, dst) in enumerate(pairs)
            ]
            return made[: 2 + pages], made[2 + pages :]

        def wait(group):
            for copy in group:
                copy.wait()

        def lanes(h, count=1):
            return slice(h * HD, (h + count) * HD)

        def side_by_side(buf, duo):
            (i, h), (other_i, other_h) = duo
            if i == other_i and other_h == h + 1:
                return buf[i, :, lanes(h, 2)]
            return jnp.concatenate([buf[i, :, lanes(h)], buf[other_i, :, lanes(other_h)]], axis=1)

        def score(duo):
            (i, h), (other_i, other_h) = duo
            blank = jnp.zeros((slots, HD), jnp.bfloat16)
            diagonal = jnp.concatenate(
                [
                    jnp.concatenate([q_buf[i, :, lanes(h)], blank], axis=1),
                    jnp.concatenate([blank, q_buf[other_i, :, lanes(other_h)]], axis=1),
                ],
                axis=0,
            )
            return lax.dot_general(
                diagonal,
                side_by_side(k_buf, duo),
                (((1,), (1,)), ((), ())),
                preferred_element_type=jnp.float32,
            )

        def weigh(duo, scores):
            column = lax.broadcasted_iota(jnp.int32, (slots, slots), 1)
            usable = jnp.concatenate([column < live[first[0] + i] for i, _ in duo], axis=0)
            scores = jnp.concatenate(
                [scores[:, :cached], jnp.where(usable, scores[:, cached:], MASKED)], axis=1
            )
            peak = jnp.max(scores, axis=1, keepdims=True)
            weights = jnp.exp2((scores - peak) * exponent_scale)
            return weights.astype(jnp.bfloat16), jnp.sum(weights, axis=1, keepdims=True)

        def blend(duo, weights, row_total):
            blended = jnp.dot(
                weights, side_by_side(v_buf, duo), preferred_element_type=jnp.float32
            )
            row = lax.broadcasted_iota(jnp.int32, (slots, HD), 0)
            for n, (i, h) in enumerate(duo):
                rows = slice(n * slots, (n + 1) * slots)
                attended = blended[rows, lanes(n)] / row_total[rows]
                attended = jnp.where(row < live[first[0] + i], attended, 0.0)
                out[i * slots : (i + 1) * slots, lanes(h)] = attended.astype(jnp.bfloat16)

        groups = [copies(i) for i in range(request_count)]
        for group in groups:
            for copy in group[0] + group[1]:
                copy.start()
        waited = set()

        def ready(duo, which):
            for i, _ in duo:
                if (i, which) not in waited:
                    waited.add((i, which))
                    wait(groups[i][which])

        units = [
            ((i, h), (i, h + 1)) for i in range(request_count) for h in range(0, heads - 1, 2)
        ]
        left = [(i, heads - 1) for i in range(request_count)] if heads % 2 else []
        units += [(left[n], left[n + 1]) for n in range(0, len(left), 2)]
        ready(units[0], 0)
        scores = score(units[0])
        for n, duo in enumerate(units):
            later = None
            if n + 1 < len(units):
                ready(units[n + 1], 0)
                later = score(units[n + 1])
            weights, row_total = weigh(duo, scores)
            ready(duo, 1)
            blend(duo, weights, row_total)
            scores = later

    extra = () if after is None else (after,)
    return pl.pallas_call(
        kernel,
        grid_spec=pltpu.PrefetchScalarGridSpec(
            num_scalar_prefetch=3,
            grid=(1,),
            in_specs=[HBM] * 5 + [ANY] * len(extra),
            out_specs=pl.BlockSpec((request_count * slots, width), lambda i, *_: (0, 0)),
            scratch_shapes=[
                pltpu.VMEM((request_count, slots, width), jnp.bfloat16),
                pltpu.VMEM((request_count, key_rows, width), jnp.bfloat16),
                pltpu.VMEM((request_count, key_rows, width), jnp.bfloat16),
                pltpu.SemaphoreType.DMA((request_count, 2 * pages + 3)),
            ],
        ),
        out_shape=jax.ShapeDtypeStruct((request_count * slots, width), jnp.bfloat16),
        compiler_params=pltpu.CompilerParams(vmem_limit_bytes=ATTEND_VMEM_LIMIT),
        cost_estimate=BRIEF,
        name="attend",
    )(
        request_page_table,
        live_token_count,
        first_request,
        queries,
        fresh_keys,
        fresh_values,
        paged_keys,
        paged_values,
        *extra,
    )


def project(own, other, weight, weight_other, cuts, kind):
    rows, width = own.shape
    columns = weight.shape[1]
    blocks = columns // BLOCK
    bounds = [sum(cuts[:n]) for n in range(len(cuts) + 1)]
    assert bounds[-1] == blocks

    def kernel(a, b, w, u, *rest):
        outs, (w_buf, out_buf, in_sems, out_sems) = rest[: len(cuts)], rest[len(cuts) :]

        def fetch(n):
            here = pl.ds(n * BLOCK, BLOCK)
            return [
                pltpu.make_async_copy(
                    src.at[:, here], w_buf.at[pl.ds(m * width, width), here], in_sems.at[n, m]
                )
                for m, src in enumerate((w, u))
            ]

        def store(n):
            part = max(m for m in range(len(cuts)) if bounds[m] <= n)
            return pltpu.make_async_copy(
                out_buf.at[:, pl.ds(n * BLOCK, BLOCK)],
                outs[part].at[:, pl.ds((n - bounds[part]) * BLOCK, BLOCK)],
                out_sems.at[n],
            )

        for n in range(blocks):
            for copy in fetch(n):
                copy.start()
        features = jnp.concatenate([a[...], b[...]], axis=1)
        for n in range(blocks):
            for copy in fetch(n):
                copy.wait()
            here = slice(n * BLOCK, (n + 1) * BLOCK)
            out_buf[:, here] = jnp.dot(
                features, w_buf[:, here], preferred_element_type=jnp.float32
            ).astype(kind)
            store(n).start()
        for n in range(blocks):
            store(n).wait()

    return pl.pallas_call(
        kernel,
        in_specs=[pl.BlockSpec(memory_space=pltpu.VMEM)] * 2 + [HBM] * 2,
        out_specs=[HBM] * len(cuts),
        out_shape=[jax.ShapeDtypeStruct((rows, cut * BLOCK), kind) for cut in cuts],
        scratch_shapes=[
            pltpu.VMEM((2 * width, columns), jnp.bfloat16),
            pltpu.VMEM((rows, columns), kind),
            pltpu.SemaphoreType.DMA((blocks, 2)),
            pltpu.SemaphoreType.DMA((blocks,)),
        ],
        compiler_params=pltpu.CompilerParams(vmem_limit_bytes=VMEM_LIMIT),
        cost_estimate=BRIEF,
        name="project",
    )(own, other, weight, weight_other)


def pool_place(request, slot, in_use, pool_row):
    return pool_row[in_use[slot[request]]]


def rank_partials(blocks, owners, pool, lookup):
    rows, width = blocks[0].shape
    slots = rows // 2
    rank = pool.shape[1]
    down_block = (pool.shape[2] - width) // width
    count = len(blocks)

    def kernel(owner, slot, in_use, pool_row, *refs):
        downs, ins, outs = refs[: 2 * count], refs[2 * count : 3 * count], refs[3 * count :]
        for n in range(count):
            for i in range(2):
                outs[n][i] = lax.dot_general(
                    downs[2 * n + i][0],
                    ins[n][i * slots : (i + 1) * slots],
                    (((1,), (1,)), ((), ())),
                    preferred_element_type=jnp.float32,
                )

    def down_spec(n, i):
        return pl.BlockSpec(
            (1, rank, width),
            lambda s, owner, *look: (pool_place(2 * owner[n] + i, *look), 0, down_block),
        )

    return pl.pallas_call(
        kernel,
        grid_spec=pltpu.PrefetchScalarGridSpec(
            num_scalar_prefetch=4,
            grid=(1,),
            in_specs=[down_spec(n, i) for n in range(count) for i in range(2)]
            + [pl.BlockSpec((rows, width), lambda s, *_: (0, 0))] * count,
            out_specs=[pl.BlockSpec((2, rank, slots), lambda s, *_: (0, 0, 0))] * count,
        ),
        out_shape=[jax.ShapeDtypeStruct((2, rank, slots), jnp.float32)] * count,
        compiler_params=pltpu.CompilerParams(vmem_limit_bytes=VMEM_LIMIT),
        cost_estimate=BRIEF,
        name="rank_partials",
    )(owners, *lookup, *([pool] * (2 * count)), *blocks)


def sum_ranks(ranks):
    requests, rank, slots = ranks[0].shape

    def kernel(r0, r1, r2, r3, acts):
        acts[...] = jnp.zeros_like(acts)
        for i in range(requests):
            total = (r0[i] + r1[i]) + (r2[i] + r3[i])
            high = total.astype(jnp.bfloat16).astype(jnp.float32)
            pair = jnp.concatenate([high, total - high], axis=0).T.astype(jnp.bfloat16)
            acts[i * slots : (i + 1) * slots, 2 * rank * i : 2 * rank * (i + 1)] = pair

    return pl.pallas_call(
        kernel,
        out_shape=jax.ShapeDtypeStruct((requests * slots, 2 * requests * rank), jnp.bfloat16),
        compiler_params=pltpu.CompilerParams(vmem_limit_bytes=VMEM_LIMIT),
        cost_estimate=BRIEF,
        name="sum_ranks",
    )(*ranks)


def finish(own_sums, received, acts, gating, pool, lookup, first_request, begin, end, so_far=None):
    rows, columns = own_sums.shape
    wide = math.gcd(math.gcd(begin, end - begin), 1024)
    steps = (end - begin) // wide
    at = begin // wide
    slots = rows // 2
    rank = pool.shape[1]
    extra = () if so_far is None else (so_far,)

    def kernel(first, slot, in_use, pool_row, sums, part, acts, gate, up_0, up_1, *rest):
        out = rest[-1]
        update = sums[...] + part[...].astype(jnp.float32)
        update += jnp.dot(
            acts[...],
            jnp.concatenate([up_0[0], up_0[0], up_1[0], up_1[0]], axis=0),
            preferred_element_type=jnp.float32,
        )
        for i in range(2):
            here = slice(i * slots, (i + 1) * slots)
            out[here] = (update[here] * gate[pl.ds(first[0] + i, 1), :]).astype(jnp.bfloat16)

    def up_spec(i):
        return pl.BlockSpec(
            (1, rank, wide), lambda j, first, *look: (pool_place(first[0] + i, *look), 0, at + j)
        )

    return pl.pallas_call(
        kernel,
        grid_spec=pltpu.PrefetchScalarGridSpec(
            num_scalar_prefetch=4,
            grid=(steps,),
            in_specs=[
                pl.BlockSpec((rows, wide), lambda j, *_: (0, at + j)),
                pl.BlockSpec((rows, wide), lambda j, *_: (0, j)),
                pl.BlockSpec(acts.shape, lambda j, *_: (0, 0)),
                pl.BlockSpec((gating.shape[0], wide), lambda j, *_: (0, at + j)),
                up_spec(0),
                up_spec(1),
            ]
            + [ANY] * len(extra),
            out_specs=pl.BlockSpec((rows, wide), lambda j, *_: (0, at + j)),
        ),
        out_shape=jax.ShapeDtypeStruct((rows, columns), jnp.bfloat16),
        input_output_aliases={10: 0} if extra else {},
        compiler_params=pltpu.CompilerParams(vmem_limit_bytes=VMEM_LIMIT),
        cost_estimate=BRIEF,
        name="finish",
    )(first_request, *lookup, own_sums, received, acts, gating, pool, pool, *extra)


def body(
    queries,
    fresh_keys,
    fresh_values,
    paged_keys,
    paged_values,
    request_page_table,
    live_token_count,
    request_adapter_slot,
    adapters_in_use,
    adapter_pool_row,
    adapter_down_factors,
    adapter_up_factors,
    output_weight,
    gating,
):
    tp = lax.axis_size("tp")
    holders = lax.axis_size("req")
    me = lax.axis_index("tp").astype(jnp.int32)
    per_owner = live_token_count.shape[0] // tp

    def swap(array, flip):
        return lax.ppermute(array, "tp", [(s, s ^ flip) for s in range(tp)])

    def attend(flip, after=None):
        return attend_owner(
            queries,
            fresh_keys,
            fresh_values,
            paged_keys,
            paged_values,
            request_page_table,
            live_token_count,
            ((me ^ flip) * per_owner).reshape(1),
            per_owner,
            after,
        )

    weight_other = swap(output_weight, 1)
    cross_away = attend(3)
    cross_other = swap(cross_away, 1)
    cross_here = attend(2, cross_away)
    sent = project(cross_here, cross_other, output_weight, weight_other, CUTS, jnp.bfloat16)
    received = [swap(sent[0], 2)]

    pool = jnp.concatenate([adapter_up_factors, adapter_down_factors], axis=2)
    pool, _ = lax.optimization_barrier((pool, sent[0]))
    pool = lax.all_to_all(
        jnp.broadcast_to(pool, (holders, *pool.shape[1:])), "req", 0, 0, tiled=True
    )
    own_away = attend(1, sent[0])
    own_other = swap(own_away, 1)
    own_here = attend(0, own_away)
    lookup = (request_adapter_slot, adapters_in_use, adapter_pool_row)
    owners = jnp.stack([me ^ 3, me ^ 2, me ^ 1, me])
    ranks = rank_partials([cross_away, cross_here, own_away, own_here], owners, pool, lookup)
    ranks = [swap(ranks[0], 3), swap(ranks[1], 2), swap(ranks[2], 1), ranks[3]]
    (own_sums,) = project(
        own_here, own_other, output_weight, weight_other, (sum(CUTS),), jnp.float32
    )
    last, own_sums = lax.optimization_barrier((sent[1], own_sums))
    received.append(swap(last, 2))
    acts = sum_ranks(ranks)
    out = None
    for n, part in enumerate(received):
        begin, end = sum(CUTS[:n]) * BLOCK, sum(CUTS[: n + 1]) * BLOCK
        out = finish(
            own_sums,
            part,
            acts,
            gating,
            pool,
            lookup,
            (me * per_owner).reshape(1),
            begin,
            end,
            out,
        )
    return out


def solution(mesh):
    return jax.shard_map(
        body,
        mesh=mesh,
        in_specs=(
            P("req", "tp"),
            P("req", "tp"),
            P("req", "tp"),
            P("req", None, "tp"),
            P("req", None, "tp"),
            P("req", None),
            P("req"),
            P("req"),
            P(),
            P(),
            P("req", None, "tp"),
            P("req", None, None),
            P("tp", None),
            P("req", None),
        ),
        out_specs=P(("req", "tp"), None),
        check_vma=False,
    )
```

```python
import math

import jax
import jax.numpy as jnp
from jax import lax
from jax.experimental import pallas as pl
from jax.experimental.pallas import tpu as pltpu
from jax.sharding import PartitionSpec as P

HD = 128
VMEM_LIMIT = 65280 * 1024
BLOCK = 512
CUTS = (3, 1, 1)
MASKED = -1e30
ANY = pl.BlockSpec(memory_space=pl.ANY)
BRIEF = pl.CostEstimate(flops=1000, bytes_accessed=1000, transcendentals=0)
HBM = pl.BlockSpec(memory_space=pltpu.HBM)


def attend_four(
    queries,
    fresh_keys,
    fresh_values,
    paged_keys,
    paged_values,
    request_page_table,
    live_token_count,
    requests,
    after=None,
):
    requests_here, pages = request_page_table.shape
    slots = queries.shape[0] // requests_here
    width = queries.shape[1]
    heads = width // HD
    pool_pages, page_rows = paged_keys.shape[:2]
    cached = pages * page_rows
    count = requests.shape[0]
    exponent_scale = math.log2(math.e) / math.sqrt(HD)

    def kernel(table, live, ids, q_hbm, fk_hbm, fv_hbm, pk_hbm, pv_hbm, *rest):
        outs, bufs = rest[-11:-9], rest[-9:]
        q_buf, fk_buf, fv_buf, pk_buf, pv_buf, out_buf, order, in_sems, out_sems = bufs

        def fetch(src, dst, sem):
            return pltpu.make_async_copy(src, dst, in_sems.at[sem])

        def rows_of(n):
            return pl.ds(pl.multiple_of(ids[n] * slots, slots), slots)

        def query_copy(n):
            return fetch(q_hbm.at[rows_of(n)], q_buf.at[n], 3 * n)

        def key_copy(n):
            return fetch(fk_hbm.at[rows_of(n)], fk_buf.at[n], 3 * n + 1)

        def value_copy(n):
            return fetch(fv_hbm.at[rows_of(n)], fv_buf.at[n], 3 * n + 2)

        def key_page(m):
            page = order[m]
            return fetch(pk_hbm.at[page], pk_buf.at[page], 3 * count + 2 * m)

        def value_page(m):
            page = order[m]
            return fetch(pv_hbm.at[page], pv_buf.at[page], 3 * count + 2 * m + 1)

        started = [0]

        def start(copies):
            for copy in copies:
                copy.start(priority=started[0] % 2)
                started[0] += 1

        for j in range(pages):
            order[j] = table[ids[0], j]
        start([query_copy(0), key_copy(0)] + [key_page(m) for m in range(pages)])
        start([value_copy(0)] + [value_page(m) for m in range(pages)])
        place = jnp.int32(pages)
        for page in range(pool_pages):
            taken = order[0] == page
            for j in range(1, pages):
                taken = taken | (order[j] == page)

            @pl.when(jnp.logical_not(taken))
            def _(place=place, page=page):
                order[place] = page

            place = place + jnp.where(taken, 0, 1)
        others = range(pages, pool_pages)
        start([query_copy(1), key_copy(1)] + [key_page(m) for m in others])
        start([value_copy(1)] + [value_page(m) for m in others])
        for n in range(2, count):
            start([query_copy(n), key_copy(n), value_copy(n)])

        waited = set()

        def wait(name, make, indices):
            if name not in waited:
                waited.add(name)
                for index in indices:
                    make(index).wait()

        def keys_ready(duo):
            for n, _ in duo:
                wait(("q", n), query_copy, [n])
                wait(("k", n), key_copy, [n])
                wait(("first k",), key_page, range(pages))
                if n:
                    wait(("other k",), key_page, others)

        def values_ready(duo):
            for n, _ in duo:
                wait(("v", n), value_copy, [n])
                wait(("first v",), value_page, range(pages))
                if n:
                    wait(("other v",), value_page, others)

        def lanes(h, several=1):
            return slice(h * HD, (h + several) * HD)

        def gather(pool, fresh, n, here):
            return jnp.concatenate(
                [pool[table[ids[n], j], :, here] for j in range(pages)] + [fresh[n, :, here]],
                axis=0,
            )

        def side_by_side(pool, fresh, duo):
            (n, h), (other_n, other_h) = duo
            if n == other_n and other_h == h + 1:
                return gather(pool, fresh, n, lanes(h, 2))
            return jnp.concatenate(
                [gather(pool, fresh, m, lanes(g)) for m, g in duo],
                axis=1,
            )

        def score(duo):
            (n, h), (other_n, other_h) = duo
            blank = jnp.zeros((slots, HD), jnp.bfloat16)
            diagonal = jnp.concatenate(
                [
                    jnp.concatenate([q_buf[n, :, lanes(h)], blank], axis=1),
                    jnp.concatenate([blank, q_buf[other_n, :, lanes(other_h)]], axis=1),
                ],
                axis=0,
            )
            return lax.dot_general(
                diagonal,
                side_by_side(pk_buf, fk_buf, duo),
                (((1,), (1,)), ((), ())),
                preferred_element_type=jnp.float32,
            )

        def weigh(duo, scores):
            column = lax.broadcasted_iota(jnp.int32, (slots, slots), 1)
            usable = jnp.concatenate([column < live[ids[n]] for n, _ in duo], axis=0)
            scores = jnp.concatenate(
                [scores[:, :cached], jnp.where(usable, scores[:, cached:], MASKED)], axis=1
            )
            peak = jnp.max(scores, axis=1, keepdims=True)
            weights = jnp.exp2((scores - peak) * exponent_scale)
            return weights.astype(jnp.bfloat16), jnp.sum(weights, axis=1, keepdims=True)

        def blend(duo, weights, row_total):
            blended = jnp.dot(
                weights, side_by_side(pv_buf, fv_buf, duo), preferred_element_type=jnp.float32
            )
            row = lax.broadcasted_iota(jnp.int32, (slots, HD), 0)
            for m, (n, h) in enumerate(duo):
                rows = slice(m * slots, (m + 1) * slots)
                attended = blended[rows, lanes(m)] / row_total[rows]
                attended = jnp.where(row < live[ids[n]], attended, 0.0)
                out_buf[n * slots : (n + 1) * slots, lanes(h)] = attended.astype(jnp.bfloat16)

        units = []
        for first in range(0, count, 2):
            units += [((n, h), (n, h + 1)) for n in (first, first + 1) for h in range(0, heads - 1, 2)]
            if heads % 2:
                units.append(((first, heads - 1), (first + 1, heads - 1)))
        half = count // 2 * slots
        stores = [
            pltpu.make_async_copy(out_buf.at[pl.ds(m * half, half)], outs[m], out_sems.at[m])
            for m in range(2)
        ]
        keys_ready(units[0])
        scores = score(units[0])
        for u, duo in enumerate(units):
            later = None
            if u + 1 < len(units):
                keys_ready(units[u + 1])
                later = score(units[u + 1])
            weights, row_total = weigh(duo, scores)
            values_ready(duo)
            blend(duo, weights, row_total)
            scores = later
            if u + 1 == len(units) // 2:
                stores[0].start()
        stores[1].start()
        for store in stores:
            store.wait()

    extra = () if after is None else (after,)
    out_shape = jax.ShapeDtypeStruct((count // 2 * slots, width), jnp.bfloat16)
    return pl.pallas_call(
        kernel,
        grid_spec=pltpu.PrefetchScalarGridSpec(
            num_scalar_prefetch=3,
            grid=(1,),
            in_specs=[HBM] * 5 + [ANY] * len(extra),
            out_specs=[HBM] * 2,
            scratch_shapes=[
                pltpu.VMEM((count, slots, width), jnp.bfloat16),
                pltpu.VMEM((count, slots, width), jnp.bfloat16),
                pltpu.VMEM((count, slots, width), jnp.bfloat16),
                pltpu.VMEM(paged_keys.shape, jnp.bfloat16),
                pltpu.VMEM(paged_values.shape, jnp.bfloat16),
                pltpu.VMEM((count * slots, width), jnp.bfloat16),
                pltpu.SMEM((pool_pages,), jnp.int32),
                pltpu.SemaphoreType.DMA((3 * count + 2 * pool_pages,)),
                pltpu.SemaphoreType.DMA((2,)),
            ],
        ),
        out_shape=[out_shape] * 2,
        compiler_params=pltpu.CompilerParams(vmem_limit_bytes=VMEM_LIMIT),
        cost_estimate=BRIEF,
        name="attend",
    )(
        request_page_table,
        live_token_count,
        requests,
        queries,
        fresh_keys,
        fresh_values,
        paged_keys,
        paged_values,
        *extra,
    )


def project(own, other, weight, weight_other, cuts, kind):
    rows, width = own.shape
    columns = weight.shape[1]
    blocks = columns // BLOCK
    bounds = [sum(cuts[:n]) for n in range(len(cuts) + 1)]
    assert bounds[-1] == blocks

    def kernel(a_hbm, b_hbm, w, u, *rest):
        outs, (a, b, w_buf, out_buf, own_sems, in_sems, out_sems) = (
            rest[: len(cuts)],
            rest[len(cuts) :],
        )

        def fetch(n):
            here = pl.ds(n * BLOCK, BLOCK)
            return [
                pltpu.make_async_copy(
                    src.at[:, here], w_buf.at[pl.ds(m * width, width), here], in_sems.at[n, m]
                )
                for m, src in enumerate((w, u))
            ]

        def store(n):
            part = max(m for m in range(len(cuts)) if bounds[m] <= n)
            return pltpu.make_async_copy(
                out_buf.at[:, pl.ds(n * BLOCK, BLOCK)],
                outs[part].at[:, pl.ds((n - bounds[part]) * BLOCK, BLOCK)],
                out_sems.at[n],
            )

        features = [
            pltpu.make_async_copy(src, dst, own_sems.at[m])
            for m, (src, dst) in enumerate(((a_hbm, a), (b_hbm, b)))
        ]
        for m, copy in enumerate(features):
            copy.start(priority=m)
        for n in range(blocks):
            for m, copy in enumerate(fetch(n)):
                copy.start(priority=m)
        for copy in features:
            copy.wait()
        for n in range(blocks):
            for copy in fetch(n):
                copy.wait()
            here = slice(n * BLOCK, (n + 1) * BLOCK)
            out_buf[:, here] = jnp.dot(
                jnp.concatenate([a[...], b[...]], axis=1),
                w_buf[:, here],
                preferred_element_type=jnp.float32,
            ).astype(kind)
            store(n).start()
        for n in range(blocks):
            store(n).wait()

    return pl.pallas_call(
        kernel,
        in_specs=[HBM] * 4,
        out_specs=[HBM] * len(cuts),
        out_shape=[jax.ShapeDtypeStruct((rows, cut * BLOCK), kind) for cut in cuts],
        scratch_shapes=[
            pltpu.VMEM((rows, width), jnp.bfloat16),
            pltpu.VMEM((rows, width), jnp.bfloat16),
            pltpu.VMEM((2 * width, columns), jnp.bfloat16),
            pltpu.VMEM((rows, columns), kind),
            pltpu.SemaphoreType.DMA((2,)),
            pltpu.SemaphoreType.DMA((blocks, 2)),
            pltpu.SemaphoreType.DMA((blocks,)),
        ],
        compiler_params=pltpu.CompilerParams(vmem_limit_bytes=VMEM_LIMIT),
        cost_estimate=BRIEF,
        name="project",
    )(own, other, weight, weight_other)


def pool_place(request, slot, in_use, pool_row):
    return pool_row[in_use[slot[request]]]


def ranks_and_part(cross, own, pool, lookup, first_requests, part):
    rows, width = cross[0].shape
    slots = rows // 2
    rank = pool.shape[1]
    assert part.shape[1] == 4 * slots
    down_block = pool.shape[2] // width - 2

    def kernel(first, slot, in_use, pool_row, *refs):
        downs, blocks, part_in, part_out, own_ranks = refs[:8], refs[8:12], *refs[12:]
        part_out[:rows] = part_in[...]
        for i in range(2):
            here = slice(i * slots, (i + 1) * slots)
            for n in range(2):
                acts = sum(
                    lax.dot_general(
                        downs[4 * n + 2 * i + m][0],
                        blocks[2 * n + m][here],
                        (((1,), (1,)), ((), ())),
                        preferred_element_type=jnp.float32,
                    )
                    for m in range(2)
                )
                if n:
                    own_ranks[i] = acts
                    continue
                high = acts.astype(jnp.bfloat16)
                low = (acts - high.astype(jnp.float32)).astype(jnp.bfloat16)
                part_out[rows:, 2 * i * slots : (2 * i + 1) * slots] = high
                part_out[rows:, (2 * i + 1) * slots : (2 * i + 2) * slots] = low

    def down_spec(n, i, m):
        return pl.BlockSpec(
            (1, rank, width),
            lambda s, first, *look: (pool_place(first[n] + i, *look), 0, down_block + m),
        )

    def whole(*shape):
        return pl.BlockSpec(shape, lambda s, *_: (0,) * len(shape))

    return pl.pallas_call(
        kernel,
        grid_spec=pltpu.PrefetchScalarGridSpec(
            num_scalar_prefetch=4,
            grid=(1,),
            in_specs=[down_spec(n, i, m) for n in range(2) for i in range(2) for m in range(2)]
            + [whole(rows, width)] * 4
            + [whole(*part.shape)],
            out_specs=[whole(rows + rank, part.shape[1]), whole(2, rank, slots)],
        ),
        out_shape=[
            jax.ShapeDtypeStruct((rows + rank, part.shape[1]), jnp.bfloat16),
            jax.ShapeDtypeStruct((2, rank, slots), jnp.float32),
        ],
        compiler_params=pltpu.CompilerParams(vmem_limit_bytes=VMEM_LIMIT),
        cost_estimate=BRIEF,
        name="ranks_and_part",
    )(first_requests, *lookup, *([pool] * 8), *cross, *own, part)


def adapter_terms(own_ranks, received, pool, lookup, gating, first_request):
    requests, rank, slots = own_ranks.shape
    rows = requests * slots
    columns = gating.shape[1]

    def kernel(first, slot, in_use, pool_row, own, other, up_0, up_1, gate, acts, ups, gates):
        acts[...] = jnp.zeros_like(acts)
        gates[...] = jnp.zeros_like(gates)
        for i, up in enumerate((up_0, up_1)):
            total = own[i]
            for m in range(2 * i, 2 * i + 2):
                total += other[:, m * slots : (m + 1) * slots].astype(jnp.float32)
            high = total.astype(jnp.bfloat16).astype(jnp.float32)
            pair = jnp.concatenate([high, total - high], axis=0).T.astype(jnp.bfloat16)
            acts[i * slots : (i + 1) * slots, 2 * rank * i : 2 * rank * (i + 1)] = pair
            for m in range(2):
                ups[(2 * i + m) * rank : (2 * i + m + 1) * rank] = up[0]
            gates[i : i + 1] = gate[pl.ds(first[0] + i, 1), :]

    def up_spec(i):
        return pl.BlockSpec(
            (1, rank, columns), lambda s, first, *look: (pool_place(first[0] + i, *look), 0, 0)
        )

    def whole(*shape):
        return pl.BlockSpec(shape, lambda s, *_: (0,) * len(shape))

    return pl.pallas_call(
        kernel,
        grid_spec=pltpu.PrefetchScalarGridSpec(
            num_scalar_prefetch=4,
            grid=(1,),
            in_specs=[
                whole(*own_ranks.shape),
                pl.BlockSpec((rank, received.shape[1]), lambda s, *_: (rows // rank, 0)),
                up_spec(0),
                up_spec(1),
                whole(*gating.shape),
            ],
            out_specs=[
                whole(rows, 2 * requests * rank),
                whole(2 * requests * rank, columns),
                whole(8, columns),
            ],
        ),
        out_shape=[
            jax.ShapeDtypeStruct((rows, 2 * requests * rank), jnp.bfloat16),
            jax.ShapeDtypeStruct((2 * requests * rank, columns), jnp.bfloat16),
            jax.ShapeDtypeStruct((8, columns), jnp.float32),
        ],
        compiler_params=pltpu.CompilerParams(vmem_limit_bytes=VMEM_LIMIT),
        cost_estimate=BRIEF,
        name="adapter_terms",
    )(first_request, *lookup, own_ranks, received, pool, pool, gating)


def project_own(own, other, weight, weight_other, received, terms):
    acts, ups, gates = terms
    rows, width = own.shape
    columns = weight.shape[1]
    blocks = columns // BLOCK
    parts = [part.shape[1] for part in received]
    arrived = sum(parts)
    covered = arrived // BLOCK
    slots = rows // 2

    def kernel(a_hbm, b_hbm, w, u, acts_hbm, ups_hbm, gates_hbm, *refs):
        parts_hbm, (out, rest_out), bufs = refs[:-14], refs[-14:-12], refs[-12:]
        a, b, w_buf, part, acts, ups, gates, out_buf, rest_buf, own_sems, in_sems, out_sems = bufs

        def fetch(n):
            here = pl.ds(n * BLOCK, BLOCK)
            return [
                pltpu.make_async_copy(
                    src.at[:, here], w_buf.at[pl.ds(m * width, width), here], in_sems.at[n, m]
                )
                for m, src in enumerate((w, u))
            ]

        def store(n):
            here = pl.ds(n * BLOCK, BLOCK)
            if n < covered:
                src, dst = out_buf.at[:, here], out.at[:, here]
            else:
                there = pl.ds((n - covered) * BLOCK, BLOCK)
                src, dst = rest_buf.at[:, there], rest_out.at[:, there]
            return pltpu.make_async_copy(src, dst, out_sems.at[n])

        whole = ((a_hbm, a), (b_hbm, b), (acts_hbm, acts), (ups_hbm, ups), (gates_hbm, gates))
        for n, part_hbm in enumerate(parts_hbm):
            there = pl.ds(sum(parts[:n]), parts[n])
            whole += ((part_hbm.at[pl.ds(0, rows)], part.at[:, there]),)
        whole = [
            pltpu.make_async_copy(src, dst, own_sems.at[m]) for m, (src, dst) in enumerate(whole)
        ]
        for m, copy in enumerate(whole):
            copy.start(priority=m % 2)
        for n in range(blocks):
            for m, copy in enumerate(fetch(n)):
                copy.start(priority=m)
        for copy in whole:
            copy.wait()
        for n in range(blocks):
            for copy in fetch(n):
                copy.wait()
            here = slice(n * BLOCK, (n + 1) * BLOCK)
            update = jnp.dot(
                jnp.concatenate([a[...], b[...]], axis=1),
                w_buf[:, here],
                preferred_element_type=jnp.float32,
            )
            update += jnp.dot(acts[...], ups[:, here], preferred_element_type=jnp.float32)
            if n < covered:
                update += part[:, here].astype(jnp.float32)
            for i in range(2):
                those = slice(i * slots, (i + 1) * slots)
                gated = update[those] * gates[i : i + 1, here]
                if n < covered:
                    out_buf[those, here] = gated.astype(jnp.bfloat16)
                else:
                    there = slice((n - covered) * BLOCK, (n - covered + 1) * BLOCK)
                    rest_buf[those, there] = gated
            store(n).start()
        for n in range(blocks):
            store(n).wait()

    left = columns - arrived
    return pl.pallas_call(
        kernel,
        in_specs=[HBM] * (7 + len(received)),
        out_specs=[HBM] * 2,
        out_shape=[
            jax.ShapeDtypeStruct((rows, columns), jnp.bfloat16),
            jax.ShapeDtypeStruct((rows, left), jnp.float32),
        ],
        scratch_shapes=[
            pltpu.VMEM((rows, width), jnp.bfloat16),
            pltpu.VMEM((rows, width), jnp.bfloat16),
            pltpu.VMEM((2 * width, columns), jnp.bfloat16),
            pltpu.VMEM((rows, arrived), jnp.bfloat16),
            pltpu.VMEM(acts.shape, jnp.bfloat16),
            pltpu.VMEM(ups.shape, jnp.bfloat16),
            pltpu.VMEM(gates.shape, jnp.float32),
            pltpu.VMEM((rows, arrived), jnp.bfloat16),
            pltpu.VMEM((rows, left), jnp.float32),
            pltpu.SemaphoreType.DMA((5 + len(received),)),
            pltpu.SemaphoreType.DMA((blocks, 2)),
            pltpu.SemaphoreType.DMA((blocks,)),
        ],
        compiler_params=pltpu.CompilerParams(vmem_limit_bytes=VMEM_LIMIT),
        cost_estimate=BRIEF,
        name="project_own",
    )(own, other, weight, weight_other, acts, ups, gates, *received)


def finish(so_far, rest, received, gates):
    rows, columns = so_far.shape
    wide = rest.shape[1]
    assert columns % wide == 0
    at = columns // wide - 1
    slots = rows // 2

    def kernel(sums, part, gate, so_far, out):
        for i in range(2):
            here = slice(i * slots, (i + 1) * slots)
            update = sums[here] + part[here].astype(jnp.float32) * gate[i : i + 1]
            out[here] = update.astype(jnp.bfloat16)

    return pl.pallas_call(
        kernel,
        grid=(1,),
        in_specs=[
            pl.BlockSpec((rows, wide), lambda j: (0, 0)),
            pl.BlockSpec((rows, wide), lambda j: (0, 0)),
            pl.BlockSpec((gates.shape[0], wide), lambda j: (0, at)),
            ANY,
        ],
        out_specs=pl.BlockSpec((rows, wide), lambda j: (0, at)),
        out_shape=jax.ShapeDtypeStruct((rows, columns), jnp.bfloat16),
        input_output_aliases={3: 0},
        compiler_params=pltpu.CompilerParams(vmem_limit_bytes=VMEM_LIMIT),
        cost_estimate=BRIEF,
        name="finish",
    )(rest, received, gates, so_far)


def body(
    queries,
    fresh_keys,
    fresh_values,
    paged_keys,
    paged_values,
    request_page_table,
    live_token_count,
    request_adapter_slot,
    adapters_in_use,
    adapter_pool_row,
    adapter_down_factors,
    adapter_up_factors,
    output_weight,
    gating,
):
    tp = lax.axis_size("tp")
    holders = lax.axis_size("req")
    me = lax.axis_index("tp").astype(jnp.int32)
    per_owner = live_token_count.shape[0] // tp

    def swap(array, flip):
        return lax.ppermute(array, "tp", [(s, s ^ flip) for s in range(tp)])

    def attend(flip, after=None):
        owners = ((me ^ flip ^ 1) * per_owner, (me ^ flip) * per_owner)
        return attend_four(
            queries,
            fresh_keys,
            fresh_values,
            paged_keys,
            paged_values,
            request_page_table,
            live_token_count,
            jnp.stack([owner + n for owner in owners for n in range(per_owner)]),
            after,
        )

    weight_other = swap(output_weight, 1)
    down_other = swap(adapter_down_factors, 1)
    cross_away, cross_here = attend(2)
    cross_other = swap(cross_away, 1)
    sent = project(cross_here, cross_other, output_weight, weight_other, CUTS, jnp.bfloat16)
    received = [swap(sent[0], 2)]

    own_away, own_here = attend(0, sent[0])
    own_other = swap(own_away, 1)
    pool = jnp.concatenate([adapter_up_factors, adapter_down_factors, down_other], axis=2)
    pool = jnp.broadcast_to(pool, (holders, *pool.shape[1:]))
    pool, _ = lax.optimization_barrier((pool, own_here))
    pool = lax.all_to_all(pool, "req", 0, 0, tiled=True)
    lookup = (request_adapter_slot, adapters_in_use, adapter_pool_row)
    second, own_ranks = ranks_and_part(
        (cross_here, cross_other),
        (own_here, own_other),
        pool,
        lookup,
        jnp.stack([me ^ 2, me]) * per_owner,
        sent[1],
    )
    received.append(swap(second, 2))
    last, received[0], _ = lax.optimization_barrier((sent[2], received[0], second))
    received.append(swap(last, 2))
    terms = adapter_terms(
        own_ranks, received[1], pool, lookup, gating, (me * per_owner).reshape(1)
    )
    out, rest = project_own(own_here, own_other, output_weight, weight_other, received[:2], terms)
    return finish(out, rest, received[2], terms[2])


def solution(mesh):
    return jax.shard_map(
        body,
        mesh=mesh,
        in_specs=(
            P("req", "tp"),
            P("req", "tp"),
            P("req", "tp"),
            P("req", None, "tp"),
            P("req", None, "tp"),
            P("req", None),
            P("req"),
            P("req"),
            P(),
            P(),
            P("req", None, "tp"),
            P("req", None, None),
            P("tp", None),
            P("req", None),
        ),
        out_specs=P(("req", "tp"), None),
        check_vma=False,
    )
```

```python
import math

import jax
import jax.numpy as jnp
from jax import lax
from jax.experimental import pallas as pl
from jax.experimental.pallas import tpu as pltpu
from jax.sharding import PartitionSpec as P

HD = 128
VMEM_LIMIT = 65280 * 1024
BLOCK = 512
CUTS = (3, 1, 1)
MASKED = -1e30
ANY = pl.BlockSpec(memory_space=pl.ANY)
BRIEF = pl.CostEstimate(flops=1000, bytes_accessed=1000, transcendentals=0)
HBM = pl.BlockSpec(memory_space=pltpu.HBM)


def attend_four(
    queries,
    fresh_keys,
    fresh_values,
    paged_keys,
    paged_values,
    request_page_table,
    live_token_count,
    requests,
    after=None,
):
    requests_here, pages = request_page_table.shape
    slots = queries.shape[0] // requests_here
    width = queries.shape[1]
    heads = width // HD
    pool_pages, page_rows = paged_keys.shape[:2]
    cached = pages * page_rows
    count = requests.shape[0]
    exponent_scale = math.log2(math.e) / math.sqrt(HD)

    def kernel(table, live, ids, q_hbm, fk_hbm, fv_hbm, pk_hbm, pv_hbm, *rest):
        outs, bufs = rest[-12:-10], rest[-10:]
        q_buf, fk_buf, fv_buf, pk_buf, pv_buf, score_buf, out_buf, order, in_sems, out_sems = bufs

        def fetch(src, dst, sem):
            return pltpu.make_async_copy(src, dst, in_sems.at[sem])

        def rows_of(n):
            return pl.ds(pl.multiple_of(ids[n] * slots, slots), slots)

        def query_copy(n):
            return fetch(q_hbm.at[rows_of(n)], q_buf.at[n], 3 * n)

        def key_copy(n):
            return fetch(fk_hbm.at[rows_of(n)], fk_buf.at[n], 3 * n + 1)

        def value_copy(n):
            return fetch(fv_hbm.at[rows_of(n)], fv_buf.at[n], 3 * n + 2)

        def key_page(m):
            page = order[m]
            return fetch(pk_hbm.at[page], pk_buf.at[page], 3 * count + 2 * m)

        def value_page(m):
            page = order[m]
            return fetch(pv_hbm.at[page], pv_buf.at[page], 3 * count + 2 * m + 1)

        def start(copies):
            for copy in copies:
                copy.start()

        for j in range(pages):
            order[j] = table[ids[0], j]
        start([query_copy(0), key_copy(0)] + [key_page(m) for m in range(pages)])
        start([value_copy(0)] + [value_page(m) for m in range(pages)])
        place = jnp.int32(pages)
        for page in range(pool_pages):
            taken = order[0] == page
            for j in range(1, pages):
                taken = taken | (order[j] == page)

            @pl.when(jnp.logical_not(taken))
            def _(place=place, page=page):
                order[place] = page

            place = place + jnp.where(taken, 0, 1)
        others = range(pages, pool_pages)
        start([query_copy(1), key_copy(1)] + [key_page(m) for m in others])
        start([value_copy(1)] + [value_page(m) for m in others])
        for n in range(2, count):
            start([query_copy(n), key_copy(n), value_copy(n)])

        def wait(make, indices):
            for index in indices:
                make(index).wait()

        def pair_of(u):
            per_two = heads
            first, step = 2 * (u // per_two), lax.rem(u, per_two)
            split = heads // 2
            lone = step == per_two - 1
            n = first + jnp.where(lone, 0, step // split)
            h = jnp.where(lone, heads - 1, 2 * lax.rem(step, split))
            return (n, h), (n + jnp.where(lone, 1, 0), h + jnp.where(lone, 0, 1))

        def lanes(h):
            return pl.ds(pl.multiple_of(h * HD, HD), HD)

        def side_by_side(pool, fresh, duo):
            return jnp.concatenate(
                [
                    jnp.concatenate(
                        [pool[table[ids[n], j], :, lanes(h)] for j in range(pages)]
                        + [fresh[n, :, lanes(h)]],
                        axis=0,
                    )
                    for n, h in duo
                ],
                axis=1,
            )

        def score(duo):
            (n, h), (other_n, other_h) = duo
            blank = jnp.zeros((slots, HD), jnp.bfloat16)
            diagonal = jnp.concatenate(
                [
                    jnp.concatenate([q_buf[n, :, lanes(h)], blank], axis=1),
                    jnp.concatenate([blank, q_buf[other_n, :, lanes(other_h)]], axis=1),
                ],
                axis=0,
            )
            return lax.dot_general(
                diagonal,
                side_by_side(pk_buf, fk_buf, duo),
                (((1,), (1,)), ((), ())),
                preferred_element_type=jnp.float32,
            )

        def weigh(duo, scores):
            column = lax.broadcasted_iota(jnp.int32, (slots, slots), 1)
            usable = jnp.concatenate([column < live[ids[n]] for n, _ in duo], axis=0)
            scores = jnp.concatenate(
                [scores[:, :cached], jnp.where(usable, scores[:, cached:], MASKED)], axis=1
            )
            peak = jnp.max(scores, axis=1, keepdims=True)
            weights = jnp.exp2((scores - peak) * exponent_scale)
            return weights.astype(jnp.bfloat16), jnp.sum(weights, axis=1, keepdims=True)

        def blend(duo, weights, row_total):
            blended = jnp.dot(
                weights, side_by_side(pv_buf, fv_buf, duo), preferred_element_type=jnp.float32
            )
            row = lax.broadcasted_iota(jnp.int32, (slots, HD), 0)
            for m, (n, h) in enumerate(duo):
                rows = slice(m * slots, (m + 1) * slots)
                attended = blended[rows, m * HD : (m + 1) * HD] / row_total[rows]
                attended = jnp.where(row < live[ids[n]], attended, 0.0)
                out_buf[
                    pl.ds(pl.multiple_of(n * slots, slots), slots), lanes(h)
                ] = attended.astype(jnp.bfloat16)

        units = count * heads // 2
        half = count // 2 * slots
        stores = [
            pltpu.make_async_copy(out_buf.at[pl.ds(m * half, half)], outs[m], out_sems.at[m])
            for m in range(2)
        ]
        wait(query_copy, [0])
        wait(key_copy, [0])
        wait(key_page, range(pages))
        score_buf[0] = score(pair_of(jnp.int32(0)))

        def step(u, _):
            @pl.when(u == 0)
            def _():
                wait(value_copy, [0])
                wait(value_page, range(pages))

            @pl.when(u == heads // 2 - 1)
            def _():
                wait(query_copy, range(1, count))
                wait(key_copy, range(1, count))
                wait(key_page, others)

            @pl.when(u == heads // 2)
            def _():
                wait(value_copy, range(1, count))
                wait(value_page, others)

            @pl.when(u == units // 2)
            def _():
                stores[0].start()

            duo = pair_of(u)
            score_buf[lax.rem(u + 1, 2)] = score(pair_of(jnp.minimum(u + 1, units - 1)))
            weights, row_total = weigh(duo, score_buf[lax.rem(u, 2)])
            blend(duo, weights, row_total)
            return 0

        lax.fori_loop(0, units, step, 0)
        stores[1].start()
        for store in stores:
            store.wait()

    extra = () if after is None else (after,)
    out_shape = jax.ShapeDtypeStruct((count // 2 * slots, width), jnp.bfloat16)
    return pl.pallas_call(
        kernel,
        grid_spec=pltpu.PrefetchScalarGridSpec(
            num_scalar_prefetch=3,
            grid=(1,),
            in_specs=[HBM] * 5 + [ANY] * len(extra),
            out_specs=[HBM] * 2,
            scratch_shapes=[
                pltpu.VMEM((count, slots, width), jnp.bfloat16),
                pltpu.VMEM((count, slots, width), jnp.bfloat16),
                pltpu.VMEM((count, slots, width), jnp.bfloat16),
                pltpu.VMEM(paged_keys.shape, jnp.bfloat16),
                pltpu.VMEM(paged_values.shape, jnp.bfloat16),
                pltpu.VMEM((2, 2 * slots, cached + slots), jnp.float32),
                pltpu.VMEM((count * slots, width), jnp.bfloat16),
                pltpu.SMEM((pool_pages,), jnp.int32),
                pltpu.SemaphoreType.DMA((3 * count + 2 * pool_pages,)),
                pltpu.SemaphoreType.DMA((2,)),
            ],
        ),
        out_shape=[out_shape] * 2,
        compiler_params=pltpu.CompilerParams(vmem_limit_bytes=VMEM_LIMIT),
        cost_estimate=BRIEF,
        name="attend",
    )(
        request_page_table,
        live_token_count,
        requests,
        queries,
        fresh_keys,
        fresh_values,
        paged_keys,
        paged_values,
        *extra,
    )


def project(own, other, weight, weight_other, cuts, kind):
    rows, width = own.shape
    columns = weight.shape[1]
    blocks = columns // BLOCK
    bounds = [sum(cuts[:n]) for n in range(len(cuts) + 1)]
    assert bounds[-1] == blocks

    def kernel(a_hbm, b_hbm, w, u, *rest):
        outs, (a, b, w_buf, out_buf, own_sems, in_sems, out_sems) = (
            rest[: len(cuts)],
            rest[len(cuts) :],
        )

        def fetch(n):
            here = pl.ds(n * BLOCK, BLOCK)
            return [
                pltpu.make_async_copy(
                    src.at[:, here], w_buf.at[pl.ds(m * width, width), here], in_sems.at[n, m]
                )
                for m, src in enumerate((w, u))
            ]

        def store(n):
            part = max(m for m in range(len(cuts)) if bounds[m] <= n)
            return pltpu.make_async_copy(
                out_buf.at[:, pl.ds(n * BLOCK, BLOCK)],
                outs[part].at[:, pl.ds((n - bounds[part]) * BLOCK, BLOCK)],
                out_sems.at[n],
            )

        features = [
            pltpu.make_async_copy(src, dst, own_sems.at[m])
            for m, (src, dst) in enumerate(((a_hbm, a), (b_hbm, b)))
        ]
        for copy in features:
            copy.start()
        for n in range(blocks):
            for copy in fetch(n):
                copy.start()
        for copy in features:
            copy.wait()
        for n in range(blocks):
            for copy in fetch(n):
                copy.wait()
            here = slice(n * BLOCK, (n + 1) * BLOCK)
            out_buf[:, here] = jnp.dot(
                jnp.concatenate([a[...], b[...]], axis=1),
                w_buf[:, here],
                preferred_element_type=jnp.float32,
            ).astype(kind)
            store(n).start()
        for n in range(blocks):
            store(n).wait()

    return pl.pallas_call(
        kernel,
        in_specs=[HBM] * 4,
        out_specs=[HBM] * len(cuts),
        out_shape=[jax.ShapeDtypeStruct((rows, cut * BLOCK), kind) for cut in cuts],
        scratch_shapes=[
            pltpu.VMEM((rows, width), jnp.bfloat16),
            pltpu.VMEM((rows, width), jnp.bfloat16),
            pltpu.VMEM((2 * width, columns), jnp.bfloat16),
            pltpu.VMEM((rows, columns), kind),
            pltpu.SemaphoreType.DMA((2,)),
            pltpu.SemaphoreType.DMA((blocks, 2)),
            pltpu.SemaphoreType.DMA((blocks,)),
        ],
        compiler_params=pltpu.CompilerParams(vmem_limit_bytes=VMEM_LIMIT),
        cost_estimate=BRIEF,
        name="project",
    )(own, other, weight, weight_other)


def pool_place(request, req, slot, in_use, pool_row, holders):
    row, me, pairs = pool_row[in_use[slot[request]]], req[0], holders // 2
    return 2 * lax.rem(me // 2 - row // 2 + pairs, pairs) + ((row ^ me) & 1)


def ranks_and_part(cross, own, pools, lookup, first_requests, part):
    rows, width = cross[0].shape
    slots = rows // 2
    holders, rank = pools[0].shape[:2]
    assert part.shape[1] == 4 * slots
    down_block = pools[0].shape[2] // width - 1

    def kernel(first, req, slot, in_use, pool_row, *refs):
        downs, blocks, part_in, part_out, own_ranks = refs[:8], refs[8:12], *refs[12:]
        part_out[:rows] = part_in[...]
        for i in range(2):
            here = slice(i * slots, (i + 1) * slots)
            for n in range(2):
                acts = sum(
                    lax.dot_general(
                        downs[4 * n + 2 * i + m][0],
                        blocks[2 * n + m][here],
                        (((1,), (1,)), ((), ())),
                        preferred_element_type=jnp.float32,
                    )
                    for m in range(2)
                )
                if n:
                    own_ranks[i] = acts
                    continue
                high = acts.astype(jnp.bfloat16)
                low = (acts - high.astype(jnp.float32)).astype(jnp.bfloat16)
                part_out[rows:, 2 * i * slots : (2 * i + 1) * slots] = high
                part_out[rows:, (2 * i + 1) * slots : (2 * i + 2) * slots] = low

    def down_spec(n, i):
        return pl.BlockSpec(
            (1, rank, width),
            lambda s, first, *look: (pool_place(first[n] + i, *look, holders), 0, down_block),
        )

    def whole(*shape):
        return pl.BlockSpec(shape, lambda s, *_: (0,) * len(shape))

    return pl.pallas_call(
        kernel,
        grid_spec=pltpu.PrefetchScalarGridSpec(
            num_scalar_prefetch=5,
            grid=(1,),
            in_specs=[down_spec(n, i) for n in range(2) for i in range(2) for _ in pools]
            + [whole(rows, width)] * 4
            + [whole(*part.shape)],
            out_specs=[whole(rows + rank, part.shape[1]), whole(2, rank, slots)],
        ),
        out_shape=[
            jax.ShapeDtypeStruct((rows + rank, part.shape[1]), jnp.bfloat16),
            jax.ShapeDtypeStruct((2, rank, slots), jnp.float32),
        ],
        compiler_params=pltpu.CompilerParams(vmem_limit_bytes=VMEM_LIMIT),
        cost_estimate=BRIEF,
        name="ranks_and_part",
    )(first_requests, *lookup, *(list(pools) * 4), *cross, *own, part)


def adapter_terms(own_ranks, received, pools, core, lookup, gating, first_request):
    requests, rank, slots = own_ranks.shape
    rows = requests * slots
    columns = gating.shape[1]
    half = columns // 2
    holders = pools[0].shape[0]

    def kernel(first, core, req, slot, in_use, pool_row, own, other, *refs):
        m0, m1, t0, t1, gate, acts, ups, gates = refs
        acts[...] = jnp.zeros_like(acts)
        gates[...] = jnp.zeros_like(gates)
        for i, halves in enumerate(((m0, t0), (m1, t1))):
            total = own[i]
            for m in range(2 * i, 2 * i + 2):
                total += other[:, m * slots : (m + 1) * slots].astype(jnp.float32)
            high = total.astype(jnp.bfloat16).astype(jnp.float32)
            pair = jnp.concatenate([high, total - high], axis=0).T.astype(jnp.bfloat16)
            acts[i * slots : (i + 1) * slots, 2 * rank * i : 2 * rank * (i + 1)] = pair
            for m in range(2):
                for away, up in enumerate(halves):
                    there = pl.ds(pl.multiple_of((core[0] ^ away) * half, half), half)
                    ups[(2 * i + m) * rank : (2 * i + m + 1) * rank, there] = up[0]
            gates[i : i + 1] = gate[pl.ds(first[0] + i, 1), :]

    def up_spec(i):
        return pl.BlockSpec(
            (1, rank, half),
            lambda s, first, core, *look: (pool_place(first[0] + i, *look, holders), 0, 0),
        )

    def whole(*shape):
        return pl.BlockSpec(shape, lambda s, *_: (0,) * len(shape))

    return pl.pallas_call(
        kernel,
        grid_spec=pltpu.PrefetchScalarGridSpec(
            num_scalar_prefetch=6,
            grid=(1,),
            in_specs=[
                whole(*own_ranks.shape),
                pl.BlockSpec((rank, received.shape[1]), lambda s, *_: (rows // rank, 0)),
                up_spec(0),
                up_spec(1),
                up_spec(0),
                up_spec(1),
                whole(*gating.shape),
            ],
            out_specs=[
                whole(rows, 2 * requests * rank),
                whole(2 * requests * rank, columns),
                whole(8, columns),
            ],
        ),
        out_shape=[
            jax.ShapeDtypeStruct((rows, 2 * requests * rank), jnp.bfloat16),
            jax.ShapeDtypeStruct((2 * requests * rank, columns), jnp.bfloat16),
            jax.ShapeDtypeStruct((8, columns), jnp.float32),
        ],
        compiler_params=pltpu.CompilerParams(vmem_limit_bytes=VMEM_LIMIT),
        cost_estimate=BRIEF,
        name="adapter_terms",
    )(
        first_request,
        core,
        *lookup,
        own_ranks,
        received,
        pools[0],
        pools[0],
        pools[1],
        pools[1],
        gating,
    )


def project_own(own, other, weight, weight_other, received, terms):
    acts, ups, gates = terms
    rows, width = own.shape
    columns = weight.shape[1]
    blocks = columns // BLOCK
    parts = [part.shape[1] for part in received]
    arrived = sum(parts)
    covered = arrived // BLOCK
    slots = rows // 2

    def kernel(a_hbm, b_hbm, w, u, acts_hbm, ups_hbm, gates_hbm, *refs):
        parts_hbm, (out, rest_out), bufs = refs[:-14], refs[-14:-12], refs[-12:]
        a, b, w_buf, part, acts, ups, gates, out_buf, rest_buf, own_sems, in_sems, out_sems = bufs

        def fetch(n):
            here = pl.ds(n * BLOCK, BLOCK)
            return [
                pltpu.make_async_copy(
                    src.at[:, here], w_buf.at[pl.ds(m * width, width), here], in_sems.at[n, m]
                )
                for m, src in enumerate((w, u))
            ]

        def store(n):
            here = pl.ds(n * BLOCK, BLOCK)
            if n < covered:
                src, dst = out_buf.at[:, here], out.at[:, here]
            else:
                there = pl.ds((n - covered) * BLOCK, BLOCK)
                src, dst = rest_buf.at[:, there], rest_out.at[:, there]
            return pltpu.make_async_copy(src, dst, out_sems.at[n])

        whole = ((a_hbm, a), (b_hbm, b), (acts_hbm, acts), (ups_hbm, ups), (gates_hbm, gates))
        for n, part_hbm in enumerate(parts_hbm):
            there = pl.ds(sum(parts[:n]), parts[n])
            whole += ((part_hbm.at[pl.ds(0, rows)], part.at[:, there]),)
        whole = [
            pltpu.make_async_copy(src, dst, own_sems.at[m]) for m, (src, dst) in enumerate(whole)
        ]
        for copy in whole:
            copy.start()
        for n in range(blocks):
            for copy in fetch(n):
                copy.start()
        for copy in whole:
            copy.wait()
        for n in range(blocks):
            for copy in fetch(n):
                copy.wait()
            here = slice(n * BLOCK, (n + 1) * BLOCK)
            update = jnp.dot(
                jnp.concatenate([a[...], b[...]], axis=1),
                w_buf[:, here],
                preferred_element_type=jnp.float32,
            )
            update += jnp.dot(acts[...], ups[:, here], preferred_element_type=jnp.float32)
            if n < covered:
                update += part[:, here].astype(jnp.float32)
            for i in range(2):
                those = slice(i * slots, (i + 1) * slots)
                gated = update[those] * gates[i : i + 1, here]
                if n < covered:
                    out_buf[those, here] = gated.astype(jnp.bfloat16)
                else:
                    there = slice((n - covered) * BLOCK, (n - covered + 1) * BLOCK)
                    rest_buf[those, there] = gated
            store(n).start()
        for n in range(blocks):
            store(n).wait()

    left = columns - arrived
    return pl.pallas_call(
        kernel,
        in_specs=[HBM] * (7 + len(received)),
        out_specs=[HBM] * 2,
        out_shape=[
            jax.ShapeDtypeStruct((rows, columns), jnp.bfloat16),
            jax.ShapeDtypeStruct((rows, left), jnp.float32),
        ],
        scratch_shapes=[
            pltpu.VMEM((rows, width), jnp.bfloat16),
            pltpu.VMEM((rows, width), jnp.bfloat16),
            pltpu.VMEM((2 * width, columns), jnp.bfloat16),
            pltpu.VMEM((rows, arrived), jnp.bfloat16),
            pltpu.VMEM(acts.shape, jnp.bfloat16),
            pltpu.VMEM(ups.shape, jnp.bfloat16),
            pltpu.VMEM(gates.shape, jnp.float32),
            pltpu.VMEM((rows, arrived), jnp.bfloat16),
            pltpu.VMEM((rows, left), jnp.float32),
            pltpu.SemaphoreType.DMA((5 + len(received),)),
            pltpu.SemaphoreType.DMA((blocks, 2)),
            pltpu.SemaphoreType.DMA((blocks,)),
        ],
        compiler_params=pltpu.CompilerParams(vmem_limit_bytes=VMEM_LIMIT),
        cost_estimate=BRIEF,
        name="project_own",
    )(own, other, weight, weight_other, acts, ups, gates, *received)


def finish(so_far, rest, received, gates):
    rows, columns = so_far.shape
    wide = rest.shape[1]
    assert columns % wide == 0
    at = columns // wide - 1
    slots = rows // 2

    def kernel(sums, part, gate, so_far, out):
        for i in range(2):
            here = slice(i * slots, (i + 1) * slots)
            update = sums[here] + part[here].astype(jnp.float32) * gate[i : i + 1]
            out[here] = update.astype(jnp.bfloat16)

    return pl.pallas_call(
        kernel,
        grid=(1,),
        in_specs=[
            pl.BlockSpec((rows, wide), lambda j: (0, 0)),
            pl.BlockSpec((rows, wide), lambda j: (0, 0)),
            pl.BlockSpec((gates.shape[0], wide), lambda j: (0, at)),
            ANY,
        ],
        out_specs=pl.BlockSpec((rows, wide), lambda j: (0, at)),
        out_shape=jax.ShapeDtypeStruct((rows, columns), jnp.bfloat16),
        input_output_aliases={3: 0},
        compiler_params=pltpu.CompilerParams(vmem_limit_bytes=VMEM_LIMIT),
        cost_estimate=BRIEF,
        name="finish",
    )(rest, received, gates, so_far)


def body(
    queries,
    fresh_keys,
    fresh_values,
    paged_keys,
    paged_values,
    request_page_table,
    live_token_count,
    request_adapter_slot,
    adapters_in_use,
    adapter_pool_row,
    adapter_down_factors,
    adapter_up_factors,
    output_weight,
    gating,
):
    tp = lax.axis_size("tp")
    holders = lax.axis_size("req")
    me = lax.axis_index("tp").astype(jnp.int32)
    core = lax.rem(me, 2)
    per_owner = live_token_count.shape[0] // tp
    columns = output_weight.shape[1]

    def swap(array, flip):
        return lax.ppermute(array, "tp", [(s, s ^ flip) for s in range(tp)])

    def attend(flip, after=None):
        owners = ((me ^ flip ^ 1) * per_owner, (me ^ flip) * per_owner)
        return attend_four(
            queries,
            fresh_keys,
            fresh_values,
            paged_keys,
            paged_values,
            request_page_table,
            live_token_count,
            jnp.stack([owner + n for owner in owners for n in range(per_owner)]),
            after,
        )

    weight_other = swap(output_weight, 1)
    cross_away, cross_here = attend(2)
    cross_other = swap(cross_away, 1)
    sent = project(cross_here, cross_other, output_weight, weight_other, CUTS, jnp.bfloat16)
    received = [swap(sent[0], 2)]

    half = columns // 2
    up_half = lax.dynamic_slice_in_dim(adapter_up_factors, core * half, half, 2)
    pair = jnp.concatenate([up_half, adapter_down_factors], axis=2)
    pair, _ = lax.optimization_barrier((pair, cross_away))
    moved = lax.ppermute(pair, "req", [(s, s ^ 1) for s in range(holders)])
    pair, moved, _ = lax.optimization_barrier((pair, moved, sent[0]))
    pair = jnp.concatenate([pair, moved], axis=0)
    pool = [pair] + [
        lax.ppermute(pair, "req", [(s, (s + d) % holders) for s in range(holders)])
        for d in range(2, holders, 2)
    ]
    own_away, own_here = attend(0, pair)
    own_other = swap(own_away, 1)
    *pool, _ = lax.optimization_barrier((*pool, own_here))
    pool = jnp.concatenate(pool, axis=0)
    pools = (pool, swap(pool, 1))
    lookup = (
        lax.axis_index("req").astype(jnp.int32).reshape(1),
        request_adapter_slot,
        adapters_in_use,
        adapter_pool_row,
    )
    second, own_ranks = ranks_and_part(
        (cross_here, cross_other),
        (own_here, own_other),
        pools,
        lookup,
        jnp.stack([me ^ 2, me]) * per_owner,
        sent[1],
    )
    received.append(swap(second, 2))
    last, received[0], _ = lax.optimization_barrier((sent[2], received[0], second))
    received.append(swap(last, 2))
    terms = adapter_terms(
        own_ranks,
        received[1],
        pools,
        core.reshape(1),
        lookup,
        gating,
        (me * per_owner).reshape(1),
    )
    out, rest = project_own(own_here, own_other, output_weight, weight_other, received[:2], terms)
    return finish(out, rest, received[2], terms[2])


def solution(mesh):
    return jax.shard_map(
        body,
        mesh=mesh,
        in_specs=(
            P("req", "tp"),
            P("req", "tp"),
            P("req", "tp"),
            P("req", None, "tp"),
            P("req", None, "tp"),
            P("req", None),
            P("req"),
            P("req"),
            P(),
            P(),
            P("req", None, "tp"),
            P("req", None, None),
            P("tp", None),
            P("req", None),
        ),
        out_specs=P(("req", "tp"), None),
        check_vma=False,
    )
```

```python
import math

import jax
import jax.numpy as jnp
from jax import lax
from jax.experimental import pallas as pl
from jax.experimental.pallas import tpu as pltpu
from jax.sharding import PartitionSpec as P

HD = 128
VMEM_LIMIT = 40 * 1024 * 1024
BLOCK = 512
CUTS = (3, 1, 1)
MASKED = -1e30
ANY = pl.BlockSpec(memory_space=pl.ANY)
BRIEF = pl.CostEstimate(flops=1000, bytes_accessed=1000, transcendentals=0)
HBM = pl.BlockSpec(memory_space=pltpu.HBM)
VMEM = pl.BlockSpec(memory_space=pltpu.VMEM)


def in_hbm(array):
    return pltpu.with_memory_space_constraint(array, pltpu.HBM)


def in_vmem(array):
    return pltpu.with_memory_space_constraint(array, pltpu.VMEM)


def attend_four(
    queries,
    fresh_keys,
    fresh_values,
    paged_keys,
    paged_values,
    request_page_table,
    live_token_count,
    requests,
    after=None,
):
    requests_here, pages = request_page_table.shape
    slots = queries.shape[0] // requests_here
    width = queries.shape[1]
    heads = width // HD
    pool_pages, page_rows = paged_keys.shape[:2]
    cached = pages * page_rows
    count = requests.shape[0]
    per_out = count // 2
    exponent_scale = math.log2(math.e) / math.sqrt(HD)

    def kernel(table, live, ids, q_hbm, fk_hbm, fv_hbm, pk_hbm, pv_hbm, *rest):
        outs, bufs = rest[-9:-7], rest[-7:]
        q_buf, fk_buf, fv_buf, pk_buf, pv_buf, order, in_sems = bufs

        def fetch(src, dst, sem):
            return pltpu.make_async_copy(src, dst, in_sems.at[sem])

        def rows_of(n):
            return pl.ds(pl.multiple_of(ids[n] * slots, slots), slots)

        def query_copy(n):
            return fetch(q_hbm.at[rows_of(n)], q_buf.at[n], 3 * n)

        def key_copy(n):
            return fetch(fk_hbm.at[rows_of(n)], fk_buf.at[n], 3 * n + 1)

        def value_copy(n):
            return fetch(fv_hbm.at[rows_of(n)], fv_buf.at[n], 3 * n + 2)

        def key_page(m):
            page = order[m]
            return fetch(pk_hbm.at[page], pk_buf.at[page], 3 * count + 2 * m)

        def value_page(m):
            page = order[m]
            return fetch(pv_hbm.at[page], pv_buf.at[page], 3 * count + 2 * m + 1)

        def start(copies):
            for copy in copies:
                copy.start()

        for j in range(pages):
            order[j] = table[ids[0], j]
        start([query_copy(0), key_copy(0)] + [key_page(m) for m in range(pages)])
        start([value_copy(0)] + [value_page(m) for m in range(pages)])
        place = jnp.int32(pages)
        for page in range(pool_pages):
            taken = order[0] == page
            for j in range(1, pages):
                taken = taken | (order[j] == page)

            @pl.when(jnp.logical_not(taken))
            def _(place=place, page=page):
                order[place] = page

            place = place + jnp.where(taken, 0, 1)
        others = range(pages, pool_pages)
        start([query_copy(1), key_copy(1)] + [key_page(m) for m in others])
        start([value_copy(1)] + [value_page(m) for m in others])
        for n in range(2, count):
            start([query_copy(n), key_copy(n), value_copy(n)])

        waited = set()

        def wait(name, make, indices):
            if name not in waited:
                waited.add(name)
                for index in indices:
                    make(index).wait()

        def keys_ready(duo):
            for n, _ in duo:
                wait(("q", n), query_copy, [n])
                wait(("k", n), key_copy, [n])
                wait(("first k",), key_page, range(pages))
                if n:
                    wait(("other k",), key_page, others)

        def values_ready(duo):
            for n, _ in duo:
                wait(("v", n), value_copy, [n])
                wait(("first v",), value_page, range(pages))
                if n:
                    wait(("other v",), value_page, others)

        def lanes(h, several=1):
            return slice(h * HD, (h + several) * HD)

        def gather(pool, fresh, n, here):
            return jnp.concatenate(
                [pool[table[ids[n], j], :, here] for j in range(pages)] + [fresh[n, :, here]],
                axis=0,
            )

        def side_by_side(pool, fresh, duo):
            (n, h), (other_n, other_h) = duo
            if n == other_n and other_h == h + 1:
                return gather(pool, fresh, n, lanes(h, 2))
            return jnp.concatenate(
                [gather(pool, fresh, m, lanes(g)) for m, g in duo],
                axis=1,
            )

        def score(duo):
            (n, h), (other_n, other_h) = duo
            blank = jnp.zeros((slots, HD), jnp.bfloat16)
            diagonal = jnp.concatenate(
                [
                    jnp.concatenate([q_buf[n, :, lanes(h)], blank], axis=1),
                    jnp.concatenate([blank, q_buf[other_n, :, lanes(other_h)]], axis=1),
                ],
                axis=0,
            )
            return lax.dot_general(
                diagonal,
                side_by_side(pk_buf, fk_buf, duo),
                (((1,), (1,)), ((), ())),
                preferred_element_type=jnp.float32,
            )

        def weigh(duo, scores):
            column = lax.broadcasted_iota(jnp.int32, (slots, slots), 1)
            usable = jnp.concatenate([column < live[ids[n]] for n, _ in duo], axis=0)
            scores = jnp.concatenate(
                [scores[:, :cached], jnp.where(usable, scores[:, cached:], MASKED)], axis=1
            )
            peak = jnp.max(scores, axis=1, keepdims=True)
            weights = jnp.exp2((scores - peak) * exponent_scale)
            return weights.astype(jnp.bfloat16), jnp.sum(weights, axis=1, keepdims=True)

        def blend(duo, weights, row_total):
            blended = jnp.dot(
                weights, side_by_side(pv_buf, fv_buf, duo), preferred_element_type=jnp.float32
            )
            row = lax.broadcasted_iota(jnp.int32, (slots, HD), 0)
            for m, (n, h) in enumerate(duo):
                rows = slice(m * slots, (m + 1) * slots)
                attended = blended[rows, lanes(m)] / row_total[rows]
                attended = jnp.where(row < live[ids[n]], attended, 0.0)
                place = (n % per_out) * slots
                outs[n // per_out][place : place + slots, lanes(h)] = attended.astype(jnp.bfloat16)

        units = []
        for first in range(0, count, 2):
            units += [((n, h), (n, h + 1)) for n in (first, first + 1) for h in range(0, heads - 1, 2)]
            if heads % 2:
                units.append(((first, heads - 1), (first + 1, heads - 1)))
        keys_ready(units[0])
        scores = score(units[0])
        for u, duo in enumerate(units):
            later = None
            if u + 1 < len(units):
                keys_ready(units[u + 1])
                later = score(units[u + 1])
            weights, row_total = weigh(duo, scores)
            values_ready(duo)
            blend(duo, weights, row_total)
            scores = later

    extra = () if after is None else (after,)
    out_shape = pltpu.VMEM((per_out * slots, width), jnp.bfloat16)
    return pl.pallas_call(
        kernel,
        grid_spec=pltpu.PrefetchScalarGridSpec(
            num_scalar_prefetch=3,
            grid=(1,),
            in_specs=[HBM] * 5 + [ANY] * len(extra),
            out_specs=[VMEM] * 2,
            scratch_shapes=[
                pltpu.VMEM((count, slots, width), jnp.bfloat16),
                pltpu.VMEM((count, slots, width), jnp.bfloat16),
                pltpu.VMEM((count, slots, width), jnp.bfloat16),
                pltpu.VMEM(paged_keys.shape, jnp.bfloat16),
                pltpu.VMEM(paged_values.shape, jnp.bfloat16),
                pltpu.SMEM((pool_pages,), jnp.int32),
                pltpu.SemaphoreType.DMA((3 * count + 2 * pool_pages,)),
            ],
        ),
        out_shape=[out_shape] * 2,
        compiler_params=pltpu.CompilerParams(vmem_limit_bytes=VMEM_LIMIT),
        cost_estimate=BRIEF,
        name="attend",
    )(
        request_page_table,
        live_token_count,
        requests,
        *map(in_hbm, (queries, fresh_keys, fresh_values, paged_keys, paged_values)),
        *extra,
    )


def project(own, other, weight, weight_other, cuts):
    rows = own.shape[0]
    bounds = [sum(cuts[:n]) for n in range(len(cuts) + 1)]
    assert bounds[-1] * BLOCK == weight.shape[1]

    def kernel(a, b, w, u, *outs):
        features = jnp.concatenate([a[...], b[...]], axis=1)
        for part, out in enumerate(outs):
            for n in range(cuts[part]):
                here = slice((bounds[part] + n) * BLOCK, (bounds[part] + n + 1) * BLOCK)
                out[:, n * BLOCK : (n + 1) * BLOCK] = jnp.dot(
                    features,
                    jnp.concatenate([w[:, here], u[:, here]], axis=0),
                    preferred_element_type=jnp.float32,
                ).astype(jnp.bfloat16)

    return pl.pallas_call(
        kernel,
        in_specs=[VMEM] * 4,
        out_specs=[VMEM] * len(cuts),
        out_shape=[pltpu.VMEM((rows, cut * BLOCK), jnp.bfloat16) for cut in cuts],
        compiler_params=pltpu.CompilerParams(vmem_limit_bytes=VMEM_LIMIT),
        cost_estimate=BRIEF,
        name="project",
    )(own, other, in_vmem(weight), in_vmem(weight_other))


def pool_place(request, slot, in_use, pool_row):
    return pool_row[in_use[slot[request]]]


def ranks_and_part(cross, own, pool, lookup, first_requests, part):
    rows, width = cross[0].shape
    slots = rows // 2
    rank = pool.shape[1]
    assert part.shape[1] == 4 * slots
    down_block = pool.shape[2] // width - 2

    def kernel(first, slot, in_use, pool_row, *refs):
        downs, blocks, part_in, part_out, own_ranks = refs[:8], refs[8:12], *refs[12:]
        part_out[:rows] = part_in[...]
        for i in range(2):
            here = slice(i * slots, (i + 1) * slots)
            for n in range(2):
                acts = sum(
                    lax.dot_general(
                        downs[4 * n + 2 * i + m][0],
                        blocks[2 * n + m][here],
                        (((1,), (1,)), ((), ())),
                        preferred_element_type=jnp.float32,
                    )
                    for m in range(2)
                )
                if n:
                    own_ranks[i] = acts
                    continue
                high = acts.astype(jnp.bfloat16)
                low = (acts - high.astype(jnp.float32)).astype(jnp.bfloat16)
                part_out[rows:, 2 * i * slots : (2 * i + 1) * slots] = high
                part_out[rows:, (2 * i + 1) * slots : (2 * i + 2) * slots] = low

    def down_spec(n, i, m):
        return pl.BlockSpec(
            (1, rank, width),
            lambda s, first, *look: (pool_place(first[n] + i, *look), 0, down_block + m),
        )

    def whole(*shape):
        return pl.BlockSpec(shape, lambda s, *_: (0,) * len(shape))

    return pl.pallas_call(
        kernel,
        grid_spec=pltpu.PrefetchScalarGridSpec(
            num_scalar_prefetch=4,
            grid=(1,),
            in_specs=[down_spec(n, i, m) for n in range(2) for i in range(2) for m in range(2)]
            + [whole(rows, width)] * 4
            + [whole(*part.shape)],
            out_specs=[whole(rows + rank, part.shape[1]), whole(2, rank, slots)],
        ),
        out_shape=[
            jax.ShapeDtypeStruct((rows + rank, part.shape[1]), jnp.bfloat16),
            jax.ShapeDtypeStruct((2, rank, slots), jnp.float32),
        ],
        compiler_params=pltpu.CompilerParams(vmem_limit_bytes=VMEM_LIMIT),
        cost_estimate=BRIEF,
        name="ranks_and_part",
    )(first_requests, *lookup, *([pool] * 8), *cross, *own, part)


def adapter_terms(own_ranks, received, pool, lookup, gating, first_request):
    requests, rank, slots = own_ranks.shape
    rows = requests * slots
    columns = gating.shape[1]

    def kernel(first, slot, in_use, pool_row, own, other, up_0, up_1, gate, acts, ups, gates):
        acts[...] = jnp.zeros_like(acts)
        gates[...] = jnp.zeros_like(gates)
        for i, up in enumerate((up_0, up_1)):
            total = own[i]
            for m in range(2 * i, 2 * i + 2):
                total += other[:, m * slots : (m + 1) * slots].astype(jnp.float32)
            high = total.astype(jnp.bfloat16).astype(jnp.float32)
            pair = jnp.concatenate([high, total - high], axis=0).T.astype(jnp.bfloat16)
            acts[i * slots : (i + 1) * slots, 2 * rank * i : 2 * rank * (i + 1)] = pair
            for m in range(2):
                ups[(2 * i + m) * rank : (2 * i + m + 1) * rank] = up[0]
            gates[i : i + 1] = gate[pl.ds(first[0] + i, 1), :]

    def up_spec(i):
        return pl.BlockSpec(
            (1, rank, columns), lambda s, first, *look: (pool_place(first[0] + i, *look), 0, 0)
        )

    def whole(*shape):
        return pl.BlockSpec(shape, lambda s, *_: (0,) * len(shape))

    return pl.pallas_call(
        kernel,
        grid_spec=pltpu.PrefetchScalarGridSpec(
            num_scalar_prefetch=4,
            grid=(1,),
            in_specs=[
                whole(*own_ranks.shape),
                pl.BlockSpec((rank, received.shape[1]), lambda s, *_: (rows // rank, 0)),
                up_spec(0),
                up_spec(1),
                whole(*gating.shape),
            ],
            out_specs=[
                whole(rows, 2 * requests * rank),
                whole(2 * requests * rank, columns),
                whole(8, columns),
            ],
        ),
        out_shape=[
            jax.ShapeDtypeStruct((rows, 2 * requests * rank), jnp.bfloat16),
            jax.ShapeDtypeStruct((2 * requests * rank, columns), jnp.bfloat16),
            jax.ShapeDtypeStruct((8, columns), jnp.float32),
        ],
        compiler_params=pltpu.CompilerParams(vmem_limit_bytes=VMEM_LIMIT),
        cost_estimate=BRIEF,
        name="adapter_terms",
    )(first_request, *lookup, own_ranks, received, pool, pool, gating)


def project_own(own, other, weight, weight_other, received, terms):
    acts, ups, gates = terms
    rows, width = own.shape
    columns = weight.shape[1]
    blocks = columns // BLOCK
    bounds = [0]
    for part in received:
        bounds.append(bounds[-1] + part.shape[1] // BLOCK)
    covered = bounds[-1]
    slots = rows // 2

    def kernel(a, b, w, u, acts, ups, gates, *refs):
        parts, (out, rest_out, out_buf, out_sems) = refs[:-4], refs[-4:]

        def store(n):
            here = pl.ds(n * BLOCK, BLOCK)
            return pltpu.make_async_copy(out_buf.at[:, here], out.at[:, here], out_sems.at[n])

        features = jnp.concatenate([a[...], b[...]], axis=1)
        for n in range(blocks):
            here = slice(n * BLOCK, (n + 1) * BLOCK)
            update = jnp.dot(
                features,
                jnp.concatenate([w[:, here], u[:, here]], axis=0),
                preferred_element_type=jnp.float32,
            )
            update += jnp.dot(acts[...], ups[:, here], preferred_element_type=jnp.float32)
            for m, part in enumerate(parts):
                if bounds[m] <= n < bounds[m + 1]:
                    there = slice((n - bounds[m]) * BLOCK, (n - bounds[m] + 1) * BLOCK)
                    update += part[:rows, there].astype(jnp.float32)
            for i in range(2):
                those = slice(i * slots, (i + 1) * slots)
                gated = update[those] * gates[i : i + 1, here]
                if n < covered:
                    out_buf[those, here] = gated.astype(jnp.bfloat16)
                else:
                    there = slice((n - covered) * BLOCK, (n - covered + 1) * BLOCK)
                    rest_out[those, there] = gated
            if n < covered:
                store(n).start()
        for n in range(covered):
            store(n).wait()

    left = columns - covered * BLOCK
    return pl.pallas_call(
        kernel,
        in_specs=[VMEM] * (7 + len(received)),
        out_specs=[HBM, VMEM],
        out_shape=[
            pltpu.HBM((rows, columns), jnp.bfloat16),
            pltpu.VMEM((rows, left), jnp.float32),
        ],
        scratch_shapes=[
            pltpu.VMEM((rows, covered * BLOCK), jnp.bfloat16),
            pltpu.SemaphoreType.DMA((covered,)),
        ],
        compiler_params=pltpu.CompilerParams(vmem_limit_bytes=VMEM_LIMIT),
        cost_estimate=BRIEF,
        name="project_own",
    )(own, other, in_vmem(weight), in_vmem(weight_other), acts, ups, gates, *received)


def finish(so_far, rest, received, gates):
    rows, columns = so_far.shape
    wide = rest.shape[1]
    assert columns % wide == 0
    at = columns // wide - 1
    slots = rows // 2

    def kernel(sums, part, gate, so_far, out):
        for i in range(2):
            here = slice(i * slots, (i + 1) * slots)
            update = sums[here] + part[here].astype(jnp.float32) * gate[i : i + 1]
            out[here] = update.astype(jnp.bfloat16)

    return pl.pallas_call(
        kernel,
        grid=(1,),
        in_specs=[
            pl.BlockSpec((rows, wide), lambda j: (0, 0)),
            pl.BlockSpec((rows, wide), lambda j: (0, 0)),
            pl.BlockSpec((gates.shape[0], wide), lambda j: (0, at)),
            ANY,
        ],
        out_specs=pl.BlockSpec((rows, wide), lambda j: (0, at)),
        out_shape=jax.ShapeDtypeStruct((rows, columns), jnp.bfloat16),
        input_output_aliases={3: 0},
        compiler_params=pltpu.CompilerParams(vmem_limit_bytes=VMEM_LIMIT),
        cost_estimate=BRIEF,
        name="finish",
    )(rest, received, gates, so_far)


def body(
    queries,
    fresh_keys,
    fresh_values,
    paged_keys,
    paged_values,
    request_page_table,
    live_token_count,
    request_adapter_slot,
    adapters_in_use,
    adapter_pool_row,
    adapter_down_factors,
    adapter_up_factors,
    output_weight,
    gating,
):
    tp = lax.axis_size("tp")
    me = lax.axis_index("tp").astype(jnp.int32)
    per_owner = live_token_count.shape[0] // tp

    def swap(array, flip):
        return lax.ppermute(array, "tp", [(s, s ^ flip) for s in range(tp)])

    def attend(flip, after=None):
        owners = ((me ^ flip ^ 1) * per_owner, (me ^ flip) * per_owner)
        return attend_four(
            queries,
            fresh_keys,
            fresh_values,
            paged_keys,
            paged_values,
            request_page_table,
            live_token_count,
            jnp.stack([owner + n for owner in owners for n in range(per_owner)]),
            after,
        )

    down_other = swap(adapter_down_factors, 1)
    pool = jnp.concatenate([adapter_up_factors, adapter_down_factors, down_other], axis=2)
    pool = lax.all_gather(pool, "req", axis=0, tiled=True)
    weight_other = swap(output_weight, 1)
    cross_away, cross_here = attend(2)
    cross_other = swap(cross_away, 1)
    sent = project(cross_here, cross_other, output_weight, weight_other, CUTS)
    received = [swap(sent[0], 2)]

    own_away, own_here = attend(0, sent[0])
    own_other = swap(own_away, 1)
    lookup = (request_adapter_slot, adapters_in_use, adapter_pool_row)
    second, own_ranks = ranks_and_part(
        (cross_here, cross_other),
        (own_here, own_other),
        pool,
        lookup,
        jnp.stack([me ^ 2, me]) * per_owner,
        sent[1],
    )
    received.append(swap(second, 2))
    last, received[0], _ = lax.optimization_barrier((sent[2], received[0], second))
    received.append(swap(last, 2))
    terms = adapter_terms(
        own_ranks, received[1], pool, lookup, gating, (me * per_owner).reshape(1)
    )
    out, rest = project_own(own_here, own_other, output_weight, weight_other, received[:2], terms)
    return finish(out, rest, received[2], terms[2])


def solution(mesh):
    return jax.shard_map(
        body,
        mesh=mesh,
        in_specs=(
            P("req", "tp"),
            P("req", "tp"),
            P("req", "tp"),
            P("req", None, "tp"),
            P("req", None, "tp"),
            P("req", None),
            P("req"),
            P("req"),
            P(),
            P(),
            P("req", None, "tp"),
            P("req", None, None),
            P("tp", None),
            P("req", None),
        ),
        out_specs=P(("req", "tp"), None),
        check_vma=False,
    )
```

```python
import math

import jax
import jax.numpy as jnp
from jax import lax
from jax.experimental import pallas as pl
from jax.experimental.pallas import tpu as pltpu
from jax.sharding import PartitionSpec as P

HD = 128
VMEM_LIMIT = 40 * 1024 * 1024
BLOCK = 512
CUTS = (3, 1, 1)
MASKED = -1e30
ANY = pl.BlockSpec(memory_space=pl.ANY)
BRIEF = pl.CostEstimate(flops=1000, bytes_accessed=1000, transcendentals=0)
HBM = pl.BlockSpec(memory_space=pltpu.HBM)
VMEM = pl.BlockSpec(memory_space=pltpu.VMEM)


def in_hbm(array):
    return pltpu.with_memory_space_constraint(array, pltpu.HBM)


def in_vmem(array):
    return pltpu.with_memory_space_constraint(array, pltpu.VMEM)


def attend_four(
    queries,
    fresh_keys,
    fresh_values,
    paged_keys,
    paged_values,
    request_page_table,
    live_token_count,
    requests,
    after=None,
):
    requests_here, pages = request_page_table.shape
    slots = queries.shape[0] // requests_here
    width = queries.shape[1]
    heads = width // HD
    pool_pages, page_rows = paged_keys.shape[:2]
    cached = pages * page_rows
    count = requests.shape[0]
    per_out = count // 2
    exponent_scale = math.log2(math.e) / math.sqrt(HD)

    def kernel(table, live, ids, q_hbm, fk_hbm, fv_hbm, pk_hbm, pv_hbm, *rest):
        outs, bufs = rest[-9:-7], rest[-7:]
        q_buf, fk_buf, fv_buf, pk_buf, pv_buf, order, in_sems = bufs

        def fetch(src, dst, sem):
            return pltpu.make_async_copy(src, dst, in_sems.at[sem])

        def rows_of(n):
            return pl.ds(pl.multiple_of(ids[n] * slots, slots), slots)

        def query_copy(n):
            return fetch(q_hbm.at[rows_of(n)], q_buf.at[n], 3 * n)

        def key_copy(n):
            return fetch(fk_hbm.at[rows_of(n)], fk_buf.at[n], 3 * n + 1)

        def value_copy(n):
            return fetch(fv_hbm.at[rows_of(n)], fv_buf.at[n], 3 * n + 2)

        def key_page(m):
            page = order[m]
            return fetch(pk_hbm.at[page], pk_buf.at[page], 3 * count + 2 * m)

        def value_page(m):
            page = order[m]
            return fetch(pv_hbm.at[page], pv_buf.at[page], 3 * count + 2 * m + 1)

        def start(copies):
            for copy in copies:
                copy.start()

        for j in range(pages):
            order[j] = table[ids[0], j]
        start([query_copy(0), key_copy(0)] + [key_page(m) for m in range(pages)])
        start([value_copy(0)] + [value_page(m) for m in range(pages)])
        place = jnp.int32(pages)
        for page in range(pool_pages):
            taken = order[0] == page
            for j in range(1, pages):
                taken = taken | (order[j] == page)

            @pl.when(jnp.logical_not(taken))
            def _(place=place, page=page):
                order[place] = page

            place = place + jnp.where(taken, 0, 1)
        others = range(pages, pool_pages)
        start([query_copy(1), key_copy(1)] + [key_page(m) for m in others])
        start([value_copy(1)] + [value_page(m) for m in others])
        for n in range(2, count):
            start([query_copy(n), key_copy(n), value_copy(n)])

        waited = set()

        def wait(name, make, indices):
            if name not in waited:
                waited.add(name)
                for index in indices:
                    make(index).wait()

        def keys_ready(duo):
            for n, _ in duo:
                wait(("q", n), query_copy, [n])
                wait(("k", n), key_copy, [n])
                wait(("first k",), key_page, range(pages))
                if n:
                    wait(("other k",), key_page, others)

        def values_ready(duo):
            for n, _ in duo:
                wait(("v", n), value_copy, [n])
                wait(("first v",), value_page, range(pages))
                if n:
                    wait(("other v",), value_page, others)

        def lanes(h, several=1):
            return slice(h * HD, (h + several) * HD)

        def gather(pool, fresh, n, here):
            return jnp.concatenate(
                [pool[table[ids[n], j], :, here] for j in range(pages)] + [fresh[n, :, here]],
                axis=0,
            )

        def side_by_side(pool, fresh, duo):
            (n, h), (other_n, other_h) = duo
            if n == other_n and other_h == h + 1:
                return gather(pool, fresh, n, lanes(h, 2))
            return jnp.concatenate(
                [gather(pool, fresh, m, lanes(g)) for m, g in duo],
                axis=1,
            )

        def score(duo):
            (n, h), (other_n, other_h) = duo
            blank = jnp.zeros((slots, HD), jnp.bfloat16)
            diagonal = jnp.concatenate(
                [
                    jnp.concatenate([q_buf[n, :, lanes(h)], blank], axis=1),
                    jnp.concatenate([blank, q_buf[other_n, :, lanes(other_h)]], axis=1),
                ],
                axis=0,
            )
            return lax.dot_general(
                diagonal,
                side_by_side(pk_buf, fk_buf, duo),
                (((1,), (1,)), ((), ())),
                preferred_element_type=jnp.float32,
            )

        def weigh(duo, scores):
            column = lax.broadcasted_iota(jnp.int32, (slots, slots), 1)
            usable = jnp.concatenate([column < live[ids[n]] for n, _ in duo], axis=0)
            scores = jnp.concatenate(
                [scores[:, :cached], jnp.where(usable, scores[:, cached:], MASKED)], axis=1
            )
            peak = jnp.max(scores, axis=1, keepdims=True)
            weights = jnp.exp2((scores - peak) * exponent_scale)
            return weights.astype(jnp.bfloat16), jnp.sum(weights, axis=1, keepdims=True)

        def blend(duo, weights, row_total):
            blended = jnp.dot(
                weights, side_by_side(pv_buf, fv_buf, duo), preferred_element_type=jnp.float32
            )
            row = lax.broadcasted_iota(jnp.int32, (slots, HD), 0)
            for m, (n, h) in enumerate(duo):
                rows = slice(m * slots, (m + 1) * slots)
                attended = blended[rows, lanes(m)] / row_total[rows]
                attended = jnp.where(row < live[ids[n]], attended, 0.0)
                place = (n % per_out) * slots
                outs[n // per_out][place : place + slots, lanes(h)] = attended.astype(jnp.bfloat16)

        units = []
        for first in range(0, count, 2):
            units += [((n, h), (n, h + 1)) for n in (first, first + 1) for h in range(0, heads - 1, 2)]
            if heads % 2:
                units.append(((first, heads - 1), (first + 1, heads - 1)))
        keys_ready(units[0])
        scores = score(units[0])
        weighed = None
        for u, duo in enumerate(units):
            later = None
            if u + 1 < len(units):
                keys_ready(units[u + 1])
                later = score(units[u + 1])
            if u:
                values_ready(units[u - 1])
                blend(units[u - 1], *weighed)
            weighed = weigh(duo, scores)
            scores = later
        values_ready(units[-1])
        blend(units[-1], *weighed)

    extra = () if after is None else (after,)
    out_shape = pltpu.VMEM((per_out * slots, width), jnp.bfloat16)
    return pl.pallas_call(
        kernel,
        grid_spec=pltpu.PrefetchScalarGridSpec(
            num_scalar_prefetch=3,
            grid=(1,),
            in_specs=[HBM] * 5 + [ANY] * len(extra),
            out_specs=[VMEM] * 2,
            scratch_shapes=[
                pltpu.VMEM((count, slots, width), jnp.bfloat16),
                pltpu.VMEM((count, slots, width), jnp.bfloat16),
                pltpu.VMEM((count, slots, width), jnp.bfloat16),
                pltpu.VMEM(paged_keys.shape, jnp.bfloat16),
                pltpu.VMEM(paged_values.shape, jnp.bfloat16),
                pltpu.SMEM((pool_pages,), jnp.int32),
                pltpu.SemaphoreType.DMA((3 * count + 2 * pool_pages,)),
            ],
        ),
        out_shape=[out_shape] * 2,
        compiler_params=pltpu.CompilerParams(vmem_limit_bytes=VMEM_LIMIT),
        cost_estimate=BRIEF,
        name="attend",
    )(
        in_hbm(request_page_table),
        in_hbm(live_token_count),
        requests,
        *map(in_hbm, (queries, fresh_keys, fresh_values, paged_keys, paged_values)),
        *extra,
    )


def project(own, other, weight, weight_other, cuts, after):
    rows = own.shape[0]
    bounds = [sum(cuts[:n]) for n in range(len(cuts) + 1)]
    assert bounds[-1] * BLOCK == weight.shape[1]

    def kernel(a, b, w, u, after, *outs):
        features = jnp.concatenate([a[...], b[...]], axis=1)
        for part, out in enumerate(outs):
            for n in range(cuts[part]):
                here = slice((bounds[part] + n) * BLOCK, (bounds[part] + n + 1) * BLOCK)
                out[:, n * BLOCK : (n + 1) * BLOCK] = jnp.dot(
                    features,
                    jnp.concatenate([w[:, here], u[:, here]], axis=0),
                    preferred_element_type=jnp.float32,
                ).astype(jnp.bfloat16)

    return pl.pallas_call(
        kernel,
        in_specs=[VMEM] * 4 + [ANY],
        out_specs=[VMEM] * len(cuts),
        out_shape=[pltpu.VMEM((rows, cut * BLOCK), jnp.bfloat16) for cut in cuts],
        compiler_params=pltpu.CompilerParams(vmem_limit_bytes=VMEM_LIMIT),
        cost_estimate=BRIEF,
        name="project",
    )(in_vmem(own), in_vmem(other), in_vmem(weight), in_vmem(weight_other), after)


def pack_pair(ups, downs, core, after):
    rank, columns = ups[0].shape[1:]
    width = downs[0].shape[2]
    half = columns // 2

    def kernel(core, up_0, up_1, down_0, down_1, after, out):
        here = pl.ds(pl.multiple_of(core[0] * half, half), half)
        for n, (up, down) in enumerate(((up_0, down_0), (up_1, down_1))):
            out[n, :, :half] = up[0, :, here]
            out[n, :, half:] = down[0]

    return pl.pallas_call(
        kernel,
        in_specs=[pl.BlockSpec(memory_space=pltpu.SMEM)] + [VMEM] * 4 + [ANY],
        out_specs=VMEM,
        out_shape=jax.ShapeDtypeStruct((2, rank, half + width), ups[0].dtype),
        compiler_params=pltpu.CompilerParams(vmem_limit_bytes=VMEM_LIMIT),
        cost_estimate=BRIEF,
        name="pack_pair",
    )(core, *ups, *downs, after)


def pick_factors(pairs, lookup, firsts, width, after):
    rank = pairs[0].shape[1]
    half = pairs[0].shape[2] - width
    count = len(pairs)

    def kernel(first, req, slot, in_use, pool_row, *refs):
        pieces, outs = refs[:count], refs[-2:]
        for n, out in enumerate(outs):
            for m in range(2):
                for i in range(2):
                    row = pool_row[in_use[slot[first[2 * n + m] + i]]]
                    apart = lax.rem(req[0] // 2 - row // 2 + count, count)
                    place = (row ^ req[0]) & 1
                    for d, piece in enumerate(pieces):

                        @pl.when(apart == d)
                        def _(piece=piece, out=out, k=2 * m + i, m=m, i=i, place=place):
                            out[:, k * width : (k + 1) * width] = piece[place, :, half:]
                            if m:
                                there = 4 * width + i * half
                                out[:, there : there + half] = piece[place, :, :half]

    shape = jax.ShapeDtypeStruct((rank, 4 * width + 2 * half), pairs[0].dtype)
    return pl.pallas_call(
        kernel,
        in_specs=[pl.BlockSpec(memory_space=pltpu.SMEM)] * 5 + [VMEM] * count + [ANY],
        out_specs=[VMEM] * 2,
        out_shape=[shape] * 2,
        compiler_params=pltpu.CompilerParams(vmem_limit_bytes=VMEM_LIMIT),
        cost_estimate=BRIEF,
        name="pick_factors",
    )(firsts, *lookup, *pairs, after)


def ranks_and_part(cross, own, factors, part):
    rows, width = cross[0].shape
    slots = rows // 2
    rank = factors[0].shape[0]
    assert part.shape[1] == 4 * slots

    def kernel(*refs):
        factors, blocks, (part_in, part_out, own_ranks) = refs[:2], refs[2:6], refs[6:]
        part_out[:rows] = part_in[...]
        for i in range(2):
            here = slice(i * slots, (i + 1) * slots)
            for n in range(2):
                k = 2 * n + i
                acts = sum(
                    lax.dot_general(
                        factors[m][:, k * width : (k + 1) * width],
                        blocks[2 * n + m][here],
                        (((1,), (1,)), ((), ())),
                        preferred_element_type=jnp.float32,
                    )
                    for m in range(2)
                )
                if n:
                    own_ranks[i] = acts
                    continue
                high = acts.astype(jnp.bfloat16)
                low = (acts - high.astype(jnp.float32)).astype(jnp.bfloat16)
                part_out[rows:, 2 * i * slots : (2 * i + 1) * slots] = high
                part_out[rows:, (2 * i + 1) * slots : (2 * i + 2) * slots] = low

    return pl.pallas_call(
        kernel,
        in_specs=[VMEM] * 7,
        out_specs=[VMEM] * 2,
        out_shape=[
            jax.ShapeDtypeStruct((rows + rank, part.shape[1]), jnp.bfloat16),
            jax.ShapeDtypeStruct((2, rank, slots), jnp.float32),
        ],
        compiler_params=pltpu.CompilerParams(vmem_limit_bytes=VMEM_LIMIT),
        cost_estimate=BRIEF,
        name="ranks_and_part",
    )(*factors, *cross, *own, part)


def adapter_terms(own_ranks, received, factors, gating, core_and_first, width):
    requests, rank, slots = own_ranks.shape
    rows = requests * slots
    columns = gating.shape[1]
    half = columns // 2

    def kernel(scalars, own, other, mine, theirs, gate, acts, ups, gates):
        core, first = scalars[0], scalars[1]
        acts[...] = jnp.zeros_like(acts)
        gates[...] = jnp.zeros_like(gates)
        for i in range(2):
            total = own[i]
            for m in range(2 * i, 2 * i + 2):
                total += other[rows:, m * slots : (m + 1) * slots].astype(jnp.float32)
            high = total.astype(jnp.bfloat16).astype(jnp.float32)
            pair = jnp.concatenate([high, total - high], axis=0).T.astype(jnp.bfloat16)
            acts[i * slots : (i + 1) * slots, 2 * rank * i : 2 * rank * (i + 1)] = pair
            here = 4 * width + i * half
            for m in range(2):
                for away, factors in enumerate((mine, theirs)):
                    there = pl.ds(pl.multiple_of((core ^ away) * half, half), half)
                    ups[(2 * i + m) * rank : (2 * i + m + 1) * rank, there] = factors[
                        :, here : here + half
                    ]
            gates[i : i + 1] = gate[pl.ds(first + i, 1), :]

    return pl.pallas_call(
        kernel,
        in_specs=[pl.BlockSpec(memory_space=pltpu.SMEM)] + [VMEM] * 5,
        out_specs=[VMEM] * 3,
        out_shape=[
            jax.ShapeDtypeStruct((rows, 2 * requests * rank), jnp.bfloat16),
            jax.ShapeDtypeStruct((2 * requests * rank, columns), jnp.bfloat16),
            jax.ShapeDtypeStruct((8, columns), jnp.float32),
        ],
        compiler_params=pltpu.CompilerParams(vmem_limit_bytes=VMEM_LIMIT),
        cost_estimate=BRIEF,
        name="adapter_terms",
    )(core_and_first, own_ranks, received, *factors, gating)


def project_own(own, other, weight, weight_other, received, terms):
    acts, ups, gates = terms
    rows, width = own.shape
    columns = weight.shape[1]
    blocks = columns // BLOCK
    bounds = [0]
    for part in received:
        bounds.append(bounds[-1] + part.shape[1] // BLOCK)
    covered = bounds[-1]
    slots = rows // 2

    def kernel(a, b, w, u, acts, ups, gates, *refs):
        parts, (out, rest_out, out_buf, out_sems) = refs[:-4], refs[-4:]

        def store(n):
            here = pl.ds(n * BLOCK, BLOCK)
            return pltpu.make_async_copy(out_buf.at[:, here], out.at[:, here], out_sems.at[n])

        features = jnp.concatenate([a[...], b[...]], axis=1)
        for n in range(blocks):
            here = slice(n * BLOCK, (n + 1) * BLOCK)
            update = jnp.dot(
                features,
                jnp.concatenate([w[:, here], u[:, here]], axis=0),
                preferred_element_type=jnp.float32,
            )
            update += jnp.dot(acts[...], ups[:, here], preferred_element_type=jnp.float32)
            for m, part in enumerate(parts):
                if bounds[m] <= n < bounds[m + 1]:
                    there = slice((n - bounds[m]) * BLOCK, (n - bounds[m] + 1) * BLOCK)
                    update += part[:rows, there].astype(jnp.float32)
            for i in range(2):
                those = slice(i * slots, (i + 1) * slots)
                gated = update[those] * gates[i : i + 1, here]
                if n < covered:
                    out_buf[those, here] = gated.astype(jnp.bfloat16)
                else:
                    there = slice((n - covered) * BLOCK, (n - covered + 1) * BLOCK)
                    rest_out[those, there] = gated
            if n < covered:
                store(n).start()
        for n in range(covered):
            store(n).wait()

    left = columns - covered * BLOCK
    return pl.pallas_call(
        kernel,
        in_specs=[VMEM] * (7 + len(received)),
        out_specs=[HBM, VMEM],
        out_shape=[
            pltpu.HBM((rows, columns), jnp.bfloat16),
            pltpu.VMEM((rows, left), jnp.float32),
        ],
        scratch_shapes=[
            pltpu.VMEM((rows, covered * BLOCK), jnp.bfloat16),
            pltpu.SemaphoreType.DMA((covered,)),
        ],
        compiler_params=pltpu.CompilerParams(vmem_limit_bytes=VMEM_LIMIT),
        cost_estimate=BRIEF,
        name="project_own",
    )(own, other, in_vmem(weight), in_vmem(weight_other), acts, ups, gates, *received)


def finish(so_far, rest, received, gates):
    rows, columns = so_far.shape
    wide = rest.shape[1]
    assert columns % wide == 0
    at = columns // wide - 1
    slots = rows // 2

    def kernel(sums, part, gate, so_far, out):
        for i in range(2):
            here = slice(i * slots, (i + 1) * slots)
            update = sums[here] + part[here].astype(jnp.float32) * gate[i : i + 1]
            out[here] = update.astype(jnp.bfloat16)

    return pl.pallas_call(
        kernel,
        grid=(1,),
        in_specs=[
            pl.BlockSpec((rows, wide), lambda j: (0, 0)),
            pl.BlockSpec((rows, wide), lambda j: (0, 0)),
            pl.BlockSpec((gates.shape[0], wide), lambda j: (0, at)),
            ANY,
        ],
        out_specs=pl.BlockSpec((rows, wide), lambda j: (0, at)),
        out_shape=jax.ShapeDtypeStruct((rows, columns), jnp.bfloat16),
        input_output_aliases={3: 0},
        compiler_params=pltpu.CompilerParams(vmem_limit_bytes=VMEM_LIMIT),
        cost_estimate=BRIEF,
        name="finish",
    )(rest, received, gates, so_far)


def body(
    queries,
    fresh_keys,
    fresh_values,
    paged_keys,
    paged_values,
    request_page_table,
    live_token_count,
    request_adapter_slot,
    adapters_in_use,
    adapter_pool_row,
    adapter_down_factors,
    adapter_up_factors,
    output_weight,
    gating,
):
    tp = lax.axis_size("tp")
    holders = lax.axis_size("req")
    me = lax.axis_index("tp").astype(jnp.int32)
    core = lax.rem(me, 2)
    per_owner = live_token_count.shape[0] // tp

    def swap(array, flip):
        return lax.ppermute(array, "tp", [(s, s ^ flip) for s in range(tp)])

    def attend(flip, after=None):
        owners = ((me ^ flip ^ 1) * per_owner, (me ^ flip) * per_owner)
        return attend_four(
            queries,
            fresh_keys,
            fresh_values,
            paged_keys,
            paged_values,
            request_page_table,
            live_token_count,
            jnp.stack([owner + n for owner in owners for n in range(per_owner)]),
            after,
        )

    ups, downs = (
        (factors, lax.ppermute(factors, "req", [(s, s ^ 1) for s in range(holders)]))
        for factors in (adapter_up_factors, adapter_down_factors)
    )
    weight_other = swap(output_weight, 1)
    cross_away, cross_here = attend(2)
    cross_other = swap(cross_away, 1)
    pair = pack_pair(ups, downs, core.reshape(1), cross_away)
    sent = project(cross_here, cross_other, output_weight, weight_other, CUTS, pair)
    received = [swap(sent[0], 2)]

    pair, _ = lax.optimization_barrier((pair, sent[0]))
    pairs = [pair] + [
        lax.ppermute(pair, "req", [(s, (s + d) % holders) for s in range(holders)])
        for d in range(2, holders, 2)
    ]
    own_away, own_here = attend(0, sent[0])
    lookup = (
        lax.axis_index("req").astype(jnp.int32).reshape(1),
        request_adapter_slot,
        adapters_in_use,
        adapter_pool_row,
    )
    firsts = jnp.stack([me ^ 2, me, me ^ 3, me ^ 1]) * per_owner
    factors, factors_away = pick_factors(
        pairs, lookup, firsts, adapter_down_factors.shape[2], own_here
    )
    factors = (factors, swap(factors_away, 1))
    own_away, _ = lax.optimization_barrier((own_away, factors_away))
    own_other = swap(own_away, 1)
    second, own_ranks = ranks_and_part(
        (cross_here, cross_other), (own_here, own_other), factors, sent[1]
    )
    received.append(swap(second, 2))
    last, received[0], _ = lax.optimization_barrier((sent[2], received[0], second))
    received.append(swap(last, 2))
    terms = adapter_terms(
        own_ranks,
        received[1],
        factors,
        gating,
        jnp.stack([core, me * per_owner]),
        adapter_down_factors.shape[2],
    )
    out, rest = project_own(own_here, own_other, output_weight, weight_other, received[:2], terms)
    return finish(out, rest, received[2], terms[2])


def solution(mesh):
    return jax.shard_map(
        body,
        mesh=mesh,
        in_specs=(
            P("req", "tp"),
            P("req", "tp"),
            P("req", "tp"),
            P("req", None, "tp"),
            P("req", None, "tp"),
            P("req", None),
            P("req"),
            P("req"),
            P(),
            P(),
            P("req", None, "tp"),
            P("req", None, None),
            P("tp", None),
            P("req", None),
        ),
        out_specs=P(("req", "tp"), None),
        check_vma=False,
    )
```

```python
import math

import jax
import jax.numpy as jnp
from jax import lax
from jax.experimental import pallas as pl
from jax.experimental.pallas import tpu as pltpu
from jax.sharding import PartitionSpec as P

HD = 128
VMEM_LIMIT = 32 * 1024 * 1024
SMEM = pl.BlockSpec(memory_space=pltpu.SMEM)
BLOCK = 512
CUTS = (3, 1, 1)
MASKED = -1e30
ANY = pl.BlockSpec(memory_space=pl.ANY)
BRIEF = pl.CostEstimate(flops=1000, bytes_accessed=1000, transcendentals=0)
HBM = pl.BlockSpec(memory_space=pltpu.HBM)
VMEM = pl.BlockSpec(memory_space=pltpu.VMEM)


def in_hbm(array):
    return pltpu.with_memory_space_constraint(array, pltpu.HBM)


def in_vmem(array):
    return pltpu.with_memory_space_constraint(array, pltpu.VMEM)


def attend_four(
    queries,
    fresh_keys,
    fresh_values,
    paged_keys,
    paged_values,
    request_page_table,
    live_token_count,
    place,
    flip,
    per_owner,
    after=None,
):
    requests_here, pages = request_page_table.shape
    slots = queries.shape[0] // requests_here
    width = queries.shape[1]
    heads = width // HD
    pool_pages, page_rows = paged_keys.shape[:2]
    cached = pages * page_rows
    per_out = per_owner
    count = 2 * per_out
    exponent_scale = math.log2(math.e) / math.sqrt(HD)

    def kernel(table, live, place, q_hbm, fk_hbm, fv_hbm, pk_hbm, pv_hbm, *rest):
        ids = [
            (place[0] ^ away) * per_owner + n for away in (flip ^ 1, flip) for n in range(per_owner)
        ]
        outs, bufs = rest[-9:-7], rest[-7:]
        q_buf, fk_buf, fv_buf, pk_buf, pv_buf, order, in_sems = bufs

        def fetch(src, dst, sem):
            return pltpu.make_async_copy(src, dst, in_sems.at[sem])

        def rows_of(n):
            return pl.ds(pl.multiple_of(ids[n] * slots, slots), slots)

        def query_copy(n):
            return fetch(q_hbm.at[rows_of(n)], q_buf.at[n], 3 * n)

        def key_copy(n):
            return fetch(fk_hbm.at[rows_of(n)], fk_buf.at[n], 3 * n + 1)

        def value_copy(n):
            return fetch(fv_hbm.at[rows_of(n)], fv_buf.at[n], 3 * n + 2)

        def key_page(m):
            page = order[m]
            return fetch(pk_hbm.at[page], pk_buf.at[page], 3 * count + 2 * m)

        def value_page(m):
            page = order[m]
            return fetch(pv_hbm.at[page], pv_buf.at[page], 3 * count + 2 * m + 1)

        def start(copies):
            for copy in copies:
                copy.start()

        for j in range(pages):
            order[j] = table[ids[0], j]
        start([query_copy(0), key_copy(0)] + [key_page(m) for m in range(pages)])
        start([value_copy(0)] + [value_page(m) for m in range(pages)])
        free = jnp.int32(pages)
        for page in range(pool_pages):
            taken = order[0] == page
            for j in range(1, pages):
                taken = taken | (order[j] == page)

            @pl.when(jnp.logical_not(taken))
            def _(free=free, page=page):
                order[free] = page

            free = free + jnp.where(taken, 0, 1)
        others = range(pages, pool_pages)
        start([query_copy(1), key_copy(1)] + [key_page(m) for m in others])
        start([value_copy(1)] + [value_page(m) for m in others])
        for n in range(2, count):
            start([query_copy(n), key_copy(n), value_copy(n)])

        waited = set()

        def wait(name, make, indices):
            if name not in waited:
                waited.add(name)
                for index in indices:
                    make(index).wait()

        def keys_ready(duo):
            for n, _ in duo:
                wait(("q", n), query_copy, [n])
                wait(("k", n), key_copy, [n])
                wait(("first k",), key_page, range(pages))
                if n:
                    wait(("other k",), key_page, others)

        def values_ready(duo):
            for n, _ in duo:
                wait(("v", n), value_copy, [n])
                wait(("first v",), value_page, range(pages))
                if n:
                    wait(("other v",), value_page, others)

        def lanes(h, several=1):
            return slice(h * HD, (h + several) * HD)

        def gather(pool, fresh, n, here):
            return jnp.concatenate(
                [pool[table[ids[n], j], :, here] for j in range(pages)] + [fresh[n, :, here]],
                axis=0,
            )

        def side_by_side(pool, fresh, duo):
            (n, h), (other_n, other_h) = duo
            if n == other_n and other_h == h + 1:
                return gather(pool, fresh, n, lanes(h, 2))
            return jnp.concatenate(
                [gather(pool, fresh, m, lanes(g)) for m, g in duo],
                axis=1,
            )

        def score(duo):
            (n, h), (other_n, other_h) = duo
            blank = jnp.zeros((slots, HD), jnp.bfloat16)
            diagonal = jnp.concatenate(
                [
                    jnp.concatenate([q_buf[n, :, lanes(h)], blank], axis=1),
                    jnp.concatenate([blank, q_buf[other_n, :, lanes(other_h)]], axis=1),
                ],
                axis=0,
            )
            return lax.dot_general(
                diagonal,
                side_by_side(pk_buf, fk_buf, duo),
                (((1,), (1,)), ((), ())),
                preferred_element_type=jnp.float32,
            )

        def weigh(duo, scores):
            column = lax.broadcasted_iota(jnp.int32, (slots, slots), 1)
            usable = jnp.concatenate([column < live[ids[n]] for n, _ in duo], axis=0)
            scores = jnp.concatenate(
                [scores[:, :cached], jnp.where(usable, scores[:, cached:], MASKED)], axis=1
            )
            peak = jnp.max(scores, axis=1, keepdims=True)
            weights = jnp.exp2((scores - peak) * exponent_scale)
            return weights.astype(jnp.bfloat16), jnp.sum(weights, axis=1, keepdims=True)

        def blend(duo, weights, row_total):
            blended = jnp.dot(
                weights, side_by_side(pv_buf, fv_buf, duo), preferred_element_type=jnp.float32
            )
            row = lax.broadcasted_iota(jnp.int32, (slots, HD), 0)
            for m, (n, h) in enumerate(duo):
                rows = slice(m * slots, (m + 1) * slots)
                attended = blended[rows, lanes(m)] / row_total[rows]
                attended = jnp.where(row < live[ids[n]], attended, 0.0)
                at = (n % per_out) * slots
                outs[n // per_out][at : at + slots, lanes(h)] = attended.astype(jnp.bfloat16)

        units = []
        for first in range(0, count, 2):
            units += [((n, h), (n, h + 1)) for n in (first, first + 1) for h in range(0, heads - 1, 2)]
            if heads % 2:
                units.append(((first, heads - 1), (first + 1, heads - 1)))
        keys_ready(units[0])
        scores = score(units[0])
        weighed = None
        for u, duo in enumerate(units):
            later = None
            if u + 1 < len(units):
                keys_ready(units[u + 1])
                later = score(units[u + 1])
            if u:
                values_ready(units[u - 1])
                blend(units[u - 1], *weighed)
            weighed = weigh(duo, scores)
            scores = later
        values_ready(units[-1])
        blend(units[-1], *weighed)

    extra = () if after is None else (after,)
    out_shape = pltpu.VMEM((per_out * slots, width), jnp.bfloat16)
    return pl.pallas_call(
        kernel,
        grid_spec=pltpu.PrefetchScalarGridSpec(
            num_scalar_prefetch=3,
            grid=(1,),
            in_specs=[HBM] * 5 + [ANY] * len(extra),
            out_specs=[VMEM] * 2,
            scratch_shapes=[
                pltpu.VMEM((count, slots, width), jnp.bfloat16),
                pltpu.VMEM((count, slots, width), jnp.bfloat16),
                pltpu.VMEM((count, slots, width), jnp.bfloat16),
                pltpu.VMEM(paged_keys.shape, jnp.bfloat16),
                pltpu.VMEM(paged_values.shape, jnp.bfloat16),
                pltpu.SMEM((pool_pages,), jnp.int32),
                pltpu.SemaphoreType.DMA((3 * count + 2 * pool_pages,)),
            ],
        ),
        out_shape=[out_shape] * 2,
        compiler_params=pltpu.CompilerParams(vmem_limit_bytes=VMEM_LIMIT),
        cost_estimate=BRIEF,
        name="attend",
    )(
        in_hbm(request_page_table),
        in_hbm(live_token_count),
        place,
        *map(in_hbm, (queries, fresh_keys, fresh_values, paged_keys, paged_values)),
        *extra,
    )


def project(own, other, weight, weight_other, cuts, after):
    rows = own.shape[0]
    bounds = [sum(cuts[:n]) for n in range(len(cuts) + 1)]
    assert bounds[-1] * BLOCK == weight.shape[1]

    def kernel(a, b, w, u, after, *outs):
        features = jnp.concatenate([a[...], b[...]], axis=1)
        for part, out in enumerate(outs):
            for n in range(cuts[part]):
                here = slice((bounds[part] + n) * BLOCK, (bounds[part] + n + 1) * BLOCK)
                out[:, n * BLOCK : (n + 1) * BLOCK] = jnp.dot(
                    features,
                    jnp.concatenate([w[:, here], u[:, here]], axis=0),
                    preferred_element_type=jnp.float32,
                ).astype(jnp.bfloat16)

    return pl.pallas_call(
        kernel,
        in_specs=[VMEM] * 4 + [ANY],
        out_specs=[VMEM] * len(cuts),
        out_shape=[pltpu.VMEM((rows, cut * BLOCK), jnp.bfloat16) for cut in cuts],
        compiler_params=pltpu.CompilerParams(vmem_limit_bytes=VMEM_LIMIT),
        cost_estimate=BRIEF,
        name="project",
    )(in_vmem(own), in_vmem(other), in_vmem(weight), in_vmem(weight_other), after)


def pack_pair(ups, downs, place, after):
    rank, columns = ups[0].shape[1:]
    width = downs[0].shape[2]
    half = columns // 2

    def kernel(place, up_0, up_1, down_0, down_1, after, out):
        here = pl.ds(pl.multiple_of((place[0] & 1) * half, half), half)
        for n, (up, down) in enumerate(((up_0, down_0), (up_1, down_1))):
            out[n, :, :half] = up[0, :, here]
            out[n, :, half:] = down[0]

    return pl.pallas_call(
        kernel,
        in_specs=[SMEM] + [VMEM] * 4 + [ANY],
        out_specs=VMEM,
        out_shape=jax.ShapeDtypeStruct((2, rank, half + width), ups[0].dtype),
        compiler_params=pltpu.CompilerParams(vmem_limit_bytes=VMEM_LIMIT),
        cost_estimate=BRIEF,
        name="pack_pair",
    )(place, *ups, *downs, after)


def pick_factors(pairs, place, lookup, per_owner, width, after):
    rank = pairs[0].shape[1]
    half = pairs[0].shape[2] - width
    count = len(pairs)

    def kernel(place, slot, in_use, pool_row, *refs):
        pieces, outs = refs[:count], refs[-2:]
        for n, out in enumerate(outs):
            for m in range(2):
                for i in range(2):
                    request = (place[0] ^ n ^ (0 if m else 2)) * per_owner + i
                    row = pool_row[in_use[slot[request]]]
                    apart = lax.rem(place[1] // 2 - row // 2 + count, count)
                    side = (row ^ place[1]) & 1
                    for d, piece in enumerate(pieces):

                        @pl.when(apart == d)
                        def _(piece=piece, out=out, k=2 * m + i, m=m, i=i, side=side):
                            out[:, k * width : (k + 1) * width] = piece[side, :, half:]
                            if m:
                                there = 4 * width + i * half
                                out[:, there : there + half] = piece[side, :, :half]

    shape = jax.ShapeDtypeStruct((rank, 4 * width + 2 * half), pairs[0].dtype)
    return pl.pallas_call(
        kernel,
        in_specs=[SMEM] * 4 + [VMEM] * count + [ANY],
        out_specs=[VMEM] * 2,
        out_shape=[shape] * 2,
        compiler_params=pltpu.CompilerParams(vmem_limit_bytes=VMEM_LIMIT),
        cost_estimate=BRIEF,
        name="pick_factors",
    )(place, *lookup, *pairs, after)


def ranks_and_part(cross, own, factors, part):
    rows, width = cross[0].shape
    slots = rows // 2
    rank = factors[0].shape[0]
    assert part.shape[1] == 4 * slots

    def kernel(*refs):
        factors, blocks, (part_in, part_out, own_ranks) = refs[:2], refs[2:6], refs[6:]
        part_out[:rows] = part_in[...]
        for i in range(2):
            here = slice(i * slots, (i + 1) * slots)
            for n in range(2):
                k = 2 * n + i
                acts = sum(
                    lax.dot_general(
                        factors[m][:, k * width : (k + 1) * width],
                        blocks[2 * n + m][here],
                        (((1,), (1,)), ((), ())),
                        preferred_element_type=jnp.float32,
                    )
                    for m in range(2)
                )
                if n:
                    own_ranks[i] = acts
                    continue
                high = acts.astype(jnp.bfloat16)
                low = (acts - high.astype(jnp.float32)).astype(jnp.bfloat16)
                part_out[rows:, 2 * i * slots : (2 * i + 1) * slots] = high
                part_out[rows:, (2 * i + 1) * slots : (2 * i + 2) * slots] = low

    return pl.pallas_call(
        kernel,
        in_specs=[VMEM] * 7,
        out_specs=[VMEM] * 2,
        out_shape=[
            jax.ShapeDtypeStruct((rows + rank, part.shape[1]), jnp.bfloat16),
            jax.ShapeDtypeStruct((2, rank, slots), jnp.float32),
        ],
        compiler_params=pltpu.CompilerParams(vmem_limit_bytes=VMEM_LIMIT),
        cost_estimate=BRIEF,
        name="ranks_and_part",
    )(*factors, *cross, *own, part)


def adapter_terms(own_ranks, received, factors, gating, place, width):
    requests, rank, slots = own_ranks.shape
    rows = requests * slots
    columns = gating.shape[1]
    half = columns // 2

    def kernel(place, own, other, mine, theirs, gate, acts, ups, gates):
        core, first = place[0] & 1, place[0] * requests
        acts[...] = jnp.zeros_like(acts)
        gates[...] = jnp.zeros_like(gates)
        for i in range(2):
            total = own[i]
            for m in range(2 * i, 2 * i + 2):
                total += other[rows:, m * slots : (m + 1) * slots].astype(jnp.float32)
            high = total.astype(jnp.bfloat16).astype(jnp.float32)
            pair = jnp.concatenate([high, total - high], axis=0).T.astype(jnp.bfloat16)
            acts[i * slots : (i + 1) * slots, 2 * rank * i : 2 * rank * (i + 1)] = pair
            here = 4 * width + i * half
            for m in range(2):
                for away, factors in enumerate((mine, theirs)):
                    there = pl.ds(pl.multiple_of((core ^ away) * half, half), half)
                    ups[(2 * i + m) * rank : (2 * i + m + 1) * rank, there] = factors[
                        :, here : here + half
                    ]
            gates[i : i + 1] = gate[pl.ds(first + i, 1), :]

    return pl.pallas_call(
        kernel,
        in_specs=[SMEM] + [VMEM] * 5,
        out_specs=[VMEM] * 3,
        out_shape=[
            jax.ShapeDtypeStruct((rows, 2 * requests * rank), jnp.bfloat16),
            jax.ShapeDtypeStruct((2 * requests * rank, columns), jnp.bfloat16),
            jax.ShapeDtypeStruct((8, columns), jnp.float32),
        ],
        compiler_params=pltpu.CompilerParams(vmem_limit_bytes=VMEM_LIMIT),
        cost_estimate=BRIEF,
        name="adapter_terms",
    )(place, own_ranks, received, *factors, gating)


def project_own(own, other, weight, weight_other, received, terms):
    acts, ups, gates = terms
    rows, width = own.shape
    columns = weight.shape[1]
    blocks = columns // BLOCK
    bounds = [0]
    for part in received:
        bounds.append(bounds[-1] + part.shape[1] // BLOCK)
    covered = bounds[-1]
    slots = rows // 2

    def kernel(a, b, w, u, acts, ups, gates, *refs):
        parts, (out, rest_out, out_buf, out_sems) = refs[:-4], refs[-4:]

        def store(n):
            here = pl.ds(n * BLOCK, BLOCK)
            return pltpu.make_async_copy(out_buf.at[:, here], out.at[:, here], out_sems.at[n])

        features = jnp.concatenate([a[...], b[...]], axis=1)
        for n in range(blocks):
            here = slice(n * BLOCK, (n + 1) * BLOCK)
            update = jnp.dot(
                features,
                jnp.concatenate([w[:, here], u[:, here]], axis=0),
                preferred_element_type=jnp.float32,
            )
            update += jnp.dot(acts[...], ups[:, here], preferred_element_type=jnp.float32)
            for m, part in enumerate(parts):
                if bounds[m] <= n < bounds[m + 1]:
                    there = slice((n - bounds[m]) * BLOCK, (n - bounds[m] + 1) * BLOCK)
                    update += part[:rows, there].astype(jnp.float32)
            for i in range(2):
                those = slice(i * slots, (i + 1) * slots)
                gated = update[those] * gates[i : i + 1, here]
                if n < covered:
                    out_buf[those, here] = gated.astype(jnp.bfloat16)
                else:
                    there = slice((n - covered) * BLOCK, (n - covered + 1) * BLOCK)
                    rest_out[those, there] = gated
            if n < covered:
                store(n).start()
        for n in range(covered):
            store(n).wait()

    left = columns - covered * BLOCK
    return pl.pallas_call(
        kernel,
        in_specs=[VMEM] * (7 + len(received)),
        out_specs=[HBM, VMEM],
        out_shape=[
            pltpu.HBM((rows, columns), jnp.bfloat16),
            pltpu.VMEM((rows, left), jnp.float32),
        ],
        scratch_shapes=[
            pltpu.VMEM((rows, covered * BLOCK), jnp.bfloat16),
            pltpu.SemaphoreType.DMA((covered,)),
        ],
        compiler_params=pltpu.CompilerParams(vmem_limit_bytes=VMEM_LIMIT),
        cost_estimate=BRIEF,
        name="project_own",
    )(own, other, in_vmem(weight), in_vmem(weight_other), acts, ups, gates, *received)


def finish(so_far, rest, received, gates):
    rows, columns = so_far.shape
    wide = rest.shape[1]
    assert columns % wide == 0
    at = columns // wide - 1
    slots = rows // 2

    def kernel(sums, part, gate, so_far, out):
        for i in range(2):
            here = slice(i * slots, (i + 1) * slots)
            update = sums[here] + part[here].astype(jnp.float32) * gate[i : i + 1]
            out[here] = update.astype(jnp.bfloat16)

    return pl.pallas_call(
        kernel,
        grid=(1,),
        in_specs=[
            pl.BlockSpec((rows, wide), lambda j: (0, 0)),
            pl.BlockSpec((rows, wide), lambda j: (0, 0)),
            pl.BlockSpec((gates.shape[0], wide), lambda j: (0, at)),
            ANY,
        ],
        out_specs=pl.BlockSpec((rows, wide), lambda j: (0, at)),
        out_shape=jax.ShapeDtypeStruct((rows, columns), jnp.bfloat16),
        input_output_aliases={3: 0},
        compiler_params=pltpu.CompilerParams(vmem_limit_bytes=VMEM_LIMIT),
        cost_estimate=BRIEF,
        name="finish",
    )(rest, received, gates, so_far)


def body(
    queries,
    fresh_keys,
    fresh_values,
    paged_keys,
    paged_values,
    request_page_table,
    live_token_count,
    request_adapter_slot,
    adapters_in_use,
    adapter_pool_row,
    adapter_down_factors,
    adapter_up_factors,
    output_weight,
    gating,
):
    tp = lax.axis_size("tp")
    holders = lax.axis_size("req")
    place = jnp.stack([lax.axis_index("tp"), lax.axis_index("req")]).astype(jnp.int32)
    per_owner = live_token_count.shape[0] // tp

    def swap(array, flip):
        return lax.ppermute(array, "tp", [(s, s ^ flip) for s in range(tp)])

    def attend(flip, after=None):
        return attend_four(
            queries,
            fresh_keys,
            fresh_values,
            paged_keys,
            paged_values,
            request_page_table,
            live_token_count,
            place,
            flip,
            per_owner,
            after,
        )

    ups, downs = (
        (factors, lax.ppermute(factors, "req", [(s, s ^ 1) for s in range(holders)]))
        for factors in (adapter_up_factors, adapter_down_factors)
    )
    weight_other = swap(output_weight, 1)
    cross_away, cross_here = attend(2)
    cross_other, ups, downs = lax.optimization_barrier((cross_away, ups, downs))
    cross_other = swap(cross_other, 1)
    pair = pack_pair(ups, downs, place, cross_away)
    sent = project(cross_here, cross_other, output_weight, weight_other, CUTS, pair)
    received = [swap(sent[0], 2)]

    pair, _ = lax.optimization_barrier((pair, sent[0]))
    pairs = [pair] + [
        lax.ppermute(pair, "req", [(s, (s + d) % holders) for s in range(holders)])
        for d in range(2, holders, 2)
    ]
    own_away, own_here = attend(0, sent[0])
    lookup = (request_adapter_slot, adapters_in_use, adapter_pool_row)
    width = output_weight.shape[0]
    factors, factors_away = pick_factors(pairs, place, lookup, per_owner, width, own_here)
    factors = (factors, swap(factors_away, 1))
    own_away, _ = lax.optimization_barrier((own_away, factors_away))
    own_other = swap(own_away, 1)
    second, own_ranks = ranks_and_part(
        (cross_here, cross_other), (own_here, own_other), factors, sent[1]
    )
    received.append(swap(second, 2))
    last, received[0], _ = lax.optimization_barrier((sent[2], received[0], second))
    received.append(swap(last, 2))
    terms = adapter_terms(own_ranks, received[1], factors, gating, place, width)
    out, rest = project_own(own_here, own_other, output_weight, weight_other, received[:2], terms)
    return finish(out, rest, received[2], terms[2])


def solution(mesh):
    return jax.shard_map(
        body,
        mesh=mesh,
        in_specs=(
            P("req", "tp"),
            P("req", "tp"),
            P("req", "tp"),
            P("req", None, "tp"),
            P("req", None, "tp"),
            P("req", None),
            P("req"),
            P("req"),
            P(),
            P(),
            P("req", None, "tp"),
            P("req", None, None),
            P("tp", None),
            P("req", None),
        ),
        out_specs=P(("req", "tp"), None),
        check_vma=False,
    )
```

```python
import math

import jax
import jax.numpy as jnp
from jax import lax
from jax.experimental import pallas as pl
from jax.experimental.pallas import tpu as pltpu
from jax.sharding import PartitionSpec as P

HD = 128
VMEM_LIMIT = 32 * 1024 * 1024
SMEM = pl.BlockSpec(memory_space=pltpu.SMEM)
BLOCK = 512
CUTS = (4, 1)
MASKED = -1e30
ANY = pl.BlockSpec(memory_space=pl.ANY)
BRIEF = pl.CostEstimate(flops=1000, bytes_accessed=1000, transcendentals=0)
HBM = pl.BlockSpec(memory_space=pltpu.HBM)
VMEM = pl.BlockSpec(memory_space=pltpu.VMEM)


def in_hbm(array):
    return pltpu.with_memory_space_constraint(array, pltpu.HBM)


def in_vmem(array):
    return pltpu.with_memory_space_constraint(array, pltpu.VMEM)


def attend_some(
    queries,
    fresh_keys,
    fresh_values,
    paged_keys,
    paged_values,
    request_page_table,
    live_token_count,
    place,
    per_owner,
    wanted,
    after=None,
):
    requests_here, pages = request_page_table.shape
    slots = queries.shape[0] // requests_here
    width = queries.shape[1]
    heads = width // HD
    pool_pages, page_rows = paged_keys.shape[:2]
    cached = pages * page_rows
    count = len(wanted)
    per_out = count // 2
    exponent_scale = math.log2(math.e) / math.sqrt(HD)

    def kernel(table, live, place, q_hbm, fk_hbm, fv_hbm, pk_hbm, pv_hbm, *rest):
        ids = [(place[0] ^ away) * per_owner + n for away, n in wanted]
        outs, bufs = rest[-10:-8], rest[-8:]
        q_buf, fk_buf, fv_buf, pk_buf, pv_buf, order, seen, in_sems = bufs

        def fetch(src, dst, sem):
            return pltpu.make_async_copy(src, dst, in_sems.at[sem])

        def rows_of(n):
            return pl.ds(pl.multiple_of(ids[n] * slots, slots), slots)

        def query_copy(n):
            return fetch(q_hbm.at[rows_of(n)], q_buf.at[n], 3 * n)

        def key_copy(n):
            return fetch(fk_hbm.at[rows_of(n)], fk_buf.at[n], 3 * n + 1)

        def value_copy(n):
            return fetch(fv_hbm.at[rows_of(n)], fv_buf.at[n], 3 * n + 2)

        def key_page(m):
            page = order[m]
            return fetch(pk_hbm.at[page], pk_buf.at[page], 3 * count + 2 * m)

        def value_page(m):
            page = order[m]
            return fetch(pv_hbm.at[page], pv_buf.at[page], 3 * count + 2 * m + 1)

        def start(copies):
            for copy in copies:
                copy.start()

        def start_pages(begin, end):
            for m in range(pages, pool_pages):

                @pl.when((m >= begin) & (m < end))
                def _(m=m):
                    key_page(m).start()

            for m in range(pages, pool_pages):

                @pl.when((m >= begin) & (m < end))
                def _(m=m):
                    value_page(m).start()

        for j in range(pages):
            order[j] = table[ids[0], j]
        start([query_copy(0), key_copy(0)] + [key_page(m) for m in range(pages)])
        start([value_copy(0)] + [value_page(m) for m in range(pages)])
        for page in range(pool_pages):
            taken = order[0] == page
            for j in range(1, pages):
                taken = taken | (order[j] == page)
            seen[page] = taken.astype(jnp.int32)
        bounds = [jnp.int32(pages)]
        for n in range(1, count):
            free = bounds[-1]
            for j in range(pages):
                page = table[ids[n], j]
                fresh = seen[page] == 0

                @pl.when(fresh)
                def _(page=page, free=free):
                    order[free] = page
                    seen[page] = 1

                free = free + fresh.astype(jnp.int32)
            bounds.append(free)
            start([query_copy(n), key_copy(n), value_copy(n)])
            start_pages(bounds[n - 1], bounds[n])

        waited = set()

        def wait(name, make, indices):
            if name not in waited:
                waited.add(name)
                for index in indices:
                    make(index).wait()

        def wait_pages(name, make, n):
            if name not in waited:
                waited.add(name)
                for m in range(pages, pool_pages):

                    @pl.when((m >= bounds[n - 1]) & (m < bounds[n]))
                    def _(m=m):
                        make(m).wait()

        def keys_ready(duo):
            for n in range(1 + max(n for n, _ in duo)):
                wait(("q", n), query_copy, [n])
                wait(("k", n), key_copy, [n])
                if n:
                    wait_pages(("k pages", n), key_page, n)
                else:
                    wait(("k pages", 0), key_page, range(pages))

        def values_ready(duo):
            for n in range(1 + max(n for n, _ in duo)):
                wait(("v", n), value_copy, [n])
                if n:
                    wait_pages(("v pages", n), value_page, n)
                else:
                    wait(("v pages", 0), value_page, range(pages))

        def lanes(h, several=1):
            return slice(h * HD, (h + several) * HD)

        def gather(pool, fresh, n, here):
            return jnp.concatenate(
                [pool[table[ids[n], j], :, here] for j in range(pages)] + [fresh[n, :, here]],
                axis=0,
            )

        def side_by_side(pool, fresh, duo):
            (n, h), (other_n, other_h) = duo
            if n == other_n and other_h == h + 1:
                return gather(pool, fresh, n, lanes(h, 2))
            return jnp.concatenate(
                [gather(pool, fresh, m, lanes(g)) for m, g in duo],
                axis=1,
            )

        def score(duo):
            (n, h), (other_n, other_h) = duo
            blank = jnp.zeros((slots, HD), jnp.bfloat16)
            diagonal = jnp.concatenate(
                [
                    jnp.concatenate([q_buf[n, :, lanes(h)], blank], axis=1),
                    jnp.concatenate([blank, q_buf[other_n, :, lanes(other_h)]], axis=1),
                ],
                axis=0,
            )
            return lax.dot_general(
                diagonal,
                side_by_side(pk_buf, fk_buf, duo),
                (((1,), (1,)), ((), ())),
                preferred_element_type=jnp.float32,
            )

        def weigh(duo, scores):
            column = lax.broadcasted_iota(jnp.int32, (slots, slots), 1)
            usable = jnp.concatenate([column < live[ids[n]] for n, _ in duo], axis=0)
            scores = jnp.concatenate(
                [scores[:, :cached], jnp.where(usable, scores[:, cached:], MASKED)], axis=1
            )
            peak = jnp.max(scores, axis=1, keepdims=True)
            weights = jnp.exp2((scores - peak) * exponent_scale)
            return weights.astype(jnp.bfloat16), jnp.sum(weights, axis=1, keepdims=True)

        def blend(duo, weights, row_total):
            blended = jnp.dot(
                weights, side_by_side(pv_buf, fv_buf, duo), preferred_element_type=jnp.float32
            )
            row = lax.broadcasted_iota(jnp.int32, (slots, HD), 0)
            for m, (n, h) in enumerate(duo):
                rows = slice(m * slots, (m + 1) * slots)
                attended = blended[rows, lanes(m)] / row_total[rows]
                attended = jnp.where(row < live[ids[n]], attended, 0.0)
                at = (n % per_out) * slots
                outs[n // per_out][at : at + slots, lanes(h)] = attended.astype(jnp.bfloat16)

        units = []
        for first in range(0, count, 2):
            units += [((n, h), (n, h + 1)) for n in (first, first + 1) for h in range(0, heads - 1, 2)]
            if heads % 2:
                units.append(((first, heads - 1), (first + 1, heads - 1)))
        keys_ready(units[0])
        scores = score(units[0])
        weighed = None
        for u, duo in enumerate(units):
            later = None
            if u + 1 < len(units):
                keys_ready(units[u + 1])
                later = score(units[u + 1])
            if u:
                values_ready(units[u - 1])
                blend(units[u - 1], *weighed)
            weighed = weigh(duo, scores)
            scores = later
        values_ready(units[-1])
        blend(units[-1], *weighed)

    extra = () if after is None else (after,)
    out_shape = pltpu.VMEM((per_out * slots, width), jnp.bfloat16)
    return pl.pallas_call(
        kernel,
        grid_spec=pltpu.PrefetchScalarGridSpec(
            num_scalar_prefetch=3,
            grid=(1,),
            in_specs=[HBM] * 5 + [ANY] * len(extra),
            out_specs=[VMEM] * 2,
            scratch_shapes=[
                pltpu.VMEM((count, slots, width), jnp.bfloat16),
                pltpu.VMEM((count, slots, width), jnp.bfloat16),
                pltpu.VMEM((count, slots, width), jnp.bfloat16),
                pltpu.VMEM(paged_keys.shape, jnp.bfloat16),
                pltpu.VMEM(paged_values.shape, jnp.bfloat16),
                pltpu.SMEM((pool_pages,), jnp.int32),
                pltpu.SMEM((pool_pages,), jnp.int32),
                pltpu.SemaphoreType.DMA((3 * count + 2 * pool_pages,)),
            ],
        ),
        out_shape=[out_shape] * 2,
        compiler_params=pltpu.CompilerParams(vmem_limit_bytes=VMEM_LIMIT),
        cost_estimate=BRIEF,
        name="attend",
    )(
        in_hbm(request_page_table),
        in_hbm(live_token_count),
        place,
        *map(in_hbm, (queries, fresh_keys, fresh_values, paged_keys, paged_values)),
        *extra,
    )


def project(own, other, weight, weight_other, cuts, after):
    rows = own.shape[0]
    bounds = [sum(cuts[:n]) for n in range(len(cuts) + 1)]
    assert bounds[-1] * BLOCK == weight.shape[1]

    def kernel(a, b, w, u, after, *outs):
        features = jnp.concatenate([a[...], b[...]], axis=1)
        for part, out in enumerate(outs):
            for n in range(cuts[part]):
                here = slice((bounds[part] + n) * BLOCK, (bounds[part] + n + 1) * BLOCK)
                out[:, n * BLOCK : (n + 1) * BLOCK] = jnp.dot(
                    features,
                    jnp.concatenate([w[:, here], u[:, here]], axis=0),
                    preferred_element_type=jnp.float32,
                ).astype(jnp.bfloat16)

    return pl.pallas_call(
        kernel,
        in_specs=[VMEM] * 4 + [ANY],
        out_specs=[VMEM] * len(cuts),
        out_shape=[pltpu.VMEM((rows, cut * BLOCK), jnp.bfloat16) for cut in cuts],
        compiler_params=pltpu.CompilerParams(vmem_limit_bytes=VMEM_LIMIT),
        cost_estimate=BRIEF,
        name="project",
    )(in_vmem(own), in_vmem(other), in_vmem(weight), in_vmem(weight_other), after)


def pack_pair(ups, downs, place, after):
    rank, columns = ups[0].shape[1:]
    width = downs[0].shape[2]
    half = columns // 2

    def kernel(place, up_0, up_1, down_0, down_1, after, out):
        here = pl.ds(pl.multiple_of((place[0] & 1) * half, half), half)
        for n, (up, down) in enumerate(((up_0, down_0), (up_1, down_1))):
            out[n, :, :half] = up[0, :, here]
            out[n, :, half:] = down[0]

    return pl.pallas_call(
        kernel,
        in_specs=[SMEM] + [VMEM] * 4 + [ANY],
        out_specs=VMEM,
        out_shape=jax.ShapeDtypeStruct((2, rank, half + width), ups[0].dtype),
        compiler_params=pltpu.CompilerParams(vmem_limit_bytes=VMEM_LIMIT),
        cost_estimate=BRIEF,
        name="pack_pair",
    )(place, *ups, *downs, after)


def pick_factors(pairs, place, lookup, per_owner, width, after):
    rank = pairs[0].shape[1]
    half = pairs[0].shape[2] - width
    count = len(pairs)

    def kernel(place, slot, in_use, pool_row, *refs):
        pieces, outs = refs[:count], refs[-2:]
        for n, out in enumerate(outs):
            for m in range(2):
                for i in range(2):
                    request = (place[0] ^ n ^ (0 if m else 2)) * per_owner + i
                    row = pool_row[in_use[slot[request]]]
                    apart = lax.rem(place[1] // 2 - row // 2 + count, count)
                    side = (row ^ place[1]) & 1
                    for d, piece in enumerate(pieces):

                        @pl.when(apart == d)
                        def _(piece=piece, out=out, k=2 * m + i, m=m, i=i, side=side):
                            out[:, k * width : (k + 1) * width] = piece[side, :, half:]
                            if m:
                                there = 4 * width + i * half
                                out[:, there : there + half] = piece[side, :, :half]

    shape = jax.ShapeDtypeStruct((rank, 4 * width + 2 * half), pairs[0].dtype)
    return pl.pallas_call(
        kernel,
        in_specs=[SMEM] * 4 + [VMEM] * count + [ANY],
        out_specs=[VMEM] * 2,
        out_shape=[shape] * 2,
        compiler_params=pltpu.CompilerParams(vmem_limit_bytes=VMEM_LIMIT),
        cost_estimate=BRIEF,
        name="pick_factors",
    )(place, *lookup, *pairs, after)


def ranks_and_part(here, other, factors, part):
    slots, width = here[0].shape
    rows = part.shape[0]
    rank = factors[0].shape[0]
    assert part.shape[1] == 4 * slots

    def kernel(*refs):
        factors, blocks, (part_in, part_out) = refs[:2], refs[2:6], refs[6:]
        part_out[:rows] = part_in[...]
        for i in range(2):
            acts = sum(
                lax.dot_general(
                    factors[m][:, i * width : (i + 1) * width],
                    blocks[2 * m + i][...],
                    (((1,), (1,)), ((), ())),
                    preferred_element_type=jnp.float32,
                )
                for m in range(2)
            )
            high = acts.astype(jnp.bfloat16)
            low = (acts - high.astype(jnp.float32)).astype(jnp.bfloat16)
            part_out[rows:, 2 * i * slots : (2 * i + 1) * slots] = high
            part_out[rows:, (2 * i + 1) * slots : (2 * i + 2) * slots] = low

    return pl.pallas_call(
        kernel,
        in_specs=[VMEM] * 7,
        out_specs=VMEM,
        out_shape=jax.ShapeDtypeStruct((rows + rank, part.shape[1]), jnp.bfloat16),
        compiler_params=pltpu.CompilerParams(vmem_limit_bytes=VMEM_LIMIT),
        cost_estimate=BRIEF,
        name="ranks_and_part",
    )(*factors, *here, *other, part)


def project_own(own, other, weight, weight_other, first, last, factors, gating, place):
    rows, width = own.shape
    columns = weight.shape[1]
    blocks = columns // BLOCK
    slots = rows // 2
    rank = factors[0].shape[0]
    half = columns // 2
    covered = (columns - last.shape[1]) // BLOCK

    def kernel(
        place, a, b, w, u, first, last, mine, theirs, gate, out, rest_out, gates, out_buf, ups, sems
    ):
        def store(i, n):
            there = (pl.ds(i * slots, slots), pl.ds(n * BLOCK, BLOCK))
            return pltpu.make_async_copy(out_buf.at[there], out.at[there], sems.at[i, n])

        core = place[0] & 1
        gates[...] = jnp.zeros_like(gates)
        pieces = []
        for i in range(2):
            here = slice(i * slots, (i + 1) * slots)
            down = slice((2 + i) * width, (3 + i) * width)
            acts = sum(
                lax.dot_general(
                    factors[:, down],
                    block[here],
                    (((1,), (1,)), ((), ())),
                    preferred_element_type=jnp.float32,
                )
                for factors, block in ((mine, a), (theirs, b))
            )
            for m in range(2 * i, 2 * i + 2):
                acts += last[slots:, m * slots : (m + 1) * slots].astype(jnp.float32)
            high = acts.astype(jnp.bfloat16).astype(jnp.float32)
            pieces.append(jnp.concatenate([high, acts - high], axis=0).T.astype(jnp.bfloat16))
            up = 4 * width + i * half
            for m in range(2):
                for away, factors in enumerate((mine, theirs)):
                    there = pl.ds(pl.multiple_of((core ^ away) * half, half), half)
                    ups[i, m * rank : (m + 1) * rank, there] = factors[:, up : up + half]
            gates[i : i + 1] = gate[pl.ds(place[0] * 2 + i, 1), :]
        features = jnp.concatenate([a[...], b[...]], axis=1)
        for n in range(blocks):
            here = slice(n * BLOCK, (n + 1) * BLOCK)
            sums = jnp.dot(
                features,
                jnp.concatenate([w[:, here], u[:, here]], axis=0),
                preferred_element_type=jnp.float32,
            )
            for i in range(2):
                those = slice(i * slots, (i + 1) * slots)
                update = sums[those] + jnp.dot(
                    pieces[i], ups[i, :, here], preferred_element_type=jnp.float32
                )
                if not i:
                    update += first[:, here].astype(jnp.float32)
                elif n >= covered:
                    there = slice((n - covered) * BLOCK, (n - covered + 1) * BLOCK)
                    update += last[:slots, there].astype(jnp.float32)
                gated = update * gates[i : i + 1, here]
                if i and n < covered:
                    rest_out[:, here] = gated
                else:
                    out_buf[those, here] = gated.astype(jnp.bfloat16)
                    store(i, n).start()
        for i in range(2):
            for n in range(covered if i else 0, blocks):
                store(i, n).wait()

    return pl.pallas_call(
        kernel,
        in_specs=[SMEM] + [VMEM] * 9,
        out_specs=[HBM, VMEM, VMEM],
        out_shape=[
            pltpu.HBM((rows, columns), jnp.bfloat16),
            jax.ShapeDtypeStruct((slots, covered * BLOCK), jnp.float32),
            jax.ShapeDtypeStruct((8, columns), jnp.float32),
        ],
        scratch_shapes=[
            pltpu.VMEM((rows, columns), jnp.bfloat16),
            pltpu.VMEM((2, 2 * rank, columns), jnp.bfloat16),
            pltpu.SemaphoreType.DMA((2, blocks)),
        ],
        compiler_params=pltpu.CompilerParams(vmem_limit_bytes=VMEM_LIMIT),
        cost_estimate=BRIEF,
        name="project_own",
    )(
        place,
        own,
        other,
        in_vmem(weight),
        in_vmem(weight_other),
        first,
        last,
        *factors,
        gating,
    )


def finish(so_far, rest, received, gates):
    rows, columns = so_far.shape
    slots, wide = rest.shape

    def kernel(sums, part, gate, so_far, out):
        out[...] = (sums[...] + part[...].astype(jnp.float32) * gate[1:2]).astype(jnp.bfloat16)

    return pl.pallas_call(
        kernel,
        grid=(wide // 1024,),
        in_specs=[
            pl.BlockSpec((slots, 1024), lambda j: (0, j)),
            pl.BlockSpec((slots, 1024), lambda j: (0, j)),
            pl.BlockSpec((gates.shape[0], 1024), lambda j: (0, j)),
            ANY,
        ],
        out_specs=pl.BlockSpec((slots, 1024), lambda j: (1, j)),
        out_shape=jax.ShapeDtypeStruct((rows, columns), jnp.bfloat16),
        input_output_aliases={3: 0},
        compiler_params=pltpu.CompilerParams(vmem_limit_bytes=VMEM_LIMIT),
        cost_estimate=BRIEF,
        name="finish",
    )(rest, received, gates, so_far)


def body(
    queries,
    fresh_keys,
    fresh_values,
    paged_keys,
    paged_values,
    request_page_table,
    live_token_count,
    request_adapter_slot,
    adapters_in_use,
    adapter_pool_row,
    adapter_down_factors,
    adapter_up_factors,
    output_weight,
    gating,
):
    tp = lax.axis_size("tp")
    holders = lax.axis_size("req")
    place = jnp.stack([lax.axis_index("tp"), lax.axis_index("req")]).astype(jnp.int32)
    per_owner = live_token_count.shape[0] // tp

    def swap(array, flip):
        return lax.ppermute(array, "tp", [(s, s ^ flip) for s in range(tp)])

    def attend(wanted, after=None):
        return attend_some(
            queries,
            fresh_keys,
            fresh_values,
            paged_keys,
            paged_values,
            request_page_table,
            live_token_count,
            place,
            per_owner,
            wanted,
            after,
        )

    ups, downs = (
        (factors, lax.ppermute(factors, "req", [(s, s ^ 1) for s in range(holders)]))
        for factors in (adapter_up_factors, adapter_down_factors)
    )
    weight_other = swap(output_weight, 1)

    away_a, here_a = attend(((3, 0), (2, 0)))
    away_a, ups, downs = lax.optimization_barrier((away_a, ups, downs))
    other_a = swap(away_a, 1)
    pair = pack_pair(ups, downs, place, away_a)
    (sent_a,) = project(here_a, other_a, output_weight, weight_other, (sum(CUTS),), pair)
    first = swap(sent_a, 2)

    pair, _ = lax.optimization_barrier((pair, sent_a))
    pairs = [pair] + [
        lax.ppermute(pair, "req", [(s, (s + d) % holders) for s in range(holders)])
        for d in range(2, holders, 2)
    ]
    away_b, here_b = attend(((3, 1), (2, 1)), sent_a)
    away_b, *pairs = lax.optimization_barrier((away_b, *pairs))
    other_b = swap(away_b, 1)
    sent_b = project(here_b, other_b, output_weight, weight_other, CUTS, sent_a)
    second = swap(sent_b[0], 2)

    first, *pairs = lax.optimization_barrier((first, *pairs))
    lookup = (request_adapter_slot, adapters_in_use, adapter_pool_row)
    width = output_weight.shape[0]
    factors, factors_away = pick_factors(pairs, place, lookup, per_owner, width, sent_b[0])
    factors = (factors, swap(factors_away, 1))
    last = ranks_and_part((here_a, here_b), (other_a, other_b), factors, sent_b[1])
    own_away, own_here = attend(((1, 0), (1, 1), (0, 0), (0, 1)), last)
    own_away, last = lax.optimization_barrier((own_away, swap(last, 2)))
    own_other = swap(own_away, 1)
    out, rest, gates = project_own(
        own_here, own_other, output_weight, weight_other, first, last, factors, gating, place
    )
    return finish(out, rest, second, gates)


def solution(mesh):
    return jax.shard_map(
        body,
        mesh=mesh,
        in_specs=(
            P("req", "tp"),
            P("req", "tp"),
            P("req", "tp"),
            P("req", None, "tp"),
            P("req", None, "tp"),
            P("req", None),
            P("req"),
            P("req"),
            P(),
            P(),
            P("req", None, "tp"),
            P("req", None, None),
            P("tp", None),
            P("req", None),
        ),
        out_specs=P(("req", "tp"), None),
        check_vma=False,
    )
```

```python
import math

import jax
import jax.numpy as jnp
from jax import lax
from jax.experimental import pallas as pl
from jax.experimental.pallas import tpu as pltpu
from jax.sharding import PartitionSpec as P

HD = 128
VMEM_LIMIT = 32 * 1024 * 1024
SMEM = pl.BlockSpec(memory_space=pltpu.SMEM)
BLOCK = 512
CUTS = (3, 1, 1)
MASKED = -1e30
ANY = pl.BlockSpec(memory_space=pl.ANY)
BRIEF = pl.CostEstimate(flops=1000, bytes_accessed=1000, transcendentals=0)
HBM = pl.BlockSpec(memory_space=pltpu.HBM)
VMEM = pl.BlockSpec(memory_space=pltpu.VMEM)


def in_hbm(array):
    return pltpu.with_memory_space_constraint(array, pltpu.HBM)


def in_vmem(array):
    return pltpu.with_memory_space_constraint(array, pltpu.VMEM)


def attend_some(
    queries,
    fresh_keys,
    fresh_values,
    paged_keys,
    paged_values,
    request_page_table,
    live_token_count,
    place,
    per_owner,
    wanted,
    after=None,
):
    requests_here, pages = request_page_table.shape
    slots = queries.shape[0] // requests_here
    width = queries.shape[1]
    heads = width // HD
    pool_pages, page_rows = paged_keys.shape[:2]
    cached = pages * page_rows
    count = len(wanted)
    per_out = count // 2
    exponent_scale = math.log2(math.e) / math.sqrt(HD)

    def kernel(table, live, place, q_hbm, fk_hbm, fv_hbm, pk_hbm, pv_hbm, *rest):
        ids = [(place[0] ^ away) * per_owner + n for away, n in wanted]
        outs, bufs = rest[-10:-8], rest[-8:]
        q_buf, fk_buf, fv_buf, pk_buf, pv_buf, order, seen, in_sems = bufs

        def fetch(src, dst, sem):
            return pltpu.make_async_copy(src, dst, in_sems.at[sem])

        def rows_of(n):
            return pl.ds(pl.multiple_of(ids[n] * slots, slots), slots)

        def query_copy(n):
            return fetch(q_hbm.at[rows_of(n)], q_buf.at[n], 3 * n)

        def key_copy(n):
            return fetch(fk_hbm.at[rows_of(n)], fk_buf.at[n], 3 * n + 1)

        def value_copy(n):
            return fetch(fv_hbm.at[rows_of(n)], fv_buf.at[n], 3 * n + 2)

        def key_page(m):
            page = order[m]
            return fetch(pk_hbm.at[page], pk_buf.at[page], 3 * count + 2 * m)

        def value_page(m):
            page = order[m]
            return fetch(pv_hbm.at[page], pv_buf.at[page], 3 * count + 2 * m + 1)

        def start(copies):
            for copy in copies:
                copy.start()

        def start_pages(begin, end):
            for m in range(pages, pool_pages):

                @pl.when((m >= begin) & (m < end))
                def _(m=m):
                    key_page(m).start()

            for m in range(pages, pool_pages):

                @pl.when((m >= begin) & (m < end))
                def _(m=m):
                    value_page(m).start()

        for j in range(pages):
            order[j] = table[ids[0], j]
        start([query_copy(0), key_copy(0)] + [key_page(m) for m in range(pages)])
        start([value_copy(0)] + [value_page(m) for m in range(pages)])
        for page in range(pool_pages):
            taken = order[0] == page
            for j in range(1, pages):
                taken = taken | (order[j] == page)
            seen[page] = taken.astype(jnp.int32)
        bounds = [jnp.int32(pages)]
        for n in range(1, count):
            free = bounds[-1]
            for j in range(pages):
                page = table[ids[n], j]
                fresh = seen[page] == 0

                @pl.when(fresh)
                def _(page=page, free=free):
                    order[free] = page
                    seen[page] = 1

                free = free + fresh.astype(jnp.int32)
            bounds.append(free)
            start([query_copy(n), key_copy(n), value_copy(n)])
            start_pages(bounds[n - 1], bounds[n])

        waited = set()

        def wait(name, make, indices):
            if name not in waited:
                waited.add(name)
                for index in indices:
                    make(index).wait()

        def wait_pages(name, make, n):
            if name not in waited:
                waited.add(name)
                for m in range(pages, pool_pages):

                    @pl.when((m >= bounds[n - 1]) & (m < bounds[n]))
                    def _(m=m):
                        make(m).wait()

        def keys_ready(duo):
            for n in range(1 + max(n for n, _ in duo)):
                wait(("q", n), query_copy, [n])
                wait(("k", n), key_copy, [n])
                if n:
                    wait_pages(("k pages", n), key_page, n)
                else:
                    wait(("k pages", 0), key_page, range(pages))

        def values_ready(duo):
            for n in range(1 + max(n for n, _ in duo)):
                wait(("v", n), value_copy, [n])
                if n:
                    wait_pages(("v pages", n), value_page, n)
                else:
                    wait(("v pages", 0), value_page, range(pages))

        def lanes(h, several=1):
            return slice(h * HD, (h + several) * HD)

        def gather(pool, fresh, n, here):
            return jnp.concatenate(
                [pool[table[ids[n], j], :, here] for j in range(pages)] + [fresh[n, :, here]],
                axis=0,
            )

        def side_by_side(pool, fresh, duo):
            (n, h), (other_n, other_h) = duo
            if n == other_n and other_h == h + 1:
                return gather(pool, fresh, n, lanes(h, 2))
            return jnp.concatenate(
                [gather(pool, fresh, m, lanes(g)) for m, g in duo],
                axis=1,
            )

        def score(duo):
            (n, h), (other_n, other_h) = duo
            blank = jnp.zeros((slots, HD), jnp.bfloat16)
            diagonal = jnp.concatenate(
                [
                    jnp.concatenate([q_buf[n, :, lanes(h)], blank], axis=1),
                    jnp.concatenate([blank, q_buf[other_n, :, lanes(other_h)]], axis=1),
                ],
                axis=0,
            )
            return lax.dot_general(
                diagonal,
                side_by_side(pk_buf, fk_buf, duo),
                (((1,), (1,)), ((), ())),
                preferred_element_type=jnp.float32,
            )

        def weigh(duo, scores):
            column = lax.broadcasted_iota(jnp.int32, (slots, slots), 1)
            usable = jnp.concatenate([column < live[ids[n]] for n, _ in duo], axis=0)
            scores = jnp.concatenate(
                [scores[:, :cached], jnp.where(usable, scores[:, cached:], MASKED)], axis=1
            )
            peak = jnp.max(scores, axis=1, keepdims=True)
            weights = jnp.exp2((scores - peak) * exponent_scale)
            return weights.astype(jnp.bfloat16), jnp.sum(weights, axis=1, keepdims=True)

        def blend(duo, weights, row_total):
            blended = jnp.dot(
                weights, side_by_side(pv_buf, fv_buf, duo), preferred_element_type=jnp.float32
            )
            row = lax.broadcasted_iota(jnp.int32, (slots, HD), 0)
            for m, (n, h) in enumerate(duo):
                rows = slice(m * slots, (m + 1) * slots)
                attended = blended[rows, lanes(m)] / row_total[rows]
                attended = jnp.where(row < live[ids[n]], attended, 0.0)
                at = (n % per_out) * slots
                outs[n // per_out][at : at + slots, lanes(h)] = attended.astype(jnp.bfloat16)

        units = []
        for first in range(0, count, 2):
            units += [((n, h), (n, h + 1)) for n in (first, first + 1) for h in range(0, heads - 1, 2)]
            if heads % 2:
                units.append(((first, heads - 1), (first + 1, heads - 1)))
        keys_ready(units[0])
        scores = score(units[0])
        weighed = None
        for u, duo in enumerate(units):
            later = None
            if u + 1 < len(units):
                keys_ready(units[u + 1])
                later = score(units[u + 1])
            if u:
                values_ready(units[u - 1])
                blend(units[u - 1], *weighed)
            weighed = weigh(duo, scores)
            scores = later
        values_ready(units[-1])
        blend(units[-1], *weighed)

    extra = () if after is None else (after,)
    out_shape = pltpu.VMEM((per_out * slots, width), jnp.bfloat16)
    return pl.pallas_call(
        kernel,
        grid_spec=pltpu.PrefetchScalarGridSpec(
            num_scalar_prefetch=3,
            grid=(1,),
            in_specs=[HBM] * 5 + [ANY] * len(extra),
            out_specs=[VMEM] * 2,
            scratch_shapes=[
                pltpu.VMEM((count, slots, width), jnp.bfloat16),
                pltpu.VMEM((count, slots, width), jnp.bfloat16),
                pltpu.VMEM((count, slots, width), jnp.bfloat16),
                pltpu.VMEM(paged_keys.shape, jnp.bfloat16),
                pltpu.VMEM(paged_values.shape, jnp.bfloat16),
                pltpu.SMEM((pool_pages,), jnp.int32),
                pltpu.SMEM((pool_pages,), jnp.int32),
                pltpu.SemaphoreType.DMA((3 * count + 2 * pool_pages,)),
            ],
        ),
        out_shape=[out_shape] * 2,
        compiler_params=pltpu.CompilerParams(vmem_limit_bytes=VMEM_LIMIT),
        cost_estimate=BRIEF,
        name="attend",
    )(
        in_hbm(request_page_table),
        in_hbm(live_token_count),
        place,
        *map(in_hbm, (queries, fresh_keys, fresh_values, paged_keys, paged_values)),
        *extra,
    )


def project(own, other, weight, weight_other, cuts, after):
    rows = own.shape[0]
    bounds = [sum(cuts[:n]) for n in range(len(cuts) + 1)]
    assert bounds[-1] * BLOCK == weight.shape[1]

    def kernel(a, b, w, u, after, *outs):
        features = jnp.concatenate([a[...], b[...]], axis=1)
        for part, out in enumerate(outs):
            for n in range(cuts[part]):
                here = slice((bounds[part] + n) * BLOCK, (bounds[part] + n + 1) * BLOCK)
                out[:, n * BLOCK : (n + 1) * BLOCK] = jnp.dot(
                    features,
                    jnp.concatenate([w[:, here], u[:, here]], axis=0),
                    preferred_element_type=jnp.float32,
                ).astype(jnp.bfloat16)

    return pl.pallas_call(
        kernel,
        in_specs=[VMEM] * 4 + [ANY],
        out_specs=[VMEM] * len(cuts),
        out_shape=[pltpu.VMEM((rows, cut * BLOCK), jnp.bfloat16) for cut in cuts],
        compiler_params=pltpu.CompilerParams(vmem_limit_bytes=VMEM_LIMIT),
        cost_estimate=BRIEF,
        name="project",
    )(in_vmem(own), in_vmem(other), in_vmem(weight), in_vmem(weight_other), after)


def pack_pair(ups, downs, place, after):
    rank, columns = ups[0].shape[1:]
    width = downs[0].shape[2]
    half = columns // 2

    def kernel(place, up_0, up_1, down_0, down_1, after, out):
        here = pl.ds(pl.multiple_of((place[0] & 1) * half, half), half)
        for n, (up, down) in enumerate(((up_0, down_0), (up_1, down_1))):
            out[n, :, :half] = up[0, :, here]
            out[n, :, half:] = down[0]

    return pl.pallas_call(
        kernel,
        in_specs=[SMEM] + [VMEM] * 4 + [ANY],
        out_specs=VMEM,
        out_shape=jax.ShapeDtypeStruct((2, rank, half + width), ups[0].dtype),
        compiler_params=pltpu.CompilerParams(vmem_limit_bytes=VMEM_LIMIT),
        cost_estimate=BRIEF,
        name="pack_pair",
    )(place, *ups, *downs, after)


def pick_factors(pairs, place, lookup, per_owner, width, after):
    rank = pairs[0].shape[1]
    half = pairs[0].shape[2] - width
    count = len(pairs)

    def kernel(place, slot, in_use, pool_row, *refs):
        pieces, outs = refs[:count], refs[-2:]
        for n, out in enumerate(outs):
            for m in range(2):
                for i in range(2):
                    request = (place[0] ^ n ^ (0 if m else 2)) * per_owner + i
                    row = pool_row[in_use[slot[request]]]
                    apart = lax.rem(place[1] // 2 - row // 2 + count, count)
                    side = (row ^ place[1]) & 1
                    for d, piece in enumerate(pieces):

                        @pl.when(apart == d)
                        def _(piece=piece, out=out, k=2 * m + i, m=m, i=i, side=side):
                            out[:, k * width : (k + 1) * width] = piece[side, :, half:]
                            if m:
                                there = 4 * width + i * half
                                out[:, there : there + half] = piece[side, :, :half]

    shape = jax.ShapeDtypeStruct((rank, 4 * width + 2 * half), pairs[0].dtype)
    return pl.pallas_call(
        kernel,
        in_specs=[SMEM] * 4 + [VMEM] * count + [ANY],
        out_specs=[VMEM] * 2,
        out_shape=[shape] * 2,
        compiler_params=pltpu.CompilerParams(vmem_limit_bytes=VMEM_LIMIT),
        cost_estimate=BRIEF,
        name="pick_factors",
    )(place, *lookup, *pairs, after)


def ranks_and_part(here, other, factors, part):
    slots, width = here[0].shape
    rows = part.shape[0]
    rank = factors[0].shape[0]
    assert part.shape[1] == 4 * slots

    def kernel(*refs):
        factors, blocks, (part_in, part_out) = refs[:2], refs[2:6], refs[6:]
        part_out[:rows] = part_in[...]
        for i in range(2):
            acts = sum(
                lax.dot_general(
                    factors[m][:, i * width : (i + 1) * width],
                    blocks[2 * m + i][...],
                    (((1,), (1,)), ((), ())),
                    preferred_element_type=jnp.float32,
                )
                for m in range(2)
            )
            high = acts.astype(jnp.bfloat16)
            low = (acts - high.astype(jnp.float32)).astype(jnp.bfloat16)
            part_out[rows:, 2 * i * slots : (2 * i + 1) * slots] = high
            part_out[rows:, (2 * i + 1) * slots : (2 * i + 2) * slots] = low

    return pl.pallas_call(
        kernel,
        in_specs=[VMEM] * 7,
        out_specs=VMEM,
        out_shape=jax.ShapeDtypeStruct((rows + rank, part.shape[1]), jnp.bfloat16),
        compiler_params=pltpu.CompilerParams(vmem_limit_bytes=VMEM_LIMIT),
        cost_estimate=BRIEF,
        name="ranks_and_part",
    )(*factors, *here, *other, part)


def project_own(
    own, other, weight, weight_other, first, second, last, factors, gating, place
):
    rows, width = own.shape
    columns = weight.shape[1]
    blocks = columns // BLOCK
    slots = rows // 2
    rank = factors[0].shape[0]
    half = columns // 2
    open_from = second.shape[1] // BLOCK
    open_to = (columns - last.shape[1]) // BLOCK

    def kernel(
        place, a, b, w, u, first, second, last, mine, theirs, gate, out, rest_out, gates, out_buf, ups, sems
    ):
        def store(i, n):
            there = (pl.ds(i * slots, slots), pl.ds(n * BLOCK, BLOCK))
            return pltpu.make_async_copy(out_buf.at[there], out.at[there], sems.at[i, n])

        core = place[0] & 1
        gates[...] = jnp.zeros_like(gates)
        pieces = []
        for i in range(2):
            here = slice(i * slots, (i + 1) * slots)
            down = slice((2 + i) * width, (3 + i) * width)
            acts = sum(
                lax.dot_general(
                    factors[:, down],
                    block[here],
                    (((1,), (1,)), ((), ())),
                    preferred_element_type=jnp.float32,
                )
                for factors, block in ((mine, a), (theirs, b))
            )
            for m in range(2 * i, 2 * i + 2):
                acts += last[slots:, m * slots : (m + 1) * slots].astype(jnp.float32)
            high = acts.astype(jnp.bfloat16).astype(jnp.float32)
            pieces.append(jnp.concatenate([high, acts - high], axis=0).T.astype(jnp.bfloat16))
            up = 4 * width + i * half
            for m in range(2):
                for away, factors in enumerate((mine, theirs)):
                    there = pl.ds(pl.multiple_of((core ^ away) * half, half), half)
                    ups[i, m * rank : (m + 1) * rank, there] = factors[:, up : up + half]
            gates[i : i + 1] = gate[pl.ds(place[0] * 2 + i, 1), :]
        features = jnp.concatenate([a[...], b[...]], axis=1)
        for n in range(blocks):
            here = slice(n * BLOCK, (n + 1) * BLOCK)
            sums = jnp.dot(
                features,
                jnp.concatenate([w[:, here], u[:, here]], axis=0),
                preferred_element_type=jnp.float32,
            )
            for i in range(2):
                those = slice(i * slots, (i + 1) * slots)
                update = sums[those] + jnp.dot(
                    pieces[i], ups[i, :, here], preferred_element_type=jnp.float32
                )
                if not i:
                    update += first[:, here].astype(jnp.float32)
                elif n < open_from:
                    update += second[:, here].astype(jnp.float32)
                elif n >= open_to:
                    there = slice((n - open_to) * BLOCK, (n - open_to + 1) * BLOCK)
                    update += last[:slots, there].astype(jnp.float32)
                gated = update * gates[i : i + 1, here]
                if i and open_from <= n < open_to:
                    there = slice((n - open_from) * BLOCK, (n - open_from + 1) * BLOCK)
                    rest_out[:, there] = gated
                else:
                    out_buf[those, here] = gated.astype(jnp.bfloat16)
                    store(i, n).start()
        for i in range(2):
            for n in range(blocks):
                if not (i and open_from <= n < open_to):
                    store(i, n).wait()

    return pl.pallas_call(
        kernel,
        in_specs=[SMEM] + [VMEM] * 10,
        out_specs=[HBM, VMEM, VMEM],
        out_shape=[
            pltpu.HBM((rows, columns), jnp.bfloat16),
            jax.ShapeDtypeStruct((slots, (open_to - open_from) * BLOCK), jnp.float32),
            jax.ShapeDtypeStruct((8, columns), jnp.float32),
        ],
        scratch_shapes=[
            pltpu.VMEM((rows, columns), jnp.bfloat16),
            pltpu.VMEM((2, 2 * rank, columns), jnp.bfloat16),
            pltpu.SemaphoreType.DMA((2, blocks)),
        ],
        compiler_params=pltpu.CompilerParams(vmem_limit_bytes=VMEM_LIMIT),
        cost_estimate=BRIEF,
        name="project_own",
    )(
        place,
        own,
        other,
        in_vmem(weight),
        in_vmem(weight_other),
        first,
        second,
        last,
        *factors,
        gating,
    )


def finish(so_far, rest, received, gates, begin):
    rows, columns = so_far.shape
    slots, wide = rest.shape
    at = begin // wide
    assert begin % wide == 0

    def kernel(sums, part, gate, so_far, out):
        out[...] = (sums[...] + part[...].astype(jnp.float32) * gate[1:2]).astype(jnp.bfloat16)

    return pl.pallas_call(
        kernel,
        grid=(1,),
        in_specs=[
            pl.BlockSpec((slots, wide), lambda j: (0, 0)),
            pl.BlockSpec((slots, wide), lambda j: (0, 0)),
            pl.BlockSpec((gates.shape[0], wide), lambda j: (0, at)),
            ANY,
        ],
        out_specs=pl.BlockSpec((slots, wide), lambda j: (1, at)),
        out_shape=jax.ShapeDtypeStruct((rows, columns), jnp.bfloat16),
        input_output_aliases={3: 0},
        compiler_params=pltpu.CompilerParams(vmem_limit_bytes=VMEM_LIMIT),
        cost_estimate=BRIEF,
        name="finish",
    )(rest, received, gates, so_far)


def body(
    queries,
    fresh_keys,
    fresh_values,
    paged_keys,
    paged_values,
    request_page_table,
    live_token_count,
    request_adapter_slot,
    adapters_in_use,
    adapter_pool_row,
    adapter_down_factors,
    adapter_up_factors,
    output_weight,
    gating,
):
    tp = lax.axis_size("tp")
    holders = lax.axis_size("req")
    place = jnp.stack([lax.axis_index("tp"), lax.axis_index("req")]).astype(jnp.int32)
    per_owner = live_token_count.shape[0] // tp

    def swap(array, flip):
        return lax.ppermute(array, "tp", [(s, s ^ flip) for s in range(tp)])

    def attend(wanted, after=None):
        return attend_some(
            queries,
            fresh_keys,
            fresh_values,
            paged_keys,
            paged_values,
            request_page_table,
            live_token_count,
            place,
            per_owner,
            wanted,
            after,
        )

    ups, downs = (
        (factors, lax.ppermute(factors, "req", [(s, s ^ 1) for s in range(holders)]))
        for factors in (adapter_up_factors, adapter_down_factors)
    )
    weight_other = swap(output_weight, 1)

    away_a, here_a = attend(((3, 0), (2, 0)))
    away_a, ups, downs = lax.optimization_barrier((away_a, ups, downs))
    other_a = swap(away_a, 1)
    pair = pack_pair(ups, downs, place, away_a)
    (sent_a,) = project(here_a, other_a, output_weight, weight_other, (sum(CUTS),), pair)
    first = swap(sent_a, 2)

    pair, _ = lax.optimization_barrier((pair, sent_a))
    pairs = [pair] + [
        lax.ppermute(pair, "req", [(s, (s + d) % holders) for s in range(holders)])
        for d in range(2, holders, 2)
    ]
    away_b, here_b = attend(((3, 1), (2, 1)), sent_a)
    away_b, *pairs = lax.optimization_barrier((away_b, *pairs))
    other_b = swap(away_b, 1)
    sent_b = project(here_b, other_b, output_weight, weight_other, CUTS, sent_a)
    second = swap(sent_b[0], 2)

    first, *pairs = lax.optimization_barrier((first, *pairs))
    lookup = (request_adapter_slot, adapters_in_use, adapter_pool_row)
    width = output_weight.shape[0]
    factors, factors_away = pick_factors(pairs, place, lookup, per_owner, width, sent_b[0])
    factors = (factors, swap(factors_away, 1))
    last = ranks_and_part((here_a, here_b), (other_a, other_b), factors, sent_b[2])
    third, first, _ = lax.optimization_barrier((sent_b[1], first, last))
    third = swap(third, 2)
    own_away, own_here = attend(((1, 0), (1, 1), (0, 0), (0, 1)), last)
    own_away, second, last = lax.optimization_barrier((own_away, second, swap(last, 2)))
    own_other = swap(own_away, 1)
    out, rest, gates = project_own(
        own_here,
        own_other,
        output_weight,
        weight_other,
        first,
        second,
        last,
        factors,
        gating,
        place,
    )
    return finish(out, rest, third, gates, CUTS[0] * BLOCK)


def solution(mesh):
    return jax.shard_map(
        body,
        mesh=mesh,
        in_specs=(
            P("req", "tp"),
            P("req", "tp"),
            P("req", "tp"),
            P("req", None, "tp"),
            P("req", None, "tp"),
            P("req", None),
            P("req"),
            P("req"),
            P(),
            P(),
            P("req", None, "tp"),
            P("req", None, None),
            P("tp", None),
            P("req", None),
        ),
        out_specs=P(("req", "tp"), None),
        check_vma=False,
    )
```

```python
import math

import jax
import jax.numpy as jnp
from jax import lax
from jax.experimental import pallas as pl
from jax.experimental.pallas import tpu as pltpu
from jax.sharding import PartitionSpec as P

HD = 128
VMEM_LIMIT = 32 * 1024 * 1024
SMEM = pl.BlockSpec(memory_space=pltpu.SMEM)
BLOCK = 512
CUTS = (3, 1, 1)
MASKED = -1e30
ANY = pl.BlockSpec(memory_space=pl.ANY)
BRIEF = pl.CostEstimate(flops=1000, bytes_accessed=1000, transcendentals=0)
HBM = pl.BlockSpec(memory_space=pltpu.HBM)
VMEM = pl.BlockSpec(memory_space=pltpu.VMEM)


def in_hbm(array):
    return pltpu.with_memory_space_constraint(array, pltpu.HBM)


def in_vmem(array):
    return pltpu.with_memory_space_constraint(array, pltpu.VMEM)


def attend_some(
    queries,
    fresh_keys,
    fresh_values,
    paged_keys,
    paged_values,
    request_page_table,
    live_token_count,
    place,
    per_owner,
    wanted,
    pools=None,
    after=None,
):
    requests_here, pages = request_page_table.shape
    slots = queries.shape[0] // requests_here
    width = queries.shape[1]
    heads = width // HD
    pool_pages, page_rows = paged_keys.shape[:2]
    cached = pages * page_rows
    load = pools is None
    count = len(wanted)
    per_out = count // 2
    exponent_scale = math.log2(math.e) / math.sqrt(HD)

    def kernel(table, live, place, q_hbm, fk_hbm, fv_hbm, pk_hbm, pv_hbm, *rest):
        ids = [(place[0] ^ away) * per_owner + n for away, n in wanted]
        q_buf, fk_buf, fv_buf, order, seen, in_sems = rest[-6:]
        if load:
            *outs, pk_buf, pv_buf = rest[-10:-6]
        else:
            outs, pk_buf, pv_buf = rest[-8:-6], pk_hbm, pv_hbm

        def fetch(src, dst, sem):
            return pltpu.make_async_copy(src, dst, in_sems.at[sem])

        def rows_of(n):
            return pl.ds(pl.multiple_of(ids[n] * slots, slots), slots)

        def query_copy(n):
            return fetch(q_hbm.at[rows_of(n)], q_buf.at[n], 3 * n)

        def key_copy(n):
            return fetch(fk_hbm.at[rows_of(n)], fk_buf.at[n], 3 * n + 1)

        def value_copy(n):
            return fetch(fv_hbm.at[rows_of(n)], fv_buf.at[n], 3 * n + 2)

        def key_page(m):
            page = order[m]
            return fetch(pk_hbm.at[page], pk_buf.at[page], 3 * count + 2 * m)

        def value_page(m):
            page = order[m]
            return fetch(pv_hbm.at[page], pv_buf.at[page], 3 * count + 2 * m + 1)

        def start(copies):
            for copy in copies:
                copy.start()

        def start_pages(begin, end):
            for m in range(pages, pool_pages):

                @pl.when((m >= begin) & (m < end))
                def _(m=m):
                    key_page(m).start()

            for m in range(pages, pool_pages):

                @pl.when((m >= begin) & (m < end))
                def _(m=m):
                    value_page(m).start()

        if load:
            for j in range(pages):
                order[j] = table[ids[0], j]
            start([query_copy(0), key_copy(0)] + [key_page(m) for m in range(pages)])
            start([value_copy(0)] + [value_page(m) for m in range(pages)])
            for page in range(pool_pages):
                taken = order[0] == page
                for j in range(1, pages):
                    taken = taken | (order[j] == page)
                seen[page] = taken.astype(jnp.int32)
            bounds = [jnp.int32(pages)]
            for n in range(1, count):
                free = bounds[-1]
                for j in range(pages):
                    page = table[ids[n], j]
                    fresh = seen[page] == 0

                    @pl.when(fresh)
                    def _(page=page, free=free):
                        order[free] = page
                        seen[page] = 1

                    free = free + fresh.astype(jnp.int32)
                bounds.append(free)
                start([query_copy(n), key_copy(n), value_copy(n)])
                start_pages(bounds[n - 1], bounds[n])
            free = bounds[-1]
            for page in range(pool_pages):
                fresh = seen[page] == 0

                @pl.when(fresh)
                def _(page=page, free=free):
                    order[free] = page

                free = free + fresh.astype(jnp.int32)
            start_pages(bounds[-1], pool_pages)
        else:
            for n in range(count):
                start([query_copy(n), key_copy(n), value_copy(n)])

        waited = set()

        def wait(name, make, indices):
            if name not in waited:
                waited.add(name)
                for index in indices:
                    make(index).wait()

        def wait_pages(name, make, begin, end):
            if name not in waited:
                waited.add(name)
                for m in range(pages, pool_pages):

                    @pl.when((m >= begin) & (m < end))
                    def _(m=m):
                        make(m).wait()

        def keys_ready(duo):
            for n in range(1 + max(n for n, _ in duo)):
                wait(("q", n), query_copy, [n])
                wait(("k", n), key_copy, [n])
                if load and n:
                    wait_pages(("k pages", n), key_page, bounds[n - 1], bounds[n])
                elif load:
                    wait(("k pages", 0), key_page, range(pages))

        def values_ready(duo):
            for n in range(1 + max(n for n, _ in duo)):
                wait(("v", n), value_copy, [n])
                if load and n:
                    wait_pages(("v pages", n), value_page, bounds[n - 1], bounds[n])
                elif load:
                    wait(("v pages", 0), value_page, range(pages))

        def lanes(h, several=1):
            return slice(h * HD, (h + several) * HD)

        def gather(pool, fresh, n, here):
            return jnp.concatenate(
                [pool[table[ids[n], j], :, here] for j in range(pages)] + [fresh[n, :, here]],
                axis=0,
            )

        def side_by_side(pool, fresh, duo):
            (n, h), (other_n, other_h) = duo
            if n == other_n and other_h == h + 1:
                return gather(pool, fresh, n, lanes(h, 2))
            return jnp.concatenate(
                [gather(pool, fresh, m, lanes(g)) for m, g in duo],
                axis=1,
            )

        def score(duo):
            (n, h), (other_n, other_h) = duo
            blank = jnp.zeros((slots, HD), jnp.bfloat16)
            diagonal = jnp.concatenate(
                [
                    jnp.concatenate([q_buf[n, :, lanes(h)], blank], axis=1),
                    jnp.concatenate([blank, q_buf[other_n, :, lanes(other_h)]], axis=1),
                ],
                axis=0,
            )
            return lax.dot_general(
                diagonal,
                side_by_side(pk_buf, fk_buf, duo),
                (((1,), (1,)), ((), ())),
                preferred_element_type=jnp.float32,
            )

        def weigh(duo, scores):
            column = lax.broadcasted_iota(jnp.int32, (slots, slots), 1)
            usable = jnp.concatenate([column < live[ids[n]] for n, _ in duo], axis=0)
            scores = jnp.concatenate(
                [scores[:, :cached], jnp.where(usable, scores[:, cached:], MASKED)], axis=1
            )
            peak = jnp.max(scores, axis=1, keepdims=True)
            weights = jnp.exp2((scores - peak) * exponent_scale)
            return weights.astype(jnp.bfloat16), jnp.sum(weights, axis=1, keepdims=True)

        def blend(duo, weights, row_total):
            blended = jnp.dot(
                weights, side_by_side(pv_buf, fv_buf, duo), preferred_element_type=jnp.float32
            )
            row = lax.broadcasted_iota(jnp.int32, (slots, HD), 0)
            for m, (n, h) in enumerate(duo):
                rows = slice(m * slots, (m + 1) * slots)
                attended = blended[rows, lanes(m)] / row_total[rows]
                attended = jnp.where(row < live[ids[n]], attended, 0.0)
                at = (n % per_out) * slots
                outs[n // per_out][at : at + slots, lanes(h)] = attended.astype(jnp.bfloat16)

        units = []
        for first in range(0, count, 2):
            units += [((n, h), (n, h + 1)) for n in (first, first + 1) for h in range(0, heads - 1, 2)]
            if heads % 2:
                units.append(((first, heads - 1), (first + 1, heads - 1)))
        keys_ready(units[0])
        scores = score(units[0])
        weighed = None
        for u, duo in enumerate(units):
            later = None
            if u + 1 < len(units):
                keys_ready(units[u + 1])
                later = score(units[u + 1])
            if u:
                values_ready(units[u - 1])
                blend(units[u - 1], *weighed)
            weighed = weigh(duo, scores)
            scores = later
        values_ready(units[-1])
        blend(units[-1], *weighed)
        if load:
            wait_pages(("k pages", count), key_page, bounds[-1], pool_pages)
            wait_pages(("v pages", count), value_page, bounds[-1], pool_pages)

    extra = () if after is None else (after,)
    out_shape = [pltpu.VMEM((per_out * slots, width), jnp.bfloat16)] * 2
    if load:
        out_shape += [pltpu.VMEM(paged_keys.shape, jnp.bfloat16)] * 2
    return pl.pallas_call(
        kernel,
        grid_spec=pltpu.PrefetchScalarGridSpec(
            num_scalar_prefetch=3,
            grid=(1,),
            in_specs=[HBM] * 3 + [HBM if load else VMEM] * 2 + [ANY] * len(extra),
            out_specs=[VMEM] * len(out_shape),
            scratch_shapes=[
                pltpu.VMEM((count, slots, width), jnp.bfloat16),
                pltpu.VMEM((count, slots, width), jnp.bfloat16),
                pltpu.VMEM((count, slots, width), jnp.bfloat16),
                pltpu.SMEM((pool_pages,), jnp.int32),
                pltpu.SMEM((pool_pages,), jnp.int32),
                pltpu.SemaphoreType.DMA((3 * count + 2 * pool_pages,)),
            ],
        ),
        out_shape=out_shape,
        compiler_params=pltpu.CompilerParams(vmem_limit_bytes=VMEM_LIMIT),
        cost_estimate=BRIEF,
        name="attend",
    )(
        in_hbm(request_page_table),
        in_hbm(live_token_count),
        place,
        *map(in_hbm, (queries, fresh_keys, fresh_values)),
        *(map(in_hbm, (paged_keys, paged_values)) if load else map(in_vmem, pools)),
        *extra,
    )


def project(own, other, weight, weight_other, cuts, after):
    rows = own.shape[0]
    bounds = [sum(cuts[:n]) for n in range(len(cuts) + 1)]
    assert bounds[-1] * BLOCK == weight.shape[1]

    def kernel(a, b, w, u, after, *outs):
        features = jnp.concatenate([a[...], b[...]], axis=1)
        for part, out in enumerate(outs):
            for n in range(cuts[part]):
                here = slice((bounds[part] + n) * BLOCK, (bounds[part] + n + 1) * BLOCK)
                out[:, n * BLOCK : (n + 1) * BLOCK] = jnp.dot(
                    features,
                    jnp.concatenate([w[:, here], u[:, here]], axis=0),
                    preferred_element_type=jnp.float32,
                ).astype(jnp.bfloat16)

    return pl.pallas_call(
        kernel,
        in_specs=[VMEM] * 4 + [ANY],
        out_specs=[VMEM] * len(cuts),
        out_shape=[pltpu.VMEM((rows, cut * BLOCK), jnp.bfloat16) for cut in cuts],
        compiler_params=pltpu.CompilerParams(vmem_limit_bytes=VMEM_LIMIT),
        cost_estimate=BRIEF,
        name="project",
    )(in_vmem(own), in_vmem(other), in_vmem(weight), in_vmem(weight_other), after)


def pack_pair(ups, downs, place, after):
    rank, columns = ups[0].shape[1:]
    width = downs[0].shape[2]
    half = columns // 2

    def kernel(place, up_0, up_1, down_0, down_1, after, out):
        here = pl.ds(pl.multiple_of((place[0] & 1) * half, half), half)
        for n, (up, down) in enumerate(((up_0, down_0), (up_1, down_1))):
            out[n, :, :half] = up[0, :, here]
            out[n, :, half:] = down[0]

    return pl.pallas_call(
        kernel,
        in_specs=[SMEM] + [VMEM] * 4 + [ANY],
        out_specs=VMEM,
        out_shape=jax.ShapeDtypeStruct((2, rank, half + width), ups[0].dtype),
        compiler_params=pltpu.CompilerParams(vmem_limit_bytes=VMEM_LIMIT),
        cost_estimate=BRIEF,
        name="pack_pair",
    )(place, *ups, *downs, after)


def pick_factors(pairs, place, lookup, per_owner, width, after):
    rank = pairs[0].shape[1]
    half = pairs[0].shape[2] - width
    count = len(pairs)

    def kernel(place, slot, in_use, pool_row, *refs):
        pieces, outs = refs[:count], refs[-2:]
        for n, out in enumerate(outs):
            for m in range(2):
                for i in range(2):
                    request = (place[0] ^ n ^ (0 if m else 2)) * per_owner + i
                    row = pool_row[in_use[slot[request]]]
                    apart = lax.rem(place[1] // 2 - row // 2 + count, count)
                    side = (row ^ place[1]) & 1
                    for d, piece in enumerate(pieces):

                        @pl.when(apart == d)
                        def _(piece=piece, out=out, k=2 * m + i, m=m, i=i, side=side):
                            out[:, k * width : (k + 1) * width] = piece[side, :, half:]
                            if m:
                                there = 4 * width + i * half
                                out[:, there : there + half] = piece[side, :, :half]

    shape = jax.ShapeDtypeStruct((rank, 4 * width + 2 * half), pairs[0].dtype)
    return pl.pallas_call(
        kernel,
        in_specs=[SMEM] * 4 + [VMEM] * count + [ANY],
        out_specs=[VMEM] * 2,
        out_shape=[shape] * 2,
        compiler_params=pltpu.CompilerParams(vmem_limit_bytes=VMEM_LIMIT),
        cost_estimate=BRIEF,
        name="pick_factors",
    )(place, *lookup, *pairs, after)


def ranks_and_part(here, other, factors, part):
    slots, width = here[0].shape
    rows = part.shape[0]
    rank = factors[0].shape[0]
    assert part.shape[1] == 4 * slots

    def kernel(*refs):
        factors, blocks, (part_in, part_out) = refs[:2], refs[2:6], refs[6:]
        part_out[:rows] = part_in[...]
        for i in range(2):
            acts = sum(
                lax.dot_general(
                    factors[m][:, i * width : (i + 1) * width],
                    blocks[2 * m + i][...],
                    (((1,), (1,)), ((), ())),
                    preferred_element_type=jnp.float32,
                )
                for m in range(2)
            )
            high = acts.astype(jnp.bfloat16)
            low = (acts - high.astype(jnp.float32)).astype(jnp.bfloat16)
            part_out[rows:, 2 * i * slots : (2 * i + 1) * slots] = high
            part_out[rows:, (2 * i + 1) * slots : (2 * i + 2) * slots] = low

    return pl.pallas_call(
        kernel,
        in_specs=[VMEM] * 7,
        out_specs=VMEM,
        out_shape=jax.ShapeDtypeStruct((rows + rank, part.shape[1]), jnp.bfloat16),
        compiler_params=pltpu.CompilerParams(vmem_limit_bytes=VMEM_LIMIT),
        cost_estimate=BRIEF,
        name="ranks_and_part",
    )(*factors, *here, *other, part)


def project_own(
    own, other, weight, weight_other, first, second, last, factors, gating, place
):
    rows, width = own.shape
    columns = weight.shape[1]
    blocks = columns // BLOCK
    slots = rows // 2
    rank = factors[0].shape[0]
    half = columns // 2
    open_from = second.shape[1] // BLOCK
    open_to = (columns - last.shape[1]) // BLOCK

    def kernel(
        place, a, b, w, u, first, second, last, mine, theirs, gate, out, rest_out, gates, out_buf, ups, sems
    ):
        def store(i, n):
            there = (pl.ds(i * slots, slots), pl.ds(n * BLOCK, BLOCK))
            return pltpu.make_async_copy(out_buf.at[there], out.at[there], sems.at[i, n])

        core = place[0] & 1
        gates[...] = jnp.zeros_like(gates)
        pieces = []
        for i in range(2):
            here = slice(i * slots, (i + 1) * slots)
            down = slice((2 + i) * width, (3 + i) * width)
            acts = sum(
                lax.dot_general(
                    factors[:, down],
                    block[here],
                    (((1,), (1,)), ((), ())),
                    preferred_element_type=jnp.float32,
                )
                for factors, block in ((mine, a), (theirs, b))
            )
            for m in range(2 * i, 2 * i + 2):
                acts += last[slots:, m * slots : (m + 1) * slots].astype(jnp.float32)
            high = acts.astype(jnp.bfloat16).astype(jnp.float32)
            pieces.append(jnp.concatenate([high, acts - high], axis=0).T.astype(jnp.bfloat16))
            up = 4 * width + i * half
            for m in range(2):
                for away, factors in enumerate((mine, theirs)):
                    there = pl.ds(pl.multiple_of((core ^ away) * half, half), half)
                    ups[i, m * rank : (m + 1) * rank, there] = factors[:, up : up + half]
            gates[i : i + 1] = gate[pl.ds(place[0] * 2 + i, 1), :]
        features = jnp.concatenate([a[...], b[...]], axis=1)
        for n in range(blocks):
            here = slice(n * BLOCK, (n + 1) * BLOCK)
            sums = jnp.dot(
                features,
                jnp.concatenate([w[:, here], u[:, here]], axis=0),
                preferred_element_type=jnp.float32,
            )
            for i in range(2):
                those = slice(i * slots, (i + 1) * slots)
                update = sums[those] + jnp.dot(
                    pieces[i], ups[i, :, here], preferred_element_type=jnp.float32
                )
                if not i:
                    update += first[:, here].astype(jnp.float32)
                elif n < open_from:
                    update += second[:, here].astype(jnp.float32)
                elif n >= open_to:
                    there = slice((n - open_to) * BLOCK, (n - open_to + 1) * BLOCK)
                    update += last[:slots, there].astype(jnp.float32)
                gated = update * gates[i : i + 1, here]
                if i and open_from <= n < open_to:
                    there = slice((n - open_from) * BLOCK, (n - open_from + 1) * BLOCK)
                    rest_out[:, there] = gated
                else:
                    out_buf[those, here] = gated.astype(jnp.bfloat16)
                    store(i, n).start()
        for i in range(2):
            for n in range(blocks):
                if not (i and open_from <= n < open_to):
                    store(i, n).wait()

    return pl.pallas_call(
        kernel,
        in_specs=[SMEM] + [VMEM] * 10,
        out_specs=[HBM, VMEM, VMEM],
        out_shape=[
            pltpu.HBM((rows, columns), jnp.bfloat16),
            jax.ShapeDtypeStruct((slots, (open_to - open_from) * BLOCK), jnp.float32),
            jax.ShapeDtypeStruct((8, columns), jnp.float32),
        ],
        scratch_shapes=[
            pltpu.VMEM((rows, columns), jnp.bfloat16),
            pltpu.VMEM((2, 2 * rank, columns), jnp.bfloat16),
            pltpu.SemaphoreType.DMA((2, blocks)),
        ],
        compiler_params=pltpu.CompilerParams(vmem_limit_bytes=VMEM_LIMIT),
        cost_estimate=BRIEF,
        name="project_own",
    )(
        place,
        own,
        other,
        in_vmem(weight),
        in_vmem(weight_other),
        first,
        second,
        last,
        *factors,
        gating,
    )


def finish(so_far, rest, received, gates, begin):
    rows, columns = so_far.shape
    slots, wide = rest.shape
    at = begin // wide
    assert begin % wide == 0

    def kernel(sums, part, gate, so_far, out):
        out[...] = (sums[...] + part[...].astype(jnp.float32) * gate[1:2]).astype(jnp.bfloat16)

    return pl.pallas_call(
        kernel,
        grid=(1,),
        in_specs=[
            pl.BlockSpec((slots, wide), lambda j: (0, 0)),
            pl.BlockSpec((slots, wide), lambda j: (0, 0)),
            pl.BlockSpec((gates.shape[0], wide), lambda j: (0, at)),
            ANY,
        ],
        out_specs=pl.BlockSpec((slots, wide), lambda j: (1, at)),
        out_shape=jax.ShapeDtypeStruct((rows, columns), jnp.bfloat16),
        input_output_aliases={3: 0},
        compiler_params=pltpu.CompilerParams(vmem_limit_bytes=VMEM_LIMIT),
        cost_estimate=BRIEF,
        name="finish",
    )(rest, received, gates, so_far)


def body(
    queries,
    fresh_keys,
    fresh_values,
    paged_keys,
    paged_values,
    request_page_table,
    live_token_count,
    request_adapter_slot,
    adapters_in_use,
    adapter_pool_row,
    adapter_down_factors,
    adapter_up_factors,
    output_weight,
    gating,
):
    tp = lax.axis_size("tp")
    holders = lax.axis_size("req")
    place = jnp.stack([lax.axis_index("tp"), lax.axis_index("req")]).astype(jnp.int32)
    per_owner = live_token_count.shape[0] // tp

    def swap(array, flip):
        return lax.ppermute(array, "tp", [(s, s ^ flip) for s in range(tp)])

    def attend(wanted, pools=None, after=None):
        return attend_some(
            queries,
            fresh_keys,
            fresh_values,
            paged_keys,
            paged_values,
            request_page_table,
            live_token_count,
            place,
            per_owner,
            wanted,
            pools,
            after,
        )

    ups, downs = (
        (factors, lax.ppermute(factors, "req", [(s, s ^ 1) for s in range(holders)]))
        for factors in (adapter_up_factors, adapter_down_factors)
    )
    weight_other = swap(output_weight, 1)

    away_a, here_a, *pools = attend(((3, 0), (2, 0)))
    away_a, ups, downs = lax.optimization_barrier((away_a, ups, downs))
    other_a = swap(away_a, 1)
    pair = pack_pair(ups, downs, place, away_a)
    (sent_a,) = project(here_a, other_a, output_weight, weight_other, (sum(CUTS),), pair)
    first = swap(sent_a, 2)

    pair, _ = lax.optimization_barrier((pair, sent_a))
    pairs = [pair] + [
        lax.ppermute(pair, "req", [(s, (s + d) % holders) for s in range(holders)])
        for d in range(2, holders, 2)
    ]
    away_b, here_b = attend(((3, 1), (2, 1)), pools, sent_a)
    away_b, *pairs = lax.optimization_barrier((away_b, *pairs))
    other_b = swap(away_b, 1)
    sent_b = project(here_b, other_b, output_weight, weight_other, CUTS, sent_a)
    second = swap(sent_b[0], 2)

    first, *pairs = lax.optimization_barrier((first, *pairs))
    lookup = (request_adapter_slot, adapters_in_use, adapter_pool_row)
    width = output_weight.shape[0]
    factors, factors_away = pick_factors(pairs, place, lookup, per_owner, width, sent_b[0])
    factors = (factors, swap(factors_away, 1))
    last = ranks_and_part((here_a, here_b), (other_a, other_b), factors, sent_b[2])
    third, first, _ = lax.optimization_barrier((sent_b[1], first, last))
    third = swap(third, 2)
    own_away, own_here = attend(((1, 0), (1, 1), (0, 0), (0, 1)), pools, last)
    own_away, second, last = lax.optimization_barrier((own_away, second, swap(last, 2)))
    own_other = swap(own_away, 1)
    out, rest, gates = project_own(
        own_here,
        own_other,
        output_weight,
        weight_other,
        first,
        second,
        last,
        factors,
        gating,
        place,
    )
    return finish(out, rest, third, gates, CUTS[0] * BLOCK)


def solution(mesh):
    return jax.shard_map(
        body,
        mesh=mesh,
        in_specs=(
            P("req", "tp"),
            P("req", "tp"),
            P("req", "tp"),
            P("req", None, "tp"),
            P("req", None, "tp"),
            P("req", None),
            P("req"),
            P("req"),
            P(),
            P(),
            P("req", None, "tp"),
            P("req", None, None),
            P("tp", None),
            P("req", None),
        ),
        out_specs=P(("req", "tp"), None),
        check_vma=False,
    )
```

```python
import math

import jax
import jax.numpy as jnp
from jax import lax
from jax.experimental import pallas as pl
from jax.experimental.pallas import tpu as pltpu
from jax.sharding import PartitionSpec as P

HD = 128
VMEM_LIMIT = 32 * 1024 * 1024
SMEM = pl.BlockSpec(memory_space=pltpu.SMEM)
BLOCK = 512
CUTS = (3, 1, 1)
MASKED = -1e30
ANY = pl.BlockSpec(memory_space=pl.ANY)
BRIEF = pl.CostEstimate(flops=1000, bytes_accessed=1000, transcendentals=0)
HBM = pl.BlockSpec(memory_space=pltpu.HBM)
VMEM = pl.BlockSpec(memory_space=pltpu.VMEM)


def in_hbm(array):
    return pltpu.with_memory_space_constraint(array, pltpu.HBM)


def in_vmem(array):
    return pltpu.with_memory_space_constraint(array, pltpu.VMEM)


def attend_some(
    queries,
    fresh_keys,
    fresh_values,
    paged_keys,
    paged_values,
    request_page_table,
    live_token_count,
    place,
    per_owner,
    wanted,
    pools=None,
    after=None,
):
    requests_here, pages = request_page_table.shape
    slots = queries.shape[0] // requests_here
    width = queries.shape[1]
    heads = width // HD
    pool_pages, page_rows = paged_keys.shape[:2]
    cached = pages * page_rows
    load = pools is None
    count = len(wanted)
    parts = len({away for away, _ in wanted})
    per_out = count // parts
    exponent_scale = math.log2(math.e) / math.sqrt(HD)

    def kernel(table, live, place, q_hbm, fk_hbm, fv_hbm, pk_hbm, pv_hbm, *rest):
        ids = [(place[0] ^ away) * per_owner + n for away, n in wanted]
        q_buf, fk_buf, fv_buf, order, seen, in_sems = rest[-6:]
        if load:
            *outs, pk_buf, pv_buf = rest[-8 - parts : -6]
        else:
            outs, pk_buf, pv_buf = rest[-6 - parts : -6], pk_hbm, pv_hbm

        def fetch(src, dst, sem):
            return pltpu.make_async_copy(src, dst, in_sems.at[sem])

        def rows_of(n):
            return pl.ds(pl.multiple_of(ids[n] * slots, slots), slots)

        def query_copy(n):
            return fetch(q_hbm.at[rows_of(n)], q_buf.at[n], 3 * n)

        def key_copy(n):
            return fetch(fk_hbm.at[rows_of(n)], fk_buf.at[n], 3 * n + 1)

        def value_copy(n):
            return fetch(fv_hbm.at[rows_of(n)], fv_buf.at[n], 3 * n + 2)

        def key_page(m):
            page = order[m]
            return fetch(pk_hbm.at[page], pk_buf.at[page], 3 * count + 2 * m)

        def value_page(m):
            page = order[m]
            return fetch(pv_hbm.at[page], pv_buf.at[page], 3 * count + 2 * m + 1)

        def start(copies):
            for copy in copies:
                copy.start()

        def start_pages(begin, end):
            for m in range(pages, pool_pages):

                @pl.when((m >= begin) & (m < end))
                def _(m=m):
                    key_page(m).start()

            for m in range(pages, pool_pages):

                @pl.when((m >= begin) & (m < end))
                def _(m=m):
                    value_page(m).start()

        if load:
            for j in range(pages):
                order[j] = table[ids[0], j]
            start([query_copy(0), key_copy(0)] + [key_page(m) for m in range(pages)])
            start([value_copy(0)] + [value_page(m) for m in range(pages)])
            for page in range(pool_pages):
                taken = order[0] == page
                for j in range(1, pages):
                    taken = taken | (order[j] == page)
                seen[page] = taken.astype(jnp.int32)
            bounds = [jnp.int32(pages)]
            for n in range(1, count):
                free = bounds[-1]
                for j in range(pages):
                    page = table[ids[n], j]
                    fresh = seen[page] == 0

                    @pl.when(fresh)
                    def _(page=page, free=free):
                        order[free] = page
                        seen[page] = 1

                    free = free + fresh.astype(jnp.int32)
                bounds.append(free)
                start([query_copy(n), key_copy(n), value_copy(n)])
                start_pages(bounds[n - 1], bounds[n])
            free = bounds[-1]
            for page in range(pool_pages):
                fresh = seen[page] == 0

                @pl.when(fresh)
                def _(page=page, free=free):
                    order[free] = page

                free = free + fresh.astype(jnp.int32)
            start_pages(bounds[-1], pool_pages)
        else:
            for n in range(count):
                start([query_copy(n), key_copy(n), value_copy(n)])

        waited = set()

        def wait(name, make, indices):
            if name not in waited:
                waited.add(name)
                for index in indices:
                    make(index).wait()

        def wait_pages(name, make, begin, end):
            if name not in waited:
                waited.add(name)
                for m in range(pages, pool_pages):

                    @pl.when((m >= begin) & (m < end))
                    def _(m=m):
                        make(m).wait()

        def keys_ready(duo):
            for n in range(1 + max(n for n, _ in duo)):
                wait(("q", n), query_copy, [n])
                wait(("k", n), key_copy, [n])
                if load and n:
                    wait_pages(("k pages", n), key_page, bounds[n - 1], bounds[n])
                elif load:
                    wait(("k pages", 0), key_page, range(pages))

        def values_ready(duo):
            for n in range(1 + max(n for n, _ in duo)):
                wait(("v", n), value_copy, [n])
                if load and n:
                    wait_pages(("v pages", n), value_page, bounds[n - 1], bounds[n])
                elif load:
                    wait(("v pages", 0), value_page, range(pages))

        def lanes(h, several=1):
            return slice(h * HD, (h + several) * HD)

        def gather(pool, fresh, n, here):
            return jnp.concatenate(
                [pool[table[ids[n], j], :, here] for j in range(pages)] + [fresh[n, :, here]],
                axis=0,
            )

        def side_by_side(pool, fresh, duo):
            (n, h), (other_n, other_h) = duo
            if n == other_n and other_h == h + 1:
                return gather(pool, fresh, n, lanes(h, 2))
            return jnp.concatenate(
                [gather(pool, fresh, m, lanes(g)) for m, g in duo],
                axis=1,
            )

        def score(duo):
            (n, h), (other_n, other_h) = duo
            blank = jnp.zeros((slots, HD), jnp.bfloat16)
            diagonal = jnp.concatenate(
                [
                    jnp.concatenate([q_buf[n, :, lanes(h)], blank], axis=1),
                    jnp.concatenate([blank, q_buf[other_n, :, lanes(other_h)]], axis=1),
                ],
                axis=0,
            )
            return lax.dot_general(
                diagonal,
                side_by_side(pk_buf, fk_buf, duo),
                (((1,), (1,)), ((), ())),
                preferred_element_type=jnp.float32,
            )

        def weigh(duo, scores):
            column = lax.broadcasted_iota(jnp.int32, (slots, slots), 1)
            usable = jnp.concatenate([column < live[ids[n]] for n, _ in duo], axis=0)
            scores = jnp.concatenate(
                [scores[:, :cached], jnp.where(usable, scores[:, cached:], MASKED)], axis=1
            )
            peak = jnp.max(scores, axis=1, keepdims=True)
            weights = jnp.exp2((scores - peak) * exponent_scale)
            return weights.astype(jnp.bfloat16), jnp.sum(weights, axis=1, keepdims=True)

        def blend(duo, weights, row_total):
            blended = jnp.dot(
                weights, side_by_side(pv_buf, fv_buf, duo), preferred_element_type=jnp.float32
            )
            row = lax.broadcasted_iota(jnp.int32, (slots, HD), 0)
            for m, (n, h) in enumerate(duo):
                rows = slice(m * slots, (m + 1) * slots)
                attended = blended[rows, lanes(m)] / row_total[rows]
                attended = jnp.where(row < live[ids[n]], attended, 0.0)
                at = (n % per_out) * slots
                outs[n // per_out][at : at + slots, lanes(h)] = attended.astype(jnp.bfloat16)

        units = []
        for first in range(0, count, 2):
            units += [((n, h), (n, h + 1)) for n in (first, first + 1) for h in range(0, heads - 1, 2)]
            if heads % 2:
                units.append(((first, heads - 1), (first + 1, heads - 1)))
        keys_ready(units[0])
        scores = score(units[0])
        weighed = None
        for u, duo in enumerate(units):
            later = None
            if u + 1 < len(units):
                keys_ready(units[u + 1])
                later = score(units[u + 1])
            if u:
                values_ready(units[u - 1])
                blend(units[u - 1], *weighed)
            weighed = weigh(duo, scores)
            scores = later
        values_ready(units[-1])
        blend(units[-1], *weighed)
        if load:
            wait_pages(("k pages", count), key_page, bounds[-1], pool_pages)
            wait_pages(("v pages", count), value_page, bounds[-1], pool_pages)

    extra = () if after is None else (after,)
    out_shape = [pltpu.VMEM((per_out * slots, width), jnp.bfloat16)] * parts
    if load:
        out_shape += [pltpu.VMEM(paged_keys.shape, jnp.bfloat16)] * 2
    return pl.pallas_call(
        kernel,
        grid_spec=pltpu.PrefetchScalarGridSpec(
            num_scalar_prefetch=3,
            grid=(1,),
            in_specs=[HBM] * 3 + [HBM if load else VMEM] * 2 + [ANY] * len(extra),
            out_specs=[VMEM] * len(out_shape),
            scratch_shapes=[
                pltpu.VMEM((count, slots, width), jnp.bfloat16),
                pltpu.VMEM((count, slots, width), jnp.bfloat16),
                pltpu.VMEM((count, slots, width), jnp.bfloat16),
                pltpu.SMEM((pool_pages,), jnp.int32),
                pltpu.SMEM((pool_pages,), jnp.int32),
                pltpu.SemaphoreType.DMA((3 * count + 2 * pool_pages,)),
            ],
        ),
        out_shape=out_shape,
        compiler_params=pltpu.CompilerParams(vmem_limit_bytes=VMEM_LIMIT),
        cost_estimate=BRIEF,
        name="attend",
    )(
        in_hbm(request_page_table),
        in_hbm(live_token_count),
        place,
        *map(in_hbm, (queries, fresh_keys, fresh_values)),
        *(map(in_hbm, (paged_keys, paged_values)) if load else map(in_vmem, pools)),
        *extra,
    )


def project(own, other, weight, weight_other, cuts, after):
    rows = own.shape[0]
    bounds = [sum(cuts[:n]) for n in range(len(cuts) + 1)]
    assert bounds[-1] * BLOCK == weight.shape[1]

    def kernel(a, b, w, u, after, *outs):
        features = jnp.concatenate([a[...], b[...]], axis=1)
        for part, out in enumerate(outs):
            for n in range(cuts[part]):
                here = slice((bounds[part] + n) * BLOCK, (bounds[part] + n + 1) * BLOCK)
                out[:, n * BLOCK : (n + 1) * BLOCK] = jnp.dot(
                    features,
                    jnp.concatenate([w[:, here], u[:, here]], axis=0),
                    preferred_element_type=jnp.float32,
                ).astype(jnp.bfloat16)

    return pl.pallas_call(
        kernel,
        in_specs=[VMEM] * 4 + [ANY],
        out_specs=[VMEM] * len(cuts),
        out_shape=[pltpu.VMEM((rows, cut * BLOCK), jnp.bfloat16) for cut in cuts],
        compiler_params=pltpu.CompilerParams(vmem_limit_bytes=VMEM_LIMIT),
        cost_estimate=BRIEF,
        name="project",
    )(in_vmem(own), in_vmem(other), in_vmem(weight), in_vmem(weight_other), after)


def pack_pair(ups, downs, place, after):
    rank, columns = ups[0].shape[1:]
    width = downs[0].shape[2]
    half = columns // 2

    def kernel(place, up_0, up_1, down_0, down_1, after, out):
        here = pl.ds(pl.multiple_of((place[0] & 1) * half, half), half)
        for n, (up, down) in enumerate(((up_0, down_0), (up_1, down_1))):
            out[n, :, :half] = up[0, :, here]
            out[n, :, half:] = down[0]

    return pl.pallas_call(
        kernel,
        in_specs=[SMEM] + [VMEM] * 4 + [ANY],
        out_specs=VMEM,
        out_shape=jax.ShapeDtypeStruct((2, rank, half + width), ups[0].dtype),
        compiler_params=pltpu.CompilerParams(vmem_limit_bytes=VMEM_LIMIT),
        cost_estimate=BRIEF,
        name="pack_pair",
    )(place, *ups, *downs, after)


def pick_factors(pairs, place, lookup, per_owner, width, after):
    rank = pairs[0].shape[1]
    half = pairs[0].shape[2] - width
    count = len(pairs)

    def kernel(place, slot, in_use, pool_row, *refs):
        pieces, outs = refs[:count], refs[-2:]
        for n, out in enumerate(outs):
            for m in range(2):
                for i in range(2):
                    request = (place[0] ^ n ^ (0 if m else 2)) * per_owner + i
                    row = pool_row[in_use[slot[request]]]
                    apart = lax.rem(place[1] // 2 - row // 2 + count, count)
                    side = (row ^ place[1]) & 1
                    for d, piece in enumerate(pieces):

                        @pl.when(apart == d)
                        def _(piece=piece, out=out, k=2 * m + i, m=m, i=i, side=side):
                            out[:, k * width : (k + 1) * width] = piece[side, :, half:]
                            if m:
                                there = 4 * width + i * half
                                out[:, there : there + half] = piece[side, :, :half]

    shape = jax.ShapeDtypeStruct((rank, 4 * width + 2 * half), pairs[0].dtype)
    return pl.pallas_call(
        kernel,
        in_specs=[SMEM] * 4 + [VMEM] * count + [ANY],
        out_specs=[VMEM] * 2,
        out_shape=[shape] * 2,
        compiler_params=pltpu.CompilerParams(vmem_limit_bytes=VMEM_LIMIT),
        cost_estimate=BRIEF,
        name="pick_factors",
    )(place, *lookup, *pairs, after)


def ranks_and_part(here, other, factors, part):
    slots, width = here[0].shape
    rows = part.shape[0]
    rank = factors[0].shape[0]
    assert part.shape[1] == 4 * slots

    def kernel(*refs):
        factors, blocks, (part_in, part_out) = refs[:2], refs[2:6], refs[6:]
        part_out[:rows] = part_in[...]
        for i in range(2):
            acts = sum(
                lax.dot_general(
                    factors[m][:, i * width : (i + 1) * width],
                    blocks[2 * m + i][...],
                    (((1,), (1,)), ((), ())),
                    preferred_element_type=jnp.float32,
                )
                for m in range(2)
            )
            high = acts.astype(jnp.bfloat16)
            low = (acts - high.astype(jnp.float32)).astype(jnp.bfloat16)
            part_out[rows:, 2 * i * slots : (2 * i + 1) * slots] = high
            part_out[rows:, (2 * i + 1) * slots : (2 * i + 2) * slots] = low

    return pl.pallas_call(
        kernel,
        in_specs=[VMEM] * 7,
        out_specs=VMEM,
        out_shape=jax.ShapeDtypeStruct((rows + rank, part.shape[1]), jnp.bfloat16),
        compiler_params=pltpu.CompilerParams(vmem_limit_bytes=VMEM_LIMIT),
        cost_estimate=BRIEF,
        name="ranks_and_part",
    )(*factors, *here, *other, part)


def project_own(
    own, other, weight, weight_other, first, second, last, factors, gating, place
):
    rows, width = own.shape
    columns = weight.shape[1]
    blocks = columns // BLOCK
    slots = rows // 2
    rank = factors[0].shape[0]
    half = columns // 2
    open_from = second.shape[1] // BLOCK
    open_to = (columns - last.shape[1]) // BLOCK

    def kernel(
        place, a, b, w, u, first, second, last, mine, theirs, gate, out, rest_out, gates, out_buf, ups, sems
    ):
        def store(i, n):
            there = (pl.ds(i * slots, slots), pl.ds(n * BLOCK, BLOCK))
            return pltpu.make_async_copy(out_buf.at[there], out.at[there], sems.at[i, n])

        core = place[0] & 1
        gates[...] = jnp.zeros_like(gates)
        pieces = []
        for i in range(2):
            here = slice(i * slots, (i + 1) * slots)
            down = slice((2 + i) * width, (3 + i) * width)
            acts = sum(
                lax.dot_general(
                    factors[:, down],
                    block[here],
                    (((1,), (1,)), ((), ())),
                    preferred_element_type=jnp.float32,
                )
                for factors, block in ((mine, a), (theirs, b))
            )
            for m in range(2 * i, 2 * i + 2):
                acts += last[slots:, m * slots : (m + 1) * slots].astype(jnp.float32)
            high = acts.astype(jnp.bfloat16).astype(jnp.float32)
            pieces.append(jnp.concatenate([high, acts - high], axis=0).T.astype(jnp.bfloat16))
            up = 4 * width + i * half
            for m in range(2):
                for away, factors in enumerate((mine, theirs)):
                    there = pl.ds(pl.multiple_of((core ^ away) * half, half), half)
                    ups[i, m * rank : (m + 1) * rank, there] = factors[:, up : up + half]
            gates[i : i + 1] = gate[pl.ds(place[0] * 2 + i, 1), :]
        features = jnp.concatenate([a[...], b[...]], axis=1)
        for n in range(blocks):
            here = slice(n * BLOCK, (n + 1) * BLOCK)
            sums = jnp.dot(
                features,
                jnp.concatenate([w[:, here], u[:, here]], axis=0),
                preferred_element_type=jnp.float32,
            )
            for i in range(2):
                those = slice(i * slots, (i + 1) * slots)
                update = sums[those] + jnp.dot(
                    pieces[i], ups[i, :, here], preferred_element_type=jnp.float32
                )
                if not i:
                    update += first[:, here].astype(jnp.float32)
                elif n < open_from:
                    update += second[:, here].astype(jnp.float32)
                elif n >= open_to:
                    there = slice((n - open_to) * BLOCK, (n - open_to + 1) * BLOCK)
                    update += last[:slots, there].astype(jnp.float32)
                gated = update * gates[i : i + 1, here]
                if i and open_from <= n < open_to:
                    there = slice((n - open_from) * BLOCK, (n - open_from + 1) * BLOCK)
                    rest_out[:, there] = gated
                else:
                    out_buf[those, here] = gated.astype(jnp.bfloat16)
                    store(i, n).start()
        for i in range(2):
            for n in range(blocks):
                if not (i and open_from <= n < open_to):
                    store(i, n).wait()

    return pl.pallas_call(
        kernel,
        in_specs=[SMEM] + [VMEM] * 10,
        out_specs=[HBM, VMEM, VMEM],
        out_shape=[
            pltpu.HBM((rows, columns), jnp.bfloat16),
            jax.ShapeDtypeStruct((slots, (open_to - open_from) * BLOCK), jnp.float32),
            jax.ShapeDtypeStruct((8, columns), jnp.float32),
        ],
        scratch_shapes=[
            pltpu.VMEM((rows, columns), jnp.bfloat16),
            pltpu.VMEM((2, 2 * rank, columns), jnp.bfloat16),
            pltpu.SemaphoreType.DMA((2, blocks)),
        ],
        compiler_params=pltpu.CompilerParams(vmem_limit_bytes=VMEM_LIMIT),
        cost_estimate=BRIEF,
        name="project_own",
    )(
        place,
        own,
        other,
        in_vmem(weight),
        in_vmem(weight_other),
        first,
        second,
        last,
        *factors,
        gating,
    )


def finish(so_far, rest, received, gates, begin):
    rows, columns = so_far.shape
    slots, wide = rest.shape
    at = begin // wide
    assert begin % wide == 0

    def kernel(sums, part, gate, so_far, out):
        out[...] = (sums[...] + part[...].astype(jnp.float32) * gate[1:2]).astype(jnp.bfloat16)

    return pl.pallas_call(
        kernel,
        grid=(1,),
        in_specs=[
            pl.BlockSpec((slots, wide), lambda j: (0, 0)),
            pl.BlockSpec((slots, wide), lambda j: (0, 0)),
            pl.BlockSpec((gates.shape[0], wide), lambda j: (0, at)),
            ANY,
        ],
        out_specs=pl.BlockSpec((slots, wide), lambda j: (1, at)),
        out_shape=jax.ShapeDtypeStruct((rows, columns), jnp.bfloat16),
        input_output_aliases={3: 0},
        compiler_params=pltpu.CompilerParams(vmem_limit_bytes=VMEM_LIMIT),
        cost_estimate=BRIEF,
        name="finish",
    )(rest, received, gates, so_far)


def body(
    queries,
    fresh_keys,
    fresh_values,
    paged_keys,
    paged_values,
    request_page_table,
    live_token_count,
    request_adapter_slot,
    adapters_in_use,
    adapter_pool_row,
    adapter_down_factors,
    adapter_up_factors,
    output_weight,
    gating,
):
    tp = lax.axis_size("tp")
    holders = lax.axis_size("req")
    place = jnp.stack([lax.axis_index("tp"), lax.axis_index("req")]).astype(jnp.int32)
    per_owner = live_token_count.shape[0] // tp

    def swap(array, flip):
        return lax.ppermute(array, "tp", [(s, s ^ flip) for s in range(tp)])

    def attend(wanted, pools=None, after=None):
        return attend_some(
            queries,
            fresh_keys,
            fresh_values,
            paged_keys,
            paged_values,
            request_page_table,
            live_token_count,
            place,
            per_owner,
            wanted,
            pools,
            after,
        )

    ups, downs = (
        (factors, lax.ppermute(factors, "req", [(s, s ^ 1) for s in range(holders)]))
        for factors in (adapter_up_factors, adapter_down_factors)
    )
    weight_other = swap(output_weight, 1)

    away_a, here_a, *pools = attend(((3, 0), (2, 0)))
    away_a, ups, downs = lax.optimization_barrier((away_a, ups, downs))
    other_a = swap(away_a, 1)
    pair = pack_pair(ups, downs, place, away_a)
    (sent_a,) = project(here_a, other_a, output_weight, weight_other, (sum(CUTS),), pair)
    first = swap(sent_a, 2)

    pair, _ = lax.optimization_barrier((pair, sent_a))
    pairs = [pair] + [
        lax.ppermute(pair, "req", [(s, (s + d) % holders) for s in range(holders)])
        for d in range(2, holders, 2)
    ]
    away_b, here_b = attend(((3, 1), (2, 1)), pools, sent_a)
    (own_away,) = attend(((1, 0), (1, 1)), pools, away_b)
    away_b, own_away, *pairs = lax.optimization_barrier((away_b, own_away, *pairs))
    other_b = swap(away_b, 1)
    own_other = swap(own_away, 1)
    sent_b = project(here_b, other_b, output_weight, weight_other, CUTS, own_away)
    second = swap(sent_b[0], 2)

    first, *pairs = lax.optimization_barrier((first, *pairs))
    lookup = (request_adapter_slot, adapters_in_use, adapter_pool_row)
    width = output_weight.shape[0]
    factors, factors_away = pick_factors(pairs, place, lookup, per_owner, width, sent_b[0])
    factors = (factors, swap(factors_away, 1))
    last = ranks_and_part((here_a, here_b), (other_a, other_b), factors, sent_b[2])
    third, first, _ = lax.optimization_barrier((sent_b[1], first, last))
    third = swap(third, 2)
    (own_here,) = attend(((0, 0), (0, 1)), pools, last)
    last = swap(last, 2)
    out, rest, gates = project_own(
        own_here,
        own_other,
        output_weight,
        weight_other,
        first,
        second,
        last,
        factors,
        gating,
        place,
    )
    return finish(out, rest, third, gates, CUTS[0] * BLOCK)


def solution(mesh):
    return jax.shard_map(
        body,
        mesh=mesh,
        in_specs=(
            P("req", "tp"),
            P("req", "tp"),
            P("req", "tp"),
            P("req", None, "tp"),
            P("req", None, "tp"),
            P("req", None),
            P("req"),
            P("req"),
            P(),
            P(),
            P("req", None, "tp"),
            P("req", None, None),
            P("tp", None),
            P("req", None),
        ),
        out_specs=P(("req", "tp"), None),
        check_vma=False,
    )
```

```python
import math

import jax
import jax.numpy as jnp
from jax import lax
from jax.experimental import pallas as pl
from jax.experimental.pallas import tpu as pltpu
from jax.sharding import PartitionSpec as P

HD = 128
VMEM_LIMIT = 32 * 1024 * 1024
SMEM = pl.BlockSpec(memory_space=pltpu.SMEM)
BLOCK = 512
MASKED = -1e30
ANY = pl.BlockSpec(memory_space=pl.ANY)
BRIEF = pl.CostEstimate(flops=1000, bytes_accessed=1000, transcendentals=0)
HBM = pl.BlockSpec(memory_space=pltpu.HBM)
VMEM = pl.BlockSpec(memory_space=pltpu.VMEM)


def in_hbm(array):
    return pltpu.with_memory_space_constraint(array, pltpu.HBM)


def in_vmem(array):
    return pltpu.with_memory_space_constraint(array, pltpu.VMEM)


def attend_some(
    queries,
    fresh_keys,
    fresh_values,
    paged_keys,
    paged_values,
    request_page_table,
    live_token_count,
    place,
    per_owner,
    wanted,
    pools=None,
    after=None,
):
    requests_here, pages = request_page_table.shape
    slots = queries.shape[0] // requests_here
    width = queries.shape[1]
    heads = width // HD
    pool_pages, page_rows = paged_keys.shape[:2]
    cached = pages * page_rows
    load = pools is None
    count = len(wanted)
    parts = len({away for away, _ in wanted})
    per_out = count // parts
    exponent_scale = math.log2(math.e) / math.sqrt(HD)

    def kernel(table, live, place, q_hbm, fk_hbm, fv_hbm, pk_hbm, pv_hbm, *rest):
        ids = [(place[0] ^ away) * per_owner + n for away, n in wanted]
        q_buf, fk_buf, fv_buf, order, seen, in_sems = rest[-6:]
        if load:
            *outs, pk_buf, pv_buf = rest[-8 - parts : -6]
        else:
            outs, pk_buf, pv_buf = rest[-6 - parts : -6], pk_hbm, pv_hbm

        def fetch(src, dst, sem):
            return pltpu.make_async_copy(src, dst, in_sems.at[sem])

        def rows_of(n):
            return pl.ds(pl.multiple_of(ids[n] * slots, slots), slots)

        def query_copy(n):
            return fetch(q_hbm.at[rows_of(n)], q_buf.at[n], 3 * n)

        def key_copy(n):
            return fetch(fk_hbm.at[rows_of(n)], fk_buf.at[n], 3 * n + 1)

        def value_copy(n):
            return fetch(fv_hbm.at[rows_of(n)], fv_buf.at[n], 3 * n + 2)

        def key_page(m):
            page = order[m]
            return fetch(pk_hbm.at[page], pk_buf.at[page], 3 * count + 2 * m)

        def value_page(m):
            page = order[m]
            return fetch(pv_hbm.at[page], pv_buf.at[page], 3 * count + 2 * m + 1)

        def start(copies):
            for copy in copies:
                copy.start()

        def start_pages(begin, end):
            for m in range(pages, pool_pages):

                @pl.when((m >= begin) & (m < end))
                def _(m=m):
                    key_page(m).start()

            for m in range(pages, pool_pages):

                @pl.when((m >= begin) & (m < end))
                def _(m=m):
                    value_page(m).start()

        if load:
            for j in range(pages):
                order[j] = table[ids[0], j]
            start([query_copy(0), key_copy(0)] + [key_page(m) for m in range(pages)])
            start([value_copy(0)] + [value_page(m) for m in range(pages)])
            for page in range(pool_pages):
                taken = order[0] == page
                for j in range(1, pages):
                    taken = taken | (order[j] == page)
                seen[page] = taken.astype(jnp.int32)
            bounds = [jnp.int32(pages)]
            for n in range(1, count):
                free = bounds[-1]
                for j in range(pages):
                    page = table[ids[n], j]
                    fresh = seen[page] == 0

                    @pl.when(fresh)
                    def _(page=page, free=free):
                        order[free] = page
                        seen[page] = 1

                    free = free + fresh.astype(jnp.int32)
                bounds.append(free)
                start([query_copy(n), key_copy(n), value_copy(n)])
                start_pages(bounds[n - 1], bounds[n])
            free = bounds[-1]
            for page in range(pool_pages):
                fresh = seen[page] == 0

                @pl.when(fresh)
                def _(page=page, free=free):
                    order[free] = page

                free = free + fresh.astype(jnp.int32)
            start_pages(bounds[-1], pool_pages)
        else:
            for n in range(count):
                start([query_copy(n), key_copy(n), value_copy(n)])

        waited = set()

        def wait(name, make, indices):
            if name not in waited:
                waited.add(name)
                for index in indices:
                    make(index).wait()

        def wait_pages(name, make, begin, end):
            if name not in waited:
                waited.add(name)
                for m in range(pages, pool_pages):

                    @pl.when((m >= begin) & (m < end))
                    def _(m=m):
                        make(m).wait()

        def keys_ready(duo):
            for n in range(1 + max(n for n, _ in duo)):
                wait(("q", n), query_copy, [n])
                wait(("k", n), key_copy, [n])
                if load and n:
                    wait_pages(("k pages", n), key_page, bounds[n - 1], bounds[n])
                elif load:
                    wait(("k pages", 0), key_page, range(pages))

        def values_ready(duo):
            for n in range(1 + max(n for n, _ in duo)):
                wait(("v", n), value_copy, [n])
                if load and n:
                    wait_pages(("v pages", n), value_page, bounds[n - 1], bounds[n])
                elif load:
                    wait(("v pages", 0), value_page, range(pages))

        def lanes(h, several=1):
            return slice(h * HD, (h + several) * HD)

        def gather(pool, fresh, n, here):
            return jnp.concatenate(
                [pool[table[ids[n], j], :, here] for j in range(pages)] + [fresh[n, :, here]],
                axis=0,
            )

        def side_by_side(pool, fresh, duo):
            (n, h), (other_n, other_h) = duo
            if n == other_n and other_h == h + 1:
                return gather(pool, fresh, n, lanes(h, 2))
            return jnp.concatenate(
                [gather(pool, fresh, m, lanes(g)) for m, g in duo],
                axis=1,
            )

        def score(duo):
            (n, h), (other_n, other_h) = duo
            blank = jnp.zeros((slots, HD), jnp.bfloat16)
            diagonal = jnp.concatenate(
                [
                    jnp.concatenate([q_buf[n, :, lanes(h)], blank], axis=1),
                    jnp.concatenate([blank, q_buf[other_n, :, lanes(other_h)]], axis=1),
                ],
                axis=0,
            )
            return lax.dot_general(
                diagonal,
                side_by_side(pk_buf, fk_buf, duo),
                (((1,), (1,)), ((), ())),
                preferred_element_type=jnp.float32,
            )

        def weigh(duo, scores):
            column = lax.broadcasted_iota(jnp.int32, (slots, slots), 1)
            usable = jnp.concatenate([column < live[ids[n]] for n, _ in duo], axis=0)
            scores = jnp.concatenate(
                [scores[:, :cached], jnp.where(usable, scores[:, cached:], MASKED)], axis=1
            )
            peak = jnp.max(scores, axis=1, keepdims=True)
            weights = jnp.exp2((scores - peak) * exponent_scale)
            return weights.astype(jnp.bfloat16), jnp.sum(weights, axis=1, keepdims=True)

        def blend(duo, weights, row_total):
            blended = jnp.dot(
                weights, side_by_side(pv_buf, fv_buf, duo), preferred_element_type=jnp.float32
            )
            row = lax.broadcasted_iota(jnp.int32, (slots, HD), 0)
            for m, (n, h) in enumerate(duo):
                rows = slice(m * slots, (m + 1) * slots)
                attended = blended[rows, lanes(m)] / row_total[rows]
                attended = jnp.where(row < live[ids[n]], attended, 0.0)
                at = (n % per_out) * slots
                outs[n // per_out][at : at + slots, lanes(h)] = attended.astype(jnp.bfloat16)

        units = []
        for first in range(0, count, 2):
            units += [((n, h), (n, h + 1)) for n in (first, first + 1) for h in range(0, heads - 1, 2)]
            if heads % 2:
                units.append(((first, heads - 1), (first + 1, heads - 1)))
        keys_ready(units[0])
        scores = score(units[0])
        weighed = None
        for u, duo in enumerate(units):
            later = None
            if u + 1 < len(units):
                keys_ready(units[u + 1])
                later = score(units[u + 1])
            if u:
                values_ready(units[u - 1])
                blend(units[u - 1], *weighed)
            weighed = weigh(duo, scores)
            scores = later
        values_ready(units[-1])
        blend(units[-1], *weighed)
        if load:
            wait_pages(("k pages", count), key_page, bounds[-1], pool_pages)
            wait_pages(("v pages", count), value_page, bounds[-1], pool_pages)

    extra = () if after is None else (after,)
    out_shape = [pltpu.VMEM((per_out * slots, width), jnp.bfloat16)] * parts
    if load:
        out_shape += [pltpu.VMEM(paged_keys.shape, jnp.bfloat16)] * 2
    return pl.pallas_call(
        kernel,
        grid_spec=pltpu.PrefetchScalarGridSpec(
            num_scalar_prefetch=3,
            grid=(1,),
            in_specs=[HBM] * 3 + [HBM if load else VMEM] * 2 + [ANY] * len(extra),
            out_specs=[VMEM] * len(out_shape),
            scratch_shapes=[
                pltpu.VMEM((count, slots, width), jnp.bfloat16),
                pltpu.VMEM((count, slots, width), jnp.bfloat16),
                pltpu.VMEM((count, slots, width), jnp.bfloat16),
                pltpu.SMEM((pool_pages,), jnp.int32),
                pltpu.SMEM((pool_pages,), jnp.int32),
                pltpu.SemaphoreType.DMA((3 * count + 2 * pool_pages,)),
            ],
        ),
        out_shape=out_shape,
        compiler_params=pltpu.CompilerParams(vmem_limit_bytes=VMEM_LIMIT),
        cost_estimate=BRIEF,
        name="attend",
    )(
        in_hbm(request_page_table),
        in_hbm(live_token_count),
        place,
        *map(in_hbm, (queries, fresh_keys, fresh_values)),
        *(map(in_hbm, (paged_keys, paged_values)) if load else map(in_vmem, pools)),
        *extra,
    )


def project(own, other, weight, weight_other, after):
    rows = own.shape[0]
    columns = weight.shape[1]

    def kernel(a, b, w, u, after, out):
        features = jnp.concatenate([a[...], b[...]], axis=1)
        for n in range(columns // BLOCK):
            here = slice(n * BLOCK, (n + 1) * BLOCK)
            out[:, here] = jnp.dot(
                features,
                jnp.concatenate([w[:, here], u[:, here]], axis=0),
                preferred_element_type=jnp.float32,
            ).astype(jnp.bfloat16)

    return pl.pallas_call(
        kernel,
        in_specs=[VMEM] * 4 + [ANY],
        out_specs=VMEM,
        out_shape=pltpu.VMEM((rows, columns), jnp.bfloat16),
        compiler_params=pltpu.CompilerParams(vmem_limit_bytes=VMEM_LIMIT),
        cost_estimate=BRIEF,
        name="project",
    )(in_vmem(own), in_vmem(other), in_vmem(weight), in_vmem(weight_other), after)


def pack_pair(ups, downs, place, after):
    rank, columns = ups[0].shape[1:]
    width = downs[0].shape[2]
    half = columns // 2

    def kernel(place, up_0, up_1, down_0, down_1, after, out):
        here = pl.ds(pl.multiple_of((place[0] & 1) * half, half), half)
        for n, (up, down) in enumerate(((up_0, down_0), (up_1, down_1))):
            out[n, :, :half] = up[0, :, here]
            out[n, :, half:] = down[0]

    return pl.pallas_call(
        kernel,
        in_specs=[SMEM] + [VMEM] * 4 + [ANY],
        out_specs=VMEM,
        out_shape=jax.ShapeDtypeStruct((2, rank, half + width), ups[0].dtype),
        compiler_params=pltpu.CompilerParams(vmem_limit_bytes=VMEM_LIMIT),
        cost_estimate=BRIEF,
        name="pack_pair",
    )(place, *ups, *downs, after)


def pick_factors(pairs, place, lookup, per_owner, width, after):
    rank = pairs[0].shape[1]
    half = pairs[0].shape[2] - width
    count = len(pairs)

    def kernel(place, slot, in_use, pool_row, *refs):
        pieces, outs = refs[:count], refs[-2:]
        for n, out in enumerate(outs):
            for m in range(2):
                for i in range(2):
                    request = (place[0] ^ n ^ (0 if m else 2)) * per_owner + i
                    row = pool_row[in_use[slot[request]]]
                    apart = lax.rem(place[1] // 2 - row // 2 + count, count)
                    side = (row ^ place[1]) & 1
                    for d, piece in enumerate(pieces):

                        @pl.when(apart == d)
                        def _(piece=piece, out=out, k=2 * m + i, m=m, i=i, side=side):
                            out[:, k * width : (k + 1) * width] = piece[side, :, half:]
                            if m:
                                there = 4 * width + i * half
                                out[:, there : there + half] = piece[side, :, :half]

    shape = jax.ShapeDtypeStruct((rank, 4 * width + 2 * half), pairs[0].dtype)
    return pl.pallas_call(
        kernel,
        in_specs=[SMEM] * 4 + [VMEM] * count + [ANY],
        out_specs=[VMEM] * 2,
        out_shape=[shape] * 2,
        compiler_params=pltpu.CompilerParams(vmem_limit_bytes=VMEM_LIMIT),
        cost_estimate=BRIEF,
        name="pick_factors",
    )(place, *lookup, *pairs, after)


def cross_ranks(here, other, factors):
    slots, width = here[0].shape
    rank = factors[0].shape[0]

    def kernel(*refs):
        factors, blocks, out = refs[:2], refs[2:6], refs[6]
        for i in range(2):
            acts = sum(
                lax.dot_general(
                    factors[m][:, i * width : (i + 1) * width],
                    blocks[2 * m + i][...],
                    (((1,), (1,)), ((), ())),
                    preferred_element_type=jnp.float32,
                )
                for m in range(2)
            )
            high = acts.astype(jnp.bfloat16)
            low = (acts - high.astype(jnp.float32)).astype(jnp.bfloat16)
            out[:, 2 * i * slots : (2 * i + 1) * slots] = high
            out[:, (2 * i + 1) * slots : (2 * i + 2) * slots] = low

    return pl.pallas_call(
        kernel,
        in_specs=[VMEM] * 6,
        out_specs=VMEM,
        out_shape=jax.ShapeDtypeStruct((rank, 4 * slots), jnp.bfloat16),
        compiler_params=pltpu.CompilerParams(vmem_limit_bytes=VMEM_LIMIT),
        cost_estimate=BRIEF,
        name="cross_ranks",
    )(*factors, *here, *other)


def project_own(
    own, other, weight, weight_other, first, ranks, factors, gating, place
):
    rows, width = own.shape
    columns = weight.shape[1]
    blocks = columns // BLOCK
    slots = rows // 2
    rank = factors[0].shape[0]
    half = columns // 2

    def kernel(
        place, a, b, w, u, first, ranks, mine, theirs, gate, out, rest_out, gates, out_buf, ups, sems
    ):
        def store(n):
            there = (pl.ds(0, slots), pl.ds(n * BLOCK, BLOCK))
            return pltpu.make_async_copy(out_buf.at[there], out.at[there], sems.at[n])

        core = place[0] & 1
        gates[...] = jnp.zeros_like(gates)
        pieces = []
        for i in range(2):
            here = slice(i * slots, (i + 1) * slots)
            down = slice((2 + i) * width, (3 + i) * width)
            acts = sum(
                lax.dot_general(
                    factors[:, down],
                    block[here],
                    (((1,), (1,)), ((), ())),
                    preferred_element_type=jnp.float32,
                )
                for factors, block in ((mine, a), (theirs, b))
            )
            for m in range(2 * i, 2 * i + 2):
                acts += ranks[:, m * slots : (m + 1) * slots].astype(jnp.float32)
            high = acts.astype(jnp.bfloat16).astype(jnp.float32)
            pieces.append(jnp.concatenate([high, acts - high], axis=0).T.astype(jnp.bfloat16))
            up = 4 * width + i * half
            for m in range(2):
                for away, factors in enumerate((mine, theirs)):
                    there = pl.ds(pl.multiple_of((core ^ away) * half, half), half)
                    ups[i, m * rank : (m + 1) * rank, there] = factors[:, up : up + half]
            gates[i : i + 1] = gate[pl.ds(place[0] * 2 + i, 1), :]
        features = jnp.concatenate([a[...], b[...]], axis=1)
        for n in range(blocks):
            here = slice(n * BLOCK, (n + 1) * BLOCK)
            sums = jnp.dot(
                features,
                jnp.concatenate([w[:, here], u[:, here]], axis=0),
                preferred_element_type=jnp.float32,
            )
            for i in range(2):
                those = slice(i * slots, (i + 1) * slots)
                update = sums[those] + jnp.dot(
                    pieces[i], ups[i, :, here], preferred_element_type=jnp.float32
                )
                if i:
                    rest_out[:, here] = update * gates[i : i + 1, here]
                else:
                    update += first[:, here].astype(jnp.float32)
                    out_buf[:, here] = (update * gates[i : i + 1, here]).astype(jnp.bfloat16)
                    store(n).start()
        for n in range(blocks):
            store(n).wait()

    return pl.pallas_call(
        kernel,
        in_specs=[SMEM] + [VMEM] * 9,
        out_specs=[HBM, VMEM, VMEM],
        out_shape=[
            pltpu.HBM((rows, columns), jnp.bfloat16),
            jax.ShapeDtypeStruct((slots, columns), jnp.float32),
            jax.ShapeDtypeStruct((8, columns), jnp.float32),
        ],
        scratch_shapes=[
            pltpu.VMEM((slots, columns), jnp.bfloat16),
            pltpu.VMEM((2, 2 * rank, columns), jnp.bfloat16),
            pltpu.SemaphoreType.DMA((blocks,)),
        ],
        compiler_params=pltpu.CompilerParams(vmem_limit_bytes=VMEM_LIMIT),
        cost_estimate=BRIEF,
        name="project_own",
    )(
        place,
        own,
        other,
        in_vmem(weight),
        in_vmem(weight_other),
        first,
        ranks,
        *factors,
        gating,
    )


def finish(so_far, rest, received, gates):
    rows, columns = so_far.shape
    slots = rest.shape[0]
    blocks = columns // BLOCK

    def kernel(sums, part, gates, so_far, out, buf, sems):
        def store(n):
            here = pl.ds(n * BLOCK, BLOCK)
            return pltpu.make_async_copy(
                buf.at[:, here], out.at[pl.ds(slots, slots), here], sems.at[n]
            )

        for n in range(blocks):
            here = slice(n * BLOCK, (n + 1) * BLOCK)
            update = sums[:, here] + part[:, here].astype(jnp.float32) * gates[1:2, here]
            buf[:, here] = update.astype(jnp.bfloat16)
            store(n).start()
        for n in range(blocks):
            store(n).wait()

    return pl.pallas_call(
        kernel,
        in_specs=[VMEM] * 3 + [HBM],
        out_specs=HBM,
        out_shape=jax.ShapeDtypeStruct((rows, columns), jnp.bfloat16),
        scratch_shapes=[
            pltpu.VMEM((slots, columns), jnp.bfloat16),
            pltpu.SemaphoreType.DMA((blocks,)),
        ],
        input_output_aliases={3: 0},
        compiler_params=pltpu.CompilerParams(vmem_limit_bytes=VMEM_LIMIT),
        cost_estimate=BRIEF,
        name="finish",
    )(rest, received, gates, so_far)


def body(
    queries,
    fresh_keys,
    fresh_values,
    paged_keys,
    paged_values,
    request_page_table,
    live_token_count,
    request_adapter_slot,
    adapters_in_use,
    adapter_pool_row,
    adapter_down_factors,
    adapter_up_factors,
    output_weight,
    gating,
):
    tp = lax.axis_size("tp")
    holders = lax.axis_size("req")
    place = jnp.stack([lax.axis_index("tp"), lax.axis_index("req")]).astype(jnp.int32)
    per_owner = live_token_count.shape[0] // tp

    def swap(array, flip):
        return lax.ppermute(array, "tp", [(s, s ^ flip) for s in range(tp)])

    def attend(wanted, pools=None, after=None):
        return attend_some(
            queries,
            fresh_keys,
            fresh_values,
            paged_keys,
            paged_values,
            request_page_table,
            live_token_count,
            place,
            per_owner,
            wanted,
            pools,
            after,
        )

    ups, downs = (
        (factors, lax.ppermute(factors, "req", [(s, s ^ 1) for s in range(holders)]))
        for factors in (adapter_up_factors, adapter_down_factors)
    )
    weight_other = swap(output_weight, 1)

    away_a, here_a, *pools = attend(((3, 0), (2, 0)))
    away_a, ups, downs = lax.optimization_barrier((away_a, ups, downs))
    other_a = swap(away_a, 1)
    pair = pack_pair(ups, downs, place, away_a)
    sent_a = project(here_a, other_a, output_weight, weight_other, pair)
    first = swap(sent_a, 2)

    pair, _ = lax.optimization_barrier((pair, sent_a))
    pairs = [pair] + [
        lax.ppermute(pair, "req", [(s, (s + d) % holders) for s in range(holders)])
        for d in range(2, holders, 2)
    ]
    away_b, here_b = attend(((3, 1), (2, 1)), pools, sent_a)
    (own_away,) = attend(((1, 0), (1, 1)), pools, away_b)
    away_b, own_away, *pairs = lax.optimization_barrier((away_b, own_away, *pairs))
    other_b = swap(away_b, 1)
    own_other = swap(own_away, 1)
    sent_b = project(here_b, other_b, output_weight, weight_other, own_away)
    second = swap(sent_b, 2)

    first, *pairs = lax.optimization_barrier((first, *pairs))
    lookup = (request_adapter_slot, adapters_in_use, adapter_pool_row)
    width = output_weight.shape[0]
    factors, factors_away = pick_factors(pairs, place, lookup, per_owner, width, sent_b)
    factors = (factors, swap(factors_away, 1))
    ranks = cross_ranks((here_a, here_b), (other_a, other_b), factors)
    (own_here,) = attend(((0, 0), (0, 1)), pools, ranks)
    ranks = swap(ranks, 2)
    out, rest, gates = project_own(
        own_here, own_other, output_weight, weight_other, first, ranks, factors, gating, place
    )
    return finish(out, rest, second, gates)


def solution(mesh):
    return jax.shard_map(
        body,
        mesh=mesh,
        in_specs=(
            P("req", "tp"),
            P("req", "tp"),
            P("req", "tp"),
            P("req", None, "tp"),
            P("req", None, "tp"),
            P("req", None),
            P("req"),
            P("req"),
            P(),
            P(),
            P("req", None, "tp"),
            P("req", None, None),
            P("tp", None),
            P("req", None),
        ),
        out_specs=P(("req", "tp"), None),
        check_vma=False,
    )
```

```python
import math

import jax
import jax.numpy as jnp
from jax import lax
from jax.experimental import pallas as pl
from jax.experimental.pallas import tpu as pltpu
from jax.sharding import PartitionSpec as P

HD = 128
VMEM_LIMIT = 32 * 1024 * 1024
SMEM = pl.BlockSpec(memory_space=pltpu.SMEM)
BLOCK = 512
CUTS = (3, 1, 1)
MASKED = -1e30
ANY = pl.BlockSpec(memory_space=pl.ANY)
BRIEF = pl.CostEstimate(flops=1000, bytes_accessed=1000, transcendentals=0)
HBM = pl.BlockSpec(memory_space=pltpu.HBM)
VMEM = pl.BlockSpec(memory_space=pltpu.VMEM)


def in_hbm(array):
    return pltpu.with_memory_space_constraint(array, pltpu.HBM)


def in_vmem(array):
    return pltpu.with_memory_space_constraint(array, pltpu.VMEM)


def attend_some(
    queries,
    fresh_keys,
    fresh_values,
    paged_keys,
    paged_values,
    request_page_table,
    live_token_count,
    place,
    per_owner,
    wanted,
    pools=None,
    after=None,
):
    requests_here, pages = request_page_table.shape
    slots = queries.shape[0] // requests_here
    width = queries.shape[1]
    heads = width // HD
    pool_pages, page_rows = paged_keys.shape[:2]
    cached = pages * page_rows
    load = pools is None
    count = len(wanted)
    parts = len({away for away, _ in wanted})
    per_out = count // parts
    exponent_scale = math.log2(math.e) / math.sqrt(HD)

    def kernel(table, live, place, q_hbm, fk_hbm, fv_hbm, pk_hbm, pv_hbm, *rest):
        ids = [(place[0] ^ away) * per_owner + n for away, n in wanted]
        q_buf, fk_buf, fv_buf, order, seen, in_sems = rest[-6:]
        if load:
            *outs, pk_buf, pv_buf = rest[-8 - parts : -6]
        else:
            outs, pk_buf, pv_buf = rest[-6 - parts : -6], pk_hbm, pv_hbm
            q_buf, fk_buf, fv_buf = q_hbm, fk_hbm, fv_hbm

        def fetch(src, dst, sem):
            return pltpu.make_async_copy(src, dst, in_sems.at[sem])

        def rows_of(n):
            return pl.ds(pl.multiple_of(ids[n] * slots, slots), slots)

        def query_copy(n):
            return fetch(q_hbm.at[rows_of(n)], q_buf.at[n], 3 * n)

        def key_copy(n):
            return fetch(fk_hbm.at[rows_of(n)], fk_buf.at[n], 3 * n + 1)

        def value_copy(n):
            return fetch(fv_hbm.at[rows_of(n)], fv_buf.at[n], 3 * n + 2)

        def key_page(m):
            page = order[m]
            return fetch(pk_hbm.at[page], pk_buf.at[page], 3 * count + 2 * m)

        def value_page(m):
            page = order[m]
            return fetch(pv_hbm.at[page], pv_buf.at[page], 3 * count + 2 * m + 1)

        def start(copies):
            for copy in copies:
                copy.start()

        def start_pages(begin, end):
            for m in range(pages, pool_pages):

                @pl.when((m >= begin) & (m < end))
                def _(m=m):
                    key_page(m).start()

            for m in range(pages, pool_pages):

                @pl.when((m >= begin) & (m < end))
                def _(m=m):
                    value_page(m).start()

        if load:
            for j in range(pages):
                order[j] = table[ids[0], j]
            start([query_copy(0), key_copy(0)] + [key_page(m) for m in range(pages)])
            start([value_copy(0)] + [value_page(m) for m in range(pages)])
            for page in range(pool_pages):
                taken = order[0] == page
                for j in range(1, pages):
                    taken = taken | (order[j] == page)
                seen[page] = taken.astype(jnp.int32)
            bounds = [jnp.int32(pages)]
            for n in range(1, count):
                free = bounds[-1]
                for j in range(pages):
                    page = table[ids[n], j]
                    fresh = seen[page] == 0

                    @pl.when(fresh)
                    def _(page=page, free=free):
                        order[free] = page
                        seen[page] = 1

                    free = free + fresh.astype(jnp.int32)
                bounds.append(free)
                start([query_copy(n), key_copy(n), value_copy(n)])
                start_pages(bounds[n - 1], bounds[n])
            free = bounds[-1]
            for page in range(pool_pages):
                fresh = seen[page] == 0

                @pl.when(fresh)
                def _(page=page, free=free):
                    order[free] = page

                free = free + fresh.astype(jnp.int32)
            start_pages(bounds[-1], pool_pages)
        waited = set()

        def wait(name, make, indices):
            if name not in waited:
                waited.add(name)
                for index in indices:
                    make(index).wait()

        def wait_pages(name, make, begin, end):
            if name not in waited:
                waited.add(name)
                for m in range(pages, pool_pages):

                    @pl.when((m >= begin) & (m < end))
                    def _(m=m):
                        make(m).wait()

        def keys_ready(duo):
            for n in range(1 + max(n for n, _ in duo)) if load else ():
                wait(("q", n), query_copy, [n])
                wait(("k", n), key_copy, [n])
                if n:
                    wait_pages(("k pages", n), key_page, bounds[n - 1], bounds[n])
                else:
                    wait(("k pages", 0), key_page, range(pages))

        def values_ready(duo):
            for n in range(1 + max(n for n, _ in duo)) if load else ():
                wait(("v", n), value_copy, [n])
                if n:
                    wait_pages(("v pages", n), value_page, bounds[n - 1], bounds[n])
                else:
                    wait(("v pages", 0), value_page, range(pages))

        def lanes(h, several=1):
            return slice(h * HD, (h + several) * HD)

        def own(buf, n, here):
            return buf[n, :, here] if load else buf[rows_of(n), here]

        def gather(pool, fresh, n, here):
            return jnp.concatenate(
                [pool[table[ids[n], j], :, here] for j in range(pages)] + [own(fresh, n, here)],
                axis=0,
            )

        def side_by_side(pool, fresh, duo):
            (n, h), (other_n, other_h) = duo
            if n == other_n and other_h == h + 1:
                return gather(pool, fresh, n, lanes(h, 2))
            return jnp.concatenate(
                [gather(pool, fresh, m, lanes(g)) for m, g in duo],
                axis=1,
            )

        def score(duo):
            (n, h), (other_n, other_h) = duo
            blank = jnp.zeros((slots, HD), jnp.bfloat16)
            diagonal = jnp.concatenate(
                [
                    jnp.concatenate([own(q_buf, n, lanes(h)), blank], axis=1),
                    jnp.concatenate([blank, own(q_buf, other_n, lanes(other_h))], axis=1),
                ],
                axis=0,
            )
            return lax.dot_general(
                diagonal,
                side_by_side(pk_buf, fk_buf, duo),
                (((1,), (1,)), ((), ())),
                preferred_element_type=jnp.float32,
            )

        def weigh(duo, scores):
            column = lax.broadcasted_iota(jnp.int32, (slots, slots), 1)
            usable = jnp.concatenate([column < live[ids[n]] for n, _ in duo], axis=0)
            scores = jnp.concatenate(
                [scores[:, :cached], jnp.where(usable, scores[:, cached:], MASKED)], axis=1
            )
            peak = jnp.max(scores, axis=1, keepdims=True)
            weights = jnp.exp2((scores - peak) * exponent_scale)
            return weights.astype(jnp.bfloat16), jnp.sum(weights, axis=1, keepdims=True)

        def blend(duo, weights, row_total):
            blended = jnp.dot(
                weights, side_by_side(pv_buf, fv_buf, duo), preferred_element_type=jnp.float32
            )
            row = lax.broadcasted_iota(jnp.int32, (slots, HD), 0)
            for m, (n, h) in enumerate(duo):
                rows = slice(m * slots, (m + 1) * slots)
                attended = blended[rows, lanes(m)] / row_total[rows]
                attended = jnp.where(row < live[ids[n]], attended, 0.0)
                at = (n % per_out) * slots
                outs[n // per_out][at : at + slots, lanes(h)] = attended.astype(jnp.bfloat16)

        units = []
        for first in range(0, count, 2):
            units += [((n, h), (n, h + 1)) for n in (first, first + 1) for h in range(0, heads - 1, 2)]
            if heads % 2:
                units.append(((first, heads - 1), (first + 1, heads - 1)))
        keys_ready(units[0])
        scores = score(units[0])
        weighed = None
        for u, duo in enumerate(units):
            later = None
            if u + 1 < len(units):
                keys_ready(units[u + 1])
                later = score(units[u + 1])
            if u:
                values_ready(units[u - 1])
                blend(units[u - 1], *weighed)
            weighed = weigh(duo, scores)
            scores = later
        values_ready(units[-1])
        blend(units[-1], *weighed)
        if load:
            wait_pages(("k pages", count), key_page, bounds[-1], pool_pages)
            wait_pages(("v pages", count), value_page, bounds[-1], pool_pages)

    extra = () if after is None else (after,)
    out_shape = [pltpu.VMEM((per_out * slots, width), jnp.bfloat16)] * parts
    if load:
        out_shape += [pltpu.VMEM(paged_keys.shape, jnp.bfloat16)] * 2
    return pl.pallas_call(
        kernel,
        grid_spec=pltpu.PrefetchScalarGridSpec(
            num_scalar_prefetch=3,
            grid=(1,),
            in_specs=[HBM if load else VMEM] * 5 + [ANY] * len(extra),
            out_specs=[VMEM] * len(out_shape),
            scratch_shapes=[
                pltpu.VMEM((count if load else 1, slots, width), jnp.bfloat16),
                pltpu.VMEM((count if load else 1, slots, width), jnp.bfloat16),
                pltpu.VMEM((count if load else 1, slots, width), jnp.bfloat16),
                pltpu.SMEM((pool_pages,), jnp.int32),
                pltpu.SMEM((pool_pages,), jnp.int32),
                pltpu.SemaphoreType.DMA((3 * count + 2 * pool_pages,)),
            ],
        ),
        out_shape=out_shape,
        compiler_params=pltpu.CompilerParams(vmem_limit_bytes=VMEM_LIMIT),
        cost_estimate=BRIEF,
        name="attend",
    )(
        in_hbm(request_page_table),
        in_hbm(live_token_count),
        place,
        *map(in_hbm if load else in_vmem, (queries, fresh_keys, fresh_values)),
        *(map(in_hbm, (paged_keys, paged_values)) if load else map(in_vmem, pools)),
        *extra,
    )


def project(own, other, weight, weight_other, cuts, after):
    rows = own.shape[0]
    bounds = [sum(cuts[:n]) for n in range(len(cuts) + 1)]
    assert bounds[-1] * BLOCK == weight.shape[1]

    def kernel(a, b, w, u, after, *outs):
        features = jnp.concatenate([a[...], b[...]], axis=1)
        for part, out in enumerate(outs):
            for n in range(cuts[part]):
                here = slice((bounds[part] + n) * BLOCK, (bounds[part] + n + 1) * BLOCK)
                out[:, n * BLOCK : (n + 1) * BLOCK] = jnp.dot(
                    features,
                    jnp.concatenate([w[:, here], u[:, here]], axis=0),
                    preferred_element_type=jnp.float32,
                ).astype(jnp.bfloat16)

    return pl.pallas_call(
        kernel,
        in_specs=[VMEM] * 4 + [ANY],
        out_specs=[VMEM] * len(cuts),
        out_shape=[pltpu.VMEM((rows, cut * BLOCK), jnp.bfloat16) for cut in cuts],
        compiler_params=pltpu.CompilerParams(vmem_limit_bytes=VMEM_LIMIT),
        cost_estimate=BRIEF,
        name="project",
    )(in_vmem(own), in_vmem(other), in_vmem(weight), in_vmem(weight_other), after)


def pack_pair(ups, downs, place, after):
    rank, columns = ups[0].shape[1:]
    width = downs[0].shape[2]
    half = columns // 2

    def kernel(place, up_0, up_1, down_0, down_1, after, out):
        here = pl.ds(pl.multiple_of((place[0] & 1) * half, half), half)
        for n, (up, down) in enumerate(((up_0, down_0), (up_1, down_1))):
            out[n, :, :half] = up[0, :, here]
            out[n, :, half:] = down[0]

    return pl.pallas_call(
        kernel,
        in_specs=[SMEM] + [VMEM] * 4 + [ANY],
        out_specs=VMEM,
        out_shape=jax.ShapeDtypeStruct((2, rank, half + width), ups[0].dtype),
        compiler_params=pltpu.CompilerParams(vmem_limit_bytes=VMEM_LIMIT),
        cost_estimate=BRIEF,
        name="pack_pair",
    )(place, *ups, *downs, after)


def pick_factors(pairs, place, lookup, per_owner, width, after):
    rank = pairs[0].shape[1]
    half = pairs[0].shape[2] - width
    count = len(pairs)

    def kernel(place, slot, in_use, pool_row, *refs):
        pieces, outs = refs[:count], refs[-2:]
        for n, out in enumerate(outs):
            for m in range(2):
                for i in range(2):
                    request = (place[0] ^ n ^ (0 if m else 2)) * per_owner + i
                    row = pool_row[in_use[slot[request]]]
                    apart = lax.rem(place[1] // 2 - row // 2 + count, count)
                    side = (row ^ place[1]) & 1
                    for d, piece in enumerate(pieces):

                        @pl.when(apart == d)
                        def _(piece=piece, out=out, k=2 * m + i, m=m, i=i, side=side):
                            out[:, k * width : (k + 1) * width] = piece[side, :, half:]
                            if m:
                                there = 4 * width + i * half
                                out[:, there : there + half] = piece[side, :, :half]

    shape = jax.ShapeDtypeStruct((rank, 4 * width + 2 * half), pairs[0].dtype)
    return pl.pallas_call(
        kernel,
        in_specs=[SMEM] * 4 + [VMEM] * count + [ANY],
        out_specs=[VMEM] * 2,
        out_shape=[shape] * 2,
        compiler_params=pltpu.CompilerParams(vmem_limit_bytes=VMEM_LIMIT),
        cost_estimate=BRIEF,
        name="pick_factors",
    )(place, *lookup, *pairs, after)


def ranks_and_part(here, other, factors, part):
    slots, width = here[0].shape
    rows = part.shape[0]
    rank = factors[0].shape[0]
    assert part.shape[1] == 4 * slots

    def kernel(*refs):
        factors, blocks, (part_in, part_out) = refs[:2], refs[2:6], refs[6:]
        part_out[:rows] = part_in[...]
        for i in range(2):
            acts = sum(
                lax.dot_general(
                    factors[m][:, i * width : (i + 1) * width],
                    blocks[2 * m + i][...],
                    (((1,), (1,)), ((), ())),
                    preferred_element_type=jnp.float32,
                )
                for m in range(2)
            )
            high = acts.astype(jnp.bfloat16)
            low = (acts - high.astype(jnp.float32)).astype(jnp.bfloat16)
            part_out[rows:, 2 * i * slots : (2 * i + 1) * slots] = high
            part_out[rows:, (2 * i + 1) * slots : (2 * i + 2) * slots] = low

    return pl.pallas_call(
        kernel,
        in_specs=[VMEM] * 7,
        out_specs=VMEM,
        out_shape=jax.ShapeDtypeStruct((rows + rank, part.shape[1]), jnp.bfloat16),
        compiler_params=pltpu.CompilerParams(vmem_limit_bytes=VMEM_LIMIT),
        cost_estimate=BRIEF,
        name="ranks_and_part",
    )(*factors, *here, *other, part)


def project_own(
    own, other, weight, weight_other, first, second, last, factors, gating, place
):
    rows, width = own.shape
    columns = weight.shape[1]
    blocks = columns // BLOCK
    slots = rows // 2
    rank = factors[0].shape[0]
    half = columns // 2
    open_from = second.shape[1] // BLOCK
    open_to = (columns - last.shape[1]) // BLOCK

    def kernel(
        place, a, b, w, u, first, second, last, mine, theirs, gate, out, rest_out, gates, out_buf, ups, sems
    ):
        def store(i, n):
            there = (pl.ds(i * slots, slots), pl.ds(n * BLOCK, BLOCK))
            return pltpu.make_async_copy(out_buf.at[there], out.at[there], sems.at[i, n])

        core = place[0] & 1
        gates[...] = jnp.zeros_like(gates)
        pieces = []
        for i in range(2):
            here = slice(i * slots, (i + 1) * slots)
            down = slice((2 + i) * width, (3 + i) * width)
            acts = sum(
                lax.dot_general(
                    factors[:, down],
                    block[here],
                    (((1,), (1,)), ((), ())),
                    preferred_element_type=jnp.float32,
                )
                for factors, block in ((mine, a), (theirs, b))
            )
            for m in range(2 * i, 2 * i + 2):
                acts += last[slots:, m * slots : (m + 1) * slots].astype(jnp.float32)
            high = acts.astype(jnp.bfloat16).astype(jnp.float32)
            pieces.append(jnp.concatenate([high, acts - high], axis=0).T.astype(jnp.bfloat16))
            up = 4 * width + i * half
            for m in range(2):
                for away, factors in enumerate((mine, theirs)):
                    there = pl.ds(pl.multiple_of((core ^ away) * half, half), half)
                    ups[i, m * rank : (m + 1) * rank, there] = factors[:, up : up + half]
            gates[i : i + 1] = gate[pl.ds(place[0] * 2 + i, 1), :]
        features = jnp.concatenate([a[...], b[...]], axis=1)
        for n in range(blocks):
            here = slice(n * BLOCK, (n + 1) * BLOCK)
            sums = jnp.dot(
                features,
                jnp.concatenate([w[:, here], u[:, here]], axis=0),
                preferred_element_type=jnp.float32,
            )
            for i in range(2):
                those = slice(i * slots, (i + 1) * slots)
                update = sums[those] + jnp.dot(
                    pieces[i], ups[i, :, here], preferred_element_type=jnp.float32
                )
                if not i:
                    update += first[:, here].astype(jnp.float32)
                elif n < open_from:
                    update += second[:, here].astype(jnp.float32)
                elif n >= open_to:
                    there = slice((n - open_to) * BLOCK, (n - open_to + 1) * BLOCK)
                    update += last[:slots, there].astype(jnp.float32)
                gated = update * gates[i : i + 1, here]
                if i and open_from <= n < open_to:
                    there = slice((n - open_from) * BLOCK, (n - open_from + 1) * BLOCK)
                    rest_out[:, there] = gated
                else:
                    out_buf[those, here] = gated.astype(jnp.bfloat16)
                    store(i, n).start()
        for i in range(2):
            for n in range(blocks):
                if not (i and open_from <= n < open_to):
                    store(i, n).wait()

    return pl.pallas_call(
        kernel,
        in_specs=[SMEM] + [VMEM] * 10,
        out_specs=[HBM, VMEM, VMEM],
        out_shape=[
            pltpu.HBM((rows, columns), jnp.bfloat16),
            jax.ShapeDtypeStruct((slots, (open_to - open_from) * BLOCK), jnp.float32),
            jax.ShapeDtypeStruct((8, columns), jnp.float32),
        ],
        scratch_shapes=[
            pltpu.VMEM((rows, columns), jnp.bfloat16),
            pltpu.VMEM((2, 2 * rank, columns), jnp.bfloat16),
            pltpu.SemaphoreType.DMA((2, blocks)),
        ],
        compiler_params=pltpu.CompilerParams(vmem_limit_bytes=VMEM_LIMIT),
        cost_estimate=BRIEF,
        name="project_own",
    )(
        place,
        own,
        other,
        in_vmem(weight),
        in_vmem(weight_other),
        first,
        second,
        last,
        *factors,
        gating,
    )


def finish(so_far, rest, received, gates, begin):
    rows, columns = so_far.shape
    slots, wide = rest.shape
    at = begin // wide
    assert begin % wide == 0

    def kernel(sums, part, gate, so_far, out):
        out[...] = (sums[...] + part[...].astype(jnp.float32) * gate[1:2]).astype(jnp.bfloat16)

    return pl.pallas_call(
        kernel,
        grid=(1,),
        in_specs=[
            pl.BlockSpec((slots, wide), lambda j: (0, 0)),
            pl.BlockSpec((slots, wide), lambda j: (0, 0)),
            pl.BlockSpec((gates.shape[0], wide), lambda j: (0, at)),
            ANY,
        ],
        out_specs=pl.BlockSpec((slots, wide), lambda j: (1, at)),
        out_shape=jax.ShapeDtypeStruct((rows, columns), jnp.bfloat16),
        input_output_aliases={3: 0},
        compiler_params=pltpu.CompilerParams(vmem_limit_bytes=VMEM_LIMIT),
        cost_estimate=BRIEF,
        name="finish",
    )(rest, received, gates, so_far)


def body(
    queries,
    fresh_keys,
    fresh_values,
    paged_keys,
    paged_values,
    request_page_table,
    live_token_count,
    request_adapter_slot,
    adapters_in_use,
    adapter_pool_row,
    adapter_down_factors,
    adapter_up_factors,
    output_weight,
    gating,
):
    tp = lax.axis_size("tp")
    holders = lax.axis_size("req")
    place = jnp.stack([lax.axis_index("tp"), lax.axis_index("req")]).astype(jnp.int32)
    per_owner = live_token_count.shape[0] // tp

    def swap(array, flip):
        return lax.ppermute(array, "tp", [(s, s ^ flip) for s in range(tp)])

    def attend(tokens, wanted, pools=None, after=None):
        return attend_some(
            *tokens,
            paged_keys,
            paged_values,
            request_page_table,
            live_token_count,
            place,
            per_owner,
            wanted,
            pools,
            after,
        )

    ups, downs = (
        (factors, lax.ppermute(factors, "req", [(s, s ^ 1) for s in range(holders)]))
        for factors in (adapter_up_factors, adapter_down_factors)
    )
    weight_other = swap(output_weight, 1)

    tokens = (queries, fresh_keys, fresh_values)
    away_a, here_a, *pools = attend(tokens, ((3, 0), (2, 0)))
    *tokens, _ = lax.optimization_barrier((*tokens, away_a))
    away_a, ups, downs = lax.optimization_barrier((away_a, ups, downs))
    other_a = swap(away_a, 1)
    pair = pack_pair(ups, downs, place, away_a)
    (sent_a,) = project(here_a, other_a, output_weight, weight_other, (sum(CUTS),), pair)
    first = swap(sent_a, 2)

    pair, _ = lax.optimization_barrier((pair, sent_a))
    pairs = [pair] + [
        lax.ppermute(pair, "req", [(s, (s + d) % holders) for s in range(holders)])
        for d in range(2, holders, 2)
    ]
    away_b, here_b = attend(tokens, ((3, 1), (2, 1)), pools, sent_a)
    (own_away,) = attend(tokens, ((1, 0), (1, 1)), pools, away_b)
    away_b, own_away, *pairs = lax.optimization_barrier((away_b, own_away, *pairs))
    other_b = swap(away_b, 1)
    own_other = swap(own_away, 1)
    sent_b = project(here_b, other_b, output_weight, weight_other, CUTS, own_away)
    second = swap(sent_b[0], 2)

    first, *pairs = lax.optimization_barrier((first, *pairs))
    lookup = (request_adapter_slot, adapters_in_use, adapter_pool_row)
    width = output_weight.shape[0]
    factors, factors_away = pick_factors(pairs, place, lookup, per_owner, width, sent_b[0])
    factors = (factors, swap(factors_away, 1))
    last = ranks_and_part((here_a, here_b), (other_a, other_b), factors, sent_b[2])
    third, first, _ = lax.optimization_barrier((sent_b[1], first, last))
    third = swap(third, 2)
    (own_here,) = attend(tokens, ((0, 0), (0, 1)), pools, last)
    last = swap(last, 2)
    out, rest, gates = project_own(
        own_here,
        own_other,
        output_weight,
        weight_other,
        first,
        second,
        last,
        factors,
        gating,
        place,
    )
    return finish(out, rest, third, gates, CUTS[0] * BLOCK)


def solution(mesh):
    return jax.shard_map(
        body,
        mesh=mesh,
        in_specs=(
            P("req", "tp"),
            P("req", "tp"),
            P("req", "tp"),
            P("req", None, "tp"),
            P("req", None, "tp"),
            P("req", None),
            P("req"),
            P("req"),
            P(),
            P(),
            P("req", None, "tp"),
            P("req", None, None),
            P("tp", None),
            P("req", None),
        ),
        out_specs=P(("req", "tp"), None),
        check_vma=False,
    )
```

```python
import math

import jax
import jax.numpy as jnp
from jax import lax
from jax.experimental import pallas as pl
from jax.experimental.pallas import tpu as pltpu
from jax.sharding import PartitionSpec as P

HD = 128
VMEM_LIMIT = 32 * 1024 * 1024
SMEM = pl.BlockSpec(memory_space=pltpu.SMEM)
BLOCK = 256
CUTS = (5, 2, 1, 2)
MASKED = -1e30
ANY = pl.BlockSpec(memory_space=pl.ANY)
BRIEF = pl.CostEstimate(flops=1000, bytes_accessed=1000, transcendentals=0)
HBM = pl.BlockSpec(memory_space=pltpu.HBM)
VMEM = pl.BlockSpec(memory_space=pltpu.VMEM)


def in_hbm(array):
    return pltpu.with_memory_space_constraint(array, pltpu.HBM)


def in_vmem(array):
    return pltpu.with_memory_space_constraint(array, pltpu.VMEM)


def attend_some(
    queries,
    fresh_keys,
    fresh_values,
    paged_keys,
    paged_values,
    request_page_table,
    live_token_count,
    place,
    per_owner,
    wanted,
    load,
    after=None,
):
    requests_here, pages = request_page_table.shape
    slots = queries.shape[0] // requests_here
    width = queries.shape[1]
    heads = width // HD
    pool_pages, page_rows = paged_keys.shape[:2]
    cached = pages * page_rows
    count = len(wanted)
    parts = len({away for away, _ in wanted})
    per_out = count // parts
    exponent_scale = math.log2(math.e) / math.sqrt(HD)

    def kernel(table, live, place, q_hbm, fk_hbm, fv_hbm, pk_hbm, pv_hbm, *rest):
        ids = [(place[0] ^ away) * per_owner + n for away, n in wanted]
        outs = rest[-8 - parts : -8]
        q_buf, fk_buf, fv_buf, pk_buf, pv_buf, order, seen, in_sems = rest[-8:]
        if not load:
            q_buf, fk_buf, fv_buf, pk_buf, pv_buf = q_hbm, fk_hbm, fv_hbm, pk_hbm, pv_hbm

        def fetch(src, dst, sem):
            return pltpu.make_async_copy(src, dst, in_sems.at[sem])

        def rows_of(n):
            return pl.ds(pl.multiple_of(ids[n] * slots, slots), slots)

        def query_copy(n):
            return fetch(q_hbm.at[rows_of(n)], q_buf.at[n], 3 * n)

        def key_copy(n):
            return fetch(fk_hbm.at[rows_of(n)], fk_buf.at[n], 3 * n + 1)

        def value_copy(n):
            return fetch(fv_hbm.at[rows_of(n)], fv_buf.at[n], 3 * n + 2)

        def key_page(m):
            page = order[m]
            return fetch(pk_hbm.at[page], pk_buf.at[page], 3 * count + 2 * m)

        def value_page(m):
            page = order[m]
            return fetch(pv_hbm.at[page], pv_buf.at[page], 3 * count + 2 * m + 1)

        def start(copies):
            for copy in copies:
                copy.start()

        def start_pages(begin, end):
            for m in range(pages, pool_pages):

                @pl.when((m >= begin) & (m < end))
                def _(m=m):
                    key_page(m).start()

            for m in range(pages, pool_pages):

                @pl.when((m >= begin) & (m < end))
                def _(m=m):
                    value_page(m).start()

        if load:
            for j in range(pages):
                order[j] = table[ids[0], j]
            start([query_copy(0), key_copy(0)] + [key_page(m) for m in range(pages)])
            start([value_copy(0)] + [value_page(m) for m in range(pages)])
            for page in range(pool_pages):
                taken = order[0] == page
                for j in range(1, pages):
                    taken = taken | (order[j] == page)
                seen[page] = taken.astype(jnp.int32)
            bounds = [jnp.int32(pages)]
            for n in range(1, count):
                free = bounds[-1]
                for j in range(pages):
                    page = table[ids[n], j]
                    fresh = seen[page] == 0

                    @pl.when(fresh)
                    def _(page=page, free=free):
                        order[free] = page
                        seen[page] = 1

                    free = free + fresh.astype(jnp.int32)
                bounds.append(free)
                start([query_copy(n), key_copy(n), value_copy(n)])
                start_pages(bounds[n - 1], bounds[n])
        waited = set()

        def wait(name, make, indices):
            if name not in waited:
                waited.add(name)
                for index in indices:
                    make(index).wait()

        def wait_pages(name, make, begin, end):
            if name not in waited:
                waited.add(name)
                for m in range(pages, pool_pages):

                    @pl.when((m >= begin) & (m < end))
                    def _(m=m):
                        make(m).wait()

        def keys_ready(duo):
            for n in range(1 + max(n for n, _ in duo)) if load else ():
                wait(("q", n), query_copy, [n])
                wait(("k", n), key_copy, [n])
                if n:
                    wait_pages(("k pages", n), key_page, bounds[n - 1], bounds[n])
                else:
                    wait(("k pages", 0), key_page, range(pages))

        def values_ready(duo):
            for n in range(1 + max(n for n, _ in duo)) if load else ():
                wait(("v", n), value_copy, [n])
                if n:
                    wait_pages(("v pages", n), value_page, bounds[n - 1], bounds[n])
                else:
                    wait(("v pages", 0), value_page, range(pages))

        def lanes(h, several=1):
            return slice(h * HD, (h + several) * HD)

        def own(buf, n, here):
            return buf[n, :, here] if load else buf[rows_of(n), here]

        def gather(pool, fresh, n, here):
            return jnp.concatenate(
                [pool[table[ids[n], j], :, here] for j in range(pages)] + [own(fresh, n, here)],
                axis=0,
            )

        def side_by_side(pool, fresh, duo):
            (n, h), (other_n, other_h) = duo
            if n == other_n and other_h == h + 1:
                return gather(pool, fresh, n, lanes(h, 2))
            return jnp.concatenate(
                [gather(pool, fresh, m, lanes(g)) for m, g in duo],
                axis=1,
            )

        def score(duo):
            (n, h), (other_n, other_h) = duo
            blank = jnp.zeros((slots, HD), jnp.bfloat16)
            diagonal = jnp.concatenate(
                [
                    jnp.concatenate([own(q_buf, n, lanes(h)), blank], axis=1),
                    jnp.concatenate([blank, own(q_buf, other_n, lanes(other_h))], axis=1),
                ],
                axis=0,
            )
            return lax.dot_general(
                diagonal,
                side_by_side(pk_buf, fk_buf, duo),
                (((1,), (1,)), ((), ())),
                preferred_element_type=jnp.float32,
            )

        def weigh(duo, scores):
            column = lax.broadcasted_iota(jnp.int32, (slots, slots), 1)
            usable = jnp.concatenate([column < live[ids[n]] for n, _ in duo], axis=0)
            scores = jnp.concatenate(
                [scores[:, :cached], jnp.where(usable, scores[:, cached:], MASKED)], axis=1
            )
            peak = jnp.max(scores, axis=1, keepdims=True)
            weights = jnp.exp2((scores - peak) * exponent_scale)
            return weights.astype(jnp.bfloat16), jnp.sum(weights, axis=1, keepdims=True)

        def blend(duo, weights, row_total):
            blended = jnp.dot(
                weights, side_by_side(pv_buf, fv_buf, duo), preferred_element_type=jnp.float32
            )
            row = lax.broadcasted_iota(jnp.int32, (slots, HD), 0)
            for m, (n, h) in enumerate(duo):
                rows = slice(m * slots, (m + 1) * slots)
                attended = blended[rows, lanes(m)] / row_total[rows]
                attended = jnp.where(row < live[ids[n]], attended, 0.0)
                at = (n % per_out) * slots
                outs[n // per_out][at : at + slots, lanes(h)] = attended.astype(jnp.bfloat16)

        units = []
        for first in range(0, count, 2):
            units += [((n, h), (n, h + 1)) for n in (first, first + 1) for h in range(0, heads - 1, 2)]
            if heads % 2:
                units.append(((first, heads - 1), (first + 1, heads - 1)))
        keys_ready(units[0])
        scores = score(units[0])
        weighed = None
        for u, duo in enumerate(units):
            later = None
            if u + 1 < len(units):
                keys_ready(units[u + 1])
                later = score(units[u + 1])
            if u:
                values_ready(units[u - 1])
                blend(units[u - 1], *weighed)
            weighed = weigh(duo, scores)
            scores = later
        values_ready(units[-1])
        blend(units[-1], *weighed)

    extra = () if after is None else (after,)
    out_shape = [pltpu.VMEM((per_out * slots, width), jnp.bfloat16)] * parts
    return pl.pallas_call(
        kernel,
        grid_spec=pltpu.PrefetchScalarGridSpec(
            num_scalar_prefetch=3,
            grid=(1,),
            in_specs=[HBM if load else VMEM] * 5 + [ANY] * len(extra),
            out_specs=[VMEM] * len(out_shape),
            scratch_shapes=[
                pltpu.VMEM((count if load else 1, slots, width), jnp.bfloat16),
                pltpu.VMEM((count if load else 1, slots, width), jnp.bfloat16),
                pltpu.VMEM((count if load else 1, slots, width), jnp.bfloat16),
                pltpu.VMEM(paged_keys.shape if load else (1, 16, width), jnp.bfloat16),
                pltpu.VMEM(paged_keys.shape if load else (1, 16, width), jnp.bfloat16),
                pltpu.SMEM((pool_pages,), jnp.int32),
                pltpu.SMEM((pool_pages,), jnp.int32),
                pltpu.SemaphoreType.DMA((3 * count + 2 * pool_pages,)),
            ],
        ),
        out_shape=out_shape,
        compiler_params=pltpu.CompilerParams(vmem_limit_bytes=VMEM_LIMIT),
        cost_estimate=BRIEF,
        name="attend",
    )(
        in_hbm(request_page_table),
        in_hbm(live_token_count),
        place,
        *map(
            in_hbm if load else in_vmem,
            (queries, fresh_keys, fresh_values, paged_keys, paged_values),
        ),
        *extra,
    )


def project(own, other, weight, weight_other, cuts, after):
    rows = own.shape[0]
    bounds = [sum(cuts[:n]) for n in range(len(cuts) + 1)]
    assert bounds[-1] * BLOCK == weight.shape[1]

    def kernel(a, b, w, u, after, *outs):
        features = jnp.concatenate([a[...], b[...]], axis=1)
        for part, out in enumerate(outs):
            for n in range(cuts[part]):
                here = slice((bounds[part] + n) * BLOCK, (bounds[part] + n + 1) * BLOCK)
                out[:, n * BLOCK : (n + 1) * BLOCK] = jnp.dot(
                    features,
                    jnp.concatenate([w[:, here], u[:, here]], axis=0),
                    preferred_element_type=jnp.float32,
                ).astype(jnp.bfloat16)

    return pl.pallas_call(
        kernel,
        in_specs=[VMEM] * 4 + [ANY],
        out_specs=[VMEM] * len(cuts),
        out_shape=[pltpu.VMEM((rows, cut * BLOCK), jnp.bfloat16) for cut in cuts],
        compiler_params=pltpu.CompilerParams(vmem_limit_bytes=VMEM_LIMIT),
        cost_estimate=BRIEF,
        name="project",
    )(in_vmem(own), in_vmem(other), in_vmem(weight), in_vmem(weight_other), after)


def pack_pair(ups, downs, place, after):
    rank, columns = ups[0].shape[1:]
    width = downs[0].shape[2]
    half = columns // 2

    def kernel(place, up_0, up_1, down_0, down_1, after, out):
        here = pl.ds(pl.multiple_of((place[0] & 1) * half, half), half)
        for n, (up, down) in enumerate(((up_0, down_0), (up_1, down_1))):
            out[n, :, :half] = up[0, :, here]
            out[n, :, half:] = down[0]

    return pl.pallas_call(
        kernel,
        in_specs=[SMEM] + [VMEM] * 4 + [ANY],
        out_specs=VMEM,
        out_shape=jax.ShapeDtypeStruct((2, rank, half + width), ups[0].dtype),
        compiler_params=pltpu.CompilerParams(vmem_limit_bytes=VMEM_LIMIT),
        cost_estimate=BRIEF,
        name="pack_pair",
    )(place, *ups, *downs, after)


def pick_factors(pairs, place, lookup, per_owner, width, after):
    rank = pairs[0].shape[1]
    half = pairs[0].shape[2] - width
    count = len(pairs)

    def kernel(place, slot, in_use, pool_row, *refs):
        pieces, outs = refs[:count], refs[-2:]
        for n, out in enumerate(outs):
            for m in range(2):
                for i in range(2):
                    request = (place[0] ^ n ^ (0 if m else 2)) * per_owner + i
                    row = pool_row[in_use[slot[request]]]
                    apart = lax.rem(place[1] // 2 - row // 2 + count, count)
                    side = (row ^ place[1]) & 1
                    for d, piece in enumerate(pieces):

                        @pl.when(apart == d)
                        def _(piece=piece, out=out, k=2 * m + i, m=m, i=i, side=side):
                            out[:, k * width : (k + 1) * width] = piece[side, :, half:]
                            if m:
                                there = 4 * width + i * half
                                out[:, there : there + half] = piece[side, :, :half]

    shape = jax.ShapeDtypeStruct((rank, 4 * width + 2 * half), pairs[0].dtype)
    return pl.pallas_call(
        kernel,
        in_specs=[SMEM] * 4 + [VMEM] * count + [ANY],
        out_specs=[VMEM] * 2,
        out_shape=[shape] * 2,
        compiler_params=pltpu.CompilerParams(vmem_limit_bytes=VMEM_LIMIT),
        cost_estimate=BRIEF,
        name="pick_factors",
    )(place, *lookup, *pairs, after)


def ranks_and_part(here, other, factors, part):
    slots, width = here[0].shape
    rows = part.shape[0]
    rank = factors[0].shape[0]
    assert part.shape[1] == 4 * slots

    def kernel(*refs):
        factors, blocks, (part_in, part_out) = refs[:2], refs[2:6], refs[6:]
        part_out[:rows] = part_in[...]
        for i in range(2):
            acts = sum(
                lax.dot_general(
                    factors[m][:, i * width : (i + 1) * width],
                    blocks[2 * m + i][...],
                    (((1,), (1,)), ((), ())),
                    preferred_element_type=jnp.float32,
                )
                for m in range(2)
            )
            high = acts.astype(jnp.bfloat16)
            low = (acts - high.astype(jnp.float32)).astype(jnp.bfloat16)
            part_out[rows:, 2 * i * slots : (2 * i + 1) * slots] = high
            part_out[rows:, (2 * i + 1) * slots : (2 * i + 2) * slots] = low

    return pl.pallas_call(
        kernel,
        in_specs=[VMEM] * 7,
        out_specs=VMEM,
        out_shape=jax.ShapeDtypeStruct((rows + rank, part.shape[1]), jnp.bfloat16),
        compiler_params=pltpu.CompilerParams(vmem_limit_bytes=VMEM_LIMIT),
        cost_estimate=BRIEF,
        name="ranks_and_part",
    )(*factors, *here, *other, part)


def project_own(
    own, other, weight, weight_other, first, second, last, factors, gating, place
):
    rows, width = own.shape
    columns = weight.shape[1]
    blocks = columns // BLOCK
    slots = rows // 2
    rank = factors[0].shape[0]
    half = columns // 2
    open_from = second.shape[1] // BLOCK
    open_to = (columns - last.shape[1]) // BLOCK

    def kernel(
        place, a, b, w, u, first, second, last, mine, theirs, gate, out, rest_out, gates, out_buf, ups, sems
    ):
        def store(i, n):
            there = (pl.ds(i * slots, slots), pl.ds(n * BLOCK, BLOCK))
            return pltpu.make_async_copy(out_buf.at[there], out.at[there], sems.at[i, n])

        core = place[0] & 1
        gates[...] = jnp.zeros_like(gates)
        pieces = []
        for i in range(2):
            here = slice(i * slots, (i + 1) * slots)
            down = slice((2 + i) * width, (3 + i) * width)
            acts = sum(
                lax.dot_general(
                    factors[:, down],
                    block[here],
                    (((1,), (1,)), ((), ())),
                    preferred_element_type=jnp.float32,
                )
                for factors, block in ((mine, a), (theirs, b))
            )
            for m in range(2 * i, 2 * i + 2):
                acts += last[slots:, m * slots : (m + 1) * slots].astype(jnp.float32)
            high = acts.astype(jnp.bfloat16).astype(jnp.float32)
            pieces.append(jnp.concatenate([high, acts - high], axis=0).T.astype(jnp.bfloat16))
            up = 4 * width + i * half
            for m in range(2):
                for away, factors in enumerate((mine, theirs)):
                    there = pl.ds(pl.multiple_of((core ^ away) * half, half), half)
                    ups[i, m * rank : (m + 1) * rank, there] = factors[:, up : up + half]
            gates[i : i + 1] = gate[pl.ds(place[0] * 2 + i, 1), :]
        features = jnp.concatenate([a[...], b[...]], axis=1)
        for n in range(blocks):
            here = slice(n * BLOCK, (n + 1) * BLOCK)
            sums = jnp.dot(
                features,
                jnp.concatenate([w[:, here], u[:, here]], axis=0),
                preferred_element_type=jnp.float32,
            )
            for i in range(2):
                those = slice(i * slots, (i + 1) * slots)
                update = sums[those] + jnp.dot(
                    pieces[i], ups[i, :, here], preferred_element_type=jnp.float32
                )
                if not i:
                    update += first[:, here].astype(jnp.float32)
                elif n < open_from:
                    update += second[:, here].astype(jnp.float32)
                elif n >= open_to:
                    there = slice((n - open_to) * BLOCK, (n - open_to + 1) * BLOCK)
                    update += last[:slots, there].astype(jnp.float32)
                gated = update * gates[i : i + 1, here]
                if i and open_from <= n < open_to:
                    there = slice((n - open_from) * BLOCK, (n - open_from + 1) * BLOCK)
                    rest_out[:, there] = gated
                else:
                    out_buf[those, here] = gated.astype(jnp.bfloat16)
                    store(i, n).start()
        for i in range(2):
            for n in range(blocks):
                if not (i and open_from <= n < open_to):
                    store(i, n).wait()

    return pl.pallas_call(
        kernel,
        in_specs=[SMEM] + [VMEM] * 10,
        out_specs=[HBM, VMEM, VMEM],
        out_shape=[
            pltpu.HBM((rows, columns), jnp.bfloat16),
            jax.ShapeDtypeStruct((slots, (open_to - open_from) * BLOCK), jnp.float32),
            jax.ShapeDtypeStruct((8, columns), jnp.float32),
        ],
        scratch_shapes=[
            pltpu.VMEM((rows, columns), jnp.bfloat16),
            pltpu.VMEM((2, 2 * rank, columns), jnp.bfloat16),
            pltpu.SemaphoreType.DMA((2, blocks)),
        ],
        compiler_params=pltpu.CompilerParams(vmem_limit_bytes=VMEM_LIMIT),
        cost_estimate=BRIEF,
        name="project_own",
    )(
        place,
        own,
        other,
        in_vmem(weight),
        in_vmem(weight_other),
        first,
        second,
        last,
        *factors,
        gating,
    )


def finish(so_far, rest, received, gates, begin):
    rows, columns = so_far.shape
    slots, wide = rest.shape
    widths = [part.shape[1] for part in received]
    assert sum(widths) == wide

    def kernel(sums, gates, so_far, *refs):
        parts, (out, buf, sems) = refs[:-3], refs[-3:]
        stores = []
        for n, part in enumerate(parts):
            at = sum(widths[:n])
            here = slice(at, at + widths[n])
            there = slice(begin + at, begin + at + widths[n])
            update = sums[:, here] + part[...].astype(jnp.float32) * gates[1:2, there]
            buf[:, here] = update.astype(jnp.bfloat16)
            stores.append(
                pltpu.make_async_copy(
                    buf.at[:, pl.ds(at, widths[n])],
                    out.at[pl.ds(slots, slots), pl.ds(begin + at, widths[n])],
                    sems.at[n],
                )
            )
            stores[-1].start()
        for store in stores:
            store.wait()

    return pl.pallas_call(
        kernel,
        in_specs=[VMEM] * 2 + [HBM] + [VMEM] * len(received),
        out_specs=HBM,
        out_shape=jax.ShapeDtypeStruct((rows, columns), jnp.bfloat16),
        scratch_shapes=[
            pltpu.VMEM((slots, wide), jnp.bfloat16),
            pltpu.SemaphoreType.DMA((len(received),)),
        ],
        input_output_aliases={2: 0},
        compiler_params=pltpu.CompilerParams(vmem_limit_bytes=VMEM_LIMIT),
        cost_estimate=BRIEF,
        name="finish",
    )(rest, gates, so_far, *received)


def body(
    queries,
    fresh_keys,
    fresh_values,
    paged_keys,
    paged_values,
    request_page_table,
    live_token_count,
    request_adapter_slot,
    adapters_in_use,
    adapter_pool_row,
    adapter_down_factors,
    adapter_up_factors,
    output_weight,
    gating,
):
    tp = lax.axis_size("tp")
    holders = lax.axis_size("req")
    place = jnp.stack([lax.axis_index("tp"), lax.axis_index("req")]).astype(jnp.int32)
    per_owner = live_token_count.shape[0] // tp

    def swap(array, flip):
        return lax.ppermute(array, "tp", [(s, s ^ flip) for s in range(tp)])

    def attend(tokens, wanted, load=False, after=None):
        return attend_some(
            *tokens,
            request_page_table,
            live_token_count,
            place,
            per_owner,
            wanted,
            load,
            after,
        )

    ups, downs = (
        (factors, lax.ppermute(factors, "req", [(s, s ^ 1) for s in range(holders)]))
        for factors in (adapter_up_factors, adapter_down_factors)
    )
    weight_other = swap(output_weight, 1)

    tokens = (queries, fresh_keys, fresh_values, paged_keys, paged_values)
    away_a, here_a = attend(tokens, ((3, 0), (2, 0)), True)
    *tokens, _ = lax.optimization_barrier((*tokens, away_a))
    away_a, ups, downs = lax.optimization_barrier((away_a, ups, downs))
    other_a = swap(away_a, 1)
    pair = pack_pair(ups, downs, place, away_a)
    (sent_a,) = project(here_a, other_a, output_weight, weight_other, (sum(CUTS),), pair)
    first = swap(sent_a, 2)

    pair, _ = lax.optimization_barrier((pair, sent_a))
    pairs = [pair] + [
        lax.ppermute(pair, "req", [(s, (s + d) % holders) for s in range(holders)])
        for d in range(2, holders, 2)
    ]
    away_b, here_b = attend(tokens, ((3, 1), (2, 1)), after=sent_a)
    (own_away,) = attend(tokens, ((1, 0), (1, 1)), after=away_b)
    away_b, own_away, *pairs = lax.optimization_barrier((away_b, own_away, *pairs))
    other_b = swap(away_b, 1)
    own_other = swap(own_away, 1)
    sent_b = project(here_b, other_b, output_weight, weight_other, CUTS, own_away)
    second = swap(sent_b[0], 2)

    first, *pairs = lax.optimization_barrier((first, *pairs))
    lookup = (request_adapter_slot, adapters_in_use, adapter_pool_row)
    width = output_weight.shape[0]
    factors, factors_away = pick_factors(pairs, place, lookup, per_owner, width, sent_b[0])
    factors = (factors, swap(factors_away, 1))
    last = ranks_and_part((here_a, here_b), (other_a, other_b), factors, sent_b[-1])
    *others, first, _ = lax.optimization_barrier((*sent_b[1:-1], first, last))
    others = [swap(part, 2) for part in others]
    (own_here,) = attend(tokens, ((0, 0), (0, 1)), after=last)
    last = swap(last, 2)
    out, rest, gates = project_own(
        own_here,
        own_other,
        output_weight,
        weight_other,
        first,
        second,
        last,
        factors,
        gating,
        place,
    )
    return finish(out, rest, others, gates, CUTS[0] * BLOCK)


def solution(mesh):
    return jax.shard_map(
        body,
        mesh=mesh,
        in_specs=(
            P("req", "tp"),
            P("req", "tp"),
            P("req", "tp"),
            P("req", None, "tp"),
            P("req", None, "tp"),
            P("req", None),
            P("req"),
            P("req"),
            P(),
            P(),
            P("req", None, "tp"),
            P("req", None, None),
            P("tp", None),
            P("req", None),
        ),
        out_specs=P(("req", "tp"), None),
        check_vma=False,
    )
```

```python
import math

import jax
import jax.numpy as jnp
from jax import lax
from jax.experimental import pallas as pl
from jax.experimental.pallas import tpu as pltpu
from jax.sharding import PartitionSpec as P

HD = 128
VMEM_LIMIT = 32 * 1024 * 1024
SMEM = pl.BlockSpec(memory_space=pltpu.SMEM)
BLOCK = 256
CUTS = (5, 2, 1, 2)
MASKED = -1e30
ANY = pl.BlockSpec(memory_space=pl.ANY)
BRIEF = pl.CostEstimate(flops=1000, bytes_accessed=1000, transcendentals=0)
HBM = pl.BlockSpec(memory_space=pltpu.HBM)
VMEM = pl.BlockSpec(memory_space=pltpu.VMEM)


def in_hbm(array):
    return pltpu.with_memory_space_constraint(array, pltpu.HBM)


def in_vmem(array):
    return pltpu.with_memory_space_constraint(array, pltpu.VMEM)


def attend_some(
    queries,
    fresh_keys,
    fresh_values,
    paged_keys,
    paged_values,
    request_page_table,
    live_token_count,
    place,
    per_owner,
    wanted,
    load,
    after=None,
):
    requests_here, pages = request_page_table.shape
    slots = queries.shape[0] // requests_here
    width = queries.shape[1]
    heads = width // HD
    pool_pages, page_rows = paged_keys.shape[:2]
    cached = pages * page_rows
    count = len(wanted)
    parts = len({away for away, _ in wanted})
    per_out = count // parts
    exponent_scale = math.log2(math.e) / math.sqrt(HD)

    def kernel(table, live, place, q_hbm, fk_hbm, fv_hbm, pk_hbm, pv_hbm, *rest):
        ids = [(place[0] ^ away) * per_owner + n for away, n in wanted]
        outs = rest[-8 - parts : -8]
        q_buf, fk_buf, fv_buf, pk_buf, pv_buf, order, seen, in_sems = rest[-8:]
        if not load:
            q_buf, fk_buf, fv_buf, pk_buf, pv_buf = q_hbm, fk_hbm, fv_hbm, pk_hbm, pv_hbm

        def fetch(src, dst, sem):
            return pltpu.make_async_copy(src, dst, in_sems.at[sem])

        def rows_of(n):
            return pl.ds(pl.multiple_of(ids[n] * slots, slots), slots)

        def query_copy(n):
            return fetch(q_hbm.at[rows_of(n)], q_buf.at[n], 3 * n)

        def key_copy(n):
            return fetch(fk_hbm.at[rows_of(n)], fk_buf.at[n], 3 * n + 1)

        def value_copy(n):
            return fetch(fv_hbm.at[rows_of(n)], fv_buf.at[n], 3 * n + 2)

        def key_page(m):
            page = order[m]
            return fetch(pk_hbm.at[page], pk_buf.at[page], 3 * count + 2 * m)

        def value_page(m):
            page = order[m]
            return fetch(pv_hbm.at[page], pv_buf.at[page], 3 * count + 2 * m + 1)

        def start(copies):
            for copy in copies:
                copy.start()

        def start_pages(begin, end):
            for m in range(pages, pool_pages):

                @pl.when((m >= begin) & (m < end))
                def _(m=m):
                    key_page(m).start()

            for m in range(pages, pool_pages):

                @pl.when((m >= begin) & (m < end))
                def _(m=m):
                    value_page(m).start()

        if load:
            for j in range(pages):
                order[j] = table[ids[0], j]
            start([query_copy(0), key_copy(0)] + [key_page(m) for m in range(pages)])
            start([value_copy(0)] + [value_page(m) for m in range(pages)])
            for page in range(pool_pages):
                taken = order[0] == page
                for j in range(1, pages):
                    taken = taken | (order[j] == page)
                seen[page] = taken.astype(jnp.int32)
            bounds = [jnp.int32(pages)]
            for n in range(1, count):
                free = bounds[-1]
                for j in range(pages):
                    page = table[ids[n], j]
                    fresh = seen[page] == 0

                    @pl.when(fresh)
                    def _(page=page, free=free):
                        order[free] = page
                        seen[page] = 1

                    free = free + fresh.astype(jnp.int32)
                bounds.append(free)
                start([query_copy(n), key_copy(n), value_copy(n)])
                start_pages(bounds[n - 1], bounds[n])
        waited = set()

        def wait(name, make, indices):
            if name not in waited:
                waited.add(name)
                for index in indices:
                    make(index).wait()

        def wait_pages(name, make, begin, end):
            if name not in waited:
                waited.add(name)
                for m in range(pages, pool_pages):

                    @pl.when((m >= begin) & (m < end))
                    def _(m=m):
                        make(m).wait()

        def keys_ready(duo):
            for n in range(1 + max(n for n, _ in duo)) if load else ():
                wait(("q", n), query_copy, [n])
                wait(("k", n), key_copy, [n])
                if n:
                    wait_pages(("k pages", n), key_page, bounds[n - 1], bounds[n])
                else:
                    wait(("k pages", 0), key_page, range(pages))

        def values_ready(duo):
            for n in range(1 + max(n for n, _ in duo)) if load else ():
                wait(("v", n), value_copy, [n])
                if n:
                    wait_pages(("v pages", n), value_page, bounds[n - 1], bounds[n])
                else:
                    wait(("v pages", 0), value_page, range(pages))

        def lanes(h, several=1):
            return slice(h * HD, (h + several) * HD)

        def own(buf, n, here):
            return buf[n, :, here] if load else buf[rows_of(n), here]

        def gather(pool, fresh, n, here):
            return jnp.concatenate(
                [pool[table[ids[n], j], :, here] for j in range(pages)] + [own(fresh, n, here)],
                axis=0,
            )

        def side_by_side(pool, fresh, duo):
            (n, h), (other_n, other_h) = duo
            if n == other_n and other_h == h + 1:
                return gather(pool, fresh, n, lanes(h, 2))
            return jnp.concatenate(
                [gather(pool, fresh, m, lanes(g)) for m, g in duo],
                axis=1,
            )

        def score(duo):
            (n, h), (other_n, other_h) = duo
            blank = jnp.zeros((slots, HD), jnp.bfloat16)
            diagonal = jnp.concatenate(
                [
                    jnp.concatenate([own(q_buf, n, lanes(h)), blank], axis=1),
                    jnp.concatenate([blank, own(q_buf, other_n, lanes(other_h))], axis=1),
                ],
                axis=0,
            )
            return lax.dot_general(
                diagonal,
                side_by_side(pk_buf, fk_buf, duo),
                (((1,), (1,)), ((), ())),
                preferred_element_type=jnp.float32,
            )

        def weigh(duo, scores):
            column = lax.broadcasted_iota(jnp.int32, (slots, slots), 1)
            usable = jnp.concatenate([column < live[ids[n]] for n, _ in duo], axis=0)
            scores = jnp.concatenate(
                [scores[:, :cached], jnp.where(usable, scores[:, cached:], MASKED)], axis=1
            )
            peak = jnp.max(scores, axis=1, keepdims=True)
            weights = jnp.exp2((scores - peak) * exponent_scale)
            return weights.astype(jnp.bfloat16), jnp.sum(weights, axis=1, keepdims=True)

        def blend(duo, weights, row_total):
            blended = jnp.dot(
                weights, side_by_side(pv_buf, fv_buf, duo), preferred_element_type=jnp.float32
            )
            row = lax.broadcasted_iota(jnp.int32, (slots, HD), 0)
            for m, (n, h) in enumerate(duo):
                rows = slice(m * slots, (m + 1) * slots)
                attended = blended[rows, lanes(m)] / row_total[rows]
                attended = jnp.where(row < live[ids[n]], attended, 0.0)
                at = (n % per_out) * slots
                outs[n // per_out][at : at + slots, lanes(h)] = attended.astype(jnp.bfloat16)

        units = []
        for first in range(0, count, 2):
            units += [((n, h), (n, h + 1)) for n in (first, first + 1) for h in range(0, heads - 1, 2)]
            if heads % 2:
                units.append(((first, heads - 1), (first + 1, heads - 1)))
        keys_ready(units[0])
        scores = score(units[0])
        weighed = None
        for u, duo in enumerate(units):
            later = None
            if u + 1 < len(units):
                keys_ready(units[u + 1])
                later = score(units[u + 1])
            if u:
                values_ready(units[u - 1])
                blend(units[u - 1], *weighed)
            weighed = weigh(duo, scores)
            scores = later
        values_ready(units[-1])
        blend(units[-1], *weighed)

    extra = () if after is None else (after,)
    out_shape = [pltpu.VMEM((per_out * slots, width), jnp.bfloat16)] * parts
    return pl.pallas_call(
        kernel,
        grid_spec=pltpu.PrefetchScalarGridSpec(
            num_scalar_prefetch=3,
            grid=(1,),
            in_specs=[HBM if load else VMEM] * 5 + [ANY] * len(extra),
            out_specs=[VMEM] * len(out_shape),
            scratch_shapes=[
                pltpu.VMEM((count if load else 1, slots, width), jnp.bfloat16),
                pltpu.VMEM((count if load else 1, slots, width), jnp.bfloat16),
                pltpu.VMEM((count if load else 1, slots, width), jnp.bfloat16),
                pltpu.VMEM(paged_keys.shape if load else (1, 16, width), jnp.bfloat16),
                pltpu.VMEM(paged_keys.shape if load else (1, 16, width), jnp.bfloat16),
                pltpu.SMEM((pool_pages,), jnp.int32),
                pltpu.SMEM((pool_pages,), jnp.int32),
                pltpu.SemaphoreType.DMA((3 * count + 2 * pool_pages,)),
            ],
        ),
        out_shape=out_shape,
        compiler_params=pltpu.CompilerParams(vmem_limit_bytes=VMEM_LIMIT),
        cost_estimate=BRIEF,
        name="attend",
    )(
        in_hbm(request_page_table),
        in_hbm(live_token_count),
        place,
        *map(
            in_hbm if load else in_vmem,
            (queries, fresh_keys, fresh_values, paged_keys, paged_values),
        ),
        *extra,
    )


def project(own, other, weight, weight_other, cuts, after):
    rows = own.shape[0]
    bounds = [sum(cuts[:n]) for n in range(len(cuts) + 1)]
    assert bounds[-1] * BLOCK == weight.shape[1]

    def kernel(a, b, w, u, after, *outs):
        features = jnp.concatenate([a[...], b[...]], axis=1)
        for part, out in enumerate(outs):
            for n in range(cuts[part]):
                here = slice((bounds[part] + n) * BLOCK, (bounds[part] + n + 1) * BLOCK)
                out[:, n * BLOCK : (n + 1) * BLOCK] = jnp.dot(
                    features,
                    jnp.concatenate([w[:, here], u[:, here]], axis=0),
                    preferred_element_type=jnp.float32,
                ).astype(jnp.bfloat16)

    return pl.pallas_call(
        kernel,
        in_specs=[VMEM] * 4 + [ANY],
        out_specs=[VMEM] * len(cuts),
        out_shape=[pltpu.VMEM((rows, cut * BLOCK), jnp.bfloat16) for cut in cuts],
        compiler_params=pltpu.CompilerParams(vmem_limit_bytes=VMEM_LIMIT),
        cost_estimate=BRIEF,
        name="project",
    )(in_vmem(own), in_vmem(other), in_vmem(weight), in_vmem(weight_other), after)


def pack_pair(ups, downs, place, after):
    rank, columns = ups[0].shape[1:]
    width = downs[0].shape[2]
    half = columns // 2

    def kernel(place, up_0, up_1, down_0, down_1, after, out):
        here = pl.ds(pl.multiple_of((place[0] & 1) * half, half), half)
        for n, (up, down) in enumerate(((up_0, down_0), (up_1, down_1))):
            out[n, :, :half] = up[0, :, here]
            out[n, :, half:] = down[0]

    return pl.pallas_call(
        kernel,
        in_specs=[SMEM] + [VMEM] * 4 + [ANY],
        out_specs=VMEM,
        out_shape=jax.ShapeDtypeStruct((2, rank, half + width), ups[0].dtype),
        compiler_params=pltpu.CompilerParams(vmem_limit_bytes=VMEM_LIMIT),
        cost_estimate=BRIEF,
        name="pack_pair",
    )(place, *ups, *downs, after)


def pick_factors(pairs, place, lookup, per_owner, width, after):
    rank = pairs[0].shape[1]
    half = pairs[0].shape[2] - width
    count = len(pairs)

    def kernel(place, slot, in_use, pool_row, *refs):
        pieces, outs = refs[:count], refs[-2:]
        for n, out in enumerate(outs):
            for m in range(2):
                for i in range(2):
                    request = (place[0] ^ n ^ (0 if m else 2)) * per_owner + i
                    row = pool_row[in_use[slot[request]]]
                    apart = lax.rem(place[1] // 2 - row // 2 + count, count)
                    side = (row ^ place[1]) & 1
                    for d, piece in enumerate(pieces):

                        @pl.when(apart == d)
                        def _(piece=piece, out=out, k=2 * m + i, m=m, i=i, side=side):
                            out[:, k * width : (k + 1) * width] = piece[side, :, half:]
                            if m:
                                there = 4 * width + i * half
                                out[:, there : there + half] = piece[side, :, :half]

    shape = jax.ShapeDtypeStruct((rank, 4 * width + 2 * half), pairs[0].dtype)
    return pl.pallas_call(
        kernel,
        in_specs=[SMEM] * 4 + [VMEM] * count + [ANY],
        out_specs=[VMEM] * 2,
        out_shape=[shape] * 2,
        compiler_params=pltpu.CompilerParams(vmem_limit_bytes=VMEM_LIMIT),
        cost_estimate=BRIEF,
        name="pick_factors",
    )(place, *lookup, *pairs, after)


def ranks_and_part(here, other, factors, part):
    slots, width = here[0].shape
    rows = part.shape[0]
    rank = factors[0].shape[0]
    assert part.shape[1] == 4 * slots

    def kernel(*refs):
        factors, blocks, (part_in, part_out) = refs[:2], refs[2:6], refs[6:]
        part_out[:rows] = part_in[...]
        for i in range(2):
            acts = sum(
                lax.dot_general(
                    factors[m][:, i * width : (i + 1) * width],
                    blocks[2 * m + i][...],
                    (((1,), (1,)), ((), ())),
                    preferred_element_type=jnp.float32,
                )
                for m in range(2)
            )
            high = acts.astype(jnp.bfloat16)
            low = (acts - high.astype(jnp.float32)).astype(jnp.bfloat16)
            part_out[rows:, 2 * i * slots : (2 * i + 1) * slots] = high
            part_out[rows:, (2 * i + 1) * slots : (2 * i + 2) * slots] = low

    return pl.pallas_call(
        kernel,
        in_specs=[VMEM] * 7,
        out_specs=VMEM,
        out_shape=jax.ShapeDtypeStruct((rows + rank, part.shape[1]), jnp.bfloat16),
        compiler_params=pltpu.CompilerParams(vmem_limit_bytes=VMEM_LIMIT),
        cost_estimate=BRIEF,
        name="ranks_and_part",
    )(*factors, *here, *other, part)


def prepare_own(own, other, weight, weight_other, factors, gating, place):
    rows, width = own.shape
    columns = weight.shape[1]
    slots = rows // 2
    rank = factors[0].shape[0]
    half = columns // 2

    def kernel(place, a, b, w, u, mine, theirs, gate, sums, ranks, ups, gates):
        core = place[0] & 1
        gates[...] = jnp.zeros_like(gates)
        for i in range(2):
            here = slice(i * slots, (i + 1) * slots)
            down = slice((2 + i) * width, (3 + i) * width)
            ranks[i] = sum(
                lax.dot_general(
                    factors[:, down],
                    block[here],
                    (((1,), (1,)), ((), ())),
                    preferred_element_type=jnp.float32,
                )
                for factors, block in ((mine, a), (theirs, b))
            )
            up = 4 * width + i * half
            for m in range(2):
                for away, factors in enumerate((mine, theirs)):
                    there = pl.ds(pl.multiple_of((core ^ away) * half, half), half)
                    ups[i, m * rank : (m + 1) * rank, there] = factors[:, up : up + half]
            gates[i : i + 1] = gate[pl.ds(place[0] * 2 + i, 1), :]
        features = jnp.concatenate([a[...], b[...]], axis=1)
        for n in range(columns // BLOCK):
            here = slice(n * BLOCK, (n + 1) * BLOCK)
            sums[:, here] = jnp.dot(
                features,
                jnp.concatenate([w[:, here], u[:, here]], axis=0),
                preferred_element_type=jnp.float32,
            )

    return pl.pallas_call(
        kernel,
        in_specs=[SMEM] + [VMEM] * 7,
        out_specs=[VMEM] * 4,
        out_shape=[
            pltpu.VMEM((rows, columns), jnp.float32),
            pltpu.VMEM((2, rank, slots), jnp.float32),
            pltpu.VMEM((2, 2 * rank, columns), jnp.bfloat16),
            pltpu.VMEM((8, columns), jnp.float32),
        ],
        compiler_params=pltpu.CompilerParams(vmem_limit_bytes=VMEM_LIMIT),
        cost_estimate=BRIEF,
        name="prepare_own",
    )(place, own, other, in_vmem(weight), in_vmem(weight_other), *factors, gating)


def combine(prepared, first, second, last):
    rows, columns = prepared[0].shape
    blocks = columns // BLOCK
    slots = rows // 2
    open_from = second.shape[1] // BLOCK
    open_to = (columns - last.shape[1]) // BLOCK

    def kernel(sums, ranks, ups, gates, first, second, last, out, rest_out, out_buf, sems):
        def store(i, n):
            there = (pl.ds(i * slots, slots), pl.ds(n * BLOCK, BLOCK))
            return pltpu.make_async_copy(out_buf.at[there], out.at[there], sems.at[i, n])

        for i in range(2):
            those = slice(i * slots, (i + 1) * slots)
            acts = ranks[i]
            for m in range(2 * i, 2 * i + 2):
                acts += last[slots:, m * slots : (m + 1) * slots].astype(jnp.float32)
            high = acts.astype(jnp.bfloat16).astype(jnp.float32)
            pair = jnp.concatenate([high, acts - high], axis=0).T.astype(jnp.bfloat16)
            for n in range(blocks):
                here = slice(n * BLOCK, (n + 1) * BLOCK)
                update = sums[those, here] + jnp.dot(
                    pair, ups[i, :, here], preferred_element_type=jnp.float32
                )
                if not i:
                    update += first[:, here].astype(jnp.float32)
                elif n < open_from:
                    update += second[:, here].astype(jnp.float32)
                elif n >= open_to:
                    there = slice((n - open_to) * BLOCK, (n - open_to + 1) * BLOCK)
                    update += last[:slots, there].astype(jnp.float32)
                gated = update * gates[i : i + 1, here]
                if i and open_from <= n < open_to:
                    there = slice((n - open_from) * BLOCK, (n - open_from + 1) * BLOCK)
                    rest_out[:, there] = gated
                else:
                    out_buf[those, here] = gated.astype(jnp.bfloat16)
                    store(i, n).start()
        for i in range(2):
            for n in range(blocks):
                if not (i and open_from <= n < open_to):
                    store(i, n).wait()

    return pl.pallas_call(
        kernel,
        in_specs=[VMEM] * 7,
        out_specs=[HBM, VMEM],
        out_shape=[
            pltpu.HBM((rows, columns), jnp.bfloat16),
            pltpu.VMEM((slots, (open_to - open_from) * BLOCK), jnp.float32),
        ],
        scratch_shapes=[
            pltpu.VMEM((rows, columns), jnp.bfloat16),
            pltpu.SemaphoreType.DMA((2, blocks)),
        ],
        compiler_params=pltpu.CompilerParams(vmem_limit_bytes=VMEM_LIMIT),
        cost_estimate=BRIEF,
        name="combine",
    )(*prepared, first, second, last)


def finish(so_far, rest, received, gates, begin):
    rows, columns = so_far.shape
    slots, wide = rest.shape
    widths = [part.shape[1] for part in received]
    assert sum(widths) == wide

    def kernel(sums, gates, so_far, *refs):
        parts, (out, buf, sems) = refs[:-3], refs[-3:]
        stores = []
        for n, part in enumerate(parts):
            at = sum(widths[:n])
            here = slice(at, at + widths[n])
            there = slice(begin + at, begin + at + widths[n])
            update = sums[:, here] + part[...].astype(jnp.float32) * gates[1:2, there]
            buf[:, here] = update.astype(jnp.bfloat16)
            stores.append(
                pltpu.make_async_copy(
                    buf.at[:, pl.ds(at, widths[n])],
                    out.at[pl.ds(slots, slots), pl.ds(begin + at, widths[n])],
                    sems.at[n],
                )
            )
            stores[-1].start()
        for store in stores:
            store.wait()

    return pl.pallas_call(
        kernel,
        in_specs=[VMEM] * 2 + [HBM] + [VMEM] * len(received),
        out_specs=HBM,
        out_shape=jax.ShapeDtypeStruct((rows, columns), jnp.bfloat16),
        scratch_shapes=[
            pltpu.VMEM((slots, wide), jnp.bfloat16),
            pltpu.SemaphoreType.DMA((len(received),)),
        ],
        input_output_aliases={2: 0},
        compiler_params=pltpu.CompilerParams(vmem_limit_bytes=VMEM_LIMIT),
        cost_estimate=BRIEF,
        name="finish",
    )(rest, gates, so_far, *received)


def body(
    queries,
    fresh_keys,
    fresh_values,
    paged_keys,
    paged_values,
    request_page_table,
    live_token_count,
    request_adapter_slot,
    adapters_in_use,
    adapter_pool_row,
    adapter_down_factors,
    adapter_up_factors,
    output_weight,
    gating,
):
    tp = lax.axis_size("tp")
    holders = lax.axis_size("req")
    place = jnp.stack([lax.axis_index("tp"), lax.axis_index("req")]).astype(jnp.int32)
    per_owner = live_token_count.shape[0] // tp

    def swap(array, flip):
        return lax.ppermute(array, "tp", [(s, s ^ flip) for s in range(tp)])

    def attend(tokens, wanted, load=False, after=None):
        return attend_some(
            *tokens,
            request_page_table,
            live_token_count,
            place,
            per_owner,
            wanted,
            load,
            after,
        )

    ups, downs = (
        (factors, lax.ppermute(factors, "req", [(s, s ^ 1) for s in range(holders)]))
        for factors in (adapter_up_factors, adapter_down_factors)
    )
    weight_other = swap(output_weight, 1)

    tokens = (queries, fresh_keys, fresh_values, paged_keys, paged_values)
    away_a, here_a = attend(tokens, ((3, 0), (2, 0)), True)
    *tokens, _ = lax.optimization_barrier((*tokens, away_a))
    away_a, ups, downs = lax.optimization_barrier((away_a, ups, downs))
    other_a = swap(away_a, 1)
    pair = pack_pair(ups, downs, place, away_a)
    (sent_a,) = project(here_a, other_a, output_weight, weight_other, (sum(CUTS),), pair)
    first = swap(sent_a, 2)

    pair, _ = lax.optimization_barrier((pair, sent_a))
    pairs = [pair] + [
        lax.ppermute(pair, "req", [(s, (s + d) % holders) for s in range(holders)])
        for d in range(2, holders, 2)
    ]
    away_b, here_b = attend(tokens, ((3, 1), (2, 1)), after=sent_a)
    (own_away,) = attend(tokens, ((1, 0), (1, 1)), after=away_b)
    away_b, own_away, *pairs = lax.optimization_barrier((away_b, own_away, *pairs))
    other_b = swap(away_b, 1)
    own_other = swap(own_away, 1)
    sent_b = project(here_b, other_b, output_weight, weight_other, CUTS, own_away)
    second = swap(sent_b[0], 2)

    first, *pairs = lax.optimization_barrier((first, *pairs))
    lookup = (request_adapter_slot, adapters_in_use, adapter_pool_row)
    width = output_weight.shape[0]
    factors, factors_away = pick_factors(pairs, place, lookup, per_owner, width, sent_b[0])
    factors = (factors, swap(factors_away, 1))
    last = ranks_and_part((here_a, here_b), (other_a, other_b), factors, sent_b[-1])
    *others, first, _ = lax.optimization_barrier((*sent_b[1:-1], first, last))
    others = [swap(part, 2) for part in others]
    (own_here,) = attend(tokens, ((0, 0), (0, 1)), after=last)
    last = swap(last, 2)
    prepared = prepare_own(
        own_here, own_other, output_weight, weight_other, factors, gating, place
    )
    out, rest = combine(prepared, first, second, last)
    return finish(out, rest, others, prepared[-1], CUTS[0] * BLOCK)


def solution(mesh):
    return jax.shard_map(
        body,
        mesh=mesh,
        in_specs=(
            P("req", "tp"),
            P("req", "tp"),
            P("req", "tp"),
            P("req", None, "tp"),
            P("req", None, "tp"),
            P("req", None),
            P("req"),
            P("req"),
            P(),
            P(),
            P("req", None, "tp"),
            P("req", None, None),
            P("tp", None),
            P("req", None),
        ),
        out_specs=P(("req", "tp"), None),
        check_vma=False,
    )
```

```python
import math

import jax
import jax.numpy as jnp
from jax import lax
from jax.experimental import pallas as pl
from jax.experimental.pallas import tpu as pltpu
from jax.sharding import PartitionSpec as P

HD = 128
VMEM_LIMIT = 32 * 1024 * 1024
SMEM = pl.BlockSpec(memory_space=pltpu.SMEM)
BLOCK = 256
CUTS = (5, 2, 1, 2)
MASKED = -1e30
ANY = pl.BlockSpec(memory_space=pl.ANY)
BRIEF = pl.CostEstimate(flops=1000, bytes_accessed=1000, transcendentals=0)
HBM = pl.BlockSpec(memory_space=pltpu.HBM)
VMEM = pl.BlockSpec(memory_space=pltpu.VMEM)


def in_hbm(array):
    return pltpu.with_memory_space_constraint(array, pltpu.HBM)


def in_vmem(array):
    return pltpu.with_memory_space_constraint(array, pltpu.VMEM)


def attend_some(
    queries,
    fresh_keys,
    fresh_values,
    paged_keys,
    paged_values,
    request_page_table,
    live_token_count,
    place,
    per_owner,
    wanted,
    load,
    after=None,
):
    requests_here, pages = request_page_table.shape
    slots = queries.shape[0] // requests_here
    width = queries.shape[1]
    heads = width // HD
    pool_pages, page_rows = paged_keys.shape[:2]
    cached = pages * page_rows
    count = len(wanted)
    parts = len({away for away, _ in wanted})
    per_out = count // parts
    exponent_scale = math.log2(math.e) / math.sqrt(HD)

    def kernel(table, live, place, q_hbm, fk_hbm, fv_hbm, pk_hbm, pv_hbm, *rest):
        ids = [(place[0] ^ away) * per_owner + n for away, n in wanted]
        outs = rest[-8 - parts : -8]
        q_buf, fk_buf, fv_buf, pk_buf, pv_buf, order, seen, in_sems = rest[-8:]
        if not load:
            q_buf, fk_buf, fv_buf, pk_buf, pv_buf = q_hbm, fk_hbm, fv_hbm, pk_hbm, pv_hbm

        def fetch(src, dst, sem):
            return pltpu.make_async_copy(src, dst, in_sems.at[sem])

        def rows_of(n):
            return pl.ds(pl.multiple_of(ids[n] * slots, slots), slots)

        def query_copy(n):
            return fetch(q_hbm.at[rows_of(n)], q_buf.at[n], 3 * n)

        def key_copy(n):
            return fetch(fk_hbm.at[rows_of(n)], fk_buf.at[n], 3 * n + 1)

        def value_copy(n):
            return fetch(fv_hbm.at[rows_of(n)], fv_buf.at[n], 3 * n + 2)

        def key_page(m):
            page = order[m]
            return fetch(pk_hbm.at[page], pk_buf.at[page], 3 * count + 2 * m)

        def value_page(m):
            page = order[m]
            return fetch(pv_hbm.at[page], pv_buf.at[page], 3 * count + 2 * m + 1)

        def start(copies):
            for copy in copies:
                copy.start()

        def start_pages(begin, end):
            for m in range(pages, pool_pages):

                @pl.when((m >= begin) & (m < end))
                def _(m=m):
                    key_page(m).start()

            for m in range(pages, pool_pages):

                @pl.when((m >= begin) & (m < end))
                def _(m=m):
                    value_page(m).start()

        if load:
            for j in range(pages):
                order[j] = table[ids[0], j]
            start([query_copy(0), key_copy(0)] + [key_page(m) for m in range(pages)])
            start([value_copy(0)] + [value_page(m) for m in range(pages)])
            for page in range(pool_pages):
                taken = order[0] == page
                for j in range(1, pages):
                    taken = taken | (order[j] == page)
                seen[page] = taken.astype(jnp.int32)
            bounds = [jnp.int32(pages)]
            for n in range(1, count):
                free = bounds[-1]
                for j in range(pages):
                    page = table[ids[n], j]
                    fresh = seen[page] == 0

                    @pl.when(fresh)
                    def _(page=page, free=free):
                        order[free] = page
                        seen[page] = 1

                    free = free + fresh.astype(jnp.int32)
                bounds.append(free)
                start([query_copy(n), key_copy(n), value_copy(n)])
                start_pages(bounds[n - 1], bounds[n])
        waited = set()

        def wait(name, make, indices):
            if name not in waited:
                waited.add(name)
                for index in indices:
                    make(index).wait()

        def wait_pages(name, make, begin, end):
            if name not in waited:
                waited.add(name)
                for m in range(pages, pool_pages):

                    @pl.when((m >= begin) & (m < end))
                    def _(m=m):
                        make(m).wait()

        def keys_ready(duo):
            for n in range(1 + max(n for n, _ in duo)) if load else ():
                wait(("q", n), query_copy, [n])
                wait(("k", n), key_copy, [n])
                if n:
                    wait_pages(("k pages", n), key_page, bounds[n - 1], bounds[n])
                else:
                    wait(("k pages", 0), key_page, range(pages))

        def values_ready(duo):
            for n in range(1 + max(n for n, _ in duo)) if load else ():
                wait(("v", n), value_copy, [n])
                if n:
                    wait_pages(("v pages", n), value_page, bounds[n - 1], bounds[n])
                else:
                    wait(("v pages", 0), value_page, range(pages))

        def lanes(h, several=1):
            return slice(h * HD, (h + several) * HD)

        def own(buf, n, here):
            return buf[n, :, here] if load else buf[rows_of(n), here]

        def gather(pool, fresh, n, here):
            return jnp.concatenate(
                [pool[table[ids[n], j], :, here] for j in range(pages)] + [own(fresh, n, here)],
                axis=0,
            )

        def side_by_side(pool, fresh, duo):
            (n, h), (other_n, other_h) = duo
            if n == other_n and other_h == h + 1:
                return gather(pool, fresh, n, lanes(h, 2))
            return jnp.concatenate(
                [gather(pool, fresh, m, lanes(g)) for m, g in duo],
                axis=1,
            )

        def score(duo):
            (n, h), (other_n, other_h) = duo
            blank = jnp.zeros((slots, HD), jnp.bfloat16)
            diagonal = jnp.concatenate(
                [
                    jnp.concatenate([own(q_buf, n, lanes(h)), blank], axis=1),
                    jnp.concatenate([blank, own(q_buf, other_n, lanes(other_h))], axis=1),
                ],
                axis=0,
            )
            return lax.dot_general(
                diagonal,
                side_by_side(pk_buf, fk_buf, duo),
                (((1,), (1,)), ((), ())),
                preferred_element_type=jnp.float32,
            )

        def weigh(duo, scores):
            column = lax.broadcasted_iota(jnp.int32, (slots, slots), 1)
            usable = jnp.concatenate([column < live[ids[n]] for n, _ in duo], axis=0)
            scores = jnp.concatenate(
                [scores[:, :cached], jnp.where(usable, scores[:, cached:], MASKED)], axis=1
            )
            peak = jnp.max(scores, axis=1, keepdims=True)
            weights = jnp.exp2((scores - peak) * exponent_scale)
            return weights.astype(jnp.bfloat16), jnp.sum(weights, axis=1, keepdims=True)

        def blend(duo, weights, row_total):
            blended = jnp.dot(
                weights, side_by_side(pv_buf, fv_buf, duo), preferred_element_type=jnp.float32
            )
            row = lax.broadcasted_iota(jnp.int32, (slots, HD), 0)
            for m, (n, h) in enumerate(duo):
                rows = slice(m * slots, (m + 1) * slots)
                attended = blended[rows, lanes(m)] / row_total[rows]
                attended = jnp.where(row < live[ids[n]], attended, 0.0)
                at = (n % per_out) * slots
                outs[n // per_out][at : at + slots, lanes(h)] = attended.astype(jnp.bfloat16)

        units = []
        for first in range(0, count, 2):
            units += [((n, h), (n, h + 1)) for n in (first, first + 1) for h in range(0, heads - 1, 2)]
            if heads % 2:
                units.append(((first, heads - 1), (first + 1, heads - 1)))
        keys_ready(units[0])
        scores = score(units[0])
        weighed = None
        for u, duo in enumerate(units):
            later = None
            if u + 1 < len(units):
                keys_ready(units[u + 1])
                later = score(units[u + 1])
            if u:
                values_ready(units[u - 1])
                blend(units[u - 1], *weighed)
            weighed = weigh(duo, scores)
            scores = later
        values_ready(units[-1])
        blend(units[-1], *weighed)

    extra = () if after is None else (after,)
    out_shape = [pltpu.VMEM((per_out * slots, width), jnp.bfloat16)] * parts
    return pl.pallas_call(
        kernel,
        grid_spec=pltpu.PrefetchScalarGridSpec(
            num_scalar_prefetch=3,
            grid=(1,),
            in_specs=[HBM if load else VMEM] * 5 + [ANY] * len(extra),
            out_specs=[VMEM] * len(out_shape),
            scratch_shapes=[
                pltpu.VMEM((count if load else 1, slots, width), jnp.bfloat16),
                pltpu.VMEM((count if load else 1, slots, width), jnp.bfloat16),
                pltpu.VMEM((count if load else 1, slots, width), jnp.bfloat16),
                pltpu.VMEM(paged_keys.shape if load else (1, 16, width), jnp.bfloat16),
                pltpu.VMEM(paged_keys.shape if load else (1, 16, width), jnp.bfloat16),
                pltpu.SMEM((pool_pages,), jnp.int32),
                pltpu.SMEM((pool_pages,), jnp.int32),
                pltpu.SemaphoreType.DMA((3 * count + 2 * pool_pages,)),
            ],
        ),
        out_shape=out_shape,
        compiler_params=pltpu.CompilerParams(vmem_limit_bytes=VMEM_LIMIT),
        cost_estimate=BRIEF,
        name="attend",
    )(
        in_hbm(request_page_table),
        in_hbm(live_token_count),
        place,
        *map(
            in_hbm if load else in_vmem,
            (queries, fresh_keys, fresh_values, paged_keys, paged_values),
        ),
        *extra,
    )


def project(own, other, weight, weight_other, cuts, after):
    rows = own.shape[0]
    bounds = [sum(cuts[:n]) for n in range(len(cuts) + 1)]
    assert bounds[-1] * BLOCK == weight.shape[1]

    def kernel(a, b, w, u, after, *outs):
        features = jnp.concatenate([a[...], b[...]], axis=1)
        for part, out in enumerate(outs):
            for n in range(cuts[part]):
                here = slice((bounds[part] + n) * BLOCK, (bounds[part] + n + 1) * BLOCK)
                out[:, n * BLOCK : (n + 1) * BLOCK] = jnp.dot(
                    features,
                    jnp.concatenate([w[:, here], u[:, here]], axis=0),
                    preferred_element_type=jnp.float32,
                ).astype(jnp.bfloat16)

    return pl.pallas_call(
        kernel,
        in_specs=[VMEM] * 4 + [ANY],
        out_specs=[VMEM] * len(cuts),
        out_shape=[pltpu.VMEM((rows, cut * BLOCK), jnp.bfloat16) for cut in cuts],
        compiler_params=pltpu.CompilerParams(vmem_limit_bytes=VMEM_LIMIT),
        cost_estimate=BRIEF,
        name="project",
    )(in_vmem(own), in_vmem(other), in_vmem(weight), in_vmem(weight_other), after)


def pack_pair(ups, downs, place, after):
    rank, columns = ups[0].shape[1:]
    width = downs[0].shape[2]
    half = columns // 2

    def kernel(place, up_0, up_1, down_0, down_1, after, out):
        here = pl.ds(pl.multiple_of((place[0] & 1) * half, half), half)
        for n, (up, down) in enumerate(((up_0, down_0), (up_1, down_1))):
            out[n, :, :half] = up[0, :, here]
            out[n, :, half:] = down[0]

    return pl.pallas_call(
        kernel,
        in_specs=[SMEM] + [VMEM] * 4 + [ANY],
        out_specs=VMEM,
        out_shape=jax.ShapeDtypeStruct((2, rank, half + width), ups[0].dtype),
        compiler_params=pltpu.CompilerParams(vmem_limit_bytes=VMEM_LIMIT),
        cost_estimate=BRIEF,
        name="pack_pair",
    )(place, *ups, *downs, after)


def pick_factors(pairs, place, lookup, per_owner, width, after):
    rank = pairs[0].shape[1]
    half = pairs[0].shape[2] - width
    count = len(pairs)

    def kernel(place, slot, in_use, pool_row, *refs):
        pieces, outs = refs[:count], refs[-2:]
        for n, out in enumerate(outs):
            for m in range(2):
                for i in range(2):
                    request = (place[0] ^ n ^ (0 if m else 2)) * per_owner + i
                    row = pool_row[in_use[slot[request]]]
                    apart = lax.rem(place[1] // 2 - row // 2 + count, count)
                    side = (row ^ place[1]) & 1
                    for d, piece in enumerate(pieces):

                        @pl.when(apart == d)
                        def _(piece=piece, out=out, k=2 * m + i, m=m, i=i, side=side):
                            out[:, k * width : (k + 1) * width] = piece[side, :, half:]
                            if m:
                                there = 4 * width + i * half
                                out[:, there : there + half] = piece[side, :, :half]

    shape = jax.ShapeDtypeStruct((rank, 4 * width + 2 * half), pairs[0].dtype)
    return pl.pallas_call(
        kernel,
        in_specs=[SMEM] * 4 + [VMEM] * count + [ANY],
        out_specs=[VMEM] * 2,
        out_shape=[shape] * 2,
        compiler_params=pltpu.CompilerParams(vmem_limit_bytes=VMEM_LIMIT),
        cost_estimate=BRIEF,
        name="pick_factors",
    )(place, *lookup, *pairs, after)


def ranks_and_part(here, other, factors, part):
    slots, width = here[0].shape
    rows = part.shape[0]
    rank = factors[0].shape[0]
    assert part.shape[1] == 4 * slots

    def kernel(*refs):
        factors, blocks, (part_in, part_out) = refs[:2], refs[2:6], refs[6:]
        part_out[:rows] = part_in[...]
        for i in range(2):
            acts = sum(
                lax.dot_general(
                    factors[m][:, i * width : (i + 1) * width],
                    blocks[2 * m + i][...],
                    (((1,), (1,)), ((), ())),
                    preferred_element_type=jnp.float32,
                )
                for m in range(2)
            )
            high = acts.astype(jnp.bfloat16)
            low = (acts - high.astype(jnp.float32)).astype(jnp.bfloat16)
            part_out[rows:, 2 * i * slots : (2 * i + 1) * slots] = high
            part_out[rows:, (2 * i + 1) * slots : (2 * i + 2) * slots] = low

    return pl.pallas_call(
        kernel,
        in_specs=[VMEM] * 7,
        out_specs=VMEM,
        out_shape=jax.ShapeDtypeStruct((rows + rank, part.shape[1]), jnp.bfloat16),
        compiler_params=pltpu.CompilerParams(vmem_limit_bytes=VMEM_LIMIT),
        cost_estimate=BRIEF,
        name="ranks_and_part",
    )(*factors, *here, *other, part)


def prepare_own(own, other, weight, weight_other, factors, gating, place):
    rows, width = own.shape
    columns = weight.shape[1]
    slots = rows // 2
    rank = factors[0].shape[0]
    half = columns // 2

    def kernel(place, a, b, w, u, mine, theirs, gate, sums, ranks, ups, gates):
        core = place[0] & 1
        gates[...] = jnp.zeros_like(gates)
        for i in range(2):
            here = slice(i * slots, (i + 1) * slots)
            down = slice((2 + i) * width, (3 + i) * width)
            ranks[i] = sum(
                lax.dot_general(
                    factors[:, down],
                    block[here],
                    (((1,), (1,)), ((), ())),
                    preferred_element_type=jnp.float32,
                )
                for factors, block in ((mine, a), (theirs, b))
            )
            up = 4 * width + i * half
            for m in range(2):
                for away, factors in enumerate((mine, theirs)):
                    there = pl.ds(pl.multiple_of((core ^ away) * half, half), half)
                    ups[i, m * rank : (m + 1) * rank, there] = factors[:, up : up + half]
            gates[i : i + 1] = gate[pl.ds(place[0] * 2 + i, 1), :]
        features = jnp.concatenate([a[...], b[...]], axis=1)
        for n in range(columns // BLOCK):
            here = slice(n * BLOCK, (n + 1) * BLOCK)
            sums[:, here] = jnp.dot(
                features,
                jnp.concatenate([w[:, here], u[:, here]], axis=0),
                preferred_element_type=jnp.float32,
            )

    return pl.pallas_call(
        kernel,
        in_specs=[SMEM] + [VMEM] * 7,
        out_specs=[VMEM] * 4,
        out_shape=[
            pltpu.VMEM((rows, columns), jnp.float32),
            pltpu.VMEM((2, rank, slots), jnp.float32),
            pltpu.VMEM((2, 2 * rank, columns), jnp.bfloat16),
            pltpu.VMEM((8, columns), jnp.float32),
        ],
        compiler_params=pltpu.CompilerParams(vmem_limit_bytes=VMEM_LIMIT),
        cost_estimate=BRIEF,
        name="prepare_own",
    )(place, own, other, in_vmem(weight), in_vmem(weight_other), *factors, gating)


def combine(prepared, first, second, last):
    rows, columns = prepared[0].shape
    blocks = columns // BLOCK
    slots = rows // 2
    open_from = second.shape[1] // BLOCK
    open_to = (columns - last.shape[1]) // BLOCK

    def kernel(sums, ranks, ups, gates, first, second, last, out, rest_out, out_buf, sems):
        def store(i, n):
            there = (pl.ds(i * slots, slots), pl.ds(n * BLOCK, BLOCK))
            return pltpu.make_async_copy(out_buf.at[there], out.at[there], sems.at[i, n])

        for i in range(2):
            those = slice(i * slots, (i + 1) * slots)
            acts = ranks[i]
            for m in range(2 * i, 2 * i + 2):
                acts += last[slots:, m * slots : (m + 1) * slots].astype(jnp.float32)
            high = acts.astype(jnp.bfloat16).astype(jnp.float32)
            pair = jnp.concatenate([high, acts - high], axis=0).T.astype(jnp.bfloat16)
            for n in range(blocks):
                here = slice(n * BLOCK, (n + 1) * BLOCK)
                update = sums[those, here] + jnp.dot(
                    pair, ups[i, :, here], preferred_element_type=jnp.float32
                )
                if not i:
                    update += first[:, here].astype(jnp.float32)
                elif n < open_from:
                    update += second[:, here].astype(jnp.float32)
                elif n >= open_to:
                    there = slice((n - open_to) * BLOCK, (n - open_to + 1) * BLOCK)
                    update += last[:slots, there].astype(jnp.float32)
                gated = update * gates[i : i + 1, here]
                if i and open_from <= n < open_to:
                    there = slice((n - open_from) * BLOCK, (n - open_from + 1) * BLOCK)
                    rest_out[:, there] = gated
                else:
                    out_buf[those, here] = gated.astype(jnp.bfloat16)
                    store(i, n).start()
        for i in range(2):
            for n in range(blocks):
                if not (i and open_from <= n < open_to):
                    store(i, n).wait()

    return pl.pallas_call(
        kernel,
        in_specs=[VMEM] * 7,
        out_specs=[HBM, VMEM],
        out_shape=[
            pltpu.HBM((rows, columns), jnp.bfloat16),
            pltpu.VMEM((slots, (open_to - open_from) * BLOCK), jnp.float32),
        ],
        scratch_shapes=[
            pltpu.VMEM((rows, columns), jnp.bfloat16),
            pltpu.SemaphoreType.DMA((2, blocks)),
        ],
        compiler_params=pltpu.CompilerParams(vmem_limit_bytes=VMEM_LIMIT),
        cost_estimate=BRIEF,
        name="combine",
    )(*prepared, first, second, last)


def finish(so_far, rest, received, gates, begin):
    rows, columns = so_far.shape
    slots, wide = rest.shape
    widths = [part.shape[1] for part in received]
    assert sum(widths) == wide

    def kernel(sums, gates, so_far, *refs):
        parts, (out, buf, sems) = refs[:-3], refs[-3:]
        stores = []
        for n, part in enumerate(parts):
            at = sum(widths[:n])
            here = slice(at, at + widths[n])
            there = slice(begin + at, begin + at + widths[n])
            update = sums[:, here] + part[...].astype(jnp.float32) * gates[1:2, there]
            buf[:, here] = update.astype(jnp.bfloat16)
            stores.append(
                pltpu.make_async_copy(
                    buf.at[:, pl.ds(at, widths[n])],
                    out.at[pl.ds(slots, slots), pl.ds(begin + at, widths[n])],
                    sems.at[n],
                )
            )
            stores[-1].start()
        for store in stores:
            store.wait()

    return pl.pallas_call(
        kernel,
        in_specs=[VMEM] * 2 + [HBM] + [VMEM] * len(received),
        out_specs=HBM,
        out_shape=jax.ShapeDtypeStruct((rows, columns), jnp.bfloat16),
        scratch_shapes=[
            pltpu.VMEM((slots, wide), jnp.bfloat16),
            pltpu.SemaphoreType.DMA((len(received),)),
        ],
        input_output_aliases={2: 0},
        compiler_params=pltpu.CompilerParams(vmem_limit_bytes=VMEM_LIMIT),
        cost_estimate=BRIEF,
        name="finish",
    )(rest, gates, so_far, *received)


def body(
    queries,
    fresh_keys,
    fresh_values,
    paged_keys,
    paged_values,
    request_page_table,
    live_token_count,
    request_adapter_slot,
    adapters_in_use,
    adapter_pool_row,
    adapter_down_factors,
    adapter_up_factors,
    output_weight,
    gating,
):
    tp = lax.axis_size("tp")
    holders = lax.axis_size("req")
    place = jnp.stack([lax.axis_index("tp"), lax.axis_index("req")]).astype(jnp.int32)
    per_owner = live_token_count.shape[0] // tp

    def swap(array, flip):
        return lax.ppermute(array, "tp", [(s, s ^ flip) for s in range(tp)])

    def attend(tokens, wanted, load=False, after=None):
        return attend_some(
            *tokens,
            request_page_table,
            live_token_count,
            place,
            per_owner,
            wanted,
            load,
            after,
        )

    ups, downs = (
        (factors, lax.ppermute(factors, "req", [(s, s ^ 1) for s in range(holders)]))
        for factors in (adapter_up_factors, adapter_down_factors)
    )
    weight_other = swap(output_weight, 1)

    tokens = (queries, fresh_keys, fresh_values, paged_keys, paged_values)
    away_a, here_a = attend(tokens, ((3, 0), (2, 0)), True)
    *tokens, _ = lax.optimization_barrier((*tokens, away_a))
    away_a, ups, downs = lax.optimization_barrier((away_a, ups, downs))
    other_a = swap(away_a, 1)
    pair = pack_pair(ups, downs, place, away_a)
    (sent_a,) = project(here_a, other_a, output_weight, weight_other, (sum(CUTS),), pair)
    first = swap(sent_a, 2)

    pair, _ = lax.optimization_barrier((pair, sent_a))
    pairs = [pair] + [
        lax.ppermute(pair, "req", [(s, (s + d) % holders) for s in range(holders)])
        for d in range(2, holders, 2)
    ]
    away_b, here_b = attend(tokens, ((3, 1), (2, 1)), after=sent_a)
    (own_away,) = attend(tokens, ((1, 0), (1, 1)), after=away_b)
    late = pairs.pop(1)
    away_b, own_away, *pairs = lax.optimization_barrier((away_b, own_away, *pairs))
    pairs.insert(1, late)
    other_b = swap(away_b, 1)
    sent_b = project(here_b, other_b, output_weight, weight_other, CUTS, own_away)
    second = swap(sent_b[0], 2)

    first, *pairs = lax.optimization_barrier((first, *pairs))
    lookup = (request_adapter_slot, adapters_in_use, adapter_pool_row)
    width = output_weight.shape[0]
    factors, factors_away = pick_factors(pairs, place, lookup, per_owner, width, sent_b[0])
    own_away, factors_away = lax.optimization_barrier((own_away, factors_away))
    factors = (factors, swap(factors_away, 1))
    own_other = swap(own_away, 1)
    last = ranks_and_part((here_a, here_b), (other_a, other_b), factors, sent_b[-1])
    *others, first, _ = lax.optimization_barrier((*sent_b[1:-1], first, last))
    others = [swap(part, 2) for part in others]
    (own_here,) = attend(tokens, ((0, 0), (0, 1)), after=last)
    last = swap(last, 2)
    prepared = prepare_own(
        own_here, own_other, output_weight, weight_other, factors, gating, place
    )
    out, rest = combine(prepared, first, second, last)
    return finish(out, rest, others, prepared[-1], CUTS[0] * BLOCK)


def solution(mesh):
    return jax.shard_map(
        body,
        mesh=mesh,
        in_specs=(
            P("req", "tp"),
            P("req", "tp"),
            P("req", "tp"),
            P("req", None, "tp"),
            P("req", None, "tp"),
            P("req", None),
            P("req"),
            P("req"),
            P(),
            P(),
            P("req", None, "tp"),
            P("req", None, None),
            P("tp", None),
            P("req", None),
        ),
        out_specs=P(("req", "tp"), None),
        check_vma=False,
    )
```

```python
import math

import jax
import jax.numpy as jnp
from jax import lax
from jax.experimental import pallas as pl
from jax.experimental.pallas import tpu as pltpu
from jax.sharding import PartitionSpec as P

HD = 128
VMEM_LIMIT = 32 * 1024 * 1024
SMEM = pl.BlockSpec(memory_space=pltpu.SMEM)
BLOCK = 256
CUTS = (5, 2, 1, 2)
MASKED = -1e30
ANY = pl.BlockSpec(memory_space=pl.ANY)
BRIEF = pl.CostEstimate(flops=1000, bytes_accessed=1000, transcendentals=0)
HBM = pl.BlockSpec(memory_space=pltpu.HBM)
VMEM = pl.BlockSpec(memory_space=pltpu.VMEM)


def in_hbm(array):
    return pltpu.with_memory_space_constraint(array, pltpu.HBM)


def in_vmem(array):
    return pltpu.with_memory_space_constraint(array, pltpu.VMEM)


def attend_some(
    queries,
    fresh_keys,
    fresh_values,
    paged_keys,
    paged_values,
    request_page_table,
    live_token_count,
    place,
    per_owner,
    wanted,
    load,
    after=None,
):
    requests_here, pages = request_page_table.shape
    slots = queries.shape[0] // requests_here
    width = queries.shape[1]
    heads = width // HD
    pool_pages, page_rows = paged_keys.shape[:2]
    cached = pages * page_rows
    count = len(wanted)
    parts = len({away for away, _ in wanted})
    per_out = count // parts
    exponent_scale = math.log2(math.e) / math.sqrt(HD)

    def kernel(table, live, place, q_hbm, fk_hbm, fv_hbm, pk_hbm, pv_hbm, *rest):
        ids = [(place[0] ^ away) * per_owner + n for away, n in wanted]
        outs = rest[-8 - parts : -8]
        q_buf, fk_buf, fv_buf, pk_buf, pv_buf, order, seen, in_sems = rest[-8:]
        if not load:
            q_buf, fk_buf, fv_buf, pk_buf, pv_buf = q_hbm, fk_hbm, fv_hbm, pk_hbm, pv_hbm

        def fetch(src, dst, sem):
            return pltpu.make_async_copy(src, dst, in_sems.at[sem])

        def rows_of(n):
            return pl.ds(pl.multiple_of(ids[n] * slots, slots), slots)

        def query_copy(n):
            return fetch(q_hbm.at[rows_of(n)], q_buf.at[n], 3 * n)

        def key_copy(n):
            return fetch(fk_hbm.at[rows_of(n)], fk_buf.at[n], 3 * n + 1)

        def value_copy(n):
            return fetch(fv_hbm.at[rows_of(n)], fv_buf.at[n], 3 * n + 2)

        def key_page(m):
            page = order[m]
            return fetch(pk_hbm.at[page], pk_buf.at[page], 3 * count + 2 * m)

        def value_page(m):
            page = order[m]
            return fetch(pv_hbm.at[page], pv_buf.at[page], 3 * count + 2 * m + 1)

        def start(copies):
            for copy in copies:
                copy.start()

        def start_pages(begin, end):
            for m in range(pages, pool_pages):

                @pl.when((m >= begin) & (m < end))
                def _(m=m):
                    key_page(m).start()

            for m in range(pages, pool_pages):

                @pl.when((m >= begin) & (m < end))
                def _(m=m):
                    value_page(m).start()

        if load:
            for j in range(pages):
                order[j] = table[ids[0], j]
            start([query_copy(0), key_copy(0)] + [key_page(m) for m in range(pages)])
            start([value_copy(0)] + [value_page(m) for m in range(pages)])
            for page in range(pool_pages):
                taken = order[0] == page
                for j in range(1, pages):
                    taken = taken | (order[j] == page)
                seen[page] = taken.astype(jnp.int32)
            bounds = [jnp.int32(pages)]
            for n in range(1, count):
                free = bounds[-1]
                for j in range(pages):
                    page = table[ids[n], j]
                    fresh = seen[page] == 0

                    @pl.when(fresh)
                    def _(page=page, free=free):
                        order[free] = page
                        seen[page] = 1

                    free = free + fresh.astype(jnp.int32)
                bounds.append(free)
                start([query_copy(n), key_copy(n), value_copy(n)])
                start_pages(bounds[n - 1], bounds[n])
        waited = set()

        def wait(name, make, indices):
            if name not in waited:
                waited.add(name)
                for index in indices:
                    make(index).wait()

        def wait_pages(name, make, begin, end):
            if name not in waited:
                waited.add(name)
                for m in range(pages, pool_pages):

                    @pl.when((m >= begin) & (m < end))
                    def _(m=m):
                        make(m).wait()

        def keys_ready(duo):
            for n in range(1 + max(n for n, _ in duo)) if load else ():
                wait(("q", n), query_copy, [n])
                wait(("k", n), key_copy, [n])
                if n:
                    wait_pages(("k pages", n), key_page, bounds[n - 1], bounds[n])
                else:
                    wait(("k pages", 0), key_page, range(pages))

        def values_ready(duo):
            for n in range(1 + max(n for n, _ in duo)) if load else ():
                wait(("v", n), value_copy, [n])
                if n:
                    wait_pages(("v pages", n), value_page, bounds[n - 1], bounds[n])
                else:
                    wait(("v pages", 0), value_page, range(pages))

        def lanes(h, several=1):
            return slice(h * HD, (h + several) * HD)

        def own(buf, n, here):
            return buf[n, :, here] if load else buf[rows_of(n), here]

        def gather(pool, fresh, n, here):
            return jnp.concatenate(
                [pool[table[ids[n], j], :, here] for j in range(pages)] + [own(fresh, n, here)],
                axis=0,
            )

        def side_by_side(pool, fresh, duo):
            (n, h), (other_n, other_h) = duo
            if n == other_n and other_h == h + 1:
                return gather(pool, fresh, n, lanes(h, 2))
            return jnp.concatenate(
                [gather(pool, fresh, m, lanes(g)) for m, g in duo],
                axis=1,
            )

        def score(duo):
            (n, h), (other_n, other_h) = duo
            blank = jnp.zeros((slots, HD), jnp.bfloat16)
            diagonal = jnp.concatenate(
                [
                    jnp.concatenate([own(q_buf, n, lanes(h)), blank], axis=1),
                    jnp.concatenate([blank, own(q_buf, other_n, lanes(other_h))], axis=1),
                ],
                axis=0,
            )
            return lax.dot_general(
                diagonal,
                side_by_side(pk_buf, fk_buf, duo),
                (((1,), (1,)), ((), ())),
                preferred_element_type=jnp.float32,
            )

        def weigh(duo, scores):
            column = lax.broadcasted_iota(jnp.int32, (slots, slots), 1)
            usable = jnp.concatenate([column < live[ids[n]] for n, _ in duo], axis=0)
            scores = jnp.concatenate(
                [scores[:, :cached], jnp.where(usable, scores[:, cached:], MASKED)], axis=1
            )
            peak = jnp.max(scores, axis=1, keepdims=True)
            weights = jnp.exp2((scores - peak) * exponent_scale)
            return weights.astype(jnp.bfloat16), jnp.sum(weights, axis=1, keepdims=True)

        def blend(duo, weights, row_total):
            blended = jnp.dot(
                weights, side_by_side(pv_buf, fv_buf, duo), preferred_element_type=jnp.float32
            )
            row = lax.broadcasted_iota(jnp.int32, (slots, HD), 0)
            for m, (n, h) in enumerate(duo):
                rows = slice(m * slots, (m + 1) * slots)
                attended = blended[rows, lanes(m)] / row_total[rows]
                attended = jnp.where(row < live[ids[n]], attended, 0.0)
                at = (n % per_out) * slots
                outs[n // per_out][at : at + slots, lanes(h)] = attended.astype(jnp.bfloat16)

        units = []
        for first in range(0, count, 2):
            units += [((n, h), (n, h + 1)) for n in (first, first + 1) for h in range(0, heads - 1, 2)]
            if heads % 2:
                units.append(((first, heads - 1), (first + 1, heads - 1)))
        keys_ready(units[0])
        scores = score(units[0])
        weighed = None
        for u, duo in enumerate(units):
            later = None
            if u + 1 < len(units):
                keys_ready(units[u + 1])
                later = score(units[u + 1])
            if u:
                values_ready(units[u - 1])
                blend(units[u - 1], *weighed)
            weighed = weigh(duo, scores)
            scores = later
        values_ready(units[-1])
        blend(units[-1], *weighed)

    extra = () if after is None else (after,)
    out_shape = [pltpu.VMEM((per_out * slots, width), jnp.bfloat16)] * parts
    return pl.pallas_call(
        kernel,
        grid_spec=pltpu.PrefetchScalarGridSpec(
            num_scalar_prefetch=3,
            grid=(1,),
            in_specs=[HBM if load else VMEM] * 5 + [ANY] * len(extra),
            out_specs=[VMEM] * len(out_shape),
            scratch_shapes=[
                pltpu.VMEM((count if load else 1, slots, width), jnp.bfloat16),
                pltpu.VMEM((count if load else 1, slots, width), jnp.bfloat16),
                pltpu.VMEM((count if load else 1, slots, width), jnp.bfloat16),
                pltpu.VMEM(paged_keys.shape if load else (1, 16, width), jnp.bfloat16),
                pltpu.VMEM(paged_keys.shape if load else (1, 16, width), jnp.bfloat16),
                pltpu.SMEM((pool_pages,), jnp.int32),
                pltpu.SMEM((pool_pages,), jnp.int32),
                pltpu.SemaphoreType.DMA((3 * count + 2 * pool_pages,)),
            ],
        ),
        out_shape=out_shape,
        compiler_params=pltpu.CompilerParams(vmem_limit_bytes=VMEM_LIMIT),
        cost_estimate=BRIEF,
        name="attend",
    )(
        in_hbm(request_page_table),
        in_hbm(live_token_count),
        place,
        *map(
            in_hbm if load else in_vmem,
            (queries, fresh_keys, fresh_values, paged_keys, paged_values),
        ),
        *extra,
    )


def project(own, other, weight, weight_other, cuts, after):
    rows = own.shape[0]
    bounds = [sum(cuts[:n]) for n in range(len(cuts) + 1)]
    assert bounds[-1] * BLOCK == weight.shape[1]

    def kernel(a, b, w, u, after, *outs):
        features = jnp.concatenate([a[...], b[...]], axis=1)
        for part, out in enumerate(outs):
            for n in range(cuts[part]):
                here = slice((bounds[part] + n) * BLOCK, (bounds[part] + n + 1) * BLOCK)
                out[:, n * BLOCK : (n + 1) * BLOCK] = jnp.dot(
                    features,
                    jnp.concatenate([w[:, here], u[:, here]], axis=0),
                    preferred_element_type=jnp.float32,
                ).astype(jnp.bfloat16)

    return pl.pallas_call(
        kernel,
        in_specs=[VMEM] * 4 + [ANY],
        out_specs=[VMEM] * len(cuts),
        out_shape=[pltpu.VMEM((rows, cut * BLOCK), jnp.bfloat16) for cut in cuts],
        compiler_params=pltpu.CompilerParams(vmem_limit_bytes=VMEM_LIMIT),
        cost_estimate=BRIEF,
        name="project",
    )(in_vmem(own), in_vmem(other), in_vmem(weight), in_vmem(weight_other), after)


def pack_pair(ups, downs, place, after):
    rank, columns = ups[0].shape[1:]
    width = downs[0].shape[2]
    half = columns // 2

    def kernel(place, up_0, up_1, down_0, down_1, after, out):
        here = pl.ds(pl.multiple_of((place[0] & 1) * half, half), half)
        for n, (up, down) in enumerate(((up_0, down_0), (up_1, down_1))):
            out[n, :, :half] = up[0, :, here]
            out[n, :, half:] = down[0]

    return pl.pallas_call(
        kernel,
        in_specs=[SMEM] + [VMEM] * 4 + [ANY],
        out_specs=VMEM,
        out_shape=jax.ShapeDtypeStruct((2, rank, half + width), ups[0].dtype),
        compiler_params=pltpu.CompilerParams(vmem_limit_bytes=VMEM_LIMIT),
        cost_estimate=BRIEF,
        name="pack_pair",
    )(place, *ups, *downs, after)


def pick_factors(pairs, place, lookup, per_owner, width, after):
    rank = pairs[0].shape[1]
    half = pairs[0].shape[2] - width
    count = len(pairs)

    def kernel(place, slot, in_use, pool_row, *refs):
        pieces, outs = refs[:count], refs[-2:]
        for n, out in enumerate(outs):
            for m in range(2):
                for i in range(2):
                    request = (place[0] ^ n ^ (0 if m else 2)) * per_owner + i
                    row = pool_row[in_use[slot[request]]]
                    apart = lax.rem(place[1] // 2 - row // 2 + count, count)
                    side = (row ^ place[1]) & 1
                    for d, piece in enumerate(pieces):

                        @pl.when(apart == d)
                        def _(piece=piece, out=out, k=2 * m + i, m=m, i=i, side=side):
                            out[:, k * width : (k + 1) * width] = piece[side, :, half:]
                            if m:
                                there = 4 * width + i * half
                                out[:, there : there + half] = piece[side, :, :half]

    shape = jax.ShapeDtypeStruct((rank, 4 * width + 2 * half), pairs[0].dtype)
    return pl.pallas_call(
        kernel,
        in_specs=[SMEM] * 4 + [VMEM] * count + [ANY],
        out_specs=[VMEM] * 2,
        out_shape=[shape] * 2,
        compiler_params=pltpu.CompilerParams(vmem_limit_bytes=VMEM_LIMIT),
        cost_estimate=BRIEF,
        name="pick_factors",
    )(place, *lookup, *pairs, after)


def ranks_and_part(here, other, factors, part):
    slots, width = here[0].shape
    rows = part.shape[0]
    rank = factors[0].shape[0]
    assert part.shape[1] == 4 * slots

    def kernel(*refs):
        factors, blocks, (part_in, part_out) = refs[:2], refs[2:6], refs[6:]
        part_out[:rows] = part_in[...]
        for i in range(2):
            acts = sum(
                lax.dot_general(
                    factors[m][:, i * width : (i + 1) * width],
                    blocks[2 * m + i][...],
                    (((1,), (1,)), ((), ())),
                    preferred_element_type=jnp.float32,
                )
                for m in range(2)
            )
            high = acts.astype(jnp.bfloat16)
            low = (acts - high.astype(jnp.float32)).astype(jnp.bfloat16)
            part_out[rows:, 2 * i * slots : (2 * i + 1) * slots] = high
            part_out[rows:, (2 * i + 1) * slots : (2 * i + 2) * slots] = low

    return pl.pallas_call(
        kernel,
        in_specs=[VMEM] * 7,
        out_specs=VMEM,
        out_shape=jax.ShapeDtypeStruct((rows + rank, part.shape[1]), jnp.bfloat16),
        compiler_params=pltpu.CompilerParams(vmem_limit_bytes=VMEM_LIMIT),
        cost_estimate=BRIEF,
        name="ranks_and_part",
    )(*factors, *here, *other, part)


def prepare_own(own, other, weight, weight_other, factors, gating, place):
    rows, width = own.shape
    columns = weight.shape[1]
    slots = rows // 2
    rank = factors[0].shape[0]
    half = columns // 2

    def kernel(place, a, b, w, u, mine, theirs, gate, sums, ranks, ups, gates):
        core = place[0] & 1
        gates[...] = jnp.zeros_like(gates)
        for i in range(2):
            here = slice(i * slots, (i + 1) * slots)
            down = slice((2 + i) * width, (3 + i) * width)
            ranks[i] = sum(
                lax.dot_general(
                    factors[:, down],
                    block[here],
                    (((1,), (1,)), ((), ())),
                    preferred_element_type=jnp.float32,
                )
                for factors, block in ((mine, a), (theirs, b))
            )
            up = 4 * width + i * half
            for m in range(2):
                for away, factors in enumerate((mine, theirs)):
                    there = pl.ds(pl.multiple_of((core ^ away) * half, half), half)
                    ups[i, m * rank : (m + 1) * rank, there] = factors[:, up : up + half]
            gates[i : i + 1] = gate[pl.ds(place[0] * 2 + i, 1), :]
        features = jnp.concatenate([a[...], b[...]], axis=1)
        for n in range(columns // BLOCK):
            here = slice(n * BLOCK, (n + 1) * BLOCK)
            sums[:, here] = jnp.dot(
                features,
                jnp.concatenate([w[:, here], u[:, here]], axis=0),
                preferred_element_type=jnp.float32,
            )

    return pl.pallas_call(
        kernel,
        in_specs=[SMEM] + [VMEM] * 7,
        out_specs=[VMEM] * 4,
        out_shape=[
            pltpu.VMEM((rows, columns), jnp.float32),
            pltpu.VMEM((2, rank, slots), jnp.float32),
            pltpu.VMEM((2, 2 * rank, columns), jnp.bfloat16),
            pltpu.VMEM((8, columns), jnp.float32),
        ],
        compiler_params=pltpu.CompilerParams(vmem_limit_bytes=VMEM_LIMIT),
        cost_estimate=BRIEF,
        name="prepare_own",
    )(place, own, other, in_vmem(weight), in_vmem(weight_other), *factors, gating)


def combine(prepared, first, second, last):
    rows, columns = prepared[0].shape
    blocks = columns // BLOCK
    slots = rows // 2
    open_from = second.shape[1] // BLOCK
    open_to = (columns - last.shape[1]) // BLOCK

    def kernel(sums, ranks, ups, gates, first, second, last, out, rest_out, out_buf, sems):
        def store(i, n):
            there = (pl.ds(i * slots, slots), pl.ds(n * BLOCK, BLOCK))
            return pltpu.make_async_copy(out_buf.at[there], out.at[there], sems.at[i, n])

        for i in range(2):
            those = slice(i * slots, (i + 1) * slots)
            acts = ranks[i]
            for m in range(2 * i, 2 * i + 2):
                acts += last[slots:, m * slots : (m + 1) * slots].astype(jnp.float32)
            high = acts.astype(jnp.bfloat16).astype(jnp.float32)
            pair = jnp.concatenate([high, acts - high], axis=0).T.astype(jnp.bfloat16)
            for n in range(blocks):
                here = slice(n * BLOCK, (n + 1) * BLOCK)
                update = sums[those, here] + jnp.dot(
                    pair, ups[i, :, here], preferred_element_type=jnp.float32
                )
                if not i:
                    update += first[:, here].astype(jnp.float32)
                elif n < open_from:
                    update += second[:, here].astype(jnp.float32)
                elif n >= open_to:
                    there = slice((n - open_to) * BLOCK, (n - open_to + 1) * BLOCK)
                    update += last[:slots, there].astype(jnp.float32)
                gated = update * gates[i : i + 1, here]
                if i and open_from <= n < open_to:
                    there = slice((n - open_from) * BLOCK, (n - open_from + 1) * BLOCK)
                    rest_out[:, there] = gated
                else:
                    out_buf[those, here] = gated.astype(jnp.bfloat16)
                    store(i, n).start()
        for i in range(2):
            for n in range(blocks):
                if not (i and open_from <= n < open_to):
                    store(i, n).wait()

    return pl.pallas_call(
        kernel,
        in_specs=[VMEM] * 7,
        out_specs=[HBM, VMEM],
        out_shape=[
            pltpu.HBM((rows, columns), jnp.bfloat16),
            pltpu.VMEM((slots, (open_to - open_from) * BLOCK), jnp.float32),
        ],
        scratch_shapes=[
            pltpu.VMEM((rows, columns), jnp.bfloat16),
            pltpu.SemaphoreType.DMA((2, blocks)),
        ],
        compiler_params=pltpu.CompilerParams(vmem_limit_bytes=VMEM_LIMIT),
        cost_estimate=BRIEF,
        name="combine",
    )(*prepared, first, second, last)


def finish(so_far, rest, received, gates, begin):
    rows, columns = so_far.shape
    slots, wide = rest.shape
    widths = [part.shape[1] for part in received]
    assert sum(widths) == wide

    def kernel(sums, gates, so_far, *refs):
        parts, (out, buf, sems) = refs[:-3], refs[-3:]
        stores = []
        for n, part in enumerate(parts):
            at = sum(widths[:n])
            here = slice(at, at + widths[n])
            there = slice(begin + at, begin + at + widths[n])
            update = sums[:, here] + part[...].astype(jnp.float32) * gates[1:2, there]
            buf[:, here] = update.astype(jnp.bfloat16)
            stores.append(
                pltpu.make_async_copy(
                    buf.at[:, pl.ds(at, widths[n])],
                    out.at[pl.ds(slots, slots), pl.ds(begin + at, widths[n])],
                    sems.at[n],
                )
            )
            stores[-1].start()
        for store in stores:
            store.wait()

    return pl.pallas_call(
        kernel,
        in_specs=[VMEM] * 2 + [HBM] + [VMEM] * len(received),
        out_specs=HBM,
        out_shape=jax.ShapeDtypeStruct((rows, columns), jnp.bfloat16),
        scratch_shapes=[
            pltpu.VMEM((slots, wide), jnp.bfloat16),
            pltpu.SemaphoreType.DMA((len(received),)),
        ],
        input_output_aliases={2: 0},
        compiler_params=pltpu.CompilerParams(vmem_limit_bytes=VMEM_LIMIT),
        cost_estimate=BRIEF,
        name="finish",
    )(rest, gates, so_far, *received)


def body(
    queries,
    fresh_keys,
    fresh_values,
    paged_keys,
    paged_values,
    request_page_table,
    live_token_count,
    request_adapter_slot,
    adapters_in_use,
    adapter_pool_row,
    adapter_down_factors,
    adapter_up_factors,
    output_weight,
    gating,
):
    tp = lax.axis_size("tp")
    holders = lax.axis_size("req")
    place = jnp.stack([lax.axis_index("tp"), lax.axis_index("req")]).astype(jnp.int32)
    per_owner = live_token_count.shape[0] // tp

    def swap(array, flip):
        return lax.ppermute(array, "tp", [(s, s ^ flip) for s in range(tp)])

    def attend(tokens, wanted, load=False, after=None):
        return attend_some(
            *tokens,
            request_page_table,
            live_token_count,
            place,
            per_owner,
            wanted,
            load,
            after,
        )

    ups, downs = (
        (factors, lax.ppermute(factors, "req", [(s, s ^ 1) for s in range(holders)]))
        for factors in (adapter_up_factors, adapter_down_factors)
    )
    weight_other = swap(output_weight, 1)

    tokens = (queries, fresh_keys, fresh_values, paged_keys, paged_values)
    away_a, here_a = attend(tokens, ((3, 0), (2, 0)), True)
    *tokens, _ = lax.optimization_barrier((*tokens, away_a))
    away_a, ups, downs = lax.optimization_barrier((away_a, ups, downs))
    other_a = swap(away_a, 1)
    pair = pack_pair(ups, downs, place, away_a)
    (sent_a,) = project(here_a, other_a, output_weight, weight_other, (sum(CUTS),), pair)
    first = swap(sent_a, 2)

    pair, _ = lax.optimization_barrier((pair, sent_a))
    pairs = [pair] + [
        lax.ppermute(pair, "req", [(s, (s + d) % holders) for s in range(holders)])
        for d in range(2, holders, 2)
    ]
    away_b, here_b = attend(tokens, ((3, 1), (2, 1)), after=sent_a)
    (own_away,) = attend(tokens, ((1, 0), (1, 1)), after=away_b)
    late = pairs.pop(1)
    away_b, own_away, *pairs = lax.optimization_barrier((away_b, own_away, *pairs))
    pairs.insert(1, late)
    other_b = swap(away_b, 1)
    sent_b = project(here_b, other_b, output_weight, weight_other, CUTS, own_away)
    second = swap(sent_b[0], 2)
    own_away, _ = lax.optimization_barrier((own_away, sent_b[0]))
    own_other = swap(own_away, 1)

    first, *pairs = lax.optimization_barrier((first, *pairs))
    lookup = (request_adapter_slot, adapters_in_use, adapter_pool_row)
    width = output_weight.shape[0]
    factors, factors_away = pick_factors(pairs, place, lookup, per_owner, width, sent_b[0])
    factors = (factors, swap(factors_away, 1))
    last = ranks_and_part((here_a, here_b), (other_a, other_b), factors, sent_b[-1])
    *others, first, _ = lax.optimization_barrier((*sent_b[1:-1], first, last))
    others = [swap(part, 2) for part in others]
    (own_here,) = attend(tokens, ((0, 0), (0, 1)), after=last)
    last = swap(last, 2)
    prepared = prepare_own(
        own_here, own_other, output_weight, weight_other, factors, gating, place
    )
    out, rest = combine(prepared, first, second, last)
    return finish(out, rest, others, prepared[-1], CUTS[0] * BLOCK)


def solution(mesh):
    return jax.shard_map(
        body,
        mesh=mesh,
        in_specs=(
            P("req", "tp"),
            P("req", "tp"),
            P("req", "tp"),
            P("req", None, "tp"),
            P("req", None, "tp"),
            P("req", None),
            P("req"),
            P("req"),
            P(),
            P(),
            P("req", None, "tp"),
            P("req", None, None),
            P("tp", None),
            P("req", None),
        ),
        out_specs=P(("req", "tp"), None),
        check_vma=False,
    )
```

```python
import math

import jax
import jax.numpy as jnp
from jax import lax
from jax.experimental import pallas as pl
from jax.experimental.pallas import tpu as pltpu
from jax.sharding import PartitionSpec as P

HD = 128
VMEM_LIMIT = 32 * 1024 * 1024
SMEM = pl.BlockSpec(memory_space=pltpu.SMEM)
BLOCK = 256
CUTS = (5, 2, 1, 2)
MASKED = -1e30
ANY = pl.BlockSpec(memory_space=pl.ANY)
BRIEF = pl.CostEstimate(flops=1000, bytes_accessed=1000, transcendentals=0)
HBM = pl.BlockSpec(memory_space=pltpu.HBM)
VMEM = pl.BlockSpec(memory_space=pltpu.VMEM)


def in_hbm(array):
    return pltpu.with_memory_space_constraint(array, pltpu.HBM)


def in_vmem(array):
    return pltpu.with_memory_space_constraint(array, pltpu.VMEM)


def attend_some(
    queries,
    fresh_keys,
    fresh_values,
    paged_keys,
    paged_values,
    request_page_table,
    live_token_count,
    place,
    per_owner,
    wanted,
    load,
    after=None,
):
    requests_here, pages = request_page_table.shape
    slots = queries.shape[0] // requests_here
    width = queries.shape[1]
    heads = width // HD
    pool_pages, page_rows = paged_keys.shape[:2]
    cached = pages * page_rows
    count = len(wanted)
    parts = len({away for away, _ in wanted})
    per_out = count // parts
    exponent_scale = math.log2(math.e) / math.sqrt(HD)

    def kernel(table, live, place, q_hbm, fk_hbm, fv_hbm, pk_hbm, pv_hbm, *rest):
        ids = [(place[0] ^ away) * per_owner + n for away, n in wanted]
        outs = rest[-8 - parts : -8]
        q_buf, fk_buf, fv_buf, pk_buf, pv_buf, order, seen, in_sems = rest[-8:]
        if not load:
            q_buf, fk_buf, fv_buf, pk_buf, pv_buf = q_hbm, fk_hbm, fv_hbm, pk_hbm, pv_hbm

        def fetch(src, dst, sem):
            return pltpu.make_async_copy(src, dst, in_sems.at[sem])

        def rows_of(n):
            return pl.ds(pl.multiple_of(ids[n] * slots, slots), slots)

        def query_copy(n):
            return fetch(q_hbm.at[rows_of(n)], q_buf.at[n], 3 * n)

        def key_copy(n):
            return fetch(fk_hbm.at[rows_of(n)], fk_buf.at[n], 3 * n + 1)

        def value_copy(n):
            return fetch(fv_hbm.at[rows_of(n)], fv_buf.at[n], 3 * n + 2)

        def key_page(m):
            page = order[m]
            return fetch(pk_hbm.at[page], pk_buf.at[page], 3 * count + 2 * m)

        def value_page(m):
            page = order[m]
            return fetch(pv_hbm.at[page], pv_buf.at[page], 3 * count + 2 * m + 1)

        def start(copies):
            for copy in copies:
                copy.start()

        def start_pages(begin, end):
            for m in range(pages, pool_pages):

                @pl.when((m >= begin) & (m < end))
                def _(m=m):
                    key_page(m).start()

            for m in range(pages, pool_pages):

                @pl.when((m >= begin) & (m < end))
                def _(m=m):
                    value_page(m).start()

        if load:
            for j in range(pages):
                order[j] = table[ids[0], j]
            start([query_copy(0), key_copy(0)] + [key_page(m) for m in range(pages)])
            start([value_copy(0)] + [value_page(m) for m in range(pages)])
            for page in range(pool_pages):
                taken = order[0] == page
                for j in range(1, pages):
                    taken = taken | (order[j] == page)
                seen[page] = taken.astype(jnp.int32)
            bounds = [jnp.int32(pages)]
            for n in range(1, count):
                free = bounds[-1]
                for j in range(pages):
                    page = table[ids[n], j]
                    fresh = seen[page] == 0

                    @pl.when(fresh)
                    def _(page=page, free=free):
                        order[free] = page
                        seen[page] = 1

                    free = free + fresh.astype(jnp.int32)
                bounds.append(free)
                start([query_copy(n), key_copy(n), value_copy(n)])
                start_pages(bounds[n - 1], bounds[n])
        waited = set()

        def wait(name, make, indices):
            if name not in waited:
                waited.add(name)
                for index in indices:
                    make(index).wait()

        def wait_pages(name, make, begin, end):
            if name not in waited:
                waited.add(name)
                for m in range(pages, pool_pages):

                    @pl.when((m >= begin) & (m < end))
                    def _(m=m):
                        make(m).wait()

        def keys_ready(duo):
            for n in range(1 + max(n for n, _ in duo)) if load else ():
                wait(("q", n), query_copy, [n])
                wait(("k", n), key_copy, [n])
                if n:
                    wait_pages(("k pages", n), key_page, bounds[n - 1], bounds[n])
                else:
                    wait(("k pages", 0), key_page, range(pages))

        def values_ready(duo):
            for n in range(1 + max(n for n, _ in duo)) if load else ():
                wait(("v", n), value_copy, [n])
                if n:
                    wait_pages(("v pages", n), value_page, bounds[n - 1], bounds[n])
                else:
                    wait(("v pages", 0), value_page, range(pages))

        def lanes(h, several=1):
            return slice(h * HD, (h + several) * HD)

        def own(buf, n, here):
            return buf[n, :, here] if load else buf[rows_of(n), here]

        def gather(pool, fresh, n, here):
            return jnp.concatenate(
                [pool[table[ids[n], j], :, here] for j in range(pages)] + [own(fresh, n, here)],
                axis=0,
            )

        def side_by_side(pool, fresh, duo):
            (n, h), (other_n, other_h) = duo
            if n == other_n and other_h == h + 1:
                return gather(pool, fresh, n, lanes(h, 2))
            return jnp.concatenate(
                [gather(pool, fresh, m, lanes(g)) for m, g in duo],
                axis=1,
            )

        def score(duo):
            (n, h), (other_n, other_h) = duo
            blank = jnp.zeros((slots, HD), jnp.bfloat16)
            diagonal = jnp.concatenate(
                [
                    jnp.concatenate([own(q_buf, n, lanes(h)), blank], axis=1),
                    jnp.concatenate([blank, own(q_buf, other_n, lanes(other_h))], axis=1),
                ],
                axis=0,
            )
            return lax.dot_general(
                diagonal,
                side_by_side(pk_buf, fk_buf, duo),
                (((1,), (1,)), ((), ())),
                preferred_element_type=jnp.float32,
            )

        def weigh(duo, scores):
            column = lax.broadcasted_iota(jnp.int32, (slots, slots), 1)
            usable = jnp.concatenate([column < live[ids[n]] for n, _ in duo], axis=0)
            scores = jnp.concatenate(
                [scores[:, :cached], jnp.where(usable, scores[:, cached:], MASKED)], axis=1
            )
            peak = jnp.max(scores, axis=1, keepdims=True)
            weights = jnp.exp2((scores - peak) * exponent_scale)
            return weights.astype(jnp.bfloat16), jnp.sum(weights, axis=1, keepdims=True)

        def blend(duo, weights, row_total):
            blended = jnp.dot(
                weights, side_by_side(pv_buf, fv_buf, duo), preferred_element_type=jnp.float32
            )
            row = lax.broadcasted_iota(jnp.int32, (slots, HD), 0)
            for m, (n, h) in enumerate(duo):
                rows = slice(m * slots, (m + 1) * slots)
                attended = blended[rows, lanes(m)] / row_total[rows]
                attended = jnp.where(row < live[ids[n]], attended, 0.0)
                at = (n % per_out) * slots
                outs[n // per_out][at : at + slots, lanes(h)] = attended.astype(jnp.bfloat16)

        units = []
        for first in range(0, count, 2):
            units += [((n, h), (n, h + 1)) for n in (first, first + 1) for h in range(0, heads - 1, 2)]
            if heads % 2:
                units.append(((first, heads - 1), (first + 1, heads - 1)))
        keys_ready(units[0])
        scores = score(units[0])
        weighed = None
        for u, duo in enumerate(units):
            later = None
            if u + 1 < len(units):
                keys_ready(units[u + 1])
                later = score(units[u + 1])
            if u:
                values_ready(units[u - 1])
                blend(units[u - 1], *weighed)
            weighed = weigh(duo, scores)
            scores = later
        values_ready(units[-1])
        blend(units[-1], *weighed)

    extra = () if after is None else (after,)
    out_shape = [pltpu.VMEM((per_out * slots, width), jnp.bfloat16)] * parts
    return pl.pallas_call(
        kernel,
        grid_spec=pltpu.PrefetchScalarGridSpec(
            num_scalar_prefetch=3,
            grid=(1,),
            in_specs=[HBM if load else VMEM] * 5 + [ANY] * len(extra),
            out_specs=[VMEM] * len(out_shape),
            scratch_shapes=[
                pltpu.VMEM((count if load else 1, slots, width), jnp.bfloat16),
                pltpu.VMEM((count if load else 1, slots, width), jnp.bfloat16),
                pltpu.VMEM((count if load else 1, slots, width), jnp.bfloat16),
                pltpu.VMEM(paged_keys.shape if load else (1, 16, width), jnp.bfloat16),
                pltpu.VMEM(paged_keys.shape if load else (1, 16, width), jnp.bfloat16),
                pltpu.SMEM((pool_pages,), jnp.int32),
                pltpu.SMEM((pool_pages,), jnp.int32),
                pltpu.SemaphoreType.DMA((3 * count + 2 * pool_pages,)),
            ],
        ),
        out_shape=out_shape,
        compiler_params=pltpu.CompilerParams(vmem_limit_bytes=VMEM_LIMIT),
        cost_estimate=BRIEF,
        name="attend",
    )(
        in_hbm(request_page_table),
        in_hbm(live_token_count),
        place,
        *map(
            in_hbm if load else in_vmem,
            (queries, fresh_keys, fresh_values, paged_keys, paged_values),
        ),
        *extra,
    )


def project(own, other, weight, weight_other, cuts, after):
    rows = own.shape[0]
    bounds = [sum(cuts[:n]) for n in range(len(cuts) + 1)]
    assert bounds[-1] * BLOCK == weight.shape[1]

    def kernel(a, b, w, u, after, *outs):
        features = jnp.concatenate([a[...], b[...]], axis=1)
        for part, out in enumerate(outs):
            for n in range(cuts[part]):
                here = slice((bounds[part] + n) * BLOCK, (bounds[part] + n + 1) * BLOCK)
                out[:, n * BLOCK : (n + 1) * BLOCK] = jnp.dot(
                    features,
                    jnp.concatenate([w[:, here], u[:, here]], axis=0),
                    preferred_element_type=jnp.float32,
                ).astype(jnp.bfloat16)

    return pl.pallas_call(
        kernel,
        in_specs=[VMEM] * 4 + [ANY],
        out_specs=[VMEM] * len(cuts),
        out_shape=[pltpu.VMEM((rows, cut * BLOCK), jnp.bfloat16) for cut in cuts],
        compiler_params=pltpu.CompilerParams(vmem_limit_bytes=VMEM_LIMIT),
        cost_estimate=BRIEF,
        name="project",
    )(in_vmem(own), in_vmem(other), in_vmem(weight), in_vmem(weight_other), after)


def pack_pair(ups, downs, place, after):
    rank, columns = ups[0].shape[1:]
    width = downs[0].shape[2]
    half = columns // 2

    def kernel(place, up_0, up_1, down_0, down_1, after, out):
        here = pl.ds(pl.multiple_of((place[0] & 1) * half, half), half)
        for n, (up, down) in enumerate(((up_0, down_0), (up_1, down_1))):
            out[n, :, :half] = up[0, :, here]
            out[n, :, half:] = down[0]

    return pl.pallas_call(
        kernel,
        in_specs=[SMEM] + [VMEM] * 4 + [ANY],
        out_specs=VMEM,
        out_shape=jax.ShapeDtypeStruct((2, rank, half + width), ups[0].dtype),
        compiler_params=pltpu.CompilerParams(vmem_limit_bytes=VMEM_LIMIT),
        cost_estimate=BRIEF,
        name="pack_pair",
    )(place, *ups, *downs, after)


def pick_factors(pairs, place, lookup, per_owner, width, after):
    rank = pairs[0].shape[1]
    half = pairs[0].shape[2] - width
    count = len(pairs)

    def kernel(place, slot, in_use, pool_row, *refs):
        pieces, outs = refs[:count], refs[-2:]
        for n, out in enumerate(outs):
            for m in range(2):
                for i in range(2):
                    request = (place[0] ^ n ^ (0 if m else 2)) * per_owner + i
                    row = pool_row[in_use[slot[request]]]
                    apart = lax.rem(place[1] // 2 - row // 2 + count, count)
                    side = (row ^ place[1]) & 1
                    for d, piece in enumerate(pieces):

                        @pl.when(apart == d)
                        def _(piece=piece, out=out, k=2 * m + i, m=m, i=i, side=side):
                            out[:, k * width : (k + 1) * width] = piece[side, :, half:]
                            if m:
                                there = 4 * width + i * half
                                out[:, there : there + half] = piece[side, :, :half]

    shape = jax.ShapeDtypeStruct((rank, 4 * width + 2 * half), pairs[0].dtype)
    return pl.pallas_call(
        kernel,
        in_specs=[SMEM] * 4 + [VMEM] * count + [ANY],
        out_specs=[VMEM] * 2,
        out_shape=[shape] * 2,
        compiler_params=pltpu.CompilerParams(vmem_limit_bytes=VMEM_LIMIT),
        cost_estimate=BRIEF,
        name="pick_factors",
    )(place, *lookup, *pairs, after)


def ranks_and_part(here, other, factors, part):
    slots, width = here[0].shape
    rows = part.shape[0]
    rank = factors[0].shape[0]
    assert part.shape[1] == 4 * slots

    def kernel(*refs):
        factors, blocks, (part_in, part_out) = refs[:2], refs[2:6], refs[6:]
        part_out[:rows] = part_in[...]
        for i in range(2):
            acts = sum(
                lax.dot_general(
                    factors[m][:, i * width : (i + 1) * width],
                    blocks[2 * m + i][...],
                    (((1,), (1,)), ((), ())),
                    preferred_element_type=jnp.float32,
                )
                for m in range(2)
            )
            high = acts.astype(jnp.bfloat16)
            low = (acts - high.astype(jnp.float32)).astype(jnp.bfloat16)
            part_out[rows:, 2 * i * slots : (2 * i + 1) * slots] = high
            part_out[rows:, (2 * i + 1) * slots : (2 * i + 2) * slots] = low

    return pl.pallas_call(
        kernel,
        in_specs=[VMEM] * 7,
        out_specs=VMEM,
        out_shape=jax.ShapeDtypeStruct((rows + rank, part.shape[1]), jnp.bfloat16),
        compiler_params=pltpu.CompilerParams(vmem_limit_bytes=VMEM_LIMIT),
        cost_estimate=BRIEF,
        name="ranks_and_part",
    )(*factors, *here, *other, part)


def prepare_own(own, other, weight, weight_other, factors, gating, place):
    rows, width = own.shape
    columns = weight.shape[1]
    slots = rows // 2
    rank = factors[0].shape[0]
    half = columns // 2

    def kernel(place, a, b, w, u, mine, theirs, gate, sums, ranks, ups, gates):
        core = place[0] & 1
        gates[...] = jnp.zeros_like(gates)
        for i in range(2):
            here = slice(i * slots, (i + 1) * slots)
            down = slice((2 + i) * width, (3 + i) * width)
            ranks[i] = sum(
                lax.dot_general(
                    factors[:, down],
                    block[here],
                    (((1,), (1,)), ((), ())),
                    preferred_element_type=jnp.float32,
                )
                for factors, block in ((mine, a), (theirs, b))
            )
            up = 4 * width + i * half
            for m in range(2):
                for away, factors in enumerate((mine, theirs)):
                    there = pl.ds(pl.multiple_of((core ^ away) * half, half), half)
                    ups[i, m * rank : (m + 1) * rank, there] = factors[:, up : up + half]
            gates[i : i + 1] = gate[pl.ds(place[0] * 2 + i, 1), :]
        features = jnp.concatenate([a[...], b[...]], axis=1)
        for n in range(columns // BLOCK):
            here = slice(n * BLOCK, (n + 1) * BLOCK)
            sums[:, here] = jnp.dot(
                features,
                jnp.concatenate([w[:, here], u[:, here]], axis=0),
                preferred_element_type=jnp.float32,
            )

    return pl.pallas_call(
        kernel,
        in_specs=[SMEM] + [VMEM] * 7,
        out_specs=[VMEM] * 4,
        out_shape=[
            pltpu.VMEM((rows, columns), jnp.float32),
            pltpu.VMEM((2, rank, slots), jnp.float32),
            pltpu.VMEM((2, 2 * rank, columns), jnp.bfloat16),
            pltpu.VMEM((8, columns), jnp.float32),
        ],
        compiler_params=pltpu.CompilerParams(vmem_limit_bytes=VMEM_LIMIT),
        cost_estimate=BRIEF,
        name="prepare_own",
    )(place, own, other, in_vmem(weight), in_vmem(weight_other), *factors, gating)


def combine(prepared, first, second, last):
    rows, columns = prepared[0].shape
    blocks = columns // BLOCK
    slots = rows // 2
    open_from = second.shape[1] // BLOCK
    open_to = (columns - last.shape[1]) // BLOCK

    def kernel(sums, ranks, ups, gates, first, second, last, out, rest_out, out_buf, sems):
        def store(i, n):
            there = (pl.ds(i * slots, slots), pl.ds(n * BLOCK, BLOCK))
            return pltpu.make_async_copy(out_buf.at[there], out.at[there], sems.at[i, n])

        for i in range(2):
            those = slice(i * slots, (i + 1) * slots)
            acts = ranks[i]
            for m in range(2 * i, 2 * i + 2):
                acts += last[slots:, m * slots : (m + 1) * slots].astype(jnp.float32)
            high = acts.astype(jnp.bfloat16).astype(jnp.float32)
            pair = jnp.concatenate([high, acts - high], axis=0).T.astype(jnp.bfloat16)
            for n in range(blocks):
                here = slice(n * BLOCK, (n + 1) * BLOCK)
                update = sums[those, here] + jnp.dot(
                    pair, ups[i, :, here], preferred_element_type=jnp.float32
                )
                if not i:
                    update += first[:, here].astype(jnp.float32)
                elif n < open_from:
                    update += second[:, here].astype(jnp.float32)
                elif n >= open_to:
                    there = slice((n - open_to) * BLOCK, (n - open_to + 1) * BLOCK)
                    update += last[:slots, there].astype(jnp.float32)
                gated = update * gates[i : i + 1, here]
                if i and open_from <= n < open_to:
                    there = slice((n - open_from) * BLOCK, (n - open_from + 1) * BLOCK)
                    rest_out[:, there] = gated
                else:
                    out_buf[those, here] = gated.astype(jnp.bfloat16)
                    store(i, n).start()
        for i in range(2):
            for n in range(blocks):
                if not (i and open_from <= n < open_to):
                    store(i, n).wait()

    return pl.pallas_call(
        kernel,
        in_specs=[VMEM] * 7,
        out_specs=[HBM, VMEM],
        out_shape=[
            pltpu.HBM((rows, columns), jnp.bfloat16),
            pltpu.VMEM((slots, (open_to - open_from) * BLOCK), jnp.float32),
        ],
        scratch_shapes=[
            pltpu.VMEM((rows, columns), jnp.bfloat16),
            pltpu.SemaphoreType.DMA((2, blocks)),
        ],
        compiler_params=pltpu.CompilerParams(vmem_limit_bytes=VMEM_LIMIT),
        cost_estimate=BRIEF,
        name="combine",
    )(*prepared, first, second, last)


def finish(so_far, rest, received, gates, begin):
    rows, columns = so_far.shape
    slots, wide = rest.shape
    widths = [part.shape[1] for part in received]
    assert sum(widths) == wide

    def kernel(sums, gates, so_far, *refs):
        parts, (out, buf, sems) = refs[:-3], refs[-3:]
        stores = []
        for n, part in enumerate(parts):
            at = sum(widths[:n])
            here = slice(at, at + widths[n])
            there = slice(begin + at, begin + at + widths[n])
            update = sums[:, here] + part[...].astype(jnp.float32) * gates[1:2, there]
            buf[:, here] = update.astype(jnp.bfloat16)
            stores.append(
                pltpu.make_async_copy(
                    buf.at[:, pl.ds(at, widths[n])],
                    out.at[pl.ds(slots, slots), pl.ds(begin + at, widths[n])],
                    sems.at[n],
                )
            )
            stores[-1].start()
        for store in stores:
            store.wait()

    return pl.pallas_call(
        kernel,
        in_specs=[VMEM] * 2 + [HBM] + [VMEM] * len(received),
        out_specs=HBM,
        out_shape=jax.ShapeDtypeStruct((rows, columns), jnp.bfloat16),
        scratch_shapes=[
            pltpu.VMEM((slots, wide), jnp.bfloat16),
            pltpu.SemaphoreType.DMA((len(received),)),
        ],
        input_output_aliases={2: 0},
        compiler_params=pltpu.CompilerParams(vmem_limit_bytes=VMEM_LIMIT),
        cost_estimate=BRIEF,
        name="finish",
    )(rest, gates, so_far, *received)


def body(
    queries,
    fresh_keys,
    fresh_values,
    paged_keys,
    paged_values,
    request_page_table,
    live_token_count,
    request_adapter_slot,
    adapters_in_use,
    adapter_pool_row,
    adapter_down_factors,
    adapter_up_factors,
    output_weight,
    gating,
):
    tp = lax.axis_size("tp")
    holders = lax.axis_size("req")
    place = jnp.stack([lax.axis_index("tp"), lax.axis_index("req")]).astype(jnp.int32)
    per_owner = live_token_count.shape[0] // tp

    def swap(array, flip):
        return lax.ppermute(array, "tp", [(s, s ^ flip) for s in range(tp)])

    def attend(tokens, wanted, load=False, after=None):
        return attend_some(
            *tokens,
            request_page_table,
            live_token_count,
            place,
            per_owner,
            wanted,
            load,
            after,
        )

    ups, downs = (
        (factors, lax.ppermute(factors, "req", [(s, s ^ 1) for s in range(holders)]))
        for factors in (adapter_up_factors, adapter_down_factors)
    )
    weight_other = swap(output_weight, 1)

    tokens = (queries, fresh_keys, fresh_values, paged_keys, paged_values)
    away_a, here_a = attend(tokens, ((3, 0), (2, 0)), True)
    *tokens, _ = lax.optimization_barrier((*tokens, away_a))
    away_a, ups, downs = lax.optimization_barrier((away_a, ups, downs))
    other_a = swap(away_a, 1)
    pair = pack_pair(ups, downs, place, away_a)
    (sent_a,) = project(here_a, other_a, output_weight, weight_other, (sum(CUTS),), pair)
    first = swap(sent_a, 2)

    pair, _ = lax.optimization_barrier((pair, sent_a))
    pairs = [pair] + [
        lax.ppermute(pair, "req", [(s, (s + d) % holders) for s in range(holders)])
        for d in range(2, holders, 2)
    ]
    away_b, here_b = attend(tokens, ((3, 1), (2, 1)), after=sent_a)
    (own_away,) = attend(tokens, ((1, 0), (1, 1)), after=away_b)
    late = pairs.pop(1)
    away_b, own_away, *pairs = lax.optimization_barrier((away_b, own_away, *pairs))
    pairs.insert(1, late)
    other_b = swap(away_b, 1)
    sent_b = project(here_b, other_b, output_weight, weight_other, CUTS, own_away)
    second = swap(sent_b[0], 2)
    own_away, _ = lax.optimization_barrier((own_away, sent_b[0]))
    own_other = swap(own_away, 1)

    (own_here,) = attend(tokens, ((0, 0), (0, 1)), after=sent_b[0])
    first, *pairs = lax.optimization_barrier((first, *pairs))
    lookup = (request_adapter_slot, adapters_in_use, adapter_pool_row)
    width = output_weight.shape[0]
    factors, factors_away = pick_factors(pairs, place, lookup, per_owner, width, own_here)
    factors = (factors, swap(factors_away, 1))
    last = ranks_and_part((here_a, here_b), (other_a, other_b), factors, sent_b[-1])
    *others, first, _ = lax.optimization_barrier((*sent_b[1:-1], first, last))
    others = [swap(part, 2) for part in others]
    last = swap(last, 2)
    prepared = prepare_own(
        own_here, own_other, output_weight, weight_other, factors, gating, place
    )
    out, rest = combine(prepared, first, second, last)
    return finish(out, rest, others, prepared[-1], CUTS[0] * BLOCK)


def solution(mesh):
    return jax.shard_map(
        body,
        mesh=mesh,
        in_specs=(
            P("req", "tp"),
            P("req", "tp"),
            P("req", "tp"),
            P("req", None, "tp"),
            P("req", None, "tp"),
            P("req", None),
            P("req"),
            P("req"),
            P(),
            P(),
            P("req", None, "tp"),
            P("req", None, None),
            P("tp", None),
            P("req", None),
        ),
        out_specs=P(("req", "tp"), None),
        check_vma=False,
    )
```
